32 devices in a mesh: dp: 8 (over y, x, core), seq: 4 (over z).
Axes of the slice: x: 2, y: 2, z: 4, core: 2. Of those that a mesh axis runs over, the one named last changes fastest.
Arguments:
- inputs: bfloat16 [16, 1024, 1024], P('dp', 'seq'), may hold values from -6 to 6
- out_grad: bfloat16 [16, 1024, 1024], P('dp', 'seq'), may hold values from -6 to 6
- norm_gain: float32 [2, 1024], replicated, may hold values from 0.3 to 2.4, as said below
- norm_bias: float32 [2, 1024], replicated, may hold values from -1.25 to 1.25
- proj_bias: float32 [4, 1024], replicated, may hold values from -1.25 to 1.25
- fc_bias: float32 [4096], replicated, may hold values from -1.25 to 1.25
- qkv_weight: bfloat16 [1024, 3072], P('dp'), may hold values from -0.1875 to 0.1875
- out_weight: bfloat16 [1024, 1024], P('dp'), may hold values from -2 to 2
- feed_input_weight: bfloat16 [1024, 4096], P('dp'), may hold values from -0.1875 to 0.1875
- proj_weight: bfloat16 [4096, 1024], P('dp'), may hold values from -0.09375 to 0.09375
- adapters: float32 [4, 4, 1024], replicated, may hold values from -0.1875 to 0.1875
- first_moment: float32 [4, 4, 1024], replicated, may hold values from -0.0048828125 to 0.0048828125
- second_moment: float32 [4, 4, 1024], replicated, may hold values from 6.103516e-08 to 2.4414064e-07
Outputs:
- mixed: bfloat16 [16, 1024, 1024], P('dp', 'seq')
- grad_in: bfloat16 [16, 1024, 1024], P('dp', 'seq')
- adapter_grad: float32 [4, 4, 1024], replicated
- grad_norm: float32 [], replicated
- new_adapters: float32 [4, 4, 1024], replicated
- new_first: float32 [4, 4, 1024], replicated
- new_second: float32 [4, 4, 1024], replicated
The draws below stay inside these ranges and needn't reach their ends.
Inputs may be any that keep to these rules, and one draw needn't show every extreme that they name: `norm_gain`: positive gains of the two layer norms.
All inputs are finite; a program needn't handle non-finite values.
Results may differ from the reference program's by a relative error of at most 0.013.
Values may be sent and summed in bfloat16 or wider, within the bound.
No kernel may reach another device: no remote copies, remote signals or barrier semaphores. Data moves between devices by JAX's collectives and lax.ppermute only.
A program may use at most 192 MiB of HBM per device.

```python
import math
import jax
import jax.numpy as jnp
from jax import lax

D = 1024
HEADS = 16
HEAD_DIM = 64
FF = 4096
ADAPTER_RANK = 4
STEP = 10
LEN = 1024
DOCS = 16


def draw_norm_gain(key, part):
    key = jax.random.fold_in(key, 11)
    place = jnp.arange(D, dtype=jnp.float32) / D
    rising = 0.5 + place
    noise = jax.random.uniform(key, (2, D), jnp.float32, 0.85, 1.15)
    return (rising[None, :] * noise).astype(jnp.float32)


def shard_levels(key, extent, pieces, low, largest):
    def one(axis_at, shards_of):
        heights = jax.random.uniform(jax.random.fold_in(jax.random.fold_in(key, 6), axis_at), (shards_of,), jnp.float32, low / len(pieces), largest / len(pieces))
        return jnp.repeat(jnp.exp(heights), extent[axis_at] // shards_of).reshape((-1,) + (1,) * (len(extent) - axis_at - 1))

    level = one(*pieces[0])
    for cut in pieces[1:]:
        level = level * one(*cut)
    return level


def scatter_about(key, shape, scale, most, pieces=(), kind=jnp.bfloat16):
    entries = jax.random.normal(key, shape, jnp.float32) * scale
    if len(pieces) > 0:
        entries = shard_levels(key, shape, pieces, -0.22, 0.18) * entries
    return jnp.clip(entries, min=-most, max=most).astype(kind)


def setup_inputs(seed: int = 0) -> dict:
    splits = jax.random.split(jax.random.key(seed), 14)
    return {
        "inputs": scatter_about(splits[0], (DOCS, LEN, D), 1.0, 6.0, ((0, 8), (1, 4))),
        "out_grad": scatter_about(splits[1], (DOCS, LEN, D), 1.0, 6.0, ((0, 8), (1, 4))),
        "norm_gain": draw_norm_gain(jax.random.fold_in(splits[13], 71), 0),
        "norm_bias": scatter_about(splits[3], (2, D), 0.2, 1.25, (), jnp.float32),
        "proj_bias": scatter_about(splits[4], (4, D), 0.2, 1.25, (), jnp.float32),
        "fc_bias": scatter_about(splits[5], (FF,), 0.2, 1.25, (), jnp.float32),
        "qkv_weight": scatter_about(splits[6], (D, 3 * D), D ** -0.5, 0.1875, ((0, 8),)),
        "out_weight": scatter_about(splits[7], (D, D), (D * 8 // LEN) ** -0.5, 2.0, ((0, 8),)),
        "feed_input_weight": scatter_about(splits[8], (D, FF), D ** -0.5, 0.1875, ((0, 8),)),
        "proj_weight": scatter_about(splits[9], (FF, D), FF ** -0.5, 0.09375, ((0, 8),)),
        "adapters": scatter_about(splits[10], (4, ADAPTER_RANK, D), 0.03, 0.1875, (), jnp.float32),
        "first_moment": scatter_about(splits[11], (4, ADAPTER_RANK, D), (0.111 / (4 * ADAPTER_RANK * D) ** 0.5), 0.0048828125, (), jnp.float32),
        "second_moment": jnp.clip(jnp.exp(jax.random.uniform(splits[12], (4, ADAPTER_RANK, D), jnp.float32, math.log(6.103515914901436e-08), math.log(2.4414063659605745e-07))), 6.103515914901436e-08, 2.4414063659605745e-07),
    }


@jax.custom_vjp
def low(v):
    return lax.optimization_barrier(v.astype(jnp.bfloat16)).astype(jnp.float32)

@jax.custom_vjp
def low_back(v):
    return v

def low_keep(v):
    return (low(v), None)

def low_pass(kept, grad):
    return (grad,)

def back_keep(v):
    return (v, None)

def back_low(kept, grad):
    return (low(grad),)
low.defvjp(low_keep, low_pass)
low_back.defvjp(back_keep, back_low)
highest = lax.Precision.HIGHEST
adapter_alpha = 32.0
beta_one = 0.9
beta_two = 0.999
adam_eps = 1e-08
decay_rate = 0.01
learning_rate = 0.02
clip_bound = 1.0
norm_eps = 1e-05

def layer_norm(value, gain, shift):
    center = lax.optimization_barrier(jnp.mean(value, axis=-1, keepdims=True))
    centered = value - center
    spread = lax.optimization_barrier(jnp.mean(centered * centered, axis=-1, keepdims=True))
    return centered * lax.rsqrt(spread + norm_eps) * gain + shift

def matmul(left, right):
    return jnp.dot(left, right, precision=highest)

def attend(packed):
    query = packed[:, 0]
    keys = packed[:, 1]
    values = packed[:, 2]
    scale = 1.0 / math.sqrt(HEAD_DIM)
    scores = low_back(jnp.einsum('qhd,khd->hqk', query, keys, precision=highest) * scale)
    position = jnp.arange(LEN)
    causal = position[None, :, None] >= position[None, None, :]
    masked = jnp.where(causal, scores, -1e+30)
    summit = lax.optimization_barrier(jnp.max(masked, axis=-1, keepdims=True))
    expo = jnp.where(causal, jnp.exp(masked - summit), 0.0)
    probs = low(expo / lax.optimization_barrier(jnp.sum(expo, axis=-1, keepdims=True)))
    context = jnp.einsum('hqk,khd->qhd', probs, values, precision=highest)
    return low(low_back(context))

def block(inputs, adapters, frozen):
    gains, shifts, bias_terms, fc_bias, qkv_w, out_w, fc_w, proj_w = frozen
    group, length, width = inputs.shape
    flat = inputs.reshape(group * length, width)
    normed = layer_norm(flat, gains[0], shifts[0])
    base = matmul(low(normed), qkv_w)
    scale_factor = adapter_alpha / ADAPTER_RANK
    down_q = matmul(normed, adapters[0].T)
    down_v = matmul(normed, adapters[2].T)
    query = base[:, :width] + bias_terms[0] + scale_factor * matmul(down_q, adapters[1])
    keys = base[:, width:2 * width]
    values = base[:, 2 * width:] + bias_terms[1] + scale_factor * matmul(down_v, adapters[3])
    joined = low(low_back(jnp.concatenate([query, keys, values], axis=1)))
    joined = joined.reshape(group, length, 3, HEADS, HEAD_DIM)
    context = lax.map(jax.checkpoint(attend), joined).reshape(group * length, width)
    attn = low_back(matmul(context, out_w) + bias_terms[2])
    middle = flat + attn
    normed_two = layer_norm(middle, gains[1], shifts[1])
    hidden = low_back(matmul(low(normed_two), fc_w) + fc_bias)
    active = low(jax.nn.gelu(hidden, approximate=True))
    result = middle + matmul(active, proj_w) + bias_terms[3]
    return result.reshape(group, length, width)

def adam_update(grad, weight, first, second, norm):
    scale_factor = clip_bound / jnp.maximum(norm, clip_bound)
    clipped = grad * scale_factor
    new_first = beta_one * first + (1.0 - beta_one) * clipped
    new_second = beta_two * second + (1.0 - beta_two) * clipped * clipped
    first_hat = new_first / (1.0 - beta_one ** STEP)
    second_hat = new_second / (1.0 - beta_two ** STEP)
    new_weight = weight - learning_rate * (first_hat / (jnp.sqrt(second_hat) + adam_eps) + decay_rate * weight)
    return (clipped, new_weight, new_first, new_second)

def reference(inputs, out_grad, norm_gain, norm_bias, proj_bias, fc_bias, qkv_weight, out_weight, feed_input_weight, proj_weight, adapters, first_moment, second_moment):
    frozen = (norm_gain, norm_bias, proj_bias, fc_bias, qkv_weight.astype(jnp.float32), out_weight.astype(jnp.float32), feed_input_weight.astype(jnp.float32), proj_weight.astype(jnp.float32))
    group = math.gcd(DOCS, max(1, 4096 // LEN))
    groups = DOCS // group
    input_groups = inputs.astype(jnp.float32).reshape(groups, group, LEN, D)
    grad_groups = out_grad.astype(jnp.float32).reshape(groups, group, LEN, D)

    def visit(total, pair):
        input_part, grad_part = pair
        result, backward = jax.vjp(lambda first, second: block(first, second, frozen), input_part, adapters)
        grad_input, grad_adapters = backward(grad_part)
        return (total + grad_adapters, (result.astype(jnp.bfloat16), grad_input.astype(jnp.bfloat16)))
    total, (mixed, grad_in) = lax.scan(visit, jnp.zeros(adapters.shape, adapters.dtype), (input_groups, grad_groups))
    grad_norm = jnp.sqrt(jnp.sum(total * total))
    clipped, new_adapters, new_first, new_second = adam_update(total, adapters, first_moment, second_moment, grad_norm)
    return (mixed.reshape(DOCS, LEN, D), grad_in.reshape(DOCS, LEN, D), clipped, grad_norm, new_adapters, new_first, new_second)
```

```python
import functools
import math

import jax
import jax.numpy as jnp
from jax import lax
from jax.experimental import pallas as pl
from jax.experimental.pallas import tpu as pltpu
from jax.sharding import Mesh
from jax.sharding import PartitionSpec as P

HEAD_DIM = 64
ADAPTER_RANK = 4
STEP = 10


highest = lax.Precision.HIGHEST
adapter_alpha = 32.0
beta_one = 0.9
beta_two = 0.999
adam_eps = 1e-08
decay_rate = 0.01
learning_rate = 0.02
clip_bound = 1.0
norm_eps = 1e-05


def layer_norm(value, gain, shift):
    center = jnp.mean(value, axis=-1, keepdims=True)
    centered = value - center
    spread = jnp.mean(centered * centered, axis=-1, keepdims=True)
    return centered * lax.rsqrt(spread + norm_eps) * gain + shift


def dot_trans(left, right):
    return lax.dot_general(
        left, right, (((1,), (1,)), ((), ())), preferred_element_type=jnp.float32
    )


def dot_first(left, right):
    return lax.dot_general(
        left, right, (((0,), (0,)), ((), ())), precision=highest, preferred_element_type=jnp.float32
    )


def adam_update(grad, weight, first, second, norm):
    scale_factor = clip_bound / jnp.maximum(norm, clip_bound)
    clipped = grad * scale_factor
    new_first = beta_one * first + (1.0 - beta_one) * clipped
    new_second = beta_two * second + (1.0 - beta_two) * clipped * clipped
    first_hat = new_first / (1.0 - beta_one**STEP)
    second_hat = new_second / (1.0 - beta_two**STEP)
    new_weight = weight - learning_rate * (
        first_hat / (jnp.sqrt(second_hat) + adam_eps) + decay_rate * weight
    )
    return (clipped, new_weight, new_first, new_second)


def split_heads(packed):
    length = packed.shape[0]
    local_heads = packed.shape[-1] // HEAD_DIM
    query = packed[:, 0, 0].reshape(length, local_heads, HEAD_DIM)
    keys = packed[:, 1, 0].reshape(length, local_heads, HEAD_DIM)
    values = packed[:, 2, 0].reshape(length, local_heads, HEAD_DIM)
    return (query, keys, values)


def doc_forward(packed):
    length = packed.shape[0]
    local_width = packed.shape[-1]
    query, keys, values = split_heads(packed)
    local_heads = query.shape[1]
    span = min(512, length)
    blocks = length // span
    scale = 1.0 / math.sqrt(HEAD_DIM)
    starts = jnp.arange(blocks, dtype=jnp.int32) * span

    def visit(pieces):
        query_block, start = pieces
        scores = (
            jnp.einsum("qhd,khd->hqk", query_block, keys, preferred_element_type=jnp.float32)
            * scale
        )
        causal = (start + jnp.arange(span))[:, None] >= jnp.arange(length)[None, :]
        masked = jnp.where(causal[None], scores, -1e30)
        summit = jnp.max(masked, axis=-1, keepdims=True)
        expo = jnp.where(causal[None], jnp.exp(masked - summit), 0.0)
        totals = jnp.sum(expo, axis=-1, keepdims=True)
        weights = (expo / totals).astype(jnp.bfloat16)
        context = jnp.einsum(
            "hqk,khd->qhd", weights, values, preferred_element_type=jnp.float32
        ).astype(jnp.bfloat16)
        return (context, summit[..., 0] + jnp.log(totals[..., 0]))

    context, log_total = lax.map(
        visit, (query.reshape(blocks, span, local_heads, HEAD_DIM), starts)
    )
    return (context.reshape(length, 1, local_width), log_total)


def doc_backward(args):
    packed, grad_context, log_total = args
    length = packed.shape[0]
    local_width = packed.shape[-1]
    query, keys, values = split_heads(packed)
    local_heads = query.shape[1]
    output_gradient = grad_context[:, 0].reshape(length, local_heads, HEAD_DIM)
    span = min(512, length)
    blocks = length // span
    scale = 1.0 / math.sqrt(HEAD_DIM)
    starts = jnp.arange(blocks, dtype=jnp.int32) * span

    def visit(carry, pieces):
        grad_keys, grad_values = carry
        query_block, grad_block, total_block, start = pieces
        scores = (
            jnp.einsum("qhd,khd->hqk", query_block, keys, preferred_element_type=jnp.float32)
            * scale
        )
        causal = (start + jnp.arange(span))[:, None] >= jnp.arange(length)[None, :]
        masked = jnp.where(causal[None], scores, -1e30)
        probs = jnp.where(causal[None], jnp.exp(masked - total_block[:, :, None]), 0.0)
        weights = probs.astype(jnp.bfloat16)
        grad_probs = jnp.einsum(
            "qhd,khd->hqk", grad_block, values, preferred_element_type=jnp.float32
        )
        inner = jnp.sum(probs * grad_probs, axis=-1, keepdims=True)
        grad_scores = (probs * (grad_probs - inner)).astype(jnp.bfloat16)
        grad_query = (
            jnp.einsum("hqk,khd->qhd", grad_scores, keys, preferred_element_type=jnp.float32)
            * scale
        )
        grad_keys = (
            grad_keys
            + jnp.einsum(
                "hqk,qhd->khd", grad_scores, query_block, preferred_element_type=jnp.float32
            )
            * scale
        )
        grad_values = grad_values + jnp.einsum(
            "hqk,qhd->khd", weights, grad_block, preferred_element_type=jnp.float32
        )
        return ((grad_keys, grad_values), grad_query)

    empty = jnp.zeros((length, local_heads, HEAD_DIM), jnp.float32)
    pieces = (
        query.reshape(blocks, span, local_heads, HEAD_DIM),
        output_gradient.reshape(blocks, span, local_heads, HEAD_DIM),
        log_total,
        starts,
    )
    (grad_keys, grad_values), grad_query = lax.scan(visit, (empty, empty), pieces)
    joined = jnp.stack(
        [
            grad_query.reshape(length, local_width),
            grad_keys.reshape(length, local_width),
            grad_values.reshape(length, local_width),
        ],
        axis=1,
    )
    return joined.astype(jnp.bfloat16)[:, :, None, :]


def on_device(
    inputs,
    out_grad,
    norm_gain,
    norm_bias,
    proj_bias,
    fc_bias,
    qkv_weight,
    out_weight,
    feed_input_weight,
    proj_weight,
    adapters,
    first_moment,
    second_moment,
):
    docs, tokens, width = inputs.shape
    count = docs * tokens
    ranks = lax.axis_size("seq")
    scale_factor = adapter_alpha / ADAPTER_RANK

    def forward(stack):
        qkv_full, out_full, fc_full, proj_full = stack
        flat = inputs.reshape(count, width).astype(jnp.float32)
        normed, norm_one_back = jax.vjp(
            lambda value: layer_norm(value, norm_gain[0], norm_bias[0]), flat
        )
        base = jnp.dot(normed.astype(jnp.bfloat16), qkv_full, preferred_element_type=jnp.float32)
        down_q = jnp.dot(normed, adapters[0].T, precision=highest)
        down_v = jnp.dot(normed, adapters[2].T, precision=highest)
        query = (
            base[:, :width]
            + proj_bias[0]
            + scale_factor * jnp.dot(down_q, adapters[1], precision=highest)
        )
        keys = base[:, width : 2 * width]
        values = (
            base[:, 2 * width :]
            + proj_bias[1]
            + scale_factor * jnp.dot(down_v, adapters[3], precision=highest)
        )
        joined = (
            jnp.concatenate([query, keys, values], axis=1)
            .astype(jnp.bfloat16)
            .reshape(docs, tokens, 3, ranks, width // ranks)
        )
        spread = lax.all_to_all(joined, "seq", split_axis=3, concat_axis=1, tiled=True)
        context, log_total = lax.map(doc_forward, spread)
        context = lax.all_to_all(context, "seq", split_axis=1, concat_axis=2, tiled=True).reshape(
            count, width
        )
        middle = (
            flat + jnp.dot(context, out_full, preferred_element_type=jnp.float32) + proj_bias[2]
        )
        normed_two, norm_two_back = jax.vjp(
            lambda value: layer_norm(value, norm_gain[1], norm_bias[1]), middle
        )
        hidden = (
            jnp.dot(normed_two.astype(jnp.bfloat16), fc_full, preferred_element_type=jnp.float32)
            + fc_bias
        )
        active, gelu_back = jax.vjp(lambda value: jax.nn.gelu(value, approximate=True), hidden)
        result = (
            middle
            + jnp.dot(active.astype(jnp.bfloat16), proj_full, preferred_element_type=jnp.float32)
            + proj_bias[3]
        )
        return (
            result,
            (normed, down_q, down_v, norm_one_back, spread, log_total, norm_two_back, gelu_back),
        )

    stack = (
        lax.all_gather(qkv_weight, "dp", axis=0, tiled=True),
        lax.all_gather(out_weight, "dp", axis=0, tiled=True),
        lax.all_gather(feed_input_weight, "dp", axis=0, tiled=True),
        lax.all_gather(proj_weight, "dp", axis=0, tiled=True),
    )
    result, kept = forward(stack)
    fenced = lax.optimization_barrier((stack, result))
    stack = fenced[0]
    again, kept = forward(stack)
    qkv_full, out_full, fc_full, proj_full = stack
    normed, down_q, down_v, norm_one_back, spread, log_total, norm_two_back, gelu_back = kept
    cotangent = out_grad.reshape(count, width)
    grad_active = dot_trans(cotangent, proj_full)
    grad_hidden = gelu_back(grad_active)[0].astype(jnp.bfloat16)
    grad_normed_two = dot_trans(grad_hidden, fc_full)
    grad_middle = cotangent.astype(jnp.float32) + norm_two_back(grad_normed_two)[0]
    grad_context = dot_trans(grad_middle.astype(jnp.bfloat16), out_full).astype(jnp.bfloat16)
    grad_context = grad_context.reshape(docs, tokens, ranks, width // ranks)
    grad_context = lax.all_to_all(grad_context, "seq", split_axis=2, concat_axis=1, tiled=True)
    grad_joined = lax.map(doc_backward, (spread, grad_context, log_total))
    grad_joined = lax.all_to_all(
        grad_joined, "seq", split_axis=1, concat_axis=3, tiled=True
    ).reshape(count, 3 * width)
    grad_normed = dot_trans(grad_joined, qkv_full)
    grad_query = grad_joined[:, :width].astype(jnp.float32)
    grad_value = grad_joined[:, 2 * width :].astype(jnp.float32)
    tilt_q = scale_factor * jnp.dot(grad_query, adapters[1].T, precision=highest)
    value_adapter_up = scale_factor * jnp.dot(grad_value, adapters[3].T, precision=highest)
    grad_normed = (
        grad_normed
        + jnp.dot(tilt_q, adapters[0], precision=highest)
        + jnp.dot(value_adapter_up, adapters[2], precision=highest)
    )
    grad_input = (
        (grad_middle + norm_one_back(grad_normed)[0])
        .astype(jnp.bfloat16)
        .reshape(docs, tokens, width)
    )
    partial_terms = jnp.stack(
        [
            dot_first(tilt_q, normed),
            scale_factor * dot_first(down_q, grad_query),
            dot_first(value_adapter_up, normed),
            scale_factor * dot_first(down_v, grad_value),
        ]
    )
    total = lax.psum(partial_terms, ("dp", "seq"))
    grad_norm = jnp.sqrt(jnp.sum(total * total))
    clipped, new_weight, new_first, new_second = adam_update(
        total, adapters, first_moment, second_moment, grad_norm
    )
    mixed = result.astype(jnp.bfloat16).reshape(docs, tokens, width)
    return (mixed, grad_input, clipped, grad_norm, new_weight, new_first, new_second)


HALF = 512
BLOCK = 256
SMEM = pl.BlockSpec(memory_space=pltpu.SMEM)
VMEM = pl.BlockSpec(memory_space=pltpu.VMEM)
HBM = pl.BlockSpec(memory_space=pl.ANY)
f32 = jnp.float32
bf16 = jnp.bfloat16
SWAP = ((0, 1), (1, 0))
GELU_A = math.sqrt(2.0 / math.pi)
GELU_B = 0.044715


def nn(left, right):
    return lax.dot_general(left, right, (((1,), (0,)), ((), ())), preferred_element_type=f32)


def nt(left, right):
    return lax.dot_general(left, right, (((1,), (1,)), ((), ())), preferred_element_type=f32)


def tn(left, right):
    return lax.dot_general(left, right, (((0,), (0,)), ((), ())), preferred_element_type=f32)


def shape(*dims, dtype=bf16):
    return jax.ShapeDtypeStruct(dims, dtype)


def params(mib):
    return pltpu.CompilerParams(vmem_limit_bytes=mib * 2**20)


def rows(index, size):
    return pl.ds(pl.multiple_of(index * size, size), size)


def parity(z, k):
    return lax.rem(z + k, 2)


class Copies:
    def __init__(self, sems):
        self.sems = sems
        self.count = 0

    def start(self, source, target):
        copy = pltpu.make_async_copy(source, target, self.sems.at[self.count])
        self.count += 1
        copy.start()
        return copy


def wait_all(copies):
    for copy in copies:
        copy.wait()


def center_scale(x):
    center = jnp.mean(x, axis=-1, keepdims=True)
    centered = x - center
    spread = jnp.mean(centered * centered, axis=-1, keepdims=True)
    inverse = lax.rsqrt(spread + norm_eps)
    return centered * inverse, inverse


def norm_back(hat, inverse, grad):
    first = jnp.mean(grad, axis=-1, keepdims=True)
    second = jnp.mean(grad * hat, axis=-1, keepdims=True)
    return inverse * (grad - first - hat * second)


def qkv_kernel(
    ids, m0, m1, o0, o1, w0, w1, w2, w3t, w3b, gain, shift, down_w, up_w, bias,
    q_out, k_out, v_out, n_out, down_out, w_out, xs, ws, sems,
):
    core, z, chip = ids[0], ids[1], ids[2]
    go = Copies(sems)
    arrive = [
        go.start(ref, xs.at[rows(2 * side + parity(z, k), BLOCK)])
        for side, pair in ((core, (m0, m1)), (1 - core, (o0, o1)))
        for k, ref in enumerate(pair)
    ]
    weights = [
        go.start(ref, ws.at[rows(chip ^ r, BLOCK)]) for r, ref in enumerate((w0, w1, w2))
    ]
    weights.append(go.start(w3t, ws.at[rows(2 * (chip ^ 3), BLOCK // 2)]))
    weights.append(go.start(w3b, ws.at[rows(2 * (chip ^ 3) + 1, BLOCK // 2)]))
    wait_all(arrive)

    @pl.loop(0, 4)
    def _(i):
        at = rows(i, BLOCK)
        hat, _ = center_scale(xs[at].astype(f32))
        n_out[at] = (hat * gain[...] + shift[...]).astype(bf16)

    wait_all(weights)
    keep = go.start(ws, w_out)

    @pl.loop(0, 4)
    def _(i):
        at = rows(i, BLOCK)
        n = n_out[at]
        down = nt(n, down_w[...]).astype(bf16)
        down_out[at] = down
        for part, out in enumerate((q_out, k_out, v_out)):
            cols = slice(part * HALF, (part + 1) * HALF)
            value = nn(n, ws[:, cols]) + bias[:, cols]
            if part != 1:
                value += nn(down, up_w[:, cols])
            value = value.astype(bf16)
            if part == 0:
                value = value * jnp.asarray(0.125, bf16)
            out[at] = value

    keep.wait()


def call_qkv(ids, x_own, x_other, pieces, gain, shift, down_w, up_w, bias):
    return pl.pallas_call(
        qkv_kernel,
        out_shape=(
            shape(1024, HALF),
            shape(1024, HALF),
            shape(1024, HALF),
            shape(1024, 1024),
            shape(1024, 128),
            shape(1024, 1536),
        ),
        in_specs=[SMEM] + [HBM] * 9 + [VMEM] * 5,
        out_specs=(VMEM,) * 5 + (HBM,),
        scratch_shapes=[
            pltpu.VMEM((1024, 1024), bf16),
            pltpu.VMEM((1024, 1536), bf16),
            pltpu.SemaphoreType.DMA((10,)),
        ],
        compiler_params=params(40),
        name="qkv",
    )(ids, *x_own, *x_other, *pieces, gain, shift, down_w, up_w, bias)


def low_half(value):
    return lax.broadcasted_iota(jnp.int32, value.shape, 1) < 64


def forward_kernel(ids, q, k, v, ctx, stat, send):
    core = ids[0]
    keys = k[...]
    values = v[...]
    low = low_half(values)
    one = jnp.ones_like(values)
    values_ab = (jnp.where(low, values, one), jnp.where(low, one, values))
    for i in range(4):
        ext = (i + 1) * BLOCK
        query = q[i * BLOCK : ext]
        mine = low_half(query)
        zero = jnp.zeros_like(query)
        heads, tops = [], []
        for a in range(2):
            part = jnp.where(mine, query, zero) if a == 0 else jnp.where(mine, zero, query)
            scores = nt(part, keys[:ext])
            last = scores[:, i * BLOCK :]
            r = lax.broadcasted_iota(jnp.int32, last.shape, 0)
            s = lax.broadcasted_iota(jnp.int32, last.shape, 1)
            last = jnp.where(r >= s, last, -1e30)
            scores = jnp.concatenate([scores[:, : i * BLOCK], last], axis=1) if i else last
            top = jnp.max(scores, axis=1, keepdims=True)
            expo = jnp.exp(scores - top).astype(bf16)
            heads.append(nn(expo, values_ab[a][:ext]))
            tops.append(top)
        wide = low_half(heads[0])
        sums = jnp.where(wide, heads[1], heads[0])
        sums = pltpu.roll(sums, 64, 1)
        ctx[i * BLOCK : ext] = (jnp.where(wide, heads[0], heads[1]) / sums).astype(bf16)
        total = jnp.where(wide, tops[0], tops[1]) + jnp.log(sums)
        total = jnp.transpose(total)
        stat[0, :, i * BLOCK : ext] = jnp.concatenate([total[0:1], total[64:65]] * 4, axis=0)
    send[...] = ctx[rows(1 - core, HALF)]


def call_forward(ids, q, k, v):
    pair = pl.BlockSpec((1024, 128), lambda p: (0, p))
    return pl.pallas_call(
        forward_kernel,
        grid=(4,),
        out_shape=(shape(1024, HALF), shape(4, 8, 1024, dtype=f32), shape(HALF, HALF)),
        in_specs=[SMEM, pair, pair, pair],
        out_specs=(
            pair,
            pl.BlockSpec((1, 8, 1024), lambda p: (p, 0, 0)),
            pl.BlockSpec((HALF, 128), lambda p: (0, p)),
        ),
        compiler_params=params(40),
        name="attention",
    )(ids, q, k, v)


def backward_kernel(ids, q, k, v, ctx, stat, g_own, g_other, dq, dk, dv, grads, acc_k, acc_v):
    core = ids[0]
    grads[rows(core, HALF)] = g_own[...]
    grads[rows(1 - core, HALF)] = g_other[...]
    keys = k[...]
    values = v[...]
    product = grads[...].astype(f32) * ctx[...].astype(f32)
    high = product.astype(bf16)
    rest = (product - high.astype(f32)).astype(bf16)
    r = lax.broadcasted_iota(jnp.int32, (16, 128), 0)
    s = lax.broadcasted_iota(jnp.int32, (16, 128), 1)
    pick = jnp.where((s < 64) == (lax.rem(r, 2) == 0), 1.0, 0.0).astype(bf16)
    inner = nt(pick, high) + nt(pick, rest)
    acc_k[...] = jnp.zeros_like(acc_k)
    acc_v[...] = jnp.zeros_like(acc_v)
    for i in range(4):
        ext = (i + 1) * BLOCK
        cols = slice(i * BLOCK, ext)
        query = q[cols]
        grad = grads[cols]
        mine = low_half(query)
        zero = jnp.zeros_like(query)
        new_q = []
        for a in range(2):
            if a == 0:
                part, part_grad = jnp.where(mine, query, zero), jnp.where(mine, grad, zero)
            else:
                part, part_grad = jnp.where(mine, zero, query), jnp.where(mine, zero, grad)
            scores = nt(keys[:ext], part)
            probs = jnp.exp(scores - stat[0, a : a + 1, cols])
            last = probs[i * BLOCK :]
            r = lax.broadcasted_iota(jnp.int32, last.shape, 0)
            s = lax.broadcasted_iota(jnp.int32, last.shape, 1)
            last = jnp.where(r <= s, last, 0.0)
            probs = jnp.concatenate([probs[: i * BLOCK], last], axis=0) if i else last
            grad_probs = nt(values[:ext], part_grad)
            grad_scores = (probs * (grad_probs - inner[a : a + 1, cols])).astype(bf16)
            acc_v[:ext] += nn(probs.astype(bf16), part_grad)
            acc_k[:ext] += nn(grad_scores, part)
            new_q.append(tn(grad_scores, keys[:ext]))
        both = jnp.where(low_half(new_q[0]), new_q[0], new_q[1])
        dq[cols] = (both * 0.125).astype(bf16)
    dk[...] = acc_k[...].astype(bf16)
    dv[...] = acc_v[...].astype(bf16)


def call_backward(ids, q, k, v, ctx, stat, g_own, g_other):
    pair = pl.BlockSpec((1024, 128), lambda p: (0, p))
    half = pl.BlockSpec((HALF, 128), lambda p: (0, p))
    return pl.pallas_call(
        backward_kernel,
        grid=(4,),
        out_shape=(shape(1024, HALF),) * 3,
        in_specs=[SMEM, pair, pair, pair, pair, pl.BlockSpec((1, 8, 1024), lambda p: (p, 0, 0)), half, half],
        out_specs=(pair,) * 3,
        scratch_shapes=[
            pltpu.VMEM((1024, 128), bf16),
            pltpu.VMEM((1024, 128), f32),
            pltpu.VMEM((1024, 128), f32),
        ],
        compiler_params=params(40),
        name="attention_back",
    )(ids, q, k, v, ctx, stat, g_own, g_other)


def start_pieces(go, pieces, target, chip, size):
    own, by_x, by_y, top, low = pieces
    return [
        go.start(own, target.at[rows(chip, size)]),
        go.start(by_x, target.at[rows(chip ^ 1, size)]),
        go.start(by_y, target.at[rows(chip ^ 2, size)]),
        go.start(top, target.at[rows(2 * (chip ^ 3), size // 2)]),
        go.start(low, target.at[rows(2 * (chip ^ 3) + 1, size // 2)]),
    ]


def start_tokens(go, pair, target, z):
    return [go.start(ref, target.at[rows(parity(z, k), BLOCK)]) for k, ref in enumerate(pair)]


def middle_kernel(*refs):
    ids, ctx, other = refs[:3]
    mine, theirs = refs[3:8], refs[8:13]
    x0, x1, bias, gain, shift, middle, normed, w_out, cs, ws, xs, sems = refs[13:]
    core, z, chip = ids[0], ids[1], ids[2]
    go = Copies(sems)
    arrive = [go.start(ctx.at[rows(core, HALF)], cs)]
    arrive += start_pieces(go, mine, ws.at[0], chip, 128)
    arrive += start_pieces(go, theirs, ws.at[1], chip, 128)
    arrive += start_tokens(go, (x0, x1), xs, z)
    wait_all(arrive)
    keep = go.start(ws, w_out)

    @pl.loop(0, 2)
    def _(i):
        at = rows(i, BLOCK)
        value = nn(cs[at], ws[0]) + nn(other[at], ws[1])
        value = value + xs[at].astype(f32) + bias[...]
        middle[at] = value
        hat, _ = center_scale(value)
        normed[at] = (hat * gain[...] + shift[...]).astype(bf16)

    keep.wait()


def call_middle(ids, ctx, other, mine, theirs, x_own, bias, gain, shift):
    return pl.pallas_call(
        middle_kernel,
        out_shape=(shape(HALF, 1024, dtype=f32), shape(HALF, 1024), shape(2, HALF, 1024)),
        in_specs=[SMEM, HBM, VMEM] + [HBM] * 12 + [VMEM] * 3,
        out_specs=(VMEM, VMEM, HBM),
        scratch_shapes=[
            pltpu.VMEM((HALF, HALF), bf16),
            pltpu.VMEM((2, HALF, 1024), bf16),
            pltpu.VMEM((HALF, 1024), bf16),
            pltpu.SemaphoreType.DMA((14,)),
        ],
        compiler_params=params(32),
        name="middle",
    )(ids, ctx, other, *mine, *theirs, *x_own, bias, gain, shift)


def hidden_kernel(*refs):
    ids, normed = refs[:2]
    mine, theirs = refs[2:7], refs[7:12]
    bias, active, slope, w_out, ws, sems = refs[12:]
    core, chip = ids[0], ids[2]
    go = Copies(sems)
    arrive = []
    for side, pieces in ((core, mine), (1 - core, theirs)):
        own, by_x, by_y, top, low = pieces
        for r, ref in enumerate((own, by_x, by_y)):
            arrive.append(go.start(ref, ws.at[rows(2 * (chip ^ r) + side, 128)]))
        arrive.append(go.start(top, ws.at[rows(4 * (chip ^ 3) + 2 * side, 64)]))
        arrive.append(go.start(low, ws.at[rows(4 * (chip ^ 3) + 2 * side + 1, 64)]))
    wait_all(arrive)
    keep = [go.start(ws.at[:, d * HALF : (d + 1) * HALF], w_out.at[d]) for d in range(8)]
    for d in range(8):
        cols = slice(d * HALF, (d + 1) * HALF)

        @pl.loop(0, 2)
        def _(i):
            at = rows(i, BLOCK)
            h = nn(normed[at], ws[:, cols]) + bias[:, cols]
            square = h * h
            t = jnp.tanh(h * (GELU_A + (GELU_A * GELU_B) * square))
            lift = 0.5 + 0.5 * t
            active[d, at] = (h * lift).astype(bf16)
            inner = GELU_A + (3.0 * GELU_A * GELU_B) * square
            slope[d, at] = (lift + (0.5 * h) * (1.0 - t * t) * inner).astype(bf16)

    wait_all(keep)


def call_hidden(ids, normed, mine, theirs, bias):
    return pl.pallas_call(
        hidden_kernel,
        out_shape=(shape(8, HALF, HALF), shape(8, HALF, HALF), shape(8, 1024, HALF)),
        in_specs=[SMEM, VMEM] + [HBM] * 10 + [VMEM],
        out_specs=(VMEM, VMEM, HBM),
        scratch_shapes=[pltpu.VMEM((1024, 4096), bf16), pltpu.SemaphoreType.DMA((18,))],
        compiler_params=params(48),
        name="hidden",
    )(ids, normed, *mine, *theirs, bias)


def feed_kernel(steps, first, *refs):
    n = len(steps)
    ids, g0, g1, active, slope, w_in = refs[:6]
    pieces = refs[6 : 6 + n]
    refs = refs[6 + n :]
    if not first:
        old_result, old_grad, refs = refs[0], refs[1], refs[2:]
    result, grad, gs, acts, slopes, w_ins, w_outs, sems = refs[:8]
    core, z, chip = ids[0], ids[1], ids[2]
    go = Copies(sems)
    tokens = start_tokens(go, (g0, g1), gs, z)
    copies = []
    for at, (r, side) in enumerate(steps):
        d = 2 * (chip ^ r) + (core ^ side)
        copies.append(
            [
                go.start(pieces[at], w_outs.at[at]),
                go.start(slope.at[d], slopes.at[at]),
                go.start(w_in.at[d], w_ins.at[at]),
                go.start(active.at[d], acts.at[at]),
            ]
        )
    wait_all(tokens)
    for at in range(n):
        wait_all(copies[at])

        @pl.loop(0, 2)
        def _(i):
            tok = rows(i, BLOCK)
            back = nt(gs[tok], w_outs[at]) * slopes[at, tok].astype(f32)
            more = nt(back.astype(bf16), w_ins[at])
            out = nn(acts[at, tok], w_outs[at])
            if at == 0:
                if first:
                    grad[tok] = more
                    result[tok] = out
                else:
                    grad[tok] = old_grad[tok] + more
                    result[tok] = old_result[tok] + out
            else:
                grad[tok] += more
                result[tok] += out


def call_feed(ids, steps, g_own, active, slope, w_in, pieces, old):
    n = len(steps)
    first = old is None
    return pl.pallas_call(
        functools.partial(feed_kernel, steps, first),
        out_shape=(shape(HALF, 1024, dtype=f32),) * 2,
        in_specs=[SMEM] + [HBM] * (5 + n) + ([] if first else [VMEM, VMEM]),
        out_specs=(VMEM, VMEM),
        scratch_shapes=[
            pltpu.VMEM((HALF, 1024), bf16),
            pltpu.VMEM((n, HALF, HALF), bf16),
            pltpu.VMEM((n, HALF, HALF), bf16),
            pltpu.VMEM((n, 1024, HALF), bf16),
            pltpu.VMEM((n, HALF, 1024), bf16),
            pltpu.SemaphoreType.DMA((2 + 4 * n,)),
        ],
        compiler_params=params(48),
        name="feed",
    )(ids, *g_own, active, slope, w_in, *pieces, *(() if first else old))


def last_grad_kernel(
    ids, g0, g1, slope, w_in, wt0, wl0, wt1, wl1, old_grad, middle, gain, w_o,
    grad_middle, ctx_own, ctx_send, gs, slopes, w_ins, w_outs, sems,
):
    core, z, chip = ids[0], ids[1], ids[2]
    go = Copies(sems)
    tokens = start_tokens(go, (g0, g1), gs, z)
    copies = []
    for at, (top, low) in enumerate(((wt0, wl0), (wt1, wl1))):
        d = 2 * (chip ^ 3) + (core ^ at)
        copies.append(
            [
                go.start(top, w_outs.at[at, :BLOCK]),
                go.start(low, w_outs.at[at, BLOCK:]),
                go.start(slope.at[d], slopes.at[at]),
                go.start(w_in.at[d], w_ins.at[at]),
            ]
        )
    wait_all(tokens)
    wait_all(copies[0])
    wait_all(copies[1])

    @pl.loop(0, 2)
    def _(i):
        tok = rows(i, BLOCK)
        grad = old_grad[tok]
        for at in range(2):
            back = nt(gs[tok], w_outs[at]) * slopes[at, tok].astype(f32)
            grad += nt(back.astype(bf16), w_ins[at])
        hat, inverse = center_scale(middle[tok])
        value = gs[tok].astype(f32) + norm_back(hat, inverse, grad * gain[...])
        grad_middle[tok] = value
        low_value = value.astype(bf16)
        ctx_own[tok] = nt(low_value, w_o[0]).astype(bf16)
        ctx_send[tok] = nt(low_value, w_o[1]).astype(bf16)


def call_last_grad(ids, g_own, slope, w_in, halves, old_grad, middle, gain, w_o):
    return pl.pallas_call(
        last_grad_kernel,
        out_shape=(shape(HALF, 1024, dtype=f32), shape(HALF, HALF), shape(HALF, HALF)),
        in_specs=[SMEM] + [HBM] * 8 + [VMEM] * 4,
        out_specs=(VMEM,) * 3,
        scratch_shapes=[
            pltpu.VMEM((HALF, 1024), bf16),
            pltpu.VMEM((2, HALF, HALF), bf16),
            pltpu.VMEM((2, 1024, HALF), bf16),
            pltpu.VMEM((2, HALF, 1024), bf16),
            pltpu.SemaphoreType.DMA((10,)),
        ],
        compiler_params=params(48),
        name="middle_grad",
    )(ids, *g_own, slope, w_in, *halves, old_grad, middle, gain, w_o)


def last_result_kernel(
    ids, active, wt0, wl0, wt1, wl1, old_result, middle, bias, out0, out1, acts, w_outs, sems
):
    core, z, chip = ids[0], ids[1], ids[2]
    go = Copies(sems)
    arrive = []
    for at, (top, low) in enumerate(((wt0, wl0), (wt1, wl1))):
        d = 2 * (chip ^ 3) + (core ^ at)
        arrive.append(go.start(top, w_outs.at[at, :BLOCK]))
        arrive.append(go.start(low, w_outs.at[at, BLOCK:]))
        arrive.append(go.start(active.at[d], acts.at[at]))
    wait_all(arrive)
    for k, out in enumerate((out0, out1)):
        tok = rows(parity(z, k), BLOCK)
        value = old_result[tok] + middle[tok] + bias[...]
        for at in range(2):
            value += nn(acts[at, tok], w_outs[at])
        out[...] = value.astype(bf16)


def call_last_result(ids, active, halves, old_result, middle, bias):
    return pl.pallas_call(
        last_result_kernel,
        out_shape=(shape(BLOCK, 1024),) * 2,
        in_specs=[SMEM] + [HBM] * 5 + [VMEM] * 3,
        out_specs=(VMEM,) * 2,
        scratch_shapes=[
            pltpu.VMEM((2, HALF, HALF), bf16),
            pltpu.VMEM((2, HALF, 1024), bf16),
            pltpu.SemaphoreType.DMA((6,)),
        ],
        compiler_params=params(32),
        name="result",
    )(ids, active, *halves, old_result, middle, bias)


def qkv_back_kernel(
    ids, dq, dk, dv, w, normed, down, down_w, up_w, own, send, g_norm, g_up, tilt_acc, up_acc
):
    core = ids[0]
    tilt_acc[...] = jnp.zeros_like(tilt_acc)
    up_acc[...] = jnp.zeros_like(up_acc)

    @pl.loop(0, 4)
    def _(i):
        at = rows(i, BLOCK)
        gq, gk, gv = dq[at], dk[at], dv[at]
        tilt = (nt(gq, up_w[:, :HALF]) + nt(gv, up_w[:, 2 * HALF :])).astype(bf16)
        value = nt(gq, w[:, :HALF]) + nt(gk, w[:, HALF : 2 * HALF]) + nt(gv, w[:, 2 * HALF :])
        value = (value + nn(tilt, down_w[...])).astype(bf16)
        place = rows(lax.rem(i, 2), BLOCK)

        @pl.when(i // 2 == core)
        def _():
            own[place] = value

        @pl.when(i // 2 != core)
        def _():
            send[place] = value

        tilt_acc[...] += tn(tilt, normed[at])
        up_acc[:, :HALF] += tn(down[at], gq)
        up_acc[:, HALF:] += tn(down[at], gv)

    g_norm[...] = tilt_acc[:8]
    g_up[...] = up_acc[:8]


def call_qkv_back(ids, dq, dk, dv, w, normed, down, down_w, up_w):
    return pl.pallas_call(
        qkv_back_kernel,
        out_shape=(
            shape(HALF, 1024),
            shape(HALF, 1024),
            shape(8, 1024, dtype=f32),
            shape(8, 1024, dtype=f32),
        ),
        in_specs=[SMEM] + [VMEM] * 8,
        out_specs=(VMEM,) * 4,
        scratch_shapes=[pltpu.VMEM((128, 1024), f32), pltpu.VMEM((128, 1024), f32)],
        compiler_params=params(40),
        name="qkv_back",
    )(ids, dq, dk, dv, w, normed, down, down_w, up_w)


def input_grad_kernel(ids, x0, x1, own, other, grad_middle, gain, out0, out1):
    z = ids[1]
    for k, (x, out) in enumerate(((x0, out0), (x1, out1))):
        tok = rows(parity(z, k), BLOCK)
        grad = own[tok].astype(f32) + other[tok].astype(f32)
        hat, inverse = center_scale(x[...].astype(f32))
        out[...] = (grad_middle[tok] + norm_back(hat, inverse, grad * gain[...])).astype(bf16)


def call_input_grad(ids, x_own, own, other, grad_middle, gain):
    return pl.pallas_call(
        input_grad_kernel,
        out_shape=(shape(BLOCK, 1024),) * 2,
        in_specs=[SMEM] + [VMEM] * 6,
        out_specs=(VMEM,) * 2,
        compiler_params=params(32),
        name="input_grad",
    )(ids, *x_own, own, other, grad_middle, gain)


def to_core(value):
    return lax.ppermute(value, "core", SWAP)


def exchange(z, pair):
    sent = []
    for k in range(2):
        perm = [
            (4 * core + at, 4 * (at // 2) + 2 * core + (at + k) % 2)
            for core in range(2)
            for at in range(4)
        ]
        sent.append(lax.ppermute(pair[k], ("core", "seq"), perm))
    return sent


def by_parity(z, pair):
    even = lax.rem(z, 2) == 0
    return jnp.where(even, pair[0], pair[1]), jnp.where(even, pair[1], pair[0])


def gather(shard):
    by_x = lax.ppermute(shard, "x", SWAP)
    by_y = lax.ppermute(shard, "y", SWAP)
    half = shard.shape[0] // 2
    top = lax.ppermute(by_x[:half], "y", SWAP)
    low = lax.ppermute(by_y[half:], "x", SWAP)
    return [shard, by_x, by_y, top, low]


def on_chip(
    inputs,
    out_grad,
    norm_gain,
    norm_bias,
    proj_bias,
    fc_bias,
    qkv_weight,
    out_weight,
    feed_input_weight,
    proj_weight,
    adapters,
    first_moment,
    second_moment,
):
    core = lax.axis_index("core")
    z = lax.axis_index("seq")
    chip = 2 * lax.axis_index("y") + lax.axis_index("x")
    ids = jnp.stack([core, z, chip]).astype(jnp.int32)

    by_core = qkv_weight.reshape(128, 12, 2, 128)
    first, second = by_core[:, :, 0].reshape(128, 1536), by_core[:, :, 1].reshape(128, 1536)
    kept = jnp.where(core == 0, first, second)
    passed = jnp.where(core == 0, second, first)
    got = to_core(passed)
    qkv_shard = jnp.concatenate(
        [jnp.where(core == 0, kept, got), jnp.where(core == 0, got, kept)], axis=0
    )
    x_own = exchange(z, by_parity(z, (inputs[0], inputs[1])))
    x_other = [to_core(part) for part in x_own]
    qkv_pieces = gather(qkv_shard)
    out_pieces = gather(out_weight)
    out_other = [to_core(part) for part in out_pieces]
    in_pieces = gather(feed_input_weight)
    in_other = [to_core(part) for part in in_pieces]
    proj_pieces = gather(proj_weight)
    proj_other = [to_core(part) for part in proj_pieces]
    g_own = exchange(z, by_parity(z, (out_grad[0], out_grad[1])))

    def columns(value):
        lead = value.shape[0]
        value = value.reshape(lead, 4, 2, 128)
        return jnp.where(core == 0, value[:, :, 0], value[:, :, 1]).reshape(lead, HALF)

    scale = adapter_alpha / ADAPTER_RANK
    up_q, up_v = scale * columns(adapters[1]), scale * columns(adapters[3])
    up_w = jnp.zeros((128, 1536), f32)
    up_w = up_w.at[0:4, :HALF].set(up_q).at[4:8, 2 * HALF :].set(up_v).astype(bf16)
    down_w = jnp.concatenate([adapters[0], adapters[2], jnp.zeros((120, 1024), f32)], axis=0)
    down_w = down_w.astype(bf16)
    head_bias = columns(proj_bias[:2])
    qkv_bias = jnp.concatenate([head_bias[0], jnp.zeros((HALF,), f32), head_bias[1]])[None]

    q, k, v, normed, down, qkv_full = call_qkv(
        ids, x_own, x_other, qkv_pieces, norm_gain[:1], norm_bias[:1], down_w, up_w, qkv_bias
    )
    ctx, stat, ctx_send = call_forward(ids, q, k, v)
    ctx_other = to_core(ctx_send)
    middle, normed_two, out_full = call_middle(
        ids, ctx, ctx_other, out_pieces, out_other, x_own, proj_bias[2:3], norm_gain[1:], norm_bias[1:]
    )
    active, slope, w_in = call_hidden(ids, normed_two, in_pieces, in_other, fc_bias[None])
    old = call_feed(
        ids, ((0, 0), (0, 1)), g_own, active, slope, w_in, (proj_pieces[0], proj_other[0]), None
    )
    result, grad = call_feed(
        ids,
        ((1, 0), (1, 1), (2, 0), (2, 1)),
        g_own,
        active,
        slope,
        w_in,
        (proj_pieces[1], proj_other[1], proj_pieces[2], proj_other[2]),
        old,
    )
    halves = (proj_pieces[3], proj_pieces[4], proj_other[3], proj_other[4])
    grad_middle, grad_ctx, grad_send = call_last_grad(
        ids, g_own, slope, w_in, halves, grad, middle, norm_gain[1:], out_full
    )
    grad_ctx_other = to_core(grad_send)
    mixed = exchange(z, call_last_result(ids, active, halves, result, middle, proj_bias[3:]))
    dq, dk, dv = call_backward(ids, q, k, v, ctx, stat, grad_ctx, grad_ctx_other)
    own, send, g_norm, g_up = call_qkv_back(
        ids, dq, dk, dv, qkv_full, normed, down, down_w, up_w
    )
    other = to_core(send)
    grad_in = exchange(z, call_input_grad(ids, x_own, own, other, grad_middle, norm_gain[:1]))

    def spread(part):
        part = part.reshape(4, 4, 1, 128)
        place = lax.broadcasted_iota(jnp.int32, (1, 1, 2, 1), 2)
        return jnp.where(place == core, part, 0.0).reshape(4, 1024)

    total = jnp.stack(
        [
            g_norm[:4],
            scale * spread(g_up[:4, :HALF]),
            g_norm[4:],
            scale * spread(g_up[4:, HALF:]),
        ]
    )
    for axis, perm in (
        ("core", SWAP),
        ("x", SWAP),
        ("y", SWAP),
        ("seq", ((0, 1), (1, 0), (2, 3), (3, 2))),
        ("seq", ((0, 2), (2, 0), (1, 3), (3, 1))),
    ):
        total = total + lax.ppermute(total, axis, perm)
    grad_norm = jnp.sqrt(jnp.sum(total * total))
    clipped, new_weight, new_first, new_second = adam_update(
        total, adapters, first_moment, second_moment, grad_norm
    )
    mixed = jnp.stack(by_parity(z, mixed))
    grad_input = jnp.stack(by_parity(z, grad_in))
    return (mixed, grad_input, clipped, grad_norm, new_weight, new_first, new_second)


def solution(mesh):
    sizes = dict(mesh.shape)
    if sizes["dp"] == 8 and sizes["seq"] == 4:
        plane = Mesh(mesh.devices.reshape(2, 2, 2, 4), ("y", "x", "core", "seq"))
        return build(plane, ("y", "x", "core"), on_chip)
    return build(mesh, "dp", on_device)


def build(mesh, dp, step):
    tokens, weight = P(dp, "seq", None), P(dp, None)
    return jax.shard_map(
        step,
        mesh=mesh,
        in_specs=(tokens, tokens) + (P(),) * 4 + (weight,) * 4 + (P(),) * 3,
        out_specs=(tokens, tokens) + (P(),) * 5,
        check_vma=False,
    )
```

```python
import functools
import math

import jax
import jax.numpy as jnp
from jax import lax
from jax.experimental import pallas as pl
from jax.experimental.pallas import tpu as pltpu
from jax.sharding import Mesh
from jax.sharding import PartitionSpec as P

HEAD_DIM = 64
ADAPTER_RANK = 4
STEP = 10


highest = lax.Precision.HIGHEST
adapter_alpha = 32.0
beta_one = 0.9
beta_two = 0.999
adam_eps = 1e-08
decay_rate = 0.01
learning_rate = 0.02
clip_bound = 1.0
norm_eps = 1e-05


def layer_norm(value, gain, shift):
    center = jnp.mean(value, axis=-1, keepdims=True)
    centered = value - center
    spread = jnp.mean(centered * centered, axis=-1, keepdims=True)
    return centered * lax.rsqrt(spread + norm_eps) * gain + shift


def dot_trans(left, right):
    return lax.dot_general(
        left, right, (((1,), (1,)), ((), ())), preferred_element_type=jnp.float32
    )


def dot_first(left, right):
    return lax.dot_general(
        left, right, (((0,), (0,)), ((), ())), precision=highest, preferred_element_type=jnp.float32
    )


def adam_update(grad, weight, first, second, norm):
    scale_factor = clip_bound / jnp.maximum(norm, clip_bound)
    clipped = grad * scale_factor
    new_first = beta_one * first + (1.0 - beta_one) * clipped
    new_second = beta_two * second + (1.0 - beta_two) * clipped * clipped
    first_hat = new_first / (1.0 - beta_one**STEP)
    second_hat = new_second / (1.0 - beta_two**STEP)
    new_weight = weight - learning_rate * (
        first_hat / (jnp.sqrt(second_hat) + adam_eps) + decay_rate * weight
    )
    return (clipped, new_weight, new_first, new_second)


def split_heads(packed):
    length = packed.shape[0]
    local_heads = packed.shape[-1] // HEAD_DIM
    query = packed[:, 0, 0].reshape(length, local_heads, HEAD_DIM)
    keys = packed[:, 1, 0].reshape(length, local_heads, HEAD_DIM)
    values = packed[:, 2, 0].reshape(length, local_heads, HEAD_DIM)
    return (query, keys, values)


def doc_forward(packed):
    length = packed.shape[0]
    local_width = packed.shape[-1]
    query, keys, values = split_heads(packed)
    local_heads = query.shape[1]
    span = min(512, length)
    blocks = length // span
    scale = 1.0 / math.sqrt(HEAD_DIM)
    starts = jnp.arange(blocks, dtype=jnp.int32) * span

    def visit(pieces):
        query_block, start = pieces
        scores = (
            jnp.einsum("qhd,khd->hqk", query_block, keys, preferred_element_type=jnp.float32)
            * scale
        )
        causal = (start + jnp.arange(span))[:, None] >= jnp.arange(length)[None, :]
        masked = jnp.where(causal[None], scores, -1e30)
        summit = jnp.max(masked, axis=-1, keepdims=True)
        expo = jnp.where(causal[None], jnp.exp(masked - summit), 0.0)
        totals = jnp.sum(expo, axis=-1, keepdims=True)
        weights = (expo / totals).astype(jnp.bfloat16)
        context = jnp.einsum(
            "hqk,khd->qhd", weights, values, preferred_element_type=jnp.float32
        ).astype(jnp.bfloat16)
        return (context, summit[..., 0] + jnp.log(totals[..., 0]))

    context, log_total = lax.map(
        visit, (query.reshape(blocks, span, local_heads, HEAD_DIM), starts)
    )
    return (context.reshape(length, 1, local_width), log_total)


def doc_backward(args):
    packed, grad_context, log_total = args
    length = packed.shape[0]
    local_width = packed.shape[-1]
    query, keys, values = split_heads(packed)
    local_heads = query.shape[1]
    output_gradient = grad_context[:, 0].reshape(length, local_heads, HEAD_DIM)
    span = min(512, length)
    blocks = length // span
    scale = 1.0 / math.sqrt(HEAD_DIM)
    starts = jnp.arange(blocks, dtype=jnp.int32) * span

    def visit(carry, pieces):
        grad_keys, grad_values = carry
        query_block, grad_block, total_block, start = pieces
        scores = (
            jnp.einsum("qhd,khd->hqk", query_block, keys, preferred_element_type=jnp.float32)
            * scale
        )
        causal = (start + jnp.arange(span))[:, None] >= jnp.arange(length)[None, :]
        masked = jnp.where(causal[None], scores, -1e30)
        probs = jnp.where(causal[None], jnp.exp(masked - total_block[:, :, None]), 0.0)
        weights = probs.astype(jnp.bfloat16)
        grad_probs = jnp.einsum(
            "qhd,khd->hqk", grad_block, values, preferred_element_type=jnp.float32
        )
        inner = jnp.sum(probs * grad_probs, axis=-1, keepdims=True)
        grad_scores = (probs * (grad_probs - inner)).astype(jnp.bfloat16)
        grad_query = (
            jnp.einsum("hqk,khd->qhd", grad_scores, keys, preferred_element_type=jnp.float32)
            * scale
        )
        grad_keys = (
            grad_keys
            + jnp.einsum(
                "hqk,qhd->khd", grad_scores, query_block, preferred_element_type=jnp.float32
            )
            * scale
        )
        grad_values = grad_values + jnp.einsum(
            "hqk,qhd->khd", weights, grad_block, preferred_element_type=jnp.float32
        )
        return ((grad_keys, grad_values), grad_query)

    empty = jnp.zeros((length, local_heads, HEAD_DIM), jnp.float32)
    pieces = (
        query.reshape(blocks, span, local_heads, HEAD_DIM),
        output_gradient.reshape(blocks, span, local_heads, HEAD_DIM),
        log_total,
        starts,
    )
    (grad_keys, grad_values), grad_query = lax.scan(visit, (empty, empty), pieces)
    joined = jnp.stack(
        [
            grad_query.reshape(length, local_width),
            grad_keys.reshape(length, local_width),
            grad_values.reshape(length, local_width),
        ],
        axis=1,
    )
    return joined.astype(jnp.bfloat16)[:, :, None, :]


def on_device(
    inputs,
    out_grad,
    norm_gain,
    norm_bias,
    proj_bias,
    fc_bias,
    qkv_weight,
    out_weight,
    feed_input_weight,
    proj_weight,
    adapters,
    first_moment,
    second_moment,
):
    docs, tokens, width = inputs.shape
    count = docs * tokens
    ranks = lax.axis_size("seq")
    scale_factor = adapter_alpha / ADAPTER_RANK

    def forward(stack):
        qkv_full, out_full, fc_full, proj_full = stack
        flat = inputs.reshape(count, width).astype(jnp.float32)
        normed, norm_one_back = jax.vjp(
            lambda value: layer_norm(value, norm_gain[0], norm_bias[0]), flat
        )
        base = jnp.dot(normed.astype(jnp.bfloat16), qkv_full, preferred_element_type=jnp.float32)
        down_q = jnp.dot(normed, adapters[0].T, precision=highest)
        down_v = jnp.dot(normed, adapters[2].T, precision=highest)
        query = (
            base[:, :width]
            + proj_bias[0]
            + scale_factor * jnp.dot(down_q, adapters[1], precision=highest)
        )
        keys = base[:, width : 2 * width]
        values = (
            base[:, 2 * width :]
            + proj_bias[1]
            + scale_factor * jnp.dot(down_v, adapters[3], precision=highest)
        )
        joined = (
            jnp.concatenate([query, keys, values], axis=1)
            .astype(jnp.bfloat16)
            .reshape(docs, tokens, 3, ranks, width // ranks)
        )
        spread = lax.all_to_all(joined, "seq", split_axis=3, concat_axis=1, tiled=True)
        context, log_total = lax.map(doc_forward, spread)
        context = lax.all_to_all(context, "seq", split_axis=1, concat_axis=2, tiled=True).reshape(
            count, width
        )
        middle = (
            flat + jnp.dot(context, out_full, preferred_element_type=jnp.float32) + proj_bias[2]
        )
        normed_two, norm_two_back = jax.vjp(
            lambda value: layer_norm(value, norm_gain[1], norm_bias[1]), middle
        )
        hidden = (
            jnp.dot(normed_two.astype(jnp.bfloat16), fc_full, preferred_element_type=jnp.float32)
            + fc_bias
        )
        active, gelu_back = jax.vjp(lambda value: jax.nn.gelu(value, approximate=True), hidden)
        result = (
            middle
            + jnp.dot(active.astype(jnp.bfloat16), proj_full, preferred_element_type=jnp.float32)
            + proj_bias[3]
        )
        return (
            result,
            (normed, down_q, down_v, norm_one_back, spread, log_total, norm_two_back, gelu_back),
        )

    stack = (
        lax.all_gather(qkv_weight, "dp", axis=0, tiled=True),
        lax.all_gather(out_weight, "dp", axis=0, tiled=True),
        lax.all_gather(feed_input_weight, "dp", axis=0, tiled=True),
        lax.all_gather(proj_weight, "dp", axis=0, tiled=True),
    )
    result, kept = forward(stack)
    fenced = lax.optimization_barrier((stack, result))
    stack = fenced[0]
    again, kept = forward(stack)
    qkv_full, out_full, fc_full, proj_full = stack
    normed, down_q, down_v, norm_one_back, spread, log_total, norm_two_back, gelu_back = kept
    cotangent = out_grad.reshape(count, width)
    grad_active = dot_trans(cotangent, proj_full)
    grad_hidden = gelu_back(grad_active)[0].astype(jnp.bfloat16)
    grad_normed_two = dot_trans(grad_hidden, fc_full)
    grad_middle = cotangent.astype(jnp.float32) + norm_two_back(grad_normed_two)[0]
    grad_context = dot_trans(grad_middle.astype(jnp.bfloat16), out_full).astype(jnp.bfloat16)
    grad_context = grad_context.reshape(docs, tokens, ranks, width // ranks)
    grad_context = lax.all_to_all(grad_context, "seq", split_axis=2, concat_axis=1, tiled=True)
    grad_joined = lax.map(doc_backward, (spread, grad_context, log_total))
    grad_joined = lax.all_to_all(
        grad_joined, "seq", split_axis=1, concat_axis=3, tiled=True
    ).reshape(count, 3 * width)
    grad_normed = dot_trans(grad_joined, qkv_full)
    grad_query = grad_joined[:, :width].astype(jnp.float32)
    grad_value = grad_joined[:, 2 * width :].astype(jnp.float32)
    tilt_q = scale_factor * jnp.dot(grad_query, adapters[1].T, precision=highest)
    value_adapter_up = scale_factor * jnp.dot(grad_value, adapters[3].T, precision=highest)
    grad_normed = (
        grad_normed
        + jnp.dot(tilt_q, adapters[0], precision=highest)
        + jnp.dot(value_adapter_up, adapters[2], precision=highest)
    )
    grad_input = (
        (grad_middle + norm_one_back(grad_normed)[0])
        .astype(jnp.bfloat16)
        .reshape(docs, tokens, width)
    )
    partial_terms = jnp.stack(
        [
            dot_first(tilt_q, normed),
            scale_factor * dot_first(down_q, grad_query),
            dot_first(value_adapter_up, normed),
            scale_factor * dot_first(down_v, grad_value),
        ]
    )
    total = lax.psum(partial_terms, ("dp", "seq"))
    grad_norm = jnp.sqrt(jnp.sum(total * total))
    clipped, new_weight, new_first, new_second = adam_update(
        total, adapters, first_moment, second_moment, grad_norm
    )
    mixed = result.astype(jnp.bfloat16).reshape(docs, tokens, width)
    return (mixed, grad_input, clipped, grad_norm, new_weight, new_first, new_second)


HALF = 512
BLOCK = 256
VMEM_MIB = 63
SMEM = pl.BlockSpec(memory_space=pltpu.SMEM)
VMEM = pl.BlockSpec(memory_space=pltpu.VMEM)
HBM = pl.BlockSpec(memory_space=pl.ANY)
f32 = jnp.float32
bf16 = jnp.bfloat16
SWAP = ((0, 1), (1, 0))
GELU_A = math.sqrt(2.0 / math.pi)
GELU_B = 0.044715


def nn(left, right):
    return lax.dot_general(left, right, (((1,), (0,)), ((), ())), preferred_element_type=f32)


def nt(left, right):
    return lax.dot_general(left, right, (((1,), (1,)), ((), ())), preferred_element_type=f32)


def tn(left, right):
    return lax.dot_general(left, right, (((0,), (0,)), ((), ())), preferred_element_type=f32)


def shape(*dims, dtype=bf16):
    return jax.ShapeDtypeStruct(dims, dtype)


def params():
    return pltpu.CompilerParams(vmem_limit_bytes=VMEM_MIB * 2**20)


def rows(index, size):
    return pl.ds(pl.multiple_of(index * size, size), size)


def parity(z, k):
    return lax.rem(z + k, 2)


class Copies:
    def __init__(self, sems):
        self.sems = sems
        self.count = 0

    def start(self, source, target):
        copy = pltpu.make_async_copy(source, target, self.sems.at[self.count])
        self.count += 1
        copy.start()
        return copy


def wait_all(copies):
    for copy in copies:
        copy.wait()


def center_scale(x):
    center = jnp.mean(x, axis=-1, keepdims=True)
    centered = x - center
    spread = jnp.mean(centered * centered, axis=-1, keepdims=True)
    inverse = lax.rsqrt(spread + norm_eps)
    return centered * inverse, inverse


def norm_back(hat, inverse, grad):
    first = jnp.mean(grad, axis=-1, keepdims=True)
    second = jnp.mean(grad * hat, axis=-1, keepdims=True)
    return inverse * (grad - first - hat * second)


def norm_kernel(ids, m0, m1, gain, shift, out, xs, sems):
    z = ids[1]
    go = Copies(sems)
    arrive = [go.start(ref, xs.at[parity(z, k)]) for k, ref in enumerate((m0, m1))]
    wait_all(arrive)
    for i in range(2):
        hat, _ = center_scale(xs[i].astype(f32))
        out[i * BLOCK : (i + 1) * BLOCK] = (hat * gain[0:1] + shift[0:1]).astype(bf16)


def call_norm(ids, x_own, gain, shift):
    return pl.pallas_call(
        norm_kernel,
        out_shape=shape(HALF, 1024),
        in_specs=[SMEM, HBM, HBM, VMEM, VMEM],
        out_specs=VMEM,
        scratch_shapes=[pltpu.VMEM((2, BLOCK, 1024), bf16), pltpu.SemaphoreType.DMA((2,))],
        compiler_params=params(),
        name="norm",
    )(ids, *x_own, gain, shift)


def start_sides(go, piece, target, chip, core, tag):
    return [
        (tag, go.start(piece.at[:128], target.at[rows(2 * chip + core, 128)])),
        (tag, go.start(piece.at[128:], target.at[rows(2 * chip + 1 - core, 128)])),
    ]


def qkv_kernel(
    ids, n_own, n_other, w0, w1, w2, w3t, w3b, down_w, up_w, bias,
    q_out, k_out, v_out, down_out, w_out, o_out, ns, ws, os, outs, downs, sems,
):
    core, chip = ids[0], ids[2]
    go = Copies(sems)
    arrive = [
        go.start(n_own, ns.at[rows(core, HALF)]),
        go.start(n_other, ns.at[rows(1 - core, HALF)]),
    ]
    weights, outer, passing = [], [], []
    for r, ref in enumerate((w0, w1, w2, (w3t, w3b))):
        part = (lambda p: ref.at[p]) if r < 3 else (lambda p: ref[p // 2].at[p % 2])
        for p in range(3):
            weights += start_sides(go, part(p), ws.at[p], chip ^ r, core, p)
        for h in range(2):
            outer.append(
                go.start(
                    part(3).at[h * 128 : (h + 1) * 128],
                    os.at[rows(chip ^ r, 128), h * HALF : (h + 1) * HALF],
                )
            )
    wait_all(arrive)
    for p, out in enumerate((q_out, k_out, v_out)):
        wait_all([copy for at, copy in weights if at == p])
        passing.append(go.start(ws.at[p], w_out.at[p]))
        for i in range(4):
            at = slice(i * BLOCK, (i + 1) * BLOCK)
            if p == 0:
                downs[at] = nt(ns[at], down_w[...]).astype(bf16)
            value = nn(ns[at], ws[p]) + bias[:, p * HALF : (p + 1) * HALF]
            if p != 1:
                value += nn(downs[at], up_w[:, p * HALF : (p + 1) * HALF])
            value = value.astype(bf16)
            if p == 0:
                value = value * jnp.asarray(0.125, bf16)
            outs[p, at] = value
        passing.append(go.start(outs.at[p], out))
    passing.append(go.start(downs, down_out))
    wait_all(outer)
    passing.append(go.start(os, o_out))
    wait_all(passing)


def call_qkv(ids, n_own, n_other, pieces, down_w, up_w, bias):
    return pl.pallas_call(
        qkv_kernel,
        out_shape=(
            shape(1024, HALF),
            shape(1024, HALF),
            shape(1024, HALF),
            shape(1024, 128),
            shape(3, 1024, HALF),
            shape(HALF, 1024),
        ),
        in_specs=[SMEM] + [HBM] * 7 + [VMEM] * 3,
        out_specs=(HBM,) * 6,
        scratch_shapes=[
            pltpu.VMEM((1024, 1024), bf16),
            pltpu.VMEM((3, 1024, HALF), bf16),
            pltpu.VMEM((HALF, 1024), bf16),
            pltpu.VMEM((3, 1024, HALF), bf16),
            pltpu.VMEM((1024, 128), bf16),
            pltpu.SemaphoreType.DMA((42,)),
        ],
        compiler_params=params(),
        name="qkv",
    )(ids, n_own, n_other, *pieces, down_w, up_w, bias)


def low_half(value):
    return lax.broadcasted_iota(jnp.int32, value.shape, 1) < 64


def forward_kernel(ids, q, k, v, w_o, ctx, stat, own, send, ctxs, wos, sems):
    core = ids[0]
    pair = pl.program_id(0)
    copy = pltpu.make_async_copy(w_o, wos, sems.at[0])

    @pl.when(pair == 0)
    def _():
        copy.start()

    keys = k[...]
    values = v[...]
    low = low_half(values)
    one = jnp.ones_like(values)
    values_ab = (jnp.where(low, values, one), jnp.where(low, one, values))
    for i in range(4):
        ext = (i + 1) * BLOCK
        query = q[i * BLOCK : ext]
        mine = low_half(query)
        zero = jnp.zeros_like(query)
        heads, tops = [], []
        for a in range(2):
            part = jnp.where(mine, query, zero) if a == 0 else jnp.where(mine, zero, query)
            scores = nt(part, keys[:ext])
            last = scores[:, i * BLOCK :]
            r = lax.broadcasted_iota(jnp.int32, last.shape, 0)
            s = lax.broadcasted_iota(jnp.int32, last.shape, 1)
            last = jnp.where(r >= s, last, -1e30)
            scores = jnp.concatenate([scores[:, : i * BLOCK], last], axis=1) if i else last
            top = jnp.max(scores, axis=1, keepdims=True)
            expo = jnp.exp(scores - top).astype(bf16)
            heads.append(nn(expo, values_ab[a][:ext]))
            tops.append(top)
        wide = low_half(heads[0])
        sums = jnp.where(wide, heads[1], heads[0])
        sums = pltpu.roll(sums, 64, 1)
        value = (jnp.where(wide, heads[0], heads[1]) / sums).astype(bf16)
        ctx[i * BLOCK : ext] = value
        ctxs[pair, i * BLOCK : ext] = value
        total = jnp.where(wide, tops[0], tops[1]) + jnp.log(sums)
        total = jnp.transpose(total)
        stat[0, :, i * BLOCK : ext] = jnp.concatenate([total[0:1], total[64:65]] * 4, axis=0)

    @pl.when(pair == 3)
    def _():
        copy.wait()
        for side, out in ((1 - core, send), (core, own)):
            for i in range(2):
                at = rows(2 * side + i, BLOCK)
                whole = jnp.concatenate([ctxs[p, at] for p in range(4)], axis=1)
                out[i * BLOCK : (i + 1) * BLOCK] = nn(whole, wos[...]).astype(out.dtype)


def call_forward(ids, q, k, v, w_o):
    pair = pl.BlockSpec((1024, 128), lambda p: (0, p))
    return pl.pallas_call(
        forward_kernel,
        grid=(4,),
        out_shape=(
            shape(1024, HALF),
            shape(4, 8, 1024, dtype=f32),
            shape(HALF, 1024, dtype=f32),
            shape(HALF, 1024),
        ),
        in_specs=[SMEM, pair, pair, pair, HBM],
        out_specs=(
            pair,
            pl.BlockSpec((1, 8, 1024), lambda p: (p, 0, 0)),
            pl.BlockSpec((HALF, 1024), lambda p: (0, 0)),
            pl.BlockSpec((HALF, 1024), lambda p: (0, 0)),
        ),
        scratch_shapes=[
            pltpu.VMEM((4, 1024, 128), bf16),
            pltpu.VMEM((HALF, 1024), bf16),
            pltpu.SemaphoreType.DMA((1,)),
        ],
        compiler_params=params(),
        name="attention",
    )(ids, q, k, v, w_o)


def backward_kernel(
    ids, q, k, v, ctx, stat, w_o, g_own, g_other, dq, dk, dv, grads, acc_k, acc_v, gs, sems
):
    core = ids[0]

    @pl.when(pl.program_id(0) == 0)
    def _():
        go = Copies(sems)
        arrive = [
            go.start(g_own, gs.at[rows(core, HALF)]),
            go.start(g_other, gs.at[rows(1 - core, HALF)]),
        ]
        wait_all(arrive)

    for i in range(4):
        at = slice(i * BLOCK, (i + 1) * BLOCK)
        grads[at] = nt(gs[at], w_o[...]).astype(bf16)
    keys = k[...]
    values = v[...]
    product = grads[...].astype(f32) * ctx[...].astype(f32)
    high = product.astype(bf16)
    rest = (product - high.astype(f32)).astype(bf16)
    r = lax.broadcasted_iota(jnp.int32, (16, 128), 0)
    s = lax.broadcasted_iota(jnp.int32, (16, 128), 1)
    pick = jnp.where((s < 64) == (lax.rem(r, 2) == 0), 1.0, 0.0).astype(bf16)
    inner = nt(pick, high) + nt(pick, rest)
    acc_k[...] = jnp.zeros_like(acc_k)
    acc_v[...] = jnp.zeros_like(acc_v)
    for i in range(4):
        ext = (i + 1) * BLOCK
        cols = slice(i * BLOCK, ext)
        query = q[cols]
        grad = grads[cols]
        mine = low_half(query)
        zero = jnp.zeros_like(query)
        new_q = []
        for a in range(2):
            if a == 0:
                part, part_grad = jnp.where(mine, query, zero), jnp.where(mine, grad, zero)
            else:
                part, part_grad = jnp.where(mine, zero, query), jnp.where(mine, zero, grad)
            scores = nt(keys[:ext], part)
            probs = jnp.exp(scores - stat[0, a : a + 1, cols])
            last = probs[i * BLOCK :]
            r = lax.broadcasted_iota(jnp.int32, last.shape, 0)
            s = lax.broadcasted_iota(jnp.int32, last.shape, 1)
            last = jnp.where(r <= s, last, 0.0)
            probs = jnp.concatenate([probs[: i * BLOCK], last], axis=0) if i else last
            grad_probs = nt(values[:ext], part_grad)
            grad_scores = (probs * (grad_probs - inner[a : a + 1, cols])).astype(bf16)
            acc_v[:ext] += nn(probs.astype(bf16), part_grad)
            acc_k[:ext] += nn(grad_scores, part)
            new_q.append(tn(grad_scores, keys[:ext]))
        both = jnp.where(low_half(new_q[0]), new_q[0], new_q[1])
        dq[cols] = (both * 0.125).astype(bf16)
    dk[...] = acc_k[...].astype(bf16)
    dv[...] = acc_v[...].astype(bf16)


def call_backward(ids, q, k, v, ctx, stat, w_o, g_own, g_other):
    pair = pl.BlockSpec((1024, 128), lambda p: (0, p))
    return pl.pallas_call(
        backward_kernel,
        grid=(4,),
        out_shape=(shape(1024, HALF),) * 3,
        in_specs=[
            SMEM,
            pair,
            pair,
            pair,
            pair,
            pl.BlockSpec((1, 8, 1024), lambda p: (p, 0, 0)),
            pl.BlockSpec((128, 1024), lambda p: (p, 0)),
            HBM,
            HBM,
        ],
        out_specs=(pair,) * 3,
        scratch_shapes=[
            pltpu.VMEM((1024, 128), bf16),
            pltpu.VMEM((1024, 128), f32),
            pltpu.VMEM((1024, 128), f32),
            pltpu.VMEM((1024, 1024), bf16),
            pltpu.SemaphoreType.DMA((2,)),
        ],
        compiler_params=params(),
        name="attention_back",
    )(ids, q, k, v, ctx, stat, w_o, g_own, g_other)


def start_tokens(go, pair, target, z):
    return [go.start(ref, target.at[parity(z, k)]) for k, ref in enumerate(pair)]


def middle_kernel(
    ids, own, other, x0, x1, bias, gain, shift, middle, normed, owns, others, xs, mids, ns, sems
):
    go = Copies(sems)
    tokens = start_tokens(go, (x0, x1), xs, ids[1])
    parts = []
    for i in range(2):
        at = slice(i * BLOCK, (i + 1) * BLOCK)
        parts.append([go.start(own.at[at], owns.at[i]), go.start(other.at[at], others.at[i])])
    wait_all(tokens)
    leave = []
    for i in range(2):
        at = slice(i * BLOCK, (i + 1) * BLOCK)
        wait_all(parts[i])
        value = owns[i] + others[i].astype(f32) + xs[i].astype(f32) + bias[2:3]
        mids[i] = value
        leave.append(go.start(mids.at[i], middle.at[at]))
        hat, _ = center_scale(value)
        ns[i] = (hat * gain[1:2] + shift[1:2]).astype(bf16)
        leave.append(go.start(ns.at[i], normed.at[at]))
    wait_all(leave)


def call_middle(ids, own, other, x_own, bias, gain, shift):
    return pl.pallas_call(
        middle_kernel,
        out_shape=(shape(HALF, 1024, dtype=f32), shape(HALF, 1024)),
        in_specs=[SMEM] + [HBM] * 4 + [VMEM] * 3,
        out_specs=(HBM, HBM),
        scratch_shapes=[
            pltpu.VMEM((2, BLOCK, 1024), f32),
            pltpu.VMEM((2, BLOCK, 1024), bf16),
            pltpu.VMEM((2, BLOCK, 1024), bf16),
            pltpu.VMEM((2, BLOCK, 1024), f32),
            pltpu.VMEM((2, BLOCK, 1024), bf16),
            pltpu.SemaphoreType.DMA((10,)),
        ],
        compiler_params=params(),
        name="middle",
    )(ids, own, other, *x_own, bias, gain, shift)


def hidden_kernel(
    ids, n_own, n_other, w0, w1, w2, w3t, w3b, bias,
    active, slope, w_out, ns, ws, acts, slopes, sems,
):
    core, chip = ids[0], ids[2]
    go = Copies(sems)
    arrive = [
        go.start(n_own, ns.at[rows(core, HALF)]),
        go.start(n_other, ns.at[rows(1 - core, HALF)]),
    ]
    weights = []
    for r, ref in enumerate((w0, w1, w2, (w3t, w3b))):
        for p in range(4):
            part = ref.at[p] if r < 3 else ref[p // 2].at[p % 2]
            weights += start_sides(go, part, ws.at[p], chip ^ r, core, p)
    wait_all(arrive)
    leave = []
    for p in range(4):
        wait_all([copy for at, copy in weights if at == p])
        leave.append(go.start(ws.at[p], w_out.at[p]))
        shift = bias[pl.ds(2 * p + core, 1)]
        for i in range(4):
            at = slice(i * BLOCK, (i + 1) * BLOCK)
            h = nn(ns[at], ws[p]) + shift
            square = h * h
            t = jnp.tanh(h * (GELU_A + (GELU_A * GELU_B) * square))
            lift = 0.5 + 0.5 * t
            acts[p, at] = (h * lift).astype(bf16)
            inner = GELU_A + (3.0 * GELU_A * GELU_B) * square
            slopes[p, at] = (lift + (0.5 * h) * (1.0 - t * t) * inner).astype(bf16)
        leave.append(go.start(acts.at[p], active.at[p]))
        leave.append(go.start(slopes.at[p], slope.at[p]))
    wait_all(leave)


def call_hidden(ids, n_own, n_other, pieces, bias):
    return pl.pallas_call(
        hidden_kernel,
        out_shape=(shape(4, 1024, HALF),) * 3,
        in_specs=[SMEM] + [HBM] * 7 + [VMEM],
        out_specs=(HBM,) * 3,
        scratch_shapes=[pltpu.VMEM((1024, 1024), bf16)]
        + [pltpu.VMEM((4, 1024, HALF), bf16)] * 3
        + [pltpu.SemaphoreType.DMA((46,))],
        compiler_params=params(),
        name="hidden",
    )(ids, n_own, n_other, *pieces, bias)


def start_grads(go, ids, g_own, g_other, gs):
    core, z = ids[0], ids[1]
    return [
        go.start(ref, gs.at[2 * side + parity(z, k)])
        for side, pair in ((core, g_own), (1 - core, g_other))
        for k, ref in enumerate(pair)
    ]


def feed_kernel(steps, first, *refs):
    n = len(steps)
    ids, g0, g1, g2, g3, active, slope, w_in = refs[:8]
    pieces, refs = refs[8 : 8 + n], refs[8 + n :]
    if not first:
        old, refs = refs[:2], refs[2:]
    result, grad, gs, acts, slopes, w_ins, w_outs, res_acc, grad_acc, sems = refs
    chip = ids[2]
    go = Copies(sems)
    tokens = start_grads(go, ids, (g0, g1), (g2, g3), gs)
    copies = []
    for at, r in enumerate(steps):
        copies.append(
            [
                go.start(pieces[at], w_outs.at[at]),
                go.start(slope.at[chip ^ r], slopes.at[at]),
                go.start(w_in.at[chip ^ r], w_ins.at[at]),
                go.start(active.at[chip ^ r], acts.at[at]),
            ]
        )
    if not first:
        loads = []
        for i in range(4):
            tok = slice(i * BLOCK, (i + 1) * BLOCK)
            loads.append(
                [
                    go.start(old[0].at[tok], res_acc.at[tok]),
                    go.start(old[1].at[tok], grad_acc.at[tok]),
                ]
            )
    wait_all(tokens)
    for at in range(n):
        wait_all(copies[at])
    leave = []
    for i in range(4):
        tok = slice(i * BLOCK, (i + 1) * BLOCK)
        more = out = None
        for at in range(n):
            back = nt(gs[i], w_outs[at]) * slopes[at, tok].astype(f32)
            term = nt(back.astype(bf16), w_ins[at])
            more = term if more is None else more + term
            term = nn(acts[at, tok], w_outs[at])
            out = term if out is None else out + term
        if not first:
            wait_all(loads[i])
            more += grad_acc[tok]
            out += res_acc[tok]
        grad_acc[tok] = more
        res_acc[tok] = out
        leave.append(go.start(res_acc.at[tok], result.at[tok]))
        leave.append(go.start(grad_acc.at[tok], grad.at[tok]))
    wait_all(leave)


def call_feed(ids, steps, g_own, g_other, active, slope, w_in, pieces, old=()):
    n = len(steps)
    return pl.pallas_call(
        functools.partial(feed_kernel, steps, not old),
        out_shape=(shape(1024, 1024, dtype=f32),) * 2,
        in_specs=[SMEM] + [HBM] * (7 + n + len(old)),
        out_specs=(HBM, HBM),
        scratch_shapes=[
            pltpu.VMEM((4, BLOCK, 1024), bf16),
            pltpu.VMEM((n, 1024, HALF), bf16),
            pltpu.VMEM((n, 1024, HALF), bf16),
            pltpu.VMEM((n, 1024, HALF), bf16),
            pltpu.VMEM((n, HALF, 1024), bf16),
            pltpu.VMEM((1024, 1024), f32),
            pltpu.VMEM((1024, 1024), f32),
            pltpu.SemaphoreType.DMA((4 + 4 * n + 16,)),
        ],
        compiler_params=params(),
        name="feed",
    )(ids, *g_own, *g_other, active, slope, w_in, *pieces, *old)


def far_send_kernel(
    ids, g0, g1, slope, w_in, top, low, old, out, gs, slopes, w_ins, w_outs, olds, outs, sems
):
    core, z, chip = ids[0], ids[1], ids[2]
    go = Copies(sems)
    arrive = start_tokens(go, (g0, g1), gs, z)
    arrive.append(go.start(top, w_outs.at[:BLOCK]))
    arrive.append(go.start(low, w_outs.at[BLOCK:]))
    arrive.append(go.start(slope.at[chip ^ 3, rows(1 - core, HALF)], slopes))
    arrive.append(go.start(w_in.at[chip ^ 3], w_ins))
    load = go.start(old.at[rows(1 - core, HALF)], olds)
    wait_all(arrive)
    leave = []
    for i in range(2):
        tok = slice(i * BLOCK, (i + 1) * BLOCK)
        back = nt(gs[i], w_outs[...]) * slopes[tok].astype(f32)
        more = nt(back.astype(bf16), w_ins[...])
        if i == 0:
            load.wait()
        outs[tok] = (more + olds[tok]).astype(bf16)
        leave.append(go.start(outs.at[tok], out.at[tok]))
    wait_all(leave)


def call_far_send(ids, g_other, slope, w_in, far, old):
    return pl.pallas_call(
        far_send_kernel,
        out_shape=shape(HALF, 1024),
        in_specs=[SMEM] + [HBM] * 7,
        out_specs=HBM,
        scratch_shapes=[
            pltpu.VMEM((2, BLOCK, 1024), bf16),
            pltpu.VMEM((HALF, HALF), bf16),
            pltpu.VMEM((1024, HALF), bf16),
            pltpu.VMEM((HALF, 1024), bf16),
            pltpu.VMEM((HALF, 1024), f32),
            pltpu.VMEM((HALF, 1024), bf16),
            pltpu.SemaphoreType.DMA((9,)),
        ],
        compiler_params=params(),
        name="far_send",
    )(ids, *g_other, slope, w_in, *far, old)


def far_own_kernel(
    ids, g0, g1, slope, w_in, top, low, old, other, middle, gain, grad_out, low_out,
    gs, slopes, w_ins, w_outs, olds, others, mids, grads, lows, sems,
):
    core, z, chip = ids[0], ids[1], ids[2]
    go = Copies(sems)
    arrive = start_tokens(go, (g0, g1), gs, z)
    arrive.append(go.start(top, w_outs.at[:BLOCK]))
    arrive.append(go.start(low, w_outs.at[BLOCK:]))
    arrive.append(go.start(slope.at[chip ^ 3, rows(core, HALF)], slopes))
    arrive.append(go.start(w_in.at[chip ^ 3], w_ins))
    loads = [
        go.start(old.at[rows(core, HALF)], olds),
        go.start(other, others),
        go.start(middle, mids),
    ]
    wait_all(arrive)
    leave = []
    for i in range(2):
        tok = slice(i * BLOCK, (i + 1) * BLOCK)
        back = nt(gs[i], w_outs[...]) * slopes[tok].astype(f32)
        more = nt(back.astype(bf16), w_ins[...])
        if i == 0:
            wait_all(loads)
        more += olds[tok] + others[tok].astype(f32)
        hat, inverse = center_scale(mids[tok])
        value = gs[i].astype(f32) + norm_back(hat, inverse, more * gain[1:2])
        grads[tok] = value
        lows[tok] = value.astype(bf16)
        leave.append(go.start(grads.at[tok], grad_out.at[tok]))
        leave.append(go.start(lows.at[tok], low_out.at[tok]))
    wait_all(leave)


def call_far_own(ids, g_own, slope, w_in, far, old, other, middle, gain):
    return pl.pallas_call(
        far_own_kernel,
        out_shape=(shape(HALF, 1024, dtype=f32), shape(HALF, 1024)),
        in_specs=[SMEM] + [HBM] * 9 + [VMEM],
        out_specs=(HBM, HBM),
        scratch_shapes=[
            pltpu.VMEM((2, BLOCK, 1024), bf16),
            pltpu.VMEM((HALF, HALF), bf16),
            pltpu.VMEM((1024, HALF), bf16),
            pltpu.VMEM((HALF, 1024), bf16),
            pltpu.VMEM((HALF, 1024), f32),
            pltpu.VMEM((HALF, 1024), bf16),
            pltpu.VMEM((HALF, 1024), f32),
            pltpu.VMEM((HALF, 1024), f32),
            pltpu.VMEM((HALF, 1024), bf16),
            pltpu.SemaphoreType.DMA((13,)),
        ],
        compiler_params=params(),
        name="far_own",
    )(ids, *g_own, slope, w_in, *far, old, other, middle, gain)


def far_result_kernel(
    ids, active, top, low, old, own, send, acts, w_outs, olds, owns, sends, sems
):
    core, chip = ids[0], ids[2]
    go = Copies(sems)
    arrive = [
        go.start(top, w_outs.at[:BLOCK]),
        go.start(low, w_outs.at[BLOCK:]),
        go.start(active.at[chip ^ 3], acts),
    ]
    load = go.start(old, olds)
    wait_all(arrive)
    load.wait()
    leave = []
    for side, values, out in ((1 - core, sends, send), (core, owns, own)):
        for i in range(2):
            at = rows(2 * side + i, BLOCK)
            tok = slice(i * BLOCK, (i + 1) * BLOCK)
            values[tok] = (olds[at] + nn(acts[at], w_outs[...])).astype(values.dtype)
            leave.append(go.start(values.at[tok], out.at[tok]))
    wait_all(leave)


def call_far_result(ids, active, far, old):
    return pl.pallas_call(
        far_result_kernel,
        out_shape=(shape(HALF, 1024, dtype=f32), shape(HALF, 1024)),
        in_specs=[SMEM] + [HBM] * 4,
        out_specs=(HBM, HBM),
        scratch_shapes=[
            pltpu.VMEM((1024, HALF), bf16),
            pltpu.VMEM((HALF, 1024), bf16),
            pltpu.VMEM((1024, 1024), f32),
            pltpu.VMEM((HALF, 1024), f32),
            pltpu.VMEM((HALF, 1024), bf16),
            pltpu.SemaphoreType.DMA((8,)),
        ],
        compiler_params=params(),
        name="far_result",
    )(ids, active, *far, old)


def mixed_kernel(ids, own, other, middle, bias, out0, out1):
    z = ids[1]
    for k, out in enumerate((out0, out1)):
        tok = rows(parity(z, k), BLOCK)
        value = own[tok] + other[tok].astype(f32) + middle[tok] + bias[3:4]
        out[...] = value.astype(bf16)


def call_mixed(ids, own, other, middle, bias):
    return pl.pallas_call(
        mixed_kernel,
        out_shape=(shape(BLOCK, 1024),) * 2,
        in_specs=[SMEM] + [VMEM] * 4,
        out_specs=(VMEM, VMEM),
        compiler_params=params(),
        name="mixed",
    )(ids, own, other, middle, bias)


def qkv_back_kernel(
    ids, dq, dk, dv, w, n_own, n_other, down, down_w, up_w, own, send, g_norm, g_up,
    qs, ks, vs, ws, ns, downs, owns, sends, tilt_acc, up_acc, sems,
):
    core = ids[0]
    go = Copies(sems)
    weights = go.start(w, ws)
    later = [
        go.start(n_own, ns.at[rows(core, HALF)]),
        go.start(n_other, ns.at[rows(1 - core, HALF)]),
        go.start(down, downs),
    ]
    order = [2 * side + i for side in (1 - core, core) for i in range(2)]
    grads = [
        [go.start(ref.at[rows(i, BLOCK)], to.at[at]) for ref, to in ((dq, qs), (dk, ks), (dv, vs))]
        for at, i in enumerate(order)
    ]
    weights.wait()
    leave = []
    for at in range(4):
        wait_all(grads[at])
        gq, gk, gv = qs[at], ks[at], vs[at]
        tilt = (nt(gq, up_w[:, :HALF]) + nt(gv, up_w[:, 2 * HALF :])).astype(bf16)
        value = nt(gq, ws[0]) + nt(gk, ws[1]) + nt(gv, ws[2]) + nn(tilt, down_w[...])
        values, out = (sends, send) if at < 2 else (owns, own)
        tok = slice(at % 2 * BLOCK, (at % 2 + 1) * BLOCK)
        values[tok] = value.astype(bf16)
        leave.append(go.start(values.at[tok], out.at[tok]))
        if at == 0:
            wait_all(later)
        here = rows(order[at], BLOCK)
        tilt_term = tn(tilt, ns[here])
        up_term = jnp.concatenate([tn(downs[here], gq), tn(downs[here], gv)], axis=1)
        if at == 0:
            tilt_acc[...] = tilt_term
            up_acc[...] = up_term
        else:
            tilt_acc[...] += tilt_term
            up_acc[...] += up_term
    g_norm[...] = tilt_acc[:8]
    g_up[...] = up_acc[:8]
    wait_all(leave)


def call_qkv_back(ids, dq, dk, dv, w, n_own, n_other, down, down_w, up_w):
    return pl.pallas_call(
        qkv_back_kernel,
        out_shape=(
            shape(HALF, 1024),
            shape(HALF, 1024),
            shape(8, 1024, dtype=f32),
            shape(8, 1024, dtype=f32),
        ),
        in_specs=[SMEM] + [HBM] * 7 + [VMEM] * 2,
        out_specs=(HBM, HBM, VMEM, VMEM),
        scratch_shapes=[pltpu.VMEM((4, BLOCK, HALF), bf16)] * 3
        + [
            pltpu.VMEM((3, 1024, HALF), bf16),
            pltpu.VMEM((1024, 1024), bf16),
            pltpu.VMEM((1024, 128), bf16),
            pltpu.VMEM((HALF, 1024), bf16),
            pltpu.VMEM((HALF, 1024), bf16),
            pltpu.VMEM((128, 1024), f32),
            pltpu.VMEM((128, 1024), f32),
            pltpu.SemaphoreType.DMA((20,)),
        ],
        compiler_params=params(),
        name="qkv_back",
    )(ids, dq, dk, dv, w, n_own, n_other, down, down_w, up_w)


def input_grad_kernel(ids, x0, x1, own, other, grad_middle, gain, out0, out1):
    z = ids[1]
    for k, (x, out) in enumerate(((x0, out0), (x1, out1))):
        tok = rows(parity(z, k), BLOCK)
        grad = own[tok].astype(f32) + other[tok].astype(f32)
        hat, inverse = center_scale(x[...].astype(f32))
        out[...] = (grad_middle[tok] + norm_back(hat, inverse, grad * gain[0:1])).astype(bf16)


def call_input_grad(ids, x_own, own, other, grad_middle, gain):
    return pl.pallas_call(
        input_grad_kernel,
        out_shape=(shape(BLOCK, 1024),) * 2,
        in_specs=[SMEM] + [VMEM] * 6,
        out_specs=(VMEM,) * 2,
        compiler_params=params(),
        name="input_grad",
    )(ids, *x_own, own, other, grad_middle, gain)


def to_core(value):
    return lax.ppermute(value, "core", SWAP)


def exchange(z, pair):
    sent = []
    for k in range(2):
        perm = [
            (4 * core + at, 4 * (at // 2) + 2 * core + (at + k) % 2)
            for core in range(2)
            for at in range(4)
        ]
        sent.append(lax.ppermute(pair[k], ("core", "seq"), perm))
    return sent


def by_parity(z, pair):
    even = lax.rem(z, 2) == 0
    return jnp.where(even, pair[0], pair[1]), jnp.where(even, pair[1], pair[0])


def after(value, *others):
    return lax.optimization_barrier((value, *others))[0]


def gather_near(shard):
    return [shard, lax.ppermute(shard, "x", SWAP), lax.ppermute(shard, "y", SWAP)]


def halves(near):
    _, by_x, by_y = near
    half = by_x.shape[0] // 2
    return by_x[:half], by_y[half:]


def gather_far(near, parts):
    return near + [lax.ppermute(parts[0], "y", SWAP), lax.ppermute(parts[1], "x", SWAP)]


def on_chip(
    inputs,
    out_grad,
    norm_gain,
    norm_bias,
    proj_bias,
    fc_bias,
    qkv_weight,
    out_weight,
    feed_input_weight,
    proj_weight,
    adapters,
    first_moment,
    second_moment,
):
    core = lax.axis_index("core")
    z = lax.axis_index("seq")
    chip = 2 * lax.axis_index("y") + lax.axis_index("x")
    ids = jnp.stack([core, z, chip]).astype(jnp.int32)

    def choose(value, axis):
        first, second = lax.index_in_dim(value, 0, axis, False), lax.index_in_dim(value, 1, axis, False)
        return jnp.where(core == 0, first, second), jnp.where(core == 0, second, first)

    qkv_own, qkv_send = choose(qkv_weight.reshape(128, 3, 4, 2, 128), 3)
    qkv_own = qkv_own.transpose(1, 0, 2, 3).reshape(3, 128, HALF)
    qkv_send = qkv_send.transpose(1, 0, 2, 3).reshape(3, 128, HALF)
    qkv_got = to_core(qkv_send)
    x_own = exchange(z, by_parity(z, after((inputs[0], inputs[1]), qkv_send)))
    out_part = out_weight.reshape(128, 2, HALF).transpose(1, 0, 2).reshape(1, BLOCK, HALF)
    first_shard = jnp.concatenate(
        [jnp.concatenate([qkv_own, qkv_got], axis=1), after(out_part, qkv_send)], axis=0
    )
    first_near = gather_near(first_shard)
    in_own, in_send = choose(after(feed_input_weight, first_shard).reshape(128, 4, 2, HALF), 2)
    in_own, in_send = in_own.transpose(1, 0, 2), in_send.transpose(1, 0, 2)
    in_shard = jnp.concatenate([in_own, to_core(in_send)], axis=1)
    n_own = call_norm(ids, x_own, norm_gain, norm_bias)
    n_other = to_core(n_own)
    first_halves = halves(first_near)
    first_pieces = gather_far(first_near, first_halves)
    in_near = gather_near(after(in_shard, *first_halves))

    def columns(value):
        lead = value.shape[0]
        return choose(value.reshape(lead, 4, 2, 128), 2)[0].reshape(lead, HALF)

    scale = adapter_alpha / ADAPTER_RANK
    up_q, up_v = scale * columns(adapters[1]), scale * columns(adapters[3])
    up_w = jnp.zeros((128, 1536), f32)
    up_w = up_w.at[0:4, :HALF].set(up_q).at[4:8, 2 * HALF :].set(up_v).astype(bf16)
    down_w = jnp.concatenate([adapters[0], adapters[2], jnp.zeros((120, 1024), f32)], axis=0)
    down_w = down_w.astype(bf16)
    head_bias = columns(proj_bias[:2])
    qkv_bias = jnp.concatenate([head_bias[0], jnp.zeros((HALF,), f32), head_bias[1]])[None]

    q, k, v, down, w_qkv, w_o = call_qkv(ids, n_own, n_other, first_pieces, down_w, up_w, qkv_bias)
    g_own = exchange(z, after(by_parity(z, (out_grad[0], out_grad[1])), q))
    ctx, stat, attn_own, attn_send = call_forward(ids, q, k, v, w_o)
    attn_other = to_core(attn_send)
    middle, n2_own = call_middle(
        ids, attn_own, attn_other, x_own, proj_bias, norm_gain, norm_bias
    )
    n2_other = to_core(n2_own)
    in_near = after(in_near, ctx)
    in_halves = halves(in_near)
    in_pieces = gather_far(in_near, in_halves)
    proj_near = gather_near(after(proj_weight, *in_halves))
    g_other = [to_core(part) for part in g_own]
    active, slope, w_in = call_hidden(ids, n2_own, n2_other, in_pieces, fc_bias.reshape(8, HALF))
    old = call_feed(ids, (0,), g_own, g_other, active, slope, w_in, proj_near[:1])
    proj_near = after(proj_near, *old)
    proj_halves = halves(proj_near)
    far = gather_far(proj_near, proj_halves)[3:]
    near = after(proj_near[1:], *proj_halves)
    result, grad = call_feed(ids, (1, 2), g_own, g_other, active, slope, w_in, near, old)
    grad_send = call_far_send(ids, g_other, slope, w_in, far, grad)
    grad_other = to_core(grad_send)
    result_own, result_send = call_far_result(ids, active, after(far, grad_send), result)
    result_other = to_core(result_send)
    grad_other = after(grad_other, result_own)
    grad_middle, low_own = call_far_own(
        ids, g_own, slope, w_in, far, grad, grad_other, middle, norm_gain
    )
    low_other = to_core(low_own)
    mixed = call_mixed(ids, after(result_own, low_own), result_other, middle, proj_bias)
    low_other = after(low_other, *mixed)
    mixed = exchange(z, mixed)
    dq, dk, dv = call_backward(ids, q, k, v, ctx, stat, w_o, low_own, low_other)
    mixed = after(mixed, dq)
    dq = after(dq, *mixed)
    own, send, g_norm, g_up = call_qkv_back(
        ids, dq, dk, dv, w_qkv, n_own, n_other, down, down_w, up_w
    )
    other = to_core(send)
    grad_in = exchange(z, call_input_grad(ids, x_own, own, other, grad_middle, norm_gain))

    def spread(part):
        part = part.reshape(4, 4, 1, 128)
        place = lax.broadcasted_iota(jnp.int32, (1, 1, 2, 1), 2)
        return jnp.where(place == core, part, 0.0).reshape(4, 1024)

    total = jnp.stack(
        [
            g_norm[:4],
            scale * spread(g_up[:4, :HALF]),
            g_norm[4:],
            scale * spread(g_up[4:, HALF:]),
        ]
    )
    for axis, perm in (
        ("core", SWAP),
        ("x", SWAP),
        ("y", SWAP),
        ("seq", ((0, 1), (1, 0), (2, 3), (3, 2))),
        ("seq", ((0, 2), (2, 0), (1, 3), (3, 1))),
    ):
        total = total + lax.ppermute(total, axis, perm)
    grad_norm = jnp.sqrt(jnp.sum(total * total))
    clipped, new_weight, new_first, new_second = adam_update(
        total, adapters, first_moment, second_moment, grad_norm
    )
    mixed = jnp.stack(by_parity(z, mixed))
    grad_input = jnp.stack(by_parity(z, grad_in))
    return (mixed, grad_input, clipped, grad_norm, new_weight, new_first, new_second)


def solution(mesh):
    sizes = dict(mesh.shape)
    if sizes["dp"] == 8 and sizes["seq"] == 4:
        plane = Mesh(mesh.devices.reshape(2, 2, 2, 4), ("y", "x", "core", "seq"))
        return build(plane, ("y", "x", "core"), on_chip)
    return build(mesh, "dp", on_device)


def build(mesh, dp, step):
    tokens, weight = P(dp, "seq", None), P(dp, None)
    return jax.shard_map(
        step,
        mesh=mesh,
        in_specs=(tokens, tokens) + (P(),) * 4 + (weight,) * 4 + (P(),) * 3,
        out_specs=(tokens, tokens) + (P(),) * 5,
        check_vma=False,
    )
```

```python
import functools
import math

import jax
import jax.numpy as jnp
from jax import lax
from jax.experimental import pallas as pl
from jax.experimental.pallas import tpu as pltpu
from jax.sharding import Mesh
from jax.sharding import PartitionSpec as P

HEAD_DIM = 64
ADAPTER_RANK = 4
STEP = 10


highest = lax.Precision.HIGHEST
adapter_alpha = 32.0
beta_one = 0.9
beta_two = 0.999
adam_eps = 1e-08
decay_rate = 0.01
learning_rate = 0.02
clip_bound = 1.0
norm_eps = 1e-05


def layer_norm(value, gain, shift):
    center = jnp.mean(value, axis=-1, keepdims=True)
    centered = value - center
    spread = jnp.mean(centered * centered, axis=-1, keepdims=True)
    return centered * lax.rsqrt(spread + norm_eps) * gain + shift


def dot_trans(left, right):
    return lax.dot_general(
        left, right, (((1,), (1,)), ((), ())), preferred_element_type=jnp.float32
    )


def dot_first(left, right):
    return lax.dot_general(
        left, right, (((0,), (0,)), ((), ())), precision=highest, preferred_element_type=jnp.float32
    )


def adam_update(grad, weight, first, second, norm):
    scale_factor = clip_bound / jnp.maximum(norm, clip_bound)
    clipped = grad * scale_factor
    new_first = beta_one * first + (1.0 - beta_one) * clipped
    new_second = beta_two * second + (1.0 - beta_two) * clipped * clipped
    first_hat = new_first / (1.0 - beta_one**STEP)
    second_hat = new_second / (1.0 - beta_two**STEP)
    new_weight = weight - learning_rate * (
        first_hat / (jnp.sqrt(second_hat) + adam_eps) + decay_rate * weight
    )
    return (clipped, new_weight, new_first, new_second)


def split_heads(packed):
    length = packed.shape[0]
    local_heads = packed.shape[-1] // HEAD_DIM
    query = packed[:, 0, 0].reshape(length, local_heads, HEAD_DIM)
    keys = packed[:, 1, 0].reshape(length, local_heads, HEAD_DIM)
    values = packed[:, 2, 0].reshape(length, local_heads, HEAD_DIM)
    return (query, keys, values)


def doc_forward(packed):
    length = packed.shape[0]
    local_width = packed.shape[-1]
    query, keys, values = split_heads(packed)
    local_heads = query.shape[1]
    span = min(512, length)
    blocks = length // span
    scale = 1.0 / math.sqrt(HEAD_DIM)
    starts = jnp.arange(blocks, dtype=jnp.int32) * span

    def visit(pieces):
        query_block, start = pieces
        scores = (
            jnp.einsum("qhd,khd->hqk", query_block, keys, preferred_element_type=jnp.float32)
            * scale
        )
        causal = (start + jnp.arange(span))[:, None] >= jnp.arange(length)[None, :]
        masked = jnp.where(causal[None], scores, -1e30)
        summit = jnp.max(masked, axis=-1, keepdims=True)
        expo = jnp.where(causal[None], jnp.exp(masked - summit), 0.0)
        totals = jnp.sum(expo, axis=-1, keepdims=True)
        weights = (expo / totals).astype(jnp.bfloat16)
        context = jnp.einsum(
            "hqk,khd->qhd", weights, values, preferred_element_type=jnp.float32
        ).astype(jnp.bfloat16)
        return (context, summit[..., 0] + jnp.log(totals[..., 0]))

    context, log_total = lax.map(
        visit, (query.reshape(blocks, span, local_heads, HEAD_DIM), starts)
    )
    return (context.reshape(length, 1, local_width), log_total)


def doc_backward(args):
    packed, grad_context, log_total = args
    length = packed.shape[0]
    local_width = packed.shape[-1]
    query, keys, values = split_heads(packed)
    local_heads = query.shape[1]
    output_gradient = grad_context[:, 0].reshape(length, local_heads, HEAD_DIM)
    span = min(512, length)
    blocks = length // span
    scale = 1.0 / math.sqrt(HEAD_DIM)
    starts = jnp.arange(blocks, dtype=jnp.int32) * span

    def visit(carry, pieces):
        grad_keys, grad_values = carry
        query_block, grad_block, total_block, start = pieces
        scores = (
            jnp.einsum("qhd,khd->hqk", query_block, keys, preferred_element_type=jnp.float32)
            * scale
        )
        causal = (start + jnp.arange(span))[:, None] >= jnp.arange(length)[None, :]
        masked = jnp.where(causal[None], scores, -1e30)
        probs = jnp.where(causal[None], jnp.exp(masked - total_block[:, :, None]), 0.0)
        weights = probs.astype(jnp.bfloat16)
        grad_probs = jnp.einsum(
            "qhd,khd->hqk", grad_block, values, preferred_element_type=jnp.float32
        )
        inner = jnp.sum(probs * grad_probs, axis=-1, keepdims=True)
        grad_scores = (probs * (grad_probs - inner)).astype(jnp.bfloat16)
        grad_query = (
            jnp.einsum("hqk,khd->qhd", grad_scores, keys, preferred_element_type=jnp.float32)
            * scale
        )
        grad_keys = (
            grad_keys
            + jnp.einsum(
                "hqk,qhd->khd", grad_scores, query_block, preferred_element_type=jnp.float32
            )
            * scale
        )
        grad_values = grad_values + jnp.einsum(
            "hqk,qhd->khd", weights, grad_block, preferred_element_type=jnp.float32
        )
        return ((grad_keys, grad_values), grad_query)

    empty = jnp.zeros((length, local_heads, HEAD_DIM), jnp.float32)
    pieces = (
        query.reshape(blocks, span, local_heads, HEAD_DIM),
        output_gradient.reshape(blocks, span, local_heads, HEAD_DIM),
        log_total,
        starts,
    )
    (grad_keys, grad_values), grad_query = lax.scan(visit, (empty, empty), pieces)
    joined = jnp.stack(
        [
            grad_query.reshape(length, local_width),
            grad_keys.reshape(length, local_width),
            grad_values.reshape(length, local_width),
        ],
        axis=1,
    )
    return joined.astype(jnp.bfloat16)[:, :, None, :]


def on_device(
    inputs,
    out_grad,
    norm_gain,
    norm_bias,
    proj_bias,
    fc_bias,
    qkv_weight,
    out_weight,
    feed_input_weight,
    proj_weight,
    adapters,
    first_moment,
    second_moment,
):
    docs, tokens, width = inputs.shape
    count = docs * tokens
    ranks = lax.axis_size("seq")
    scale_factor = adapter_alpha / ADAPTER_RANK

    def forward(stack):
        qkv_full, out_full, fc_full, proj_full = stack
        flat = inputs.reshape(count, width).astype(jnp.float32)
        normed, norm_one_back = jax.vjp(
            lambda value: layer_norm(value, norm_gain[0], norm_bias[0]), flat
        )
        base = jnp.dot(normed.astype(jnp.bfloat16), qkv_full, preferred_element_type=jnp.float32)
        down_q = jnp.dot(normed, adapters[0].T, precision=highest)
        down_v = jnp.dot(normed, adapters[2].T, precision=highest)
        query = (
            base[:, :width]
            + proj_bias[0]
            + scale_factor * jnp.dot(down_q, adapters[1], precision=highest)
        )
        keys = base[:, width : 2 * width]
        values = (
            base[:, 2 * width :]
            + proj_bias[1]
            + scale_factor * jnp.dot(down_v, adapters[3], precision=highest)
        )
        joined = (
            jnp.concatenate([query, keys, values], axis=1)
            .astype(jnp.bfloat16)
            .reshape(docs, tokens, 3, ranks, width // ranks)
        )
        spread = lax.all_to_all(joined, "seq", split_axis=3, concat_axis=1, tiled=True)
        context, log_total = lax.map(doc_forward, spread)
        context = lax.all_to_all(context, "seq", split_axis=1, concat_axis=2, tiled=True).reshape(
            count, width
        )
        middle = (
            flat + jnp.dot(context, out_full, preferred_element_type=jnp.float32) + proj_bias[2]
        )
        normed_two, norm_two_back = jax.vjp(
            lambda value: layer_norm(value, norm_gain[1], norm_bias[1]), middle
        )
        hidden = (
            jnp.dot(normed_two.astype(jnp.bfloat16), fc_full, preferred_element_type=jnp.float32)
            + fc_bias
        )
        active, gelu_back = jax.vjp(lambda value: jax.nn.gelu(value, approximate=True), hidden)
        result = (
            middle
            + jnp.dot(active.astype(jnp.bfloat16), proj_full, preferred_element_type=jnp.float32)
            + proj_bias[3]
        )
        return (
            result,
            (normed, down_q, down_v, norm_one_back, spread, log_total, norm_two_back, gelu_back),
        )

    stack = (
        lax.all_gather(qkv_weight, "dp", axis=0, tiled=True),
        lax.all_gather(out_weight, "dp", axis=0, tiled=True),
        lax.all_gather(feed_input_weight, "dp", axis=0, tiled=True),
        lax.all_gather(proj_weight, "dp", axis=0, tiled=True),
    )
    result, kept = forward(stack)
    fenced = lax.optimization_barrier((stack, result))
    stack = fenced[0]
    again, kept = forward(stack)
    qkv_full, out_full, fc_full, proj_full = stack
    normed, down_q, down_v, norm_one_back, spread, log_total, norm_two_back, gelu_back = kept
    cotangent = out_grad.reshape(count, width)
    grad_active = dot_trans(cotangent, proj_full)
    grad_hidden = gelu_back(grad_active)[0].astype(jnp.bfloat16)
    grad_normed_two = dot_trans(grad_hidden, fc_full)
    grad_middle = cotangent.astype(jnp.float32) + norm_two_back(grad_normed_two)[0]
    grad_context = dot_trans(grad_middle.astype(jnp.bfloat16), out_full).astype(jnp.bfloat16)
    grad_context = grad_context.reshape(docs, tokens, ranks, width // ranks)
    grad_context = lax.all_to_all(grad_context, "seq", split_axis=2, concat_axis=1, tiled=True)
    grad_joined = lax.map(doc_backward, (spread, grad_context, log_total))
    grad_joined = lax.all_to_all(
        grad_joined, "seq", split_axis=1, concat_axis=3, tiled=True
    ).reshape(count, 3 * width)
    grad_normed = dot_trans(grad_joined, qkv_full)
    grad_query = grad_joined[:, :width].astype(jnp.float32)
    grad_value = grad_joined[:, 2 * width :].astype(jnp.float32)
    tilt_q = scale_factor * jnp.dot(grad_query, adapters[1].T, precision=highest)
    value_adapter_up = scale_factor * jnp.dot(grad_value, adapters[3].T, precision=highest)
    grad_normed = (
        grad_normed
        + jnp.dot(tilt_q, adapters[0], precision=highest)
        + jnp.dot(value_adapter_up, adapters[2], precision=highest)
    )
    grad_input = (
        (grad_middle + norm_one_back(grad_normed)[0])
        .astype(jnp.bfloat16)
        .reshape(docs, tokens, width)
    )
    partial_terms = jnp.stack(
        [
            dot_first(tilt_q, normed),
            scale_factor * dot_first(down_q, grad_query),
            dot_first(value_adapter_up, normed),
            scale_factor * dot_first(down_v, grad_value),
        ]
    )
    total = lax.psum(partial_terms, ("dp", "seq"))
    grad_norm = jnp.sqrt(jnp.sum(total * total))
    clipped, new_weight, new_first, new_second = adam_update(
        total, adapters, first_moment, second_moment, grad_norm
    )
    mixed = result.astype(jnp.bfloat16).reshape(docs, tokens, width)
    return (mixed, grad_input, clipped, grad_norm, new_weight, new_first, new_second)


HALF = 512
BLOCK = 256
VMEM_MIB = 63
SMEM = pl.BlockSpec(memory_space=pltpu.SMEM)
VMEM = pl.BlockSpec(memory_space=pltpu.VMEM)
HBM = pl.BlockSpec(memory_space=pl.ANY)
f32 = jnp.float32
bf16 = jnp.bfloat16
SWAP = ((0, 1), (1, 0))
GELU_A = math.sqrt(2.0 / math.pi)
GELU_B = 0.044715


def nn(left, right):
    return lax.dot_general(left, right, (((1,), (0,)), ((), ())), preferred_element_type=f32)


def nt(left, right):
    return lax.dot_general(left, right, (((1,), (1,)), ((), ())), preferred_element_type=f32)


def tn(left, right):
    return lax.dot_general(left, right, (((0,), (0,)), ((), ())), preferred_element_type=f32)


def shape(*dims, dtype=bf16):
    return jax.ShapeDtypeStruct(dims, dtype)


def params():
    return pltpu.CompilerParams(vmem_limit_bytes=VMEM_MIB * 2**20)


def rows(index, size):
    return pl.ds(pl.multiple_of(index * size, size), size)


def parity(z, k):
    return lax.rem(z + k, 2)


class Copies:
    def __init__(self, sems):
        self.sems = sems
        self.count = 0

    def start(self, source, target):
        copy = pltpu.make_async_copy(source, target, self.sems.at[self.count])
        self.count += 1
        copy.start()
        return copy


def wait_all(copies):
    for copy in copies:
        copy.wait()


def center_scale(x):
    center = jnp.mean(x, axis=-1, keepdims=True)
    centered = x - center
    spread = jnp.mean(centered * centered, axis=-1, keepdims=True)
    inverse = lax.rsqrt(spread + norm_eps)
    return centered * inverse, inverse


def norm_back(hat, inverse, grad):
    first = jnp.mean(grad, axis=-1, keepdims=True)
    second = jnp.mean(grad * hat, axis=-1, keepdims=True)
    return inverse * (grad - first - hat * second)


def cut_kernel(ids, w, w_o, own, send, out_part):
    core = ids[0]
    for p in range(3):
        for i in range(4):
            base = 1024 * p + 256 * i
            to = slice(128 * i, 128 * (i + 1))
            send[p, :, to] = w[:, pl.ds(pl.multiple_of(base + 128 * (1 - core), 128), 128)]
            own[p, :, to] = w[:, pl.ds(pl.multiple_of(base + 128 * core, 128), 128)]
    out_part[0, :128] = w_o[:, :HALF]
    out_part[0, 128:] = w_o[:, HALF:]


def call_cut(ids, w, w_o):
    return pl.pallas_call(
        cut_kernel,
        out_shape=(shape(3, 128, HALF), shape(3, 128, HALF), shape(1, BLOCK, HALF)),
        in_specs=[SMEM, VMEM, VMEM],
        out_specs=(VMEM,) * 3,
        compiler_params=params(),
        name="cut_qkv",
    )(ids, w, w_o)


def cut_feed_kernel(ids, w, own, send):
    core = ids[0]
    for i in range(4):
        send[i] = w[:, pl.ds(pl.multiple_of(1024 * i + HALF * (1 - core), HALF), HALF)]
        own[i] = w[:, pl.ds(pl.multiple_of(1024 * i + HALF * core, HALF), HALF)]


def call_cut_feed(ids, w):
    return pl.pallas_call(
        cut_feed_kernel,
        out_shape=(shape(4, 128, HALF), shape(4, 128, HALF)),
        in_specs=[SMEM, VMEM],
        out_specs=(VMEM,) * 2,
        compiler_params=params(),
        name="cut_feed",
    )(ids, w)


def norm_kernel(ids, m0, m1, gain, shift, out, xs, sems):
    z = ids[1]
    go = Copies(sems)
    arrive = [go.start(ref, xs.at[parity(z, k)]) for k, ref in enumerate((m0, m1))]
    wait_all(arrive)
    for i in range(2):
        hat, _ = center_scale(xs[i].astype(f32))
        out[i * BLOCK : (i + 1) * BLOCK] = (hat * gain[0:1] + shift[0:1]).astype(bf16)


def call_norm(ids, x_own, gain, shift):
    return pl.pallas_call(
        norm_kernel,
        out_shape=shape(HALF, 1024),
        in_specs=[SMEM, HBM, HBM, VMEM, VMEM],
        out_specs=VMEM,
        scratch_shapes=[pltpu.VMEM((2, BLOCK, 1024), bf16), pltpu.SemaphoreType.DMA((2,))],
        compiler_params=params(),
        name="norm",
    )(ids, *x_own, gain, shift)


def start_sides(go, piece, target, chip, core, tag):
    return [
        (tag, go.start(piece.at[:128], target.at[rows(2 * chip + core, 128)])),
        (tag, go.start(piece.at[128:], target.at[rows(2 * chip + 1 - core, 128)])),
    ]


def attend(pair, qs, ks, vs, ctxs, stats):
    keys = ks[pair]
    values = jnp.concatenate([jnp.transpose(vs[pair]), jnp.ones((128, 1024), bf16)], axis=0)
    for i in range(4):
        ext = (i + 1) * BLOCK
        cols = slice(i * BLOCK, ext)
        query = qs[pair, cols]
        low = low_half(query)
        zero = jnp.zeros_like(query)
        parts = []
        for a in range(2):
            part = jnp.where(low, query, zero) if a == 0 else jnp.where(low, zero, query)
            scores = nt(keys[:ext], part)
            last = scores[i * BLOCK :]
            r = lax.broadcasted_iota(jnp.int32, last.shape, 0)
            c = lax.broadcasted_iota(jnp.int32, last.shape, 1)
            last = jnp.where(r <= c, last, -1e30)
            scores = jnp.concatenate([scores[: i * BLOCK], last], axis=0) if i else last
            top = jnp.max(scores, axis=0, keepdims=True)
            expo = jnp.exp(scores - top).astype(bf16)
            wide = nn(values[:, :ext], expo)
            total = wide[128:129]
            parts.append(wide[64 * a : 64 * a + 64] * (1.0 / total))
            stats[pair, a : a + 1, cols] = top + jnp.log(total)
        ctxs[pair, cols] = jnp.transpose(jnp.concatenate(parts, axis=0).astype(bf16))


def first_kernel(
    ids, n_own, n_other, w0, w1, w2, w3t, w3b, down_w, up_w, bias,
    q_out, k_out, v_out, down_out, w_out, o_out, ctx_out, stat_out, own, send,
    ns, ws, os, qs, ks, vs, downs, ctxs, stats, owns, sends, sems,
):
    core, chip = ids[0], ids[2]
    go = Copies(sems)
    arrive = [
        go.start(n_own, ns.at[rows(core, HALF)]),
        go.start(n_other, ns.at[rows(1 - core, HALF)]),
    ]
    weights, outer, leave = [], [], []
    pieces = (w0, w1, w2, (w3t, w3b))
    part = lambda r, p: pieces[r].at[p] if r < 3 else pieces[r][p // 2].at[p % 2]
    for p in range(3):
        for r in range(4):
            weights += start_sides(go, part(r, p), ws.at[p], chip ^ r, core, p)
    for r in range(4):
        for h in range(2):
            outer.append(
                go.start(
                    part(r, 3).at[h * 128 : (h + 1) * 128],
                    os.at[rows(chip ^ r, 128), h * HALF : (h + 1) * HALF],
                )
            )
    wait_all(arrive)
    for p, (to, out) in enumerate(((qs, q_out), (ks, k_out), (vs, v_out))):
        wait_all([copy for at, copy in weights if at == p])
        leave.append(go.start(ws.at[p], w_out.at[p]))
        for i in range(4):
            at = slice(i * BLOCK, (i + 1) * BLOCK)
            value = nn(ns[at], ws[p]) + bias[:, p * HALF : (p + 1) * HALF]
            if p == 0:
                downs[at] = nt(ns[at], down_w[...]).astype(bf16)
            if p != 1:
                value += nn(downs[at], up_w[:, p * HALF : (p + 1) * HALF])
            value = value.astype(bf16)
            if p == 0:
                value = value * jnp.asarray(0.125, bf16)
            for pair in range(4):
                to[pair, at] = value[:, 128 * pair : 128 * (pair + 1)]
        leave.append(go.start(to, out))
    down_out[...] = nt(down_w[:16], ns[...]).astype(bf16)

    @pl.loop(0, 4)
    def _(pair):
        attend(pair, qs, ks, vs, ctxs, stats)

    leave.append(go.start(ctxs, ctx_out))
    leave.append(go.start(stats, stat_out))
    wait_all(outer)
    leave.append(go.start(os, o_out))
    for side, to, out in ((1 - core, sends, send), (core, owns, own)):
        for i in range(2):
            at = rows(2 * side + i, BLOCK)
            tok = slice(i * BLOCK, (i + 1) * BLOCK)
            whole = jnp.concatenate([ctxs[p, at] for p in range(4)], axis=1)
            to[tok] = nn(whole, os[...]).astype(to.dtype)
            leave.append(go.start(to.at[tok], out.at[tok]))
    wait_all(leave)


def call_first(ids, n_own, n_other, pieces, down_w, up_w, bias):
    heads = shape(4, 1024, 128)
    return pl.pallas_call(
        first_kernel,
        out_shape=(
            heads,
            heads,
            heads,
            shape(16, 1024),
            shape(3, 1024, HALF),
            shape(HALF, 1024),
            heads,
            shape(4, 8, 1024, dtype=f32),
            shape(HALF, 1024, dtype=f32),
            shape(HALF, 1024),
        ),
        in_specs=[SMEM] + [HBM] * 7 + [VMEM] * 3,
        out_specs=(HBM,) * 3 + (VMEM,) + (HBM,) * 6,
        scratch_shapes=[
            pltpu.VMEM((1024, 1024), bf16),
            pltpu.VMEM((3, 1024, HALF), bf16),
            pltpu.VMEM((HALF, 1024), bf16),
            pltpu.VMEM((4, 1024, 128), bf16),
            pltpu.VMEM((4, 1024, 128), bf16),
            pltpu.VMEM((4, 1024, 128), bf16),
            pltpu.VMEM((1024, 128), bf16),
            pltpu.VMEM((4, 1024, 128), bf16),
            pltpu.VMEM((4, 8, 1024), f32),
            pltpu.VMEM((HALF, 1024), f32),
            pltpu.VMEM((HALF, 1024), bf16),
            pltpu.SemaphoreType.DMA((50,)),
        ],
        compiler_params=params(),
        name="qkv_attention",
    )(ids, n_own, n_other, *pieces, down_w, up_w, bias)


def attend_back(pair, qs, ks, vs, ctxs, stats, gs, dqs, dks, dvs, acc_k, acc_v):
    keys, values = ks[pair], vs[pair]
    place = pl.ds(pl.multiple_of(pair * 128, 128), 128)
    for i in range(4):
        ext = (i + 1) * BLOCK
        cols = slice(i * BLOCK, ext)
        query, grad = qs[pair, cols], gs[pair, cols]
        low = low_half(query)
        zero = jnp.zeros_like(query)
        product = grad.astype(f32) * ctxs[pair, cols].astype(f32)
        stat = jnp.transpose(stats[pair, :, cols])
        turned_query, turned_grad = jnp.transpose(query), jnp.transpose(grad)
        new_q = []
        for a in range(2):
            pick = (lambda x, y: jnp.where(low, x, y)) if a == 0 else (lambda x, y: jnp.where(low, y, x))
            half = slice(64 * a, 64 * a + 64)
            scores = nt(pick(query, zero), keys[:ext])
            probs = jnp.exp(scores - stat[:, a : a + 1])
            last = probs[:, i * BLOCK :]
            r = lax.broadcasted_iota(jnp.int32, last.shape, 0)
            c = lax.broadcasted_iota(jnp.int32, last.shape, 1)
            last = jnp.where(r >= c, last, 0.0)
            probs = jnp.concatenate([probs[:, : i * BLOCK], last], axis=1) if i else last
            inner = jnp.sum(pick(product, 0.0), axis=1, keepdims=True)
            grad_probs = nt(pick(grad, zero), values[:ext])
            grad_scores = (probs * (grad_probs - inner)).astype(bf16)
            more_v = nn(turned_grad[half], probs.astype(bf16))
            more_k = nn(turned_query[half], grad_scores)
            if i:
                acc_v[half, : i * BLOCK] += more_v[:, : i * BLOCK]
                acc_k[half, : i * BLOCK] += more_k[:, : i * BLOCK]
            acc_v[half, cols] = more_v[:, i * BLOCK :]
            acc_k[half, cols] = more_k[:, i * BLOCK :]
            new_q.append(nn(grad_scores, keys[:ext]))
        both = jnp.where(low, new_q[0], new_q[1])
        dqs[cols, place] = (both * 0.125).astype(bf16)
    dks[:, place] = jnp.transpose(acc_k[...].astype(bf16))
    dvs[:, place] = jnp.transpose(acc_v[...].astype(bf16))


def attention_back_kernel(
    ids, q, k, v, ctx, stat, w_o, g_own, g_other, n_own, n_other, downs, up_w,
    dq, dk, dv, g_norm, g_up,
    gms, os, qs, ks, vs, ctxs, stats, gs, dqs, dks, dvs, acc_k, acc_v, ns, tilts, sems,
):
    core = ids[0]
    go = Copies(sems)
    first = [
        go.start(g_own, gms.at[rows(core, HALF)]),
        go.start(g_other, gms.at[rows(1 - core, HALF)]),
        go.start(w_o, os),
    ]
    then = [
        go.start(ref, to)
        for ref, to in ((q, qs), (k, ks), (v, vs), (ctx, ctxs), (stat, stats))
    ]
    later = [
        go.start(n_own, ns.at[rows(core, HALF)]),
        go.start(n_other, ns.at[rows(1 - core, HALF)]),
    ]
    wait_all(first)
    for i in range(4):
        at = slice(i * BLOCK, (i + 1) * BLOCK)
        value = nt(gms[at], os[...]).astype(bf16)
        for pair in range(4):
            gs[pair, at] = value[:, 128 * pair : 128 * (pair + 1)]
    wait_all(then)

    @pl.loop(0, 4)
    def _(pair):
        attend_back(pair, qs, ks, vs, ctxs, stats, gs, dqs, dks, dvs, acc_k, acc_v)

    leave = [go.start(ref, to) for ref, to in ((dqs, dq), (dks, dk), (dvs, dv))]
    tilts[...] = (nt(up_w[:16, :HALF], dqs[...]) + nt(up_w[:16, 2 * HALF :], dvs[...])).astype(bf16)
    wait_all(later)
    g_norm[...] = nn(tilts[...], ns[...])[:8]
    g_up[:, :HALF] = nn(downs[...], dqs[...])[:8]
    g_up[:, HALF:] = nn(downs[...], dvs[...])[:8]
    wait_all(leave)


def call_attention_back(ids, q, k, v, ctx, stat, w_o, g_own, g_other, n_own, n_other, downs, up_w):
    return pl.pallas_call(
        attention_back_kernel,
        out_shape=(shape(1024, HALF),) * 3 + (shape(8, 1024, dtype=f32),) * 2,
        in_specs=[SMEM] + [HBM] * 10 + [VMEM] * 2,
        out_specs=(HBM, HBM, HBM, VMEM, VMEM),
        scratch_shapes=[
            pltpu.VMEM((1024, 1024), bf16),
            pltpu.VMEM((HALF, 1024), bf16),
            pltpu.VMEM((4, 1024, 128), bf16),
            pltpu.VMEM((4, 1024, 128), bf16),
            pltpu.VMEM((4, 1024, 128), bf16),
            pltpu.VMEM((4, 1024, 128), bf16),
            pltpu.VMEM((4, 8, 1024), f32),
            pltpu.VMEM((4, 1024, 128), bf16),
            pltpu.VMEM((1024, HALF), bf16),
            pltpu.VMEM((1024, HALF), bf16),
            pltpu.VMEM((1024, HALF), bf16),
            pltpu.VMEM((128, 1024), f32),
            pltpu.VMEM((128, 1024), f32),
            pltpu.VMEM((1024, 1024), bf16),
            pltpu.VMEM((16, 1024), bf16),
            pltpu.SemaphoreType.DMA((13,)),
        ],
        compiler_params=params(),
        name="attention_back",
    )(ids, q, k, v, ctx, stat, w_o, g_own, g_other, n_own, n_other, downs, up_w)


def qkv_back_kernel(
    ids, dq, dk, dv, w, down_w, up_w, own, send, dqs, dks, dvs, ws, owns, sends, sems
):
    core = ids[0]
    go = Copies(sems)
    sides = (1 - core, core)
    loads = [
        [
            go.start(dq.at[rows(side, HALF)], dqs.at[at]),
            go.start(w.at[0], ws.at[0]) if at == 0 else None,
            go.start(dk.at[rows(side, HALF)], dks.at[at]),
            go.start(w.at[1], ws.at[1]) if at == 0 else None,
            go.start(dv.at[rows(side, HALF)], dvs.at[at]),
            go.start(w.at[2], ws.at[2]) if at == 0 else None,
        ]
        for at, side in enumerate(sides)
    ]
    leave = []
    for at, (values, out) in enumerate(((sends, send), (owns, own))):
        wait_all([copy for copy in loads[at] if copy is not None])
        for i in range(2):
            tok = slice(i * BLOCK, (i + 1) * BLOCK)
            gq, gk, gv = dqs[at, tok], dks[at, tok], dvs[at, tok]
            tilt = (nt(gq, up_w[:, :HALF]) + nt(gv, up_w[:, 2 * HALF :])).astype(bf16)
            value = nt(gq, ws[0]) + nt(gk, ws[1]) + nt(gv, ws[2]) + nn(tilt, down_w[...])
            values[tok] = value.astype(bf16)
            leave.append(go.start(values.at[tok], out.at[tok]))
    wait_all(leave)


def call_qkv_back(ids, dq, dk, dv, w, down_w, up_w):
    return pl.pallas_call(
        qkv_back_kernel,
        out_shape=(shape(HALF, 1024), shape(HALF, 1024)),
        in_specs=[SMEM] + [HBM] * 4 + [VMEM] * 2,
        out_specs=(HBM, HBM),
        scratch_shapes=[pltpu.VMEM((2, HALF, HALF), bf16)] * 3
        + [
            pltpu.VMEM((3, 1024, HALF), bf16),
            pltpu.VMEM((HALF, 1024), bf16),
            pltpu.VMEM((HALF, 1024), bf16),
            pltpu.SemaphoreType.DMA((13,)),
        ],
        compiler_params=params(),
        name="qkv_back",
    )(ids, dq, dk, dv, w, down_w, up_w)


def low_half(value):
    return lax.broadcasted_iota(jnp.int32, value.shape, 1) < 64


def start_tokens(go, pair, target, z):
    return [go.start(ref, target.at[parity(z, k)]) for k, ref in enumerate(pair)]


def middle_kernel(
    ids, own, other, x0, x1, bias, gain, shift, middle, normed, owns, others, xs, mids, ns, sems
):
    go = Copies(sems)
    tokens = start_tokens(go, (x0, x1), xs, ids[1])
    parts = []
    for i in range(2):
        at = slice(i * BLOCK, (i + 1) * BLOCK)
        parts.append([go.start(own.at[at], owns.at[i]), go.start(other.at[at], others.at[i])])
    wait_all(tokens)
    leave = []
    for i in range(2):
        at = slice(i * BLOCK, (i + 1) * BLOCK)
        wait_all(parts[i])
        value = owns[i] + others[i].astype(f32) + xs[i].astype(f32) + bias[2:3]
        mids[i] = value
        leave.append(go.start(mids.at[i], middle.at[at]))
        hat, _ = center_scale(value)
        ns[i] = (hat * gain[1:2] + shift[1:2]).astype(bf16)
        leave.append(go.start(ns.at[i], normed.at[at]))
    wait_all(leave)


def call_middle(ids, own, other, x_own, bias, gain, shift):
    return pl.pallas_call(
        middle_kernel,
        out_shape=(shape(HALF, 1024, dtype=f32), shape(HALF, 1024)),
        in_specs=[SMEM] + [HBM] * 4 + [VMEM] * 3,
        out_specs=(HBM, HBM),
        scratch_shapes=[
            pltpu.VMEM((2, BLOCK, 1024), f32),
            pltpu.VMEM((2, BLOCK, 1024), bf16),
            pltpu.VMEM((2, BLOCK, 1024), bf16),
            pltpu.VMEM((2, BLOCK, 1024), f32),
            pltpu.VMEM((2, BLOCK, 1024), bf16),
            pltpu.SemaphoreType.DMA((10,)),
        ],
        compiler_params=params(),
        name="middle",
    )(ids, own, other, *x_own, bias, gain, shift)


def start_grads(go, ids, g_own, g_other, gs):
    core, z = ids[0], ids[1]
    return [
        go.start(ref, gs.at[2 * side + parity(z, k)])
        for side, pair in ((core, g_own), (1 - core, g_other))
        for k, ref in enumerate(pair)
    ]


def hidden_kernel(
    ids, n_own, n_other, w0, w1, w2, w3t, w3b, bias, g0, g1, g2, g3, piece,
    active, slope, w_out, result, grad,
    ns, ws, acts, slopes, gs, wo, results, grads, sems,
):
    core, chip = ids[0], ids[2]
    go = Copies(sems)
    arrive = [
        go.start(n_own, ns.at[rows(core, HALF)]),
        go.start(n_other, ns.at[rows(1 - core, HALF)]),
    ]
    weights = []
    for p in range(4):
        for r, ref in enumerate((w0, w1, w2, (w3t, w3b))):
            part = ref.at[p] if r < 3 else ref[p // 2].at[p % 2]
            weights += start_sides(go, part, ws.at[p], chip ^ r, core, p)
    later = start_grads(go, ids, (g0, g1), (g2, g3), gs)
    later.append(go.start(piece, wo))
    wait_all(arrive)
    leave = []

    def finish(p, i, h):
        at = slice(i * BLOCK, (i + 1) * BLOCK)
        square = h * h
        lift = 0.5 + 0.5 * jnp.tanh(h * (GELU_A + (GELU_A * GELU_B) * square))
        act = h * lift
        acts[p, at] = act.astype(bf16)
        rise = 2.0 * GELU_A + (6.0 * GELU_A * GELU_B) * square
        slopes[p, at] = (lift + (act - act * lift) * rise).astype(bf16)
        if i == 3:
            leave.append(go.start(acts.at[p], active.at[p]))
            leave.append(go.start(slopes.at[p], slope.at[p]))

    before = None
    for p in range(4):
        wait_all([copy for at, copy in weights if at == p])
        leave.append(go.start(ws.at[p], w_out.at[p]))
        shift = bias[pl.ds(2 * p + core, 1)]
        for i in range(4):
            h = nn(ns[i * BLOCK : (i + 1) * BLOCK], ws[p]) + shift
            if before is not None:
                finish(*before)
            before = (p, i, h)
    finish(*before)
    wait_all(later)
    for i in range(4):
        tok = slice(i * BLOCK, (i + 1) * BLOCK)
        back = nt(gs[i], wo[...]) * slopes[chip, tok].astype(f32)
        results[tok] = nn(acts[chip, tok], wo[...]).astype(bf16)
        grads[tok] = nt(back.astype(bf16), ws[chip]).astype(bf16)
        leave.append(go.start(results.at[tok], result.at[tok]))
        leave.append(go.start(grads.at[tok], grad.at[tok]))
    wait_all(leave)


def call_hidden(ids, n_own, n_other, pieces, bias, g_own, g_other, piece):
    return pl.pallas_call(
        hidden_kernel,
        out_shape=(shape(4, 1024, HALF),) * 3 + (shape(1024, 1024),) * 2,
        in_specs=[SMEM] + [HBM] * 7 + [VMEM] + [HBM] * 5,
        out_specs=(HBM,) * 5,
        scratch_shapes=[pltpu.VMEM((1024, 1024), bf16)]
        + [pltpu.VMEM((4, 1024, HALF), bf16)] * 3
        + [
            pltpu.VMEM((4, BLOCK, 1024), bf16),
            pltpu.VMEM((HALF, 1024), bf16),
            pltpu.VMEM((1024, 1024), bf16),
            pltpu.VMEM((1024, 1024), bf16),
            pltpu.SemaphoreType.DMA((59,)),
        ],
        compiler_params=params(),
        name="hidden",
    )(ids, n_own, n_other, *pieces, bias, *g_own, *g_other, piece)


def feed_kernel(
    ids, g0, g1, g2, g3, active, slope, w_in, x_piece, y_piece, old_result, old_grad,
    result, grad, gs, acts, slopes, w_ins, w_outs, olds, old_gs, results, grads, sems,
):
    core, z, chip = ids[0], ids[1], ids[2]
    go = Copies(sems)
    pieces = (x_piece, y_piece)
    sources = [(core, 0, g0), (core, 1, g1), (1 - core, 0, g2), (1 - core, 1, g3)]
    blocks = [2 * side + parity(z, k) for side, k, _ in sources]
    tokens, wide, loads = [], [], []

    def start_wide(at):
        here = chip ^ (at + 1)
        wide.append((go.start(pieces[at], w_outs.at[at]), go.start(w_in.at[here], w_ins.at[at])))

    def start_block(i):
        tok = rows(blocks[i], BLOCK)
        copies = []
        for at in range(2):
            here = chip ^ (at + 1)
            copies.append(go.start(slope.at[here, tok], slopes.at[at, i]))
            copies.append(go.start(active.at[here, tok], acts.at[at, i]))
        copies.append(go.start(old_grad.at[tok], old_gs.at[i]))
        copies.append(go.start(old_result.at[tok], olds.at[i]))
        loads.append(copies)

    tokens.append(go.start(sources[0][2], gs.at[0]))
    start_wide(0)
    start_block(0)
    start_wide(1)
    for i in range(1, 4):
        tokens.append(go.start(sources[i][2], gs.at[i]))
        start_block(i)
    leave = []
    for i in range(4):
        tokens[i].wait()
        sums = [None, None]
        for at in range(2):
            if i == 0:
                wide[at][0].wait()
            back = nt(gs[i], w_outs[at])
            if at == 0:
                wait_all(loads[i])
            if i == 0:
                wide[at][1].wait()
            back = (back * slopes[at, i].astype(f32)).astype(bf16)
            terms = nn(acts[at, i], w_outs[at]), nt(back, w_ins[at])
            sums = [term if have is None else have + term for have, term in zip(sums, terms)]
        results[i] = (sums[0] + olds[i].astype(f32)).astype(bf16)
        grads[i] = (sums[1] + old_gs[i].astype(f32)).astype(bf16)
        tok = rows(blocks[i], BLOCK)
        leave.append(go.start(results.at[i], result.at[tok]))
        leave.append(go.start(grads.at[i], grad.at[tok]))
    wait_all(leave)


def call_feed(ids, g_own, g_other, active, slope, w_in, pieces, old):
    return pl.pallas_call(
        feed_kernel,
        out_shape=(shape(1024, 1024),) * 2,
        in_specs=[SMEM] + [HBM] * 11,
        out_specs=(HBM, HBM),
        scratch_shapes=[
            pltpu.VMEM((4, BLOCK, 1024), bf16),
            pltpu.VMEM((2, 4, BLOCK, HALF), bf16),
            pltpu.VMEM((2, 4, BLOCK, HALF), bf16),
            pltpu.VMEM((2, 1024, HALF), bf16),
            pltpu.VMEM((2, HALF, 1024), bf16),
        ]
        + [pltpu.VMEM((4, BLOCK, 1024), bf16)] * 4
        + [pltpu.SemaphoreType.DMA((40,))],
        compiler_params=params(),
        name="feed",
    )(ids, *g_own, *g_other, active, slope, w_in, *pieces, *old)


def far_send_kernel(
    ids, g0, g1, slope, w_in, top, low, old, out, gs, slopes, w_ins, w_outs, olds, outs, sems
):
    core, z, chip = ids[0], ids[1], ids[2]
    go = Copies(sems)
    arrive = start_tokens(go, (g0, g1), gs, z)
    arrive.append(go.start(top, w_outs.at[:BLOCK]))
    arrive.append(go.start(low, w_outs.at[BLOCK:]))
    near = [
        go.start(slope.at[chip ^ 3, rows(1 - core, HALF)], slopes),
        go.start(w_in.at[chip ^ 3], w_ins),
    ]
    load = go.start(old.at[rows(1 - core, HALF)], olds)
    wait_all(arrive)
    leave = []
    for i in range(2):
        tok = slice(i * BLOCK, (i + 1) * BLOCK)
        back = nt(gs[i], w_outs[...])
        if i == 0:
            wait_all(near)
        back = back * slopes[tok].astype(f32)
        more = nt(back.astype(bf16), w_ins[...])
        if i == 0:
            load.wait()
        outs[tok] = (more + olds[tok].astype(f32)).astype(bf16)
        leave.append(go.start(outs.at[tok], out.at[tok]))
    wait_all(leave)


def call_far_send(ids, g_other, slope, w_in, far, old):
    return pl.pallas_call(
        far_send_kernel,
        out_shape=shape(HALF, 1024),
        in_specs=[SMEM] + [HBM] * 7,
        out_specs=HBM,
        scratch_shapes=[
            pltpu.VMEM((2, BLOCK, 1024), bf16),
            pltpu.VMEM((HALF, HALF), bf16),
            pltpu.VMEM((1024, HALF), bf16),
            pltpu.VMEM((HALF, 1024), bf16),
            pltpu.VMEM((HALF, 1024), bf16),
            pltpu.VMEM((HALF, 1024), bf16),
            pltpu.SemaphoreType.DMA((9,)),
        ],
        compiler_params=params(),
        name="far_send",
    )(ids, *g_other, slope, w_in, *far, old)


def far_own_kernel(
    ids, g0, g1, slope, w_in, top, low, old, other, middle, gain, grad_out, low_out,
    gs, slopes, w_ins, w_outs, olds, others, mids, grads, lows, sems,
):
    core, z, chip = ids[0], ids[1], ids[2]
    go = Copies(sems)
    arrive = start_tokens(go, (g0, g1), gs, z)
    arrive.append(go.start(top, w_outs.at[:BLOCK]))
    arrive.append(go.start(low, w_outs.at[BLOCK:]))
    near = [
        go.start(slope.at[chip ^ 3, rows(core, HALF)], slopes),
        go.start(w_in.at[chip ^ 3], w_ins),
    ]
    loads = [
        go.start(old.at[rows(core, HALF)], olds),
        go.start(other, others),
        go.start(middle, mids),
    ]
    wait_all(arrive)
    leave = []
    for i in range(2):
        tok = slice(i * BLOCK, (i + 1) * BLOCK)
        back = nt(gs[i], w_outs[...])
        if i == 0:
            wait_all(near)
        back = back * slopes[tok].astype(f32)
        more = nt(back.astype(bf16), w_ins[...])
        if i == 0:
            wait_all(loads)
        more += olds[tok].astype(f32) + others[tok].astype(f32)
        hat, inverse = center_scale(mids[tok])
        value = gs[i].astype(f32) + norm_back(hat, inverse, more * gain[1:2])
        grads[tok] = value
        lows[tok] = value.astype(bf16)
        leave.append(go.start(grads.at[tok], grad_out.at[tok]))
        leave.append(go.start(lows.at[tok], low_out.at[tok]))
    wait_all(leave)


def call_far_own(ids, g_own, slope, w_in, far, old, other, middle, gain):
    return pl.pallas_call(
        far_own_kernel,
        out_shape=(shape(HALF, 1024, dtype=f32), shape(HALF, 1024)),
        in_specs=[SMEM] + [HBM] * 9 + [VMEM],
        out_specs=(HBM, HBM),
        scratch_shapes=[
            pltpu.VMEM((2, BLOCK, 1024), bf16),
            pltpu.VMEM((HALF, HALF), bf16),
            pltpu.VMEM((1024, HALF), bf16),
            pltpu.VMEM((HALF, 1024), bf16),
            pltpu.VMEM((HALF, 1024), bf16),
            pltpu.VMEM((HALF, 1024), bf16),
            pltpu.VMEM((HALF, 1024), f32),
            pltpu.VMEM((HALF, 1024), f32),
            pltpu.VMEM((HALF, 1024), bf16),
            pltpu.SemaphoreType.DMA((13,)),
        ],
        compiler_params=params(),
        name="far_own",
    )(ids, *g_own, slope, w_in, *far, old, other, middle, gain)


def far_result_kernel(
    ids, active, top, low, old, own, send, acts, w_outs, olds, owns, sends, sems
):
    core, chip = ids[0], ids[2]
    go = Copies(sems)
    arrive = [
        go.start(top, w_outs.at[:BLOCK]),
        go.start(low, w_outs.at[BLOCK:]),
        go.start(active.at[chip ^ 3], acts),
    ]
    load = go.start(old, olds)
    wait_all(arrive)
    load.wait()
    leave = []
    for side, values, out in ((1 - core, sends, send), (core, owns, own)):
        for i in range(2):
            at = rows(2 * side + i, BLOCK)
            tok = slice(i * BLOCK, (i + 1) * BLOCK)
            values[tok] = (olds[at].astype(f32) + nn(acts[at], w_outs[...])).astype(values.dtype)
            leave.append(go.start(values.at[tok], out.at[tok]))
    wait_all(leave)


def call_far_result(ids, active, far, old):
    return pl.pallas_call(
        far_result_kernel,
        out_shape=(shape(HALF, 1024), shape(HALF, 1024)),
        in_specs=[SMEM] + [HBM] * 4,
        out_specs=(HBM, HBM),
        scratch_shapes=[
            pltpu.VMEM((1024, HALF), bf16),
            pltpu.VMEM((HALF, 1024), bf16),
            pltpu.VMEM((1024, 1024), bf16),
            pltpu.VMEM((HALF, 1024), bf16),
            pltpu.VMEM((HALF, 1024), bf16),
            pltpu.SemaphoreType.DMA((8,)),
        ],
        compiler_params=params(),
        name="far_result",
    )(ids, active, *far, old)


def mixed_kernel(ids, own, other, middle, bias, out0, out1):
    z = ids[1]
    for k, out in enumerate((out0, out1)):
        tok = rows(parity(z, k), BLOCK)
        value = own[tok].astype(f32) + other[tok].astype(f32) + middle[tok] + bias[3:4]
        out[...] = value.astype(bf16)


def call_mixed(ids, own, other, middle, bias):
    return pl.pallas_call(
        mixed_kernel,
        out_shape=(shape(BLOCK, 1024),) * 2,
        in_specs=[SMEM] + [VMEM] * 4,
        out_specs=(VMEM, VMEM),
        compiler_params=params(),
        name="mixed",
    )(ids, own, other, middle, bias)


def input_grad_kernel(ids, x0, x1, own, other, grad_middle, gain, out0, out1):
    z = ids[1]
    for k, (x, out) in enumerate(((x0, out0), (x1, out1))):
        tok = rows(parity(z, k), BLOCK)
        grad = own[tok].astype(f32) + other[tok].astype(f32)
        hat, inverse = center_scale(x[...].astype(f32))
        out[...] = (grad_middle[tok] + norm_back(hat, inverse, grad * gain[0:1])).astype(bf16)


def call_input_grad(ids, x_own, own, other, grad_middle, gain):
    return pl.pallas_call(
        input_grad_kernel,
        out_shape=(shape(BLOCK, 1024),) * 2,
        in_specs=[SMEM] + [VMEM] * 6,
        out_specs=(VMEM,) * 2,
        compiler_params=params(),
        name="input_grad",
    )(ids, *x_own, own, other, grad_middle, gain)


def to_core(value):
    return lax.ppermute(value, "core", SWAP)


def exchange(z, pair):
    sent = []
    for k in range(2):
        perm = [
            (4 * core + at, 4 * (at // 2) + 2 * core + (at + k) % 2)
            for core in range(2)
            for at in range(4)
        ]
        sent.append(lax.ppermute(pair[k], ("core", "seq"), perm))
    return sent


def by_parity(z, pair):
    even = lax.rem(z, 2) == 0
    return jnp.where(even, pair[0], pair[1]), jnp.where(even, pair[1], pair[0])


def after(value, *others):
    return lax.optimization_barrier((value, *others))[0]


def gather_near(shard):
    return [shard, lax.ppermute(shard, "x", SWAP), lax.ppermute(shard, "y", SWAP)]


def halves(near):
    _, by_x, by_y = near
    half = by_x.shape[0] // 2
    return by_x[:half], by_y[half:]


def gather_far(near, parts):
    return near + [lax.ppermute(parts[0], "y", SWAP), lax.ppermute(parts[1], "x", SWAP)]


def on_chip(
    inputs,
    out_grad,
    norm_gain,
    norm_bias,
    proj_bias,
    fc_bias,
    qkv_weight,
    out_weight,
    feed_input_weight,
    proj_weight,
    adapters,
    first_moment,
    second_moment,
):
    core = lax.axis_index("core")
    z = lax.axis_index("seq")
    chip = 2 * lax.axis_index("y") + lax.axis_index("x")
    ids = jnp.stack([core, z, chip]).astype(jnp.int32)

    qkv_own, qkv_send, out_part = call_cut(ids, qkv_weight, out_weight)
    qkv_got = to_core(qkv_send)
    first_shard = jnp.concatenate([jnp.concatenate([qkv_own, qkv_got], axis=1), out_part], axis=0)
    first_near = gather_near(first_shard)
    x_own = exchange(z, by_parity(z, after((inputs[0], inputs[1]), first_shard)))
    in_own, in_send = call_cut_feed(ids, after(feed_input_weight, first_shard))
    in_shard = jnp.concatenate([in_own, to_core(in_send)], axis=1)
    first_near = after(first_near, in_own)
    first_halves = halves(first_near)
    n_own = call_norm(ids, after(x_own, *first_halves), norm_gain, norm_bias)
    n_other = to_core(n_own)
    first_pieces = gather_far(first_near, first_halves)
    in_near = gather_near(after(in_shard, *first_halves))

    def columns(value):
        lead = value.shape[0]
        value = value.reshape(lead, 4, 2, 128)
        return jnp.where(core == 0, value[:, :, 0], value[:, :, 1]).reshape(lead, HALF)

    scale = adapter_alpha / ADAPTER_RANK
    adapters, proj_bias = after((adapters, proj_bias), first_shard)
    up_q, up_v = scale * columns(adapters[1]), scale * columns(adapters[3])
    up_w = jnp.zeros((128, 1536), f32)
    up_w = up_w.at[0:4, :HALF].set(up_q).at[4:8, 2 * HALF :].set(up_v).astype(bf16)
    down_w = jnp.concatenate([adapters[0], adapters[2], jnp.zeros((120, 1024), f32)], axis=0)
    down_w = down_w.astype(bf16)
    head_bias = columns(proj_bias[:2])
    qkv_bias = jnp.concatenate([head_bias[0], jnp.zeros((HALF,), f32), head_bias[1]])[None]

    g_own = exchange(z, after(by_parity(z, (out_grad[0], out_grad[1])), n_other))
    q, k, v, down, w_qkv, w_o, ctx, stat, attn_own, attn_send = call_first(
        ids, n_own, n_other, first_pieces, down_w, up_w, qkv_bias
    )
    attn_other = to_core(after(attn_send, *g_own))
    in_near = after(in_near, ctx)
    in_halves = halves(in_near)
    in_pieces = gather_far(in_near, in_halves)
    middle, n2_own = call_middle(
        ids, attn_own, after(attn_other, *in_halves), x_own, proj_bias, norm_gain, norm_bias
    )
    n2_other = to_core(n2_own)
    proj_near = gather_near(after(proj_weight, *in_halves))
    g_other = [to_core(part) for part in g_own]
    active, slope, w_in, *old = call_hidden(
        ids, n2_own, n2_other, in_pieces, fc_bias.reshape(8, HALF), g_own, g_other, proj_near[0]
    )
    proj_near = after(proj_near, *old)
    proj_halves = halves(proj_near)
    far = gather_far(proj_near, proj_halves)[3:]
    near = after(proj_near[1:], *proj_halves)
    result, grad = call_feed(ids, g_own, g_other, active, slope, w_in, near, old)
    grad_send = call_far_send(ids, g_other, slope, w_in, far, grad)
    grad_other = to_core(grad_send)
    result_own, result_send = call_far_result(ids, active, after(far, grad_send), result)
    result_other = to_core(result_send)
    grad_other = after(grad_other, result_own)
    grad_middle, low_own = call_far_own(
        ids, g_own, slope, w_in, far, grad, grad_other, middle, norm_gain
    )
    low_other = to_core(low_own)
    mixed = call_mixed(ids, after(result_own, low_own), result_other, middle, proj_bias)
    low_other = after(low_other, *mixed)
    mixed = exchange(z, mixed)
    dq, dk, dv, g_norm, g_up = call_attention_back(
        ids, q, k, v, ctx, stat, w_o, low_own, low_other, n_own, n_other, down, up_w
    )
    dq = after(dq, *mixed)
    own, send = call_qkv_back(ids, dq, dk, dv, w_qkv, down_w, up_w)
    other = to_core(send)

    def spread(part):
        part = part.reshape(4, 4, 1, 128)
        place = lax.broadcasted_iota(jnp.int32, (1, 1, 2, 1), 2)
        return jnp.where(place == core, part, 0.0).reshape(4, 1024)

    total = jnp.stack(
        [
            g_norm[:4],
            scale * spread(g_up[:4, :HALF]),
            g_norm[4:],
            scale * spread(g_up[4:, HALF:]),
        ]
    )
    total = after(total + to_core(total), send)
    total = after(total + lax.ppermute(total, "x", SWAP), other)
    grad_in = call_input_grad(ids, x_own, own, after(other, total), grad_middle, norm_gain)
    total = total + lax.ppermute(total, "y", SWAP)
    total = after(total, *grad_in)
    grad_in = exchange(z, grad_in)
    for perm in (((0, 1), (1, 0), (2, 3), (3, 2)), ((0, 2), (2, 0), (1, 3), (3, 1))):
        total = total + lax.ppermute(total, "seq", perm)
    grad_norm = jnp.sqrt(jnp.sum(total * total))
    clipped, new_weight, new_first, new_second = adam_update(
        total, adapters, first_moment, second_moment, grad_norm
    )
    mixed = jnp.stack(by_parity(z, mixed))
    grad_input = jnp.stack(by_parity(z, grad_in))
    return (mixed, grad_input, clipped, grad_norm, new_weight, new_first, new_second)


def solution(mesh):
    sizes = dict(mesh.shape)
    if sizes["dp"] == 8 and sizes["seq"] == 4:
        plane = Mesh(mesh.devices.reshape(2, 2, 2, 4), ("y", "x", "core", "seq"))
        return build(plane, ("y", "x", "core"), on_chip)
    return build(mesh, "dp", on_device)


def build(mesh, dp, step):
    tokens, weight = P(dp, "seq", None), P(dp, None)
    return jax.shard_map(
        step,
        mesh=mesh,
        in_specs=(tokens, tokens) + (P(),) * 4 + (weight,) * 4 + (P(),) * 3,
        out_specs=(tokens, tokens) + (P(),) * 5,
        check_vma=False,
    )
```

```python
import functools
import math

import jax
import jax.numpy as jnp
from jax import lax
from jax.experimental import pallas as pl
from jax.experimental.pallas import tpu as pltpu
from jax.sharding import Mesh
from jax.sharding import PartitionSpec as P

HEAD_DIM = 64
ADAPTER_RANK = 4
STEP = 10


highest = lax.Precision.HIGHEST
adapter_alpha = 32.0
beta_one = 0.9
beta_two = 0.999
adam_eps = 1e-08
decay_rate = 0.01
learning_rate = 0.02
clip_bound = 1.0
norm_eps = 1e-05


def layer_norm(value, gain, shift):
    center = jnp.mean(value, axis=-1, keepdims=True)
    centered = value - center
    spread = jnp.mean(centered * centered, axis=-1, keepdims=True)
    return centered * lax.rsqrt(spread + norm_eps) * gain + shift


def dot_trans(left, right):
    return lax.dot_general(
        left, right, (((1,), (1,)), ((), ())), preferred_element_type=jnp.float32
    )


def dot_first(left, right):
    return lax.dot_general(
        left, right, (((0,), (0,)), ((), ())), precision=highest, preferred_element_type=jnp.float32
    )


def adam_update(grad, weight, first, second, norm):
    scale_factor = clip_bound / jnp.maximum(norm, clip_bound)
    clipped = grad * scale_factor
    new_first = beta_one * first + (1.0 - beta_one) * clipped
    new_second = beta_two * second + (1.0 - beta_two) * clipped * clipped
    first_hat = new_first / (1.0 - beta_one**STEP)
    second_hat = new_second / (1.0 - beta_two**STEP)
    new_weight = weight - learning_rate * (
        first_hat / (jnp.sqrt(second_hat) + adam_eps) + decay_rate * weight
    )
    return (clipped, new_weight, new_first, new_second)


def split_heads(packed):
    length = packed.shape[0]
    local_heads = packed.shape[-1] // HEAD_DIM
    query = packed[:, 0, 0].reshape(length, local_heads, HEAD_DIM)
    keys = packed[:, 1, 0].reshape(length, local_heads, HEAD_DIM)
    values = packed[:, 2, 0].reshape(length, local_heads, HEAD_DIM)
    return (query, keys, values)


def doc_forward(packed):
    length = packed.shape[0]
    local_width = packed.shape[-1]
    query, keys, values = split_heads(packed)
    local_heads = query.shape[1]
    span = min(512, length)
    blocks = length // span
    scale = 1.0 / math.sqrt(HEAD_DIM)
    starts = jnp.arange(blocks, dtype=jnp.int32) * span

    def visit(pieces):
        query_block, start = pieces
        scores = (
            jnp.einsum("qhd,khd->hqk", query_block, keys, preferred_element_type=jnp.float32)
            * scale
        )
        causal = (start + jnp.arange(span))[:, None] >= jnp.arange(length)[None, :]
        masked = jnp.where(causal[None], scores, -1e30)
        summit = jnp.max(masked, axis=-1, keepdims=True)
        expo = jnp.where(causal[None], jnp.exp(masked - summit), 0.0)
        totals = jnp.sum(expo, axis=-1, keepdims=True)
        weights = (expo / totals).astype(jnp.bfloat16)
        context = jnp.einsum(
            "hqk,khd->qhd", weights, values, preferred_element_type=jnp.float32
        ).astype(jnp.bfloat16)
        return (context, summit[..., 0] + jnp.log(totals[..., 0]))

    context, log_total = lax.map(
        visit, (query.reshape(blocks, span, local_heads, HEAD_DIM), starts)
    )
    return (context.reshape(length, 1, local_width), log_total)


def doc_backward(args):
    packed, grad_context, log_total = args
    length = packed.shape[0]
    local_width = packed.shape[-1]
    query, keys, values = split_heads(packed)
    local_heads = query.shape[1]
    output_gradient = grad_context[:, 0].reshape(length, local_heads, HEAD_DIM)
    span = min(512, length)
    blocks = length // span
    scale = 1.0 / math.sqrt(HEAD_DIM)
    starts = jnp.arange(blocks, dtype=jnp.int32) * span

    def visit(carry, pieces):
        grad_keys, grad_values = carry
        query_block, grad_block, total_block, start = pieces
        scores = (
            jnp.einsum("qhd,khd->hqk", query_block, keys, preferred_element_type=jnp.float32)
            * scale
        )
        causal = (start + jnp.arange(span))[:, None] >= jnp.arange(length)[None, :]
        masked = jnp.where(causal[None], scores, -1e30)
        probs = jnp.where(causal[None], jnp.exp(masked - total_block[:, :, None]), 0.0)
        weights = probs.astype(jnp.bfloat16)
        grad_probs = jnp.einsum(
            "qhd,khd->hqk", grad_block, values, preferred_element_type=jnp.float32
        )
        inner = jnp.sum(probs * grad_probs, axis=-1, keepdims=True)
        grad_scores = (probs * (grad_probs - inner)).astype(jnp.bfloat16)
        grad_query = (
            jnp.einsum("hqk,khd->qhd", grad_scores, keys, preferred_element_type=jnp.float32)
            * scale
        )
        grad_keys = (
            grad_keys
            + jnp.einsum(
                "hqk,qhd->khd", grad_scores, query_block, preferred_element_type=jnp.float32
            )
            * scale
        )
        grad_values = grad_values + jnp.einsum(
            "hqk,qhd->khd", weights, grad_block, preferred_element_type=jnp.float32
        )
        return ((grad_keys, grad_values), grad_query)

    empty = jnp.zeros((length, local_heads, HEAD_DIM), jnp.float32)
    pieces = (
        query.reshape(blocks, span, local_heads, HEAD_DIM),
        output_gradient.reshape(blocks, span, local_heads, HEAD_DIM),
        log_total,
        starts,
    )
    (grad_keys, grad_values), grad_query = lax.scan(visit, (empty, empty), pieces)
    joined = jnp.stack(
        [
            grad_query.reshape(length, local_width),
            grad_keys.reshape(length, local_width),
            grad_values.reshape(length, local_width),
        ],
        axis=1,
    )
    return joined.astype(jnp.bfloat16)[:, :, None, :]


def on_device(
    inputs,
    out_grad,
    norm_gain,
    norm_bias,
    proj_bias,
    fc_bias,
    qkv_weight,
    out_weight,
    feed_input_weight,
    proj_weight,
    adapters,
    first_moment,
    second_moment,
):
    docs, tokens, width = inputs.shape
    count = docs * tokens
    ranks = lax.axis_size("seq")
    scale_factor = adapter_alpha / ADAPTER_RANK

    def forward(stack):
        qkv_full, out_full, fc_full, proj_full = stack
        flat = inputs.reshape(count, width).astype(jnp.float32)
        normed, norm_one_back = jax.vjp(
            lambda value: layer_norm(value, norm_gain[0], norm_bias[0]), flat
        )
        base = jnp.dot(normed.astype(jnp.bfloat16), qkv_full, preferred_element_type=jnp.float32)
        down_q = jnp.dot(normed, adapters[0].T, precision=highest)
        down_v = jnp.dot(normed, adapters[2].T, precision=highest)
        query = (
            base[:, :width]
            + proj_bias[0]
            + scale_factor * jnp.dot(down_q, adapters[1], precision=highest)
        )
        keys = base[:, width : 2 * width]
        values = (
            base[:, 2 * width :]
            + proj_bias[1]
            + scale_factor * jnp.dot(down_v, adapters[3], precision=highest)
        )
        joined = (
            jnp.concatenate([query, keys, values], axis=1)
            .astype(jnp.bfloat16)
            .reshape(docs, tokens, 3, ranks, width // ranks)
        )
        spread = lax.all_to_all(joined, "seq", split_axis=3, concat_axis=1, tiled=True)
        context, log_total = lax.map(doc_forward, spread)
        context = lax.all_to_all(context, "seq", split_axis=1, concat_axis=2, tiled=True).reshape(
            count, width
        )
        middle = (
            flat + jnp.dot(context, out_full, preferred_element_type=jnp.float32) + proj_bias[2]
        )
        normed_two, norm_two_back = jax.vjp(
            lambda value: layer_norm(value, norm_gain[1], norm_bias[1]), middle
        )
        hidden = (
            jnp.dot(normed_two.astype(jnp.bfloat16), fc_full, preferred_element_type=jnp.float32)
            + fc_bias
        )
        active, gelu_back = jax.vjp(lambda value: jax.nn.gelu(value, approximate=True), hidden)
        result = (
            middle
            + jnp.dot(active.astype(jnp.bfloat16), proj_full, preferred_element_type=jnp.float32)
            + proj_bias[3]
        )
        return (
            result,
            (normed, down_q, down_v, norm_one_back, spread, log_total, norm_two_back, gelu_back),
        )

    stack = (
        lax.all_gather(qkv_weight, "dp", axis=0, tiled=True),
        lax.all_gather(out_weight, "dp", axis=0, tiled=True),
        lax.all_gather(feed_input_weight, "dp", axis=0, tiled=True),
        lax.all_gather(proj_weight, "dp", axis=0, tiled=True),
    )
    result, kept = forward(stack)
    fenced = lax.optimization_barrier((stack, result))
    stack = fenced[0]
    again, kept = forward(stack)
    qkv_full, out_full, fc_full, proj_full = stack
    normed, down_q, down_v, norm_one_back, spread, log_total, norm_two_back, gelu_back = kept
    cotangent = out_grad.reshape(count, width)
    grad_active = dot_trans(cotangent, proj_full)
    grad_hidden = gelu_back(grad_active)[0].astype(jnp.bfloat16)
    grad_normed_two = dot_trans(grad_hidden, fc_full)
    grad_middle = cotangent.astype(jnp.float32) + norm_two_back(grad_normed_two)[0]
    grad_context = dot_trans(grad_middle.astype(jnp.bfloat16), out_full).astype(jnp.bfloat16)
    grad_context = grad_context.reshape(docs, tokens, ranks, width // ranks)
    grad_context = lax.all_to_all(grad_context, "seq", split_axis=2, concat_axis=1, tiled=True)
    grad_joined = lax.map(doc_backward, (spread, grad_context, log_total))
    grad_joined = lax.all_to_all(
        grad_joined, "seq", split_axis=1, concat_axis=3, tiled=True
    ).reshape(count, 3 * width)
    grad_normed = dot_trans(grad_joined, qkv_full)
    grad_query = grad_joined[:, :width].astype(jnp.float32)
    grad_value = grad_joined[:, 2 * width :].astype(jnp.float32)
    tilt_q = scale_factor * jnp.dot(grad_query, adapters[1].T, precision=highest)
    value_adapter_up = scale_factor * jnp.dot(grad_value, adapters[3].T, precision=highest)
    grad_normed = (
        grad_normed
        + jnp.dot(tilt_q, adapters[0], precision=highest)
        + jnp.dot(value_adapter_up, adapters[2], precision=highest)
    )
    grad_input = (
        (grad_middle + norm_one_back(grad_normed)[0])
        .astype(jnp.bfloat16)
        .reshape(docs, tokens, width)
    )
    partial_terms = jnp.stack(
        [
            dot_first(tilt_q, normed),
            scale_factor * dot_first(down_q, grad_query),
            dot_first(value_adapter_up, normed),
            scale_factor * dot_first(down_v, grad_value),
        ]
    )
    total = lax.psum(partial_terms, ("dp", "seq"))
    grad_norm = jnp.sqrt(jnp.sum(total * total))
    clipped, new_weight, new_first, new_second = adam_update(
        total, adapters, first_moment, second_moment, grad_norm
    )
    mixed = result.astype(jnp.bfloat16).reshape(docs, tokens, width)
    return (mixed, grad_input, clipped, grad_norm, new_weight, new_first, new_second)


HALF = 512
BLOCK = 256
VMEM_MIB = 63
SMEM = pl.BlockSpec(memory_space=pltpu.SMEM)
VMEM = pl.BlockSpec(memory_space=pltpu.VMEM)
HBM = pl.BlockSpec(memory_space=pl.ANY)
f32 = jnp.float32
bf16 = jnp.bfloat16
SWAP = ((0, 1), (1, 0))
GELU_A = math.sqrt(2.0 / math.pi)
GELU_B = 0.044715


def nn(left, right):
    return lax.dot_general(left, right, (((1,), (0,)), ((), ())), preferred_element_type=f32)


def nt(left, right):
    return lax.dot_general(left, right, (((1,), (1,)), ((), ())), preferred_element_type=f32)


def tn(left, right):
    return lax.dot_general(left, right, (((0,), (0,)), ((), ())), preferred_element_type=f32)


def shape(*dims, dtype=bf16):
    return jax.ShapeDtypeStruct(dims, dtype)


def params():
    return pltpu.CompilerParams(vmem_limit_bytes=VMEM_MIB * 2**20)


def rows(index, size):
    return pl.ds(pl.multiple_of(index * size, size), size)


def parity(z, k):
    return lax.rem(z + k, 2)


class Copies:
    def __init__(self, sems):
        self.sems = sems
        self.count = 0

    def start(self, source, target):
        copy = pltpu.make_async_copy(source, target, self.sems.at[self.count])
        self.count += 1
        copy.start()
        return copy


def wait_all(copies):
    for copy in copies:
        copy.wait()


def center_scale(x):
    center = jnp.mean(x, axis=-1, keepdims=True)
    centered = x - center
    spread = jnp.mean(centered * centered, axis=-1, keepdims=True)
    inverse = lax.rsqrt(spread + norm_eps)
    return centered * inverse, inverse


def norm_back(hat, inverse, grad):
    first = jnp.mean(grad, axis=-1, keepdims=True)
    second = jnp.mean(grad * hat, axis=-1, keepdims=True)
    return inverse * (grad - first - hat * second)


def cut_kernel(ids, w, w_o, own, send, out_part):
    core = ids[0]
    for p in range(3):
        for i in range(4):
            base = 1024 * p + 256 * i
            to = slice(128 * i, 128 * (i + 1))
            send[p, :, to] = w[:, pl.ds(pl.multiple_of(base + 128 * (1 - core), 128), 128)]
            own[p, :, to] = w[:, pl.ds(pl.multiple_of(base + 128 * core, 128), 128)]
    out_part[0, :128] = w_o[:, :HALF]
    out_part[0, 128:] = w_o[:, HALF:]


def call_cut(ids, w, w_o):
    return pl.pallas_call(
        cut_kernel,
        out_shape=(shape(3, 128, HALF), shape(3, 128, HALF), shape(1, BLOCK, HALF)),
        in_specs=[SMEM, VMEM, VMEM],
        out_specs=(VMEM,) * 3,
        compiler_params=params(),
        name="cut_qkv",
    )(ids, w, w_o)


def cut_feed_kernel(ids, w, own, send):
    core = ids[0]
    for i in range(4):
        send[i] = w[:, pl.ds(pl.multiple_of(1024 * i + HALF * (1 - core), HALF), HALF)]
        own[i] = w[:, pl.ds(pl.multiple_of(1024 * i + HALF * core, HALF), HALF)]


def call_cut_feed(ids, w):
    return pl.pallas_call(
        cut_feed_kernel,
        out_shape=(shape(4, 128, HALF), shape(4, 128, HALF)),
        in_specs=[SMEM, VMEM],
        out_specs=(VMEM,) * 2,
        compiler_params=params(),
        name="cut_feed",
    )(ids, w)


def start_sides(go, piece, target, chip, core, tag):
    return [
        (tag, go.start(piece.at[:128], target.at[rows(2 * chip + core, 128)])),
        (tag, go.start(piece.at[128:], target.at[rows(2 * chip + 1 - core, 128)])),
    ]


def attend(pair, qs, ks, vs, ctxs, stats):
    keys = ks[pair]
    values = jnp.concatenate([jnp.transpose(vs[pair]), jnp.ones((128, 1024), bf16)], axis=0)
    for i in range(4):
        ext = (i + 1) * BLOCK
        cols = slice(i * BLOCK, ext)
        query = qs[pair, cols]
        low = low_half(query)
        zero = jnp.zeros_like(query)
        parts = []
        for a in range(2):
            part = jnp.where(low, query, zero) if a == 0 else jnp.where(low, zero, query)
            scores = nt(keys[:ext], part)
            last = scores[i * BLOCK :]
            r = lax.broadcasted_iota(jnp.int32, last.shape, 0)
            c = lax.broadcasted_iota(jnp.int32, last.shape, 1)
            last = jnp.where(r <= c, last, -1e30)
            scores = jnp.concatenate([scores[: i * BLOCK], last], axis=0) if i else last
            top = jnp.max(scores, axis=0, keepdims=True)
            expo = jnp.exp(scores - top).astype(bf16)
            wide = nn(values[:, :ext], expo)
            total = wide[128:129]
            parts.append(wide[64 * a : 64 * a + 64] * (1.0 / total))
            stats[pair, a : a + 1, cols] = top + jnp.log(total)
        ctxs[pair, cols] = jnp.transpose(jnp.concatenate(parts, axis=0).astype(bf16))


def first_kernel(
    ids, m0, m1, others, w0, w1, w2, w3t, w3b, gain, shift, down_w, up_w, bias,
    q_out, k_out, v_out, n_out, down_out, w_out, o_out, ctx_out, stat_out, own, send,
    xs, ns, ws, os, qs, ks, vs, downs, ctxs, stats, owns, sends, sems,
):
    core, chip = ids[0], ids[2]
    go = Copies(sems)
    arrive = start_grads(go, ids, (m0, m1), (others.at[0], others.at[1]), xs)
    weights, outer, leave = [], [], []
    pieces = (w0, w1, w2, (w3t, w3b))
    part = lambda r, p: pieces[r].at[p] if r < 3 else pieces[r][p // 2].at[p % 2]
    for p in range(3):
        for r in range(4):
            weights += start_sides(go, part(r, p), ws.at[p], chip ^ r, core, p)
    for r in range(4):
        for h in range(2):
            outer.append(
                go.start(
                    part(r, 3).at[h * 128 : (h + 1) * 128],
                    os.at[rows(chip ^ r, 128), h * HALF : (h + 1) * HALF],
                )
            )
    wait_all(arrive)
    for i in range(4):
        hat, _ = center_scale(xs[i].astype(f32))
        ns[i * BLOCK : (i + 1) * BLOCK] = (hat * gain[0:1] + shift[0:1]).astype(bf16)
    leave.append(go.start(ns, n_out))
    for p, (to, out) in enumerate(((qs, q_out), (ks, k_out), (vs, v_out))):
        wait_all([copy for at, copy in weights if at == p])
        leave.append(go.start(ws.at[p], w_out.at[p]))
        for i in range(4):
            at = slice(i * BLOCK, (i + 1) * BLOCK)
            value = nn(ns[at], ws[p]) + bias[:, p * HALF : (p + 1) * HALF]
            if p == 0:
                downs[at] = nt(ns[at], down_w[...]).astype(bf16)
            if p != 1:
                value += nn(downs[at], up_w[:, p * HALF : (p + 1) * HALF])
            value = value.astype(bf16)
            if p == 0:
                value = value * jnp.asarray(0.125, bf16)
            for pair in range(4):
                to[pair, at] = value[:, 128 * pair : 128 * (pair + 1)]
        leave.append(go.start(to, out))
    down_out[...] = nt(down_w[:16], ns[...]).astype(bf16)

    @pl.loop(0, 4)
    def _(pair):
        attend(pair, qs, ks, vs, ctxs, stats)

    leave.append(go.start(ctxs, ctx_out))
    leave.append(go.start(stats, stat_out))
    wait_all(outer)
    leave.append(go.start(os, o_out))
    for side, to, out in ((1 - core, sends, send), (core, owns, own)):
        for i in range(2):
            at = rows(2 * side + i, BLOCK)
            tok = slice(i * BLOCK, (i + 1) * BLOCK)
            whole = jnp.concatenate([ctxs[p, at] for p in range(4)], axis=1)
            to[tok] = nn(whole, os[...]).astype(to.dtype)
            leave.append(go.start(to.at[tok], out.at[tok]))
    wait_all(leave)


def call_first(ids, x_own, x_other, pieces, gain, shift, down_w, up_w, bias):
    heads = shape(4, 1024, 128)
    return pl.pallas_call(
        first_kernel,
        out_shape=(
            heads,
            heads,
            heads,
            shape(1024, 1024),
            shape(16, 1024),
            shape(3, 1024, HALF),
            shape(HALF, 1024),
            heads,
            shape(4, 8, 1024, dtype=f32),
            shape(HALF, 1024, dtype=f32),
            shape(HALF, 1024),
        ),
        in_specs=[SMEM] + [HBM] * 8 + [VMEM] * 5,
        out_specs=(HBM,) * 4 + (VMEM,) + (HBM,) * 6,
        scratch_shapes=[
            pltpu.VMEM((4, BLOCK, 1024), bf16),
            pltpu.VMEM((1024, 1024), bf16),
            pltpu.VMEM((3, 1024, HALF), bf16),
            pltpu.VMEM((HALF, 1024), bf16),
            pltpu.VMEM((4, 1024, 128), bf16),
            pltpu.VMEM((4, 1024, 128), bf16),
            pltpu.VMEM((4, 1024, 128), bf16),
            pltpu.VMEM((1024, 128), bf16),
            pltpu.VMEM((4, 1024, 128), bf16),
            pltpu.VMEM((4, 8, 1024), f32),
            pltpu.VMEM((HALF, 1024), f32),
            pltpu.VMEM((HALF, 1024), bf16),
            pltpu.SemaphoreType.DMA((53,)),
        ],
        compiler_params=params(),
        name="qkv_attention",
    )(ids, *x_own, x_other, *pieces, gain, shift, down_w, up_w, bias)


def attend_back(pair, qs, ks, vs, ctxs, stats, gs, dqs, dks, dvs, acc_k, acc_v):
    keys, values = ks[pair], vs[pair]
    place = pl.ds(pl.multiple_of(pair * 128, 128), 128)
    for i in range(4):
        ext = (i + 1) * BLOCK
        cols = slice(i * BLOCK, ext)
        query, grad = qs[pair, cols], gs[pair, cols]
        low = low_half(query)
        zero = jnp.zeros_like(query)
        product = grad.astype(f32) * ctxs[pair, cols].astype(f32)
        stat = jnp.transpose(stats[pair, :, cols])
        turned_query, turned_grad = jnp.transpose(query), jnp.transpose(grad)
        new_q = []
        for a in range(2):
            pick = (lambda x, y: jnp.where(low, x, y)) if a == 0 else (lambda x, y: jnp.where(low, y, x))
            half = slice(64 * a, 64 * a + 64)
            scores = nt(pick(query, zero), keys[:ext])
            probs = jnp.exp(scores - stat[:, a : a + 1])
            last = probs[:, i * BLOCK :]
            r = lax.broadcasted_iota(jnp.int32, last.shape, 0)
            c = lax.broadcasted_iota(jnp.int32, last.shape, 1)
            last = jnp.where(r >= c, last, 0.0)
            probs = jnp.concatenate([probs[:, : i * BLOCK], last], axis=1) if i else last
            inner = jnp.sum(pick(product, 0.0), axis=1, keepdims=True)
            grad_probs = nt(pick(grad, zero), values[:ext])
            grad_scores = (probs * (grad_probs - inner)).astype(bf16)
            more_v = nn(turned_grad[half], probs.astype(bf16))
            more_k = nn(turned_query[half], grad_scores)
            if i:
                acc_v[half, : i * BLOCK] += more_v[:, : i * BLOCK]
                acc_k[half, : i * BLOCK] += more_k[:, : i * BLOCK]
            acc_v[half, cols] = more_v[:, i * BLOCK :]
            acc_k[half, cols] = more_k[:, i * BLOCK :]
            new_q.append(nn(grad_scores, keys[:ext]))
        both = jnp.where(low, new_q[0], new_q[1])
        dqs[cols, place] = (both * 0.125).astype(bf16)
    dks[:, place] = jnp.transpose(acc_k[...].astype(bf16))
    dvs[:, place] = jnp.transpose(acc_v[...].astype(bf16))


def attention_back_kernel(
    ids, q, k, v, ctx, stat, w_o, part, other, g0, g1, g2, g3, mid_own, mid_other, w, n_all, downs,
    gain, down_w, up_w,
    own, send, grad_middle, total,
    parts, others, gs, mids, gms, os, qs, ks, vs, ctxs, stats, heads, dqs, dks, dvs, acc_k, acc_v,
    ws, ns, tilts, owns, sends, sems,
):
    core = ids[0]
    go = Copies(sems)
    tokens = start_grads(go, ids, (g0, g1), (g2, g3), gs)
    first = []
    for i in range(4):
        at = slice(i * BLOCK, (i + 1) * BLOCK)
        first.append([go.start(part.at[at], parts.at[i]), go.start(other.at[at], others.at[i])])
        if i == 0:
            middles = [
                go.start(mid_own.at[1], mids.at[rows(core, HALF)]),
                go.start(mid_other.at[1], mids.at[rows(1 - core, HALF)]),
            ]
            outer = go.start(w_o, os)
    then = [
        go.start(ref, to)
        for ref, to in ((q, qs), (k, ks), (v, vs), (ctx, ctxs), (stat, stats))
    ]
    weights = [go.start(w, ws), go.start(n_all, ns)]
    wait_all(tokens)
    for i in range(4):
        at = slice(i * BLOCK, (i + 1) * BLOCK)
        wait_all(first[i])
        if i == 0:
            wait_all(middles)
        hat, inverse = center_scale(mids[at].astype(f32))
        grad = (parts[i].astype(f32) + others[i].astype(f32)) * gain[1:2]
        value = gs[i].astype(f32) + norm_back(hat, inverse, grad)
        gms[at] = value
        if i == 0:
            outer.wait()
        value = nt(value.astype(bf16), os[...]).astype(bf16)
        for pair in range(4):
            heads[pair, at] = value[:, 128 * pair : 128 * (pair + 1)]
    leave = [go.start(gms.at[rows(core, HALF)], grad_middle)]
    wait_all(then)

    @pl.loop(0, 4)
    def _(pair):
        attend_back(pair, qs, ks, vs, ctxs, stats, heads, dqs, dks, dvs, acc_k, acc_v)

    wait_all(weights)
    for side, values, out in ((1 - core, sends, send), (core, owns, own)):
        for i in range(2):
            at = rows(2 * side + i, BLOCK)
            tok = slice(i * BLOCK, (i + 1) * BLOCK)
            gq, gk, gv = dqs[at], dks[at], dvs[at]
            tilt = (nt(gq, up_w[:, :HALF]) + nt(gv, up_w[:, 2 * HALF :])).astype(bf16)
            value = nt(gq, ws[0]) + nt(gk, ws[1]) + nt(gv, ws[2]) + nn(tilt, down_w[...])
            values[tok] = value.astype(bf16)
            leave.append(go.start(values.at[tok], out.at[tok]))
    tilts[...] = (nt(up_w[:16, :HALF], dqs[...]) + nt(up_w[:16, 2 * HALF :], dvs[...])).astype(bf16)
    down_terms = nn(tilts[...], ns[...])
    total[...] = jnp.zeros_like(total)
    total[0:4] = down_terms[0:4]
    total[8:12] = down_terms[4:8]
    up_q = 8.0 * nn(downs[...], dqs[...])
    up_v = 8.0 * nn(downs[...], dvs[...])
    for pair in range(4):
        here = pl.ds(pl.multiple_of(256 * pair + 128 * core, 128), 128)
        total[4:8, here] = up_q[0:4, 128 * pair : 128 * (pair + 1)]
        total[12:16, here] = up_v[4:8, 128 * pair : 128 * (pair + 1)]
    wait_all(leave)


def call_attention_back(
    ids, q, k, v, ctx, stat, w_o, part, other, g_own, g_other, mid_own, mid_other,
    w, n_all, downs, gain, down_w, up_w,
):
    pairs = pltpu.VMEM((4, 1024, 128), bf16)
    wide = pltpu.VMEM((1024, HALF), bf16)
    return pl.pallas_call(
        attention_back_kernel,
        out_shape=(
            shape(HALF, 1024),
            shape(HALF, 1024),
            shape(HALF, 1024, dtype=f32),
            shape(16, 1024, dtype=f32),
        ),
        in_specs=[SMEM] + [HBM] * 16 + [VMEM] * 4,
        out_specs=(HBM, HBM, HBM, VMEM),
        scratch_shapes=[
            pltpu.VMEM((4, BLOCK, 1024), bf16),
            pltpu.VMEM((4, BLOCK, 1024), bf16),
            pltpu.VMEM((4, BLOCK, 1024), bf16),
            pltpu.VMEM((1024, 1024), bf16),
            pltpu.VMEM((1024, 1024), f32),
            pltpu.VMEM((HALF, 1024), bf16),
            pairs,
            pairs,
            pairs,
            pairs,
            pltpu.VMEM((4, 8, 1024), f32),
            pairs,
            wide,
            wide,
            wide,
            pltpu.VMEM((128, 1024), f32),
            pltpu.VMEM((128, 1024), f32),
            pltpu.VMEM((3, 1024, HALF), bf16),
            pltpu.VMEM((1024, 1024), bf16),
            pltpu.VMEM((16, 1024), bf16),
            pltpu.VMEM((HALF, 1024), bf16),
            pltpu.VMEM((HALF, 1024), bf16),
            pltpu.SemaphoreType.DMA((28,)),
        ],
        compiler_params=params(),
        name="attention_back",
    )(
        ids, q, k, v, ctx, stat, w_o, part, other, *g_own, *g_other, mid_own, mid_other,
        w, n_all, downs, gain, down_w, up_w,
    )


def low_half(value):
    return lax.broadcasted_iota(jnp.int32, value.shape, 1) < 64


def start_tokens(go, pair, target, z):
    return [go.start(ref, target.at[parity(z, k)]) for k, ref in enumerate(pair)]


def middle_kernel(
    ids, own, other, x0, x1, bias, gain, shift, middle, both, owns, others, xs, mids, lows, ns, sems
):
    go = Copies(sems)
    tokens = start_tokens(go, (x0, x1), xs, ids[1])
    parts = []
    for i in range(2):
        at = slice(i * BLOCK, (i + 1) * BLOCK)
        parts.append([go.start(own.at[at], owns.at[i]), go.start(other.at[at], others.at[i])])
    wait_all(tokens)
    leave = []
    for i in range(2):
        at = slice(i * BLOCK, (i + 1) * BLOCK)
        wait_all(parts[i])
        value = owns[i] + others[i].astype(f32) + xs[i].astype(f32) + bias[2:3]
        mids[i] = value
        leave.append(go.start(mids.at[i], middle.at[at]))
        lows[i] = value.astype(bf16)
        leave.append(go.start(lows.at[i], both.at[1, at]))
        hat, _ = center_scale(value)
        ns[i] = (hat * gain[1:2] + shift[1:2]).astype(bf16)
        leave.append(go.start(ns.at[i], both.at[0, at]))
    wait_all(leave)


def call_middle(ids, own, other, x_own, bias, gain, shift):
    return pl.pallas_call(
        middle_kernel,
        out_shape=(shape(HALF, 1024, dtype=f32), shape(2, HALF, 1024)),
        in_specs=[SMEM] + [HBM] * 4 + [VMEM] * 3,
        out_specs=(HBM, HBM),
        scratch_shapes=[
            pltpu.VMEM((2, BLOCK, 1024), f32),
            pltpu.VMEM((2, BLOCK, 1024), bf16),
            pltpu.VMEM((2, BLOCK, 1024), bf16),
            pltpu.VMEM((2, BLOCK, 1024), f32),
            pltpu.VMEM((2, BLOCK, 1024), bf16),
            pltpu.VMEM((2, BLOCK, 1024), bf16),
            pltpu.SemaphoreType.DMA((12,)),
        ],
        compiler_params=params(),
        name="middle",
    )(ids, own, other, *x_own, bias, gain, shift)


def start_grads(go, ids, g_own, g_other, gs):
    core, z = ids[0], ids[1]
    return [
        go.start(ref, gs.at[2 * side + parity(z, k)])
        for side, pair in ((core, g_own), (1 - core, g_other))
        for k, ref in enumerate(pair)
    ]


def hidden_kernel(
    ids, n_own, n_other, w0, w1, w2, w3t, w3b, bias, piece,
    active, slope, w_out, result, ns, ws, acts, slopes, wo, results, sems,
):
    core, chip = ids[0], ids[2]
    go = Copies(sems)
    arrive = [
        go.start(n_own.at[0], ns.at[rows(core, HALF)]),
        go.start(n_other.at[0], ns.at[rows(1 - core, HALF)]),
    ]
    weights = []
    for p in range(4):
        for r, ref in enumerate((w0, w1, w2, (w3t, w3b))):
            part = ref.at[p] if r < 3 else ref[p // 2].at[p % 2]
            weights += start_sides(go, part, ws.at[p], chip ^ r, core, p)
    later = go.start(piece, wo)
    wait_all(arrive)
    leave = []

    def finish(p, i, h):
        at = slice(i * BLOCK, (i + 1) * BLOCK)
        square = h * h
        lift = 0.5 + 0.5 * jnp.tanh(h * (GELU_A + (GELU_A * GELU_B) * square))
        act = h * lift
        acts[p, at] = act.astype(bf16)
        rise = 2.0 * GELU_A + (6.0 * GELU_A * GELU_B) * square
        slopes[p, at] = (lift + (act - act * lift) * rise).astype(bf16)
        if i == 3:
            leave.append(go.start(acts.at[p], active.at[p]))
            leave.append(go.start(slopes.at[p], slope.at[p]))

    before = None
    for p in range(4):
        wait_all([copy for at, copy in weights if at == p])
        leave.append(go.start(ws.at[p], w_out.at[p]))
        shift = bias[pl.ds(2 * p + core, 1)]
        for i in range(4):
            h = nn(ns[i * BLOCK : (i + 1) * BLOCK], ws[p]) + shift
            if before is not None:
                finish(*before)
            before = (p, i, h)
    finish(*before)
    later.wait()
    for i in range(4):
        tok = slice(i * BLOCK, (i + 1) * BLOCK)
        results[tok] = nn(acts[chip, tok], wo[...]).astype(bf16)
        leave.append(go.start(results.at[tok], result.at[tok]))
    wait_all(leave)


def call_hidden(ids, n_own, n_other, pieces, bias, piece):
    return pl.pallas_call(
        hidden_kernel,
        out_shape=(shape(4, 1024, HALF),) * 3 + (shape(1024, 1024),),
        in_specs=[SMEM] + [HBM] * 7 + [VMEM, HBM],
        out_specs=(HBM,) * 4,
        scratch_shapes=[pltpu.VMEM((1024, 1024), bf16)]
        + [pltpu.VMEM((4, 1024, HALF), bf16)] * 3
        + [
            pltpu.VMEM((HALF, 1024), bf16),
            pltpu.VMEM((1024, 1024), bf16),
            pltpu.SemaphoreType.DMA((59,)),
        ],
        compiler_params=params(),
        name="hidden",
    )(ids, n_own, n_other, *pieces, bias, piece)


def feed_kernel(
    ids, g0, g1, g2, g3, active, slope, w_in, own_piece, x_piece, y_piece, old_result,
    result, grad, gs, acts, slopes, w_ins, w_outs, olds, results, grads, sems,
):
    core, z, chip = ids[0], ids[1], ids[2]
    go = Copies(sems)
    pieces = (own_piece, x_piece, y_piece)
    sources = [(core, 0, g0), (core, 1, g1), (1 - core, 0, g2), (1 - core, 1, g3)]
    blocks = [2 * side + parity(z, k) for side, k, _ in sources]
    tokens, wide, loads = [], [], [[] for _ in range(4)]

    def start_wide(r):
        wide.append((go.start(pieces[r], w_outs.at[r]), go.start(w_in.at[chip ^ r], w_ins.at[r])))

    def start_block(i, r):
        tok = rows(blocks[i], BLOCK)
        copies = [go.start(slope.at[chip ^ r, tok], slopes.at[r, i])]
        if r == 0:
            copies.append(go.start(old_result.at[tok], olds.at[i]))
        else:
            copies.append(go.start(active.at[chip ^ r, tok], acts.at[r, i]))
        loads[i].append(copies)

    tokens.append(go.start(sources[0][2], gs.at[0]))
    for r in range(3):
        start_wide(r)
        start_block(0, r)
    for i in range(1, 4):
        tokens.append(go.start(sources[i][2], gs.at[i]))
        for r in range(3):
            start_block(i, r)
    leave = []
    for i in range(4):
        tokens[i].wait()
        grad_sum = out_sum = None
        for r in range(3):
            if i == 0:
                wide[r][0].wait()
            back = nt(gs[i], w_outs[r])
            wait_all(loads[i][r])
            if i == 0:
                wide[r][1].wait()
            back = (back * slopes[r, i].astype(f32)).astype(bf16)
            if r == 0:
                grad_sum = nt(back, w_ins[r])
                out_sum = olds[i].astype(f32)
            else:
                grad_sum += nt(back, w_ins[r])
                out_sum += nn(acts[r, i], w_outs[r])
        results[i] = out_sum.astype(bf16)
        grads[i] = grad_sum.astype(bf16)
        tok = rows(blocks[i], BLOCK)
        leave.append(go.start(results.at[i], result.at[tok]))
        leave.append(go.start(grads.at[i], grad.at[tok]))
    wait_all(leave)


def call_feed(ids, g_own, g_other, active, slope, w_in, pieces, old):
    return pl.pallas_call(
        feed_kernel,
        out_shape=(shape(1024, 1024),) * 2,
        in_specs=[SMEM] + [HBM] * 11,
        out_specs=(HBM, HBM),
        scratch_shapes=[
            pltpu.VMEM((4, BLOCK, 1024), bf16),
            pltpu.VMEM((3, 4, BLOCK, HALF), bf16),
            pltpu.VMEM((3, 4, BLOCK, HALF), bf16),
            pltpu.VMEM((3, 1024, HALF), bf16),
            pltpu.VMEM((3, HALF, 1024), bf16),
        ]
        + [pltpu.VMEM((4, BLOCK, 1024), bf16)] * 3
        + [pltpu.SemaphoreType.DMA((50,))],
        compiler_params=params(),
        name="feed",
    )(ids, *g_own, *g_other, active, slope, w_in, *pieces, old)


def far_grad_kernel(
    ids, g0, g1, g2, g3, slope, w_in, top, low, old, out, gs, slopes, w_ins, w_outs, olds, outs, sems
):
    chip = ids[2]
    go = Copies(sems)
    arrive = [go.start(top, w_outs.at[:BLOCK]), go.start(low, w_outs.at[BLOCK:])]
    tokens = start_grads(go, ids, (g0, g1), (g2, g3), gs)
    near = [go.start(slope.at[chip ^ 3], slopes), go.start(w_in.at[chip ^ 3], w_ins)]
    load = go.start(old, olds)
    wait_all(arrive)
    wait_all(tokens)
    leave = []
    for i in range(4):
        tok = slice(i * BLOCK, (i + 1) * BLOCK)
        back = nt(gs[i], w_outs[...])
        if i == 0:
            wait_all(near)
        back = back * slopes[tok].astype(f32)
        more = nt(back.astype(bf16), w_ins[...])
        if i == 0:
            load.wait()
        outs[tok] = (more + olds[tok].astype(f32)).astype(bf16)
        leave.append(go.start(outs.at[tok], out.at[tok]))
    wait_all(leave)


def call_far_grad(ids, g_own, g_other, slope, w_in, far, old):
    return pl.pallas_call(
        far_grad_kernel,
        out_shape=shape(1024, 1024),
        in_specs=[SMEM] + [HBM] * 9,
        out_specs=HBM,
        scratch_shapes=[
            pltpu.VMEM((4, BLOCK, 1024), bf16),
            pltpu.VMEM((1024, HALF), bf16),
            pltpu.VMEM((1024, HALF), bf16),
            pltpu.VMEM((HALF, 1024), bf16),
            pltpu.VMEM((1024, 1024), bf16),
            pltpu.VMEM((1024, 1024), bf16),
            pltpu.SemaphoreType.DMA((13,)),
        ],
        compiler_params=params(),
        name="far_grad",
    )(ids, *g_own, *g_other, slope, w_in, *far, old)


def far_result_kernel(
    ids, active, top, low, old, own, send, acts, w_outs, olds, owns, sends, sems
):
    core, chip = ids[0], ids[2]
    go = Copies(sems)
    arrive = [
        go.start(top, w_outs.at[:BLOCK]),
        go.start(low, w_outs.at[BLOCK:]),
        go.start(active.at[chip ^ 3], acts),
    ]
    load = go.start(old, olds)
    wait_all(arrive)
    load.wait()
    leave = []
    for side, values, out in ((1 - core, sends, send), (core, owns, own)):
        for i in range(2):
            at = rows(2 * side + i, BLOCK)
            tok = slice(i * BLOCK, (i + 1) * BLOCK)
            values[tok] = (olds[at].astype(f32) + nn(acts[at], w_outs[...])).astype(values.dtype)
            leave.append(go.start(values.at[tok], out.at[tok]))
    wait_all(leave)


def call_far_result(ids, active, far, old):
    return pl.pallas_call(
        far_result_kernel,
        out_shape=(shape(HALF, 1024), shape(HALF, 1024)),
        in_specs=[SMEM] + [HBM] * 4,
        out_specs=(HBM, HBM),
        scratch_shapes=[
            pltpu.VMEM((1024, HALF), bf16),
            pltpu.VMEM((HALF, 1024), bf16),
            pltpu.VMEM((1024, 1024), bf16),
            pltpu.VMEM((HALF, 1024), bf16),
            pltpu.VMEM((HALF, 1024), bf16),
            pltpu.SemaphoreType.DMA((8,)),
        ],
        compiler_params=params(),
        name="far_result",
    )(ids, active, *far, old)


def mixed_kernel(ids, own, other, middle, bias, out0, out1, owns, others, mids, outs, sems):
    z = ids[1]
    go = Copies(sems)
    loads = []
    for at in range(4):
        tok = rows(2 * parity(z, at // 2) + at % 2, 128)
        loads.append(
            [go.start(ref.at[tok], to.at[at]) for ref, to in ((own, owns), (other, others), (middle, mids))]
        )
    leave = []
    for at in range(4):
        wait_all(loads[at])
        value = owns[at].astype(f32) + others[at].astype(f32) + mids[at] + bias[3:4]
        outs[at] = value.astype(bf16)
        to = (out0, out1)[at // 2].at[at % 2 * 128 : (at % 2 + 1) * 128]
        leave.append(go.start(outs.at[at], to))
    wait_all(leave)


def call_mixed(ids, own, other, middle, bias):
    return pl.pallas_call(
        mixed_kernel,
        out_shape=(shape(BLOCK, 1024),) * 2,
        in_specs=[SMEM] + [HBM] * 3 + [VMEM],
        out_specs=(HBM, HBM),
        scratch_shapes=[
            pltpu.VMEM((4, 128, 1024), bf16),
            pltpu.VMEM((4, 128, 1024), bf16),
            pltpu.VMEM((4, 128, 1024), f32),
            pltpu.VMEM((4, 128, 1024), bf16),
            pltpu.SemaphoreType.DMA((16,)),
        ],
        compiler_params=params(),
        name="mixed",
    )(ids, own, other, middle, bias)


def input_grad_kernel(
    ids, x0, x1, own, other, grad_middle, gain, out0, out1, xs, owns, others, grads, outs, sems
):
    z = ids[1]
    go = Copies(sems)
    loads = []
    for at in range(4):
        tok = rows(2 * parity(z, at // 2) + at % 2, 128)
        here = slice(at % 2 * 128, (at % 2 + 1) * 128)
        copies = [go.start((x0, x1)[at // 2].at[here], xs.at[at])]
        for ref, to in ((own, owns), (other, others), (grad_middle, grads)):
            copies.append(go.start(ref.at[tok], to.at[at]))
        loads.append(copies)
    leave = []
    for at in range(4):
        wait_all(loads[at])
        grad = (owns[at].astype(f32) + others[at].astype(f32)) * gain[0:1]
        hat, inverse = center_scale(xs[at].astype(f32))
        outs[at] = (grads[at] + norm_back(hat, inverse, grad)).astype(bf16)
        to = (out0, out1)[at // 2].at[at % 2 * 128 : (at % 2 + 1) * 128]
        leave.append(go.start(outs.at[at], to))
    wait_all(leave)


def call_input_grad(ids, x_own, own, other, grad_middle, gain):
    return pl.pallas_call(
        input_grad_kernel,
        out_shape=(shape(BLOCK, 1024),) * 2,
        in_specs=[SMEM] + [HBM] * 5 + [VMEM],
        out_specs=(HBM, HBM),
        scratch_shapes=[
            pltpu.VMEM((4, 128, 1024), bf16),
            pltpu.VMEM((4, 128, 1024), bf16),
            pltpu.VMEM((4, 128, 1024), bf16),
            pltpu.VMEM((4, 128, 1024), f32),
            pltpu.VMEM((4, 128, 1024), bf16),
            pltpu.SemaphoreType.DMA((20,)),
        ],
        compiler_params=params(),
        name="input_grad",
    )(ids, *x_own, own, other, grad_middle, gain)


def to_core(value):
    return lax.ppermute(value, "core", SWAP)


def total_over(value, axis, *others):
    flip = [lax.ppermute(value, axis, [(i, i ^ by) for i in range(4)]) for by in (1, 2, 3)]
    flip = after(flip, *others)
    return (value + flip[0]) + (flip[1] + flip[2])


def exchange(z, pair):
    sent = []
    for k in range(2):
        perm = [
            (4 * core + at, 4 * (at // 2) + 2 * core + (at + k) % 2)
            for core in range(2)
            for at in range(4)
        ]
        sent.append(lax.ppermute(pair[k], ("core", "seq"), perm))
    return sent


def by_parity(z, pair):
    even = lax.rem(z, 2) == 0
    return jnp.where(even, pair[0], pair[1]), jnp.where(even, pair[1], pair[0])


def after(value, *others):
    return lax.optimization_barrier((value, *others))[0]


def gather_near(shard):
    return [shard, lax.ppermute(shard, "x", SWAP), lax.ppermute(shard, "y", SWAP)]


def halves(near):
    return call_halves(near[1], near[2])


def halves_kernel(by_x, by_y, first, second, held, sems):
    half = first.shape[0]
    go = Copies(sems)
    loads = [go.start(by_x.at[:half], held.at[0]), go.start(by_y.at[half:], held.at[1])]
    leave = []
    for at, out in enumerate((first, second)):
        loads[at].wait()
        leave.append(go.start(held.at[at], out))
    wait_all(leave)


def call_halves(by_x, by_y):
    dims = (by_x.shape[0] // 2, *by_x.shape[1:])
    return pl.pallas_call(
        halves_kernel,
        out_shape=(shape(*dims), shape(*dims)),
        in_specs=[HBM, HBM],
        out_specs=(HBM, HBM),
        scratch_shapes=[pltpu.VMEM((2, *dims), bf16), pltpu.SemaphoreType.DMA((4,))],
        compiler_params=params(),
        name="halves",
    )(by_x, by_y)


def gather_far(near, parts):
    return near + [lax.ppermute(parts[0], "y", SWAP), lax.ppermute(parts[1], "x", SWAP)]


def on_chip(
    inputs,
    out_grad,
    norm_gain,
    norm_bias,
    proj_bias,
    fc_bias,
    qkv_weight,
    out_weight,
    feed_input_weight,
    proj_weight,
    adapters,
    first_moment,
    second_moment,
):
    width = inputs.shape[2]
    core = lax.axis_index("core")
    z = lax.axis_index("seq")
    chip = 2 * lax.axis_index("y") + lax.axis_index("x")
    ids = jnp.stack([core, z, chip]).astype(jnp.int32)

    qkv_own, qkv_send, out_part = call_cut(ids, qkv_weight, out_weight)
    qkv_got = to_core(qkv_send)
    first_shard = jnp.concatenate([jnp.concatenate([qkv_own, qkv_got], axis=1), out_part], axis=0)
    first_near = gather_near(first_shard)
    x_own = exchange(z, by_parity(z, after((inputs[0], inputs[1]), first_shard)))
    in_own, in_send = call_cut_feed(ids, after(feed_input_weight, first_shard))
    in_shard = jnp.concatenate([in_own, to_core(in_send)], axis=1)

    def columns(value):
        lead = value.shape[0]
        value = value.reshape(lead, 4, 2, 128)
        return jnp.where(core == 0, value[:, :, 0], value[:, :, 1]).reshape(lead, HALF)

    scale = adapter_alpha / ADAPTER_RANK
    adapters, proj_bias = after((adapters, proj_bias), first_shard)
    up_q, up_v = scale * columns(adapters[1]), scale * columns(adapters[3])
    up_w = jnp.zeros((128, 1536), f32)
    up_w = up_w.at[0:4, :HALF].set(up_q).at[4:8, 2 * HALF :].set(up_v).astype(bf16)
    down_w = jnp.concatenate([adapters[0], adapters[2], jnp.zeros((120, 1024), f32)], axis=0)
    down_w = down_w.astype(bf16)
    head_bias = columns(proj_bias[:2])
    qkv_bias = jnp.concatenate([head_bias[0], jnp.zeros((HALF,), f32), head_bias[1]])[None]

    first_near = after(first_near, up_w, down_w, qkv_bias, in_shard)
    first_halves = halves(first_near)
    first_pieces = gather_far(first_near, first_halves)
    x_own = after(x_own, *first_halves)
    x_other = to_core(jnp.stack(x_own))
    in_near = gather_near(after(in_shard, *first_pieces[3:]))
    q, k, v, n_all, down, w_qkv, w_o, ctx, stat, attn_own, attn_send = call_first(
        ids, x_own, x_other, first_pieces, norm_gain, norm_bias, down_w, up_w, qkv_bias
    )
    in_near = after(in_near, ctx)
    in_halves = halves(in_near)
    in_pieces = gather_far(in_near, in_halves)
    attn_other = to_core(after(attn_send, *in_halves))
    middle, n2_own = call_middle(
        ids, attn_own, after(attn_other, *in_halves), x_own, proj_bias, norm_gain, norm_bias
    )
    g_pair = by_parity(z, after((out_grad[0], out_grad[1]), n2_own))
    in_pieces[3:] = after(in_pieces[3:], *g_pair)
    g_own = exchange(z, g_pair)
    n2_other = to_core(after(n2_own, *in_pieces[3:]))
    proj_near = gather_near(after(proj_weight, *in_pieces[3:]))
    active, slope, w_in, old = call_hidden(
        ids, n2_own, n2_other, in_pieces, fc_bias.reshape(8, HALF), proj_near[0]
    )
    proj_near = after(proj_near, old)
    proj_halves = halves(proj_near)
    far = gather_far(proj_near, proj_halves)[3:]
    near = after(proj_near, *proj_halves)
    g_own = after(g_own, *proj_halves)
    g_other = [to_core(part) for part in g_own]
    result, grad = call_feed(ids, g_own, g_other, active, slope, w_in, near, old)
    result_own, result_send = call_far_result(ids, active, far, result)
    result_other = to_core(result_send)
    part = call_far_grad(ids, g_own, g_other, slope, w_in, after(far, result_own), grad)
    part = after(part, result_other)
    part_other = to_core(part)
    mixed = call_mixed(ids, result_own, after(result_other, part), middle, proj_bias)
    part_other = after(part_other, *mixed)
    mixed = exchange(z, mixed)
    own, send, grad_middle, total = call_attention_back(
        ids, q, k, v, ctx, stat, w_o, part, part_other, g_own, g_other, n2_own, n2_other,
        w_qkv, n_all, down, norm_gain, down_w, up_w,
    )
    other = to_core(after(send, *mixed))
    grad_in = call_input_grad(ids, x_own, own, other, grad_middle, norm_gain)
    total = total_over(total, "seq", *grad_in)
    grad_in = exchange(z, grad_in)
    total = total + to_core(total)
    total = total_over(total, ("y", "x"))
    total = total.reshape(4, ADAPTER_RANK, width)
    grad_norm = jnp.sqrt(jnp.sum(total * total))
    clipped, new_weight, new_first, new_second = adam_update(
        total, adapters, first_moment, second_moment, grad_norm
    )
    mixed = jnp.stack(by_parity(z, after(mixed, new_weight)))
    grad_input = jnp.stack(by_parity(z, grad_in))
    return (mixed, grad_input, clipped, grad_norm, new_weight, new_first, new_second)


def solution(mesh):
    sizes = dict(mesh.shape)
    if sizes["dp"] == 8 and sizes["seq"] == 4:
        plane = Mesh(mesh.devices.reshape(2, 2, 2, 4), ("y", "x", "core", "seq"))
        return build(plane, ("y", "x", "core"), on_chip)
    return build(mesh, "dp", on_device)


def build(mesh, dp, step):
    tokens, weight = P(dp, "seq", None), P(dp, None)
    return jax.shard_map(
        step,
        mesh=mesh,
        in_specs=(tokens, tokens) + (P(),) * 4 + (weight,) * 4 + (P(),) * 3,
        out_specs=(tokens, tokens) + (P(),) * 5,
        check_vma=False,
    )
```

```python
import functools
import math

import jax
import jax.numpy as jnp
from jax import lax
from jax.experimental import pallas as pl
from jax.experimental.pallas import tpu as pltpu
from jax.sharding import Mesh
from jax.sharding import PartitionSpec as P

HEAD_DIM = 64
ADAPTER_RANK = 4
STEP = 10


highest = lax.Precision.HIGHEST
adapter_alpha = 32.0
beta_one = 0.9
beta_two = 0.999
adam_eps = 1e-08
decay_rate = 0.01
learning_rate = 0.02
clip_bound = 1.0
norm_eps = 1e-05


def layer_norm(value, gain, shift):
    center = jnp.mean(value, axis=-1, keepdims=True)
    centered = value - center
    spread = jnp.mean(centered * centered, axis=-1, keepdims=True)
    return centered * lax.rsqrt(spread + norm_eps) * gain + shift


def dot_trans(left, right):
    return lax.dot_general(
        left, right, (((1,), (1,)), ((), ())), preferred_element_type=jnp.float32
    )


def dot_first(left, right):
    return lax.dot_general(
        left, right, (((0,), (0,)), ((), ())), precision=highest, preferred_element_type=jnp.float32
    )


def adam_update(grad, weight, first, second, norm):
    scale_factor = clip_bound / jnp.maximum(norm, clip_bound)
    clipped = grad * scale_factor
    new_first = beta_one * first + (1.0 - beta_one) * clipped
    new_second = beta_two * second + (1.0 - beta_two) * clipped * clipped
    first_hat = new_first / (1.0 - beta_one**STEP)
    second_hat = new_second / (1.0 - beta_two**STEP)
    new_weight = weight - learning_rate * (
        first_hat / (jnp.sqrt(second_hat) + adam_eps) + decay_rate * weight
    )
    return (clipped, new_weight, new_first, new_second)


def split_heads(packed):
    length = packed.shape[0]
    local_heads = packed.shape[-1] // HEAD_DIM
    query = packed[:, 0, 0].reshape(length, local_heads, HEAD_DIM)
    keys = packed[:, 1, 0].reshape(length, local_heads, HEAD_DIM)
    values = packed[:, 2, 0].reshape(length, local_heads, HEAD_DIM)
    return (query, keys, values)


def doc_forward(packed):
    length = packed.shape[0]
    local_width = packed.shape[-1]
    query, keys, values = split_heads(packed)
    local_heads = query.shape[1]
    span = min(512, length)
    blocks = length // span
    scale = 1.0 / math.sqrt(HEAD_DIM)
    starts = jnp.arange(blocks, dtype=jnp.int32) * span

    def visit(pieces):
        query_block, start = pieces
        scores = (
            jnp.einsum("qhd,khd->hqk", query_block, keys, preferred_element_type=jnp.float32)
            * scale
        )
        causal = (start + jnp.arange(span))[:, None] >= jnp.arange(length)[None, :]
        masked = jnp.where(causal[None], scores, -1e30)
        summit = jnp.max(masked, axis=-1, keepdims=True)
        expo = jnp.where(causal[None], jnp.exp(masked - summit), 0.0)
        totals = jnp.sum(expo, axis=-1, keepdims=True)
        weights = (expo / totals).astype(jnp.bfloat16)
        context = jnp.einsum(
            "hqk,khd->qhd", weights, values, preferred_element_type=jnp.float32
        ).astype(jnp.bfloat16)
        return (context, summit[..., 0] + jnp.log(totals[..., 0]))

    context, log_total = lax.map(
        visit, (query.reshape(blocks, span, local_heads, HEAD_DIM), starts)
    )
    return (context.reshape(length, 1, local_width), log_total)


def doc_backward(args):
    packed, grad_context, log_total = args
    length = packed.shape[0]
    local_width = packed.shape[-1]
    query, keys, values = split_heads(packed)
    local_heads = query.shape[1]
    output_gradient = grad_context[:, 0].reshape(length, local_heads, HEAD_DIM)
    span = min(512, length)
    blocks = length // span
    scale = 1.0 / math.sqrt(HEAD_DIM)
    starts = jnp.arange(blocks, dtype=jnp.int32) * span

    def visit(carry, pieces):
        grad_keys, grad_values = carry
        query_block, grad_block, total_block, start = pieces
        scores = (
            jnp.einsum("qhd,khd->hqk", query_block, keys, preferred_element_type=jnp.float32)
            * scale
        )
        causal = (start + jnp.arange(span))[:, None] >= jnp.arange(length)[None, :]
        masked = jnp.where(causal[None], scores, -1e30)
        probs = jnp.where(causal[None], jnp.exp(masked - total_block[:, :, None]), 0.0)
        weights = probs.astype(jnp.bfloat16)
        grad_probs = jnp.einsum(
            "qhd,khd->hqk", grad_block, values, preferred_element_type=jnp.float32
        )
        inner = jnp.sum(probs * grad_probs, axis=-1, keepdims=True)
        grad_scores = (probs * (grad_probs - inner)).astype(jnp.bfloat16)
        grad_query = (
            jnp.einsum("hqk,khd->qhd", grad_scores, keys, preferred_element_type=jnp.float32)
            * scale
        )
        grad_keys = (
            grad_keys
            + jnp.einsum(
                "hqk,qhd->khd", grad_scores, query_block, preferred_element_type=jnp.float32
            )
            * scale
        )
        grad_values = grad_values + jnp.einsum(
            "hqk,qhd->khd", weights, grad_block, preferred_element_type=jnp.float32
        )
        return ((grad_keys, grad_values), grad_query)

    empty = jnp.zeros((length, local_heads, HEAD_DIM), jnp.float32)
    pieces = (
        query.reshape(blocks, span, local_heads, HEAD_DIM),
        output_gradient.reshape(blocks, span, local_heads, HEAD_DIM),
        log_total,
        starts,
    )
    (grad_keys, grad_values), grad_query = lax.scan(visit, (empty, empty), pieces)
    joined = jnp.stack(
        [
            grad_query.reshape(length, local_width),
            grad_keys.reshape(length, local_width),
            grad_values.reshape(length, local_width),
        ],
        axis=1,
    )
    return joined.astype(jnp.bfloat16)[:, :, None, :]


def on_device(
    inputs,
    out_grad,
    norm_gain,
    norm_bias,
    proj_bias,
    fc_bias,
    qkv_weight,
    out_weight,
    feed_input_weight,
    proj_weight,
    adapters,
    first_moment,
    second_moment,
):
    docs, tokens, width = inputs.shape
    count = docs * tokens
    ranks = lax.axis_size("seq")
    scale_factor = adapter_alpha / ADAPTER_RANK

    def forward(stack):
        qkv_full, out_full, fc_full, proj_full = stack
        flat = inputs.reshape(count, width).astype(jnp.float32)
        normed, norm_one_back = jax.vjp(
            lambda value: layer_norm(value, norm_gain[0], norm_bias[0]), flat
        )
        base = jnp.dot(normed.astype(jnp.bfloat16), qkv_full, preferred_element_type=jnp.float32)
        down_q = jnp.dot(normed, adapters[0].T, precision=highest)
        down_v = jnp.dot(normed, adapters[2].T, precision=highest)
        query = (
            base[:, :width]
            + proj_bias[0]
            + scale_factor * jnp.dot(down_q, adapters[1], precision=highest)
        )
        keys = base[:, width : 2 * width]
        values = (
            base[:, 2 * width :]
            + proj_bias[1]
            + scale_factor * jnp.dot(down_v, adapters[3], precision=highest)
        )
        joined = (
            jnp.concatenate([query, keys, values], axis=1)
            .astype(jnp.bfloat16)
            .reshape(docs, tokens, 3, ranks, width // ranks)
        )
        spread = lax.all_to_all(joined, "seq", split_axis=3, concat_axis=1, tiled=True)
        context, log_total = lax.map(doc_forward, spread)
        context = lax.all_to_all(context, "seq", split_axis=1, concat_axis=2, tiled=True).reshape(
            count, width
        )
        middle = (
            flat + jnp.dot(context, out_full, preferred_element_type=jnp.float32) + proj_bias[2]
        )
        normed_two, norm_two_back = jax.vjp(
            lambda value: layer_norm(value, norm_gain[1], norm_bias[1]), middle
        )
        hidden = (
            jnp.dot(normed_two.astype(jnp.bfloat16), fc_full, preferred_element_type=jnp.float32)
            + fc_bias
        )
        active, gelu_back = jax.vjp(lambda value: jax.nn.gelu(value, approximate=True), hidden)
        result = (
            middle
            + jnp.dot(active.astype(jnp.bfloat16), proj_full, preferred_element_type=jnp.float32)
            + proj_bias[3]
        )
        return (
            result,
            (normed, down_q, down_v, norm_one_back, spread, log_total, norm_two_back, gelu_back),
        )

    stack = (
        lax.all_gather(qkv_weight, "dp", axis=0, tiled=True),
        lax.all_gather(out_weight, "dp", axis=0, tiled=True),
        lax.all_gather(feed_input_weight, "dp", axis=0, tiled=True),
        lax.all_gather(proj_weight, "dp", axis=0, tiled=True),
    )
    result, kept = forward(stack)
    fenced = lax.optimization_barrier((stack, result))
    stack = fenced[0]
    again, kept = forward(stack)
    qkv_full, out_full, fc_full, proj_full = stack
    normed, down_q, down_v, norm_one_back, spread, log_total, norm_two_back, gelu_back = kept
    cotangent = out_grad.reshape(count, width)
    grad_active = dot_trans(cotangent, proj_full)
    grad_hidden = gelu_back(grad_active)[0].astype(jnp.bfloat16)
    grad_normed_two = dot_trans(grad_hidden, fc_full)
    grad_middle = cotangent.astype(jnp.float32) + norm_two_back(grad_normed_two)[0]
    grad_context = dot_trans(grad_middle.astype(jnp.bfloat16), out_full).astype(jnp.bfloat16)
    grad_context = grad_context.reshape(docs, tokens, ranks, width // ranks)
    grad_context = lax.all_to_all(grad_context, "seq", split_axis=2, concat_axis=1, tiled=True)
    grad_joined = lax.map(doc_backward, (spread, grad_context, log_total))
    grad_joined = lax.all_to_all(
        grad_joined, "seq", split_axis=1, concat_axis=3, tiled=True
    ).reshape(count, 3 * width)
    grad_normed = dot_trans(grad_joined, qkv_full)
    grad_query = grad_joined[:, :width].astype(jnp.float32)
    grad_value = grad_joined[:, 2 * width :].astype(jnp.float32)
    tilt_q = scale_factor * jnp.dot(grad_query, adapters[1].T, precision=highest)
    value_adapter_up = scale_factor * jnp.dot(grad_value, adapters[3].T, precision=highest)
    grad_normed = (
        grad_normed
        + jnp.dot(tilt_q, adapters[0], precision=highest)
        + jnp.dot(value_adapter_up, adapters[2], precision=highest)
    )
    grad_input = (
        (grad_middle + norm_one_back(grad_normed)[0])
        .astype(jnp.bfloat16)
        .reshape(docs, tokens, width)
    )
    partial_terms = jnp.stack(
        [
            dot_first(tilt_q, normed),
            scale_factor * dot_first(down_q, grad_query),
            dot_first(value_adapter_up, normed),
            scale_factor * dot_first(down_v, grad_value),
        ]
    )
    total = lax.psum(partial_terms, ("dp", "seq"))
    grad_norm = jnp.sqrt(jnp.sum(total * total))
    clipped, new_weight, new_first, new_second = adam_update(
        total, adapters, first_moment, second_moment, grad_norm
    )
    mixed = result.astype(jnp.bfloat16).reshape(docs, tokens, width)
    return (mixed, grad_input, clipped, grad_norm, new_weight, new_first, new_second)


HALF = 512
BLOCK = 256
PICK = 20
SMEM = pl.BlockSpec(memory_space=pltpu.SMEM)
VMEM = pl.BlockSpec(memory_space=pltpu.VMEM)
HBM = pl.BlockSpec(memory_space=pltpu.HBM)
FREE = pl.BlockSpec(memory_space=pl.ANY)
KEEP = pl.BlockSpec(memory_space=pltpu.VMEM)
f32 = jnp.float32
bf16 = jnp.bfloat16
SWAP = ((0, 1), (1, 0))
GELU_A = math.sqrt(2.0 / math.pi)
GELU_B = 0.044715


def nn(left, right):
    return lax.dot_general(left, right, (((1,), (0,)), ((), ())), preferred_element_type=f32)


def nt(left, right):
    return lax.dot_general(left, right, (((1,), (1,)), ((), ())), preferred_element_type=f32)


def tn(left, right):
    return lax.dot_general(left, right, (((0,), (0,)), ((), ())), preferred_element_type=f32)


def shape(*dims, dtype=bf16):
    return jax.ShapeDtypeStruct(dims, dtype)


def params(mib):
    return pltpu.CompilerParams(vmem_limit_bytes=mib * 2**20)


def call(kernel, *, out_shape, in_specs, out_specs, **options):
    spaces = {id(HBM): pltpu.HBM, id(KEEP): pltpu.VMEM}
    single = not isinstance(out_shape, tuple)
    shapes, specs = ((out_shape,), (out_specs,)) if single else (out_shape, out_specs)
    shapes = tuple(
        spaces[id(spec)](each.shape, each.dtype) if id(spec) in spaces else each
        for each, spec in zip(shapes, specs, strict=True)
    )

    def run(*values):
        values = [
            pltpu.with_memory_space_constraint(value, spaces[id(spec)]) if id(spec) in spaces else value
            for value, spec in zip(values, in_specs, strict=True)
        ]
        return pl.pallas_call(
            kernel,
            out_shape=shapes[0] if single else shapes,
            in_specs=in_specs,
            out_specs=out_specs,
            **options,
        )(*values)

    return run


def rows(index, size):
    return pl.ds(pl.multiple_of(index * size, size), size)


def parity(z, k):
    return lax.rem(z + k, 2)


class Copies:
    def __init__(self, sems):
        self.sems = sems
        self.count = 0

    def start(self, source, target):
        copy = pltpu.make_async_copy(source, target, self.sems.at[self.count])
        self.count += 1
        copy.start()
        return copy


def wait_all(copies):
    for copy in copies:
        copy.wait()


def center_scale(x):
    center = jnp.mean(x, axis=-1, keepdims=True)
    centered = x - center
    spread = jnp.mean(centered * centered, axis=-1, keepdims=True)
    inverse = lax.rsqrt(spread + norm_eps)
    return centered * inverse, inverse


def norm_back(hat, inverse, grad):
    first = jnp.mean(grad, axis=-1, keepdims=True)
    second = jnp.mean(grad * hat, axis=-1, keepdims=True)
    return inverse * (grad - first - hat * second)


def cut_kernel(ids, w, w_o, own, send, out_part):
    core = ids[0]
    for p in range(3):
        for i in range(4):
            base = 1024 * p + 256 * i
            to = slice(128 * i, 128 * (i + 1))
            send[p, :, to] = w[:, pl.ds(pl.multiple_of(base + 128 * (1 - core), 128), 128)]
            own[p, :, to] = w[:, pl.ds(pl.multiple_of(base + 128 * core, 128), 128)]
    out_part[0, :128] = w_o[:, :HALF]
    out_part[0, 128:] = w_o[:, HALF:]


def call_cut(ids, w, w_o):
    return call(
        cut_kernel,
        out_shape=(shape(3, 128, HALF), shape(3, 128, HALF), shape(1, BLOCK, HALF)),
        in_specs=[SMEM, VMEM, VMEM],
        out_specs=(VMEM,) * 3,
        compiler_params=params(60),
        name="cut_qkv",
    )(ids, w, w_o)


def cut_feed_kernel(ids, w, own, send):
    core = ids[0]
    for i in range(4):
        send[i] = w[:, pl.ds(pl.multiple_of(1024 * i + HALF * (1 - core), HALF), HALF)]
        own[i] = w[:, pl.ds(pl.multiple_of(1024 * i + HALF * core, HALF), HALF)]


def call_cut_feed(ids, w):
    return call(
        cut_feed_kernel,
        out_shape=(shape(4, 128, HALF), shape(4, 128, HALF)),
        in_specs=[SMEM, VMEM],
        out_specs=(VMEM,) * 2,
        compiler_params=params(60),
        name="cut_feed",
    )(ids, w)


def start_sides(go, piece, target, chip, core, tag):
    return [
        (tag, go.start(piece.at[:128], target.at[rows(2 * chip + core, 128)])),
        (tag, go.start(piece.at[128:], target.at[rows(2 * chip + 1 - core, 128)])),
    ]


def attend(pair, qs, ks, vs, ctxs, stats):
    keys = ks[pair]
    values = jnp.concatenate([jnp.transpose(vs[pair]), jnp.ones((128, 1024), bf16)], axis=0)
    for i in range(4):
        ext = (i + 1) * BLOCK
        cols = slice(i * BLOCK, ext)
        query = qs[pair, cols]
        low = low_half(query)
        zero = jnp.zeros_like(query)
        parts = []
        for a in range(2):
            part = jnp.where(low, query, zero) if a == 0 else jnp.where(low, zero, query)
            scores = nt(keys[:ext], part)
            last = scores[i * BLOCK :]
            r = lax.broadcasted_iota(jnp.int32, last.shape, 0)
            c = lax.broadcasted_iota(jnp.int32, last.shape, 1)
            last = jnp.where(r <= c, last, -1e30)
            scores = jnp.concatenate([scores[: i * BLOCK], last], axis=0) if i else last
            top = jnp.max(scores, axis=0, keepdims=True)
            expo = jnp.exp(scores - top).astype(bf16)
            wide = nn(values[:, :ext], expo)
            total = wide[128:129]
            parts.append(wide[64 * a : 64 * a + 64] * (1.0 / total))
            stats[pair, a : a + 1, cols] = top + jnp.log(total)
        ctxs[pair, cols] = jnp.transpose(jnp.concatenate(parts, axis=0).astype(bf16))


def first_kernel(
    ids, m0, m1, others, w0, w1, w2, w3t, w3b, gain, shift, down_w, up_w, bias,
    q_out, k_out, v_out, n_out, down_out, w_out, o_out, ctx_out, stat_out, own, send,
    xs, ns, ws, os, qs, ks, vs, downs, ctxs, stats, owns, sends, sems,
):
    core, chip = ids[0], ids[2]
    go = Copies(sems)
    arrive = start_grads(go, ids, (m0, m1), (others.at[0], others.at[1]), xs)
    weights, outer, leave = [], [], []
    pieces = (w0, w1, w2, (w3t, w3b))
    part = lambda r, p: pieces[r].at[p] if r < 3 else pieces[r][p // 2].at[p % 2]
    for p in range(3):
        for r in range(4):
            weights += start_sides(go, part(r, p), ws.at[p], chip ^ r, core, p)
    for r in range(4):
        for h in range(2):
            outer.append(
                go.start(
                    part(r, 3).at[h * 128 : (h + 1) * 128],
                    os.at[rows(chip ^ r, 128), h * HALF : (h + 1) * HALF],
                )
            )
    wait_all(arrive)
    for i in range(4):
        hat, _ = center_scale(xs[i].astype(f32))
        ns[i * BLOCK : (i + 1) * BLOCK] = (hat * gain[0:1] + shift[0:1]).astype(bf16)
    leave.append(go.start(ns, n_out))
    for p, (to, out) in enumerate(((qs, q_out), (ks, k_out), (vs, v_out))):
        wait_all([copy for at, copy in weights if at == p])
        leave.append(go.start(ws.at[p], w_out.at[p]))
        for i in range(4):
            at = slice(i * BLOCK, (i + 1) * BLOCK)
            value = nn(ns[at], ws[p]) + bias[:, p * HALF : (p + 1) * HALF]
            if p == 0:
                downs[at] = nt(ns[at], down_w[...]).astype(bf16)
            if p != 1:
                value += nn(downs[at], up_w[:, p * HALF : (p + 1) * HALF])
            value = value.astype(bf16)
            if p == 0:
                value = value * jnp.asarray(0.125, bf16)
            for pair in range(4):
                to[pair, at] = value[:, 128 * pair : 128 * (pair + 1)]
        leave.append(go.start(to, out))
    down_out[...] = nt(down_w[:16], ns[...]).astype(bf16)

    @pl.loop(0, 4)
    def _(pair):
        attend(pair, qs, ks, vs, ctxs, stats)

    leave.append(go.start(ctxs, ctx_out))
    leave.append(go.start(stats, stat_out))
    wait_all(outer)
    leave.append(go.start(os, o_out))
    for side, to, out in ((1 - core, sends, send), (core, owns, own)):
        for i in range(2):
            at = rows(2 * side + i, BLOCK)
            tok = slice(i * BLOCK, (i + 1) * BLOCK)
            whole = jnp.concatenate([ctxs[p, at] for p in range(4)], axis=1)
            to[tok] = nn(whole, os[...]).astype(to.dtype)
            leave.append(go.start(to.at[tok], out.at[tok]))
    wait_all(leave)


def call_first(ids, x_own, x_other, pieces, gain, shift, down_w, up_w, bias):
    heads = shape(4, 1024, 128)
    return call(
        first_kernel,
        out_shape=(
            heads,
            heads,
            heads,
            shape(1024, 1024),
            shape(16, 1024),
            shape(3, 1024, HALF),
            shape(HALF, 1024),
            heads,
            shape(4, 8, 1024, dtype=f32),
            shape(HALF, 1024),
            shape(HALF, 1024),
        ),
        in_specs=[SMEM] + [HBM] * 8 + [VMEM] * 5,
        out_specs=(HBM,) * 4 + (VMEM,) + (HBM,) * 6,
        scratch_shapes=[
            pltpu.VMEM((4, BLOCK, 1024), bf16),
            pltpu.VMEM((1024, 1024), bf16),
            pltpu.VMEM((3, 1024, HALF), bf16),
            pltpu.VMEM((HALF, 1024), bf16),
            pltpu.VMEM((4, 1024, 128), bf16),
            pltpu.VMEM((4, 1024, 128), bf16),
            pltpu.VMEM((4, 1024, 128), bf16),
            pltpu.VMEM((1024, 128), bf16),
            pltpu.VMEM((4, 1024, 128), bf16),
            pltpu.VMEM((4, 8, 1024), f32),
            pltpu.VMEM((HALF, 1024), bf16),
            pltpu.VMEM((HALF, 1024), bf16),
            pltpu.SemaphoreType.DMA((53,)),
        ],
        compiler_params=params(60),
        name="qkv_attention",
    )(ids, *x_own, x_other, *pieces, gain, shift, down_w, up_w, bias)


def attend_back(pair, qs, ks, vs, ctxs, stats, gs, dqs, dks, dvs, acc_k, acc_v):
    keys, values = ks[pair], vs[pair]
    place = pl.ds(pl.multiple_of(pair * 128, 128), 128)
    for i in range(4):
        ext = (i + 1) * BLOCK
        cols = slice(i * BLOCK, ext)
        query, grad = qs[pair, cols], gs[pair, cols]
        low = low_half(query)
        zero = jnp.zeros_like(query)
        product = grad.astype(f32) * ctxs[pair, cols].astype(f32)
        stat = jnp.transpose(stats[pair, :, cols])
        turned_query, turned_grad = jnp.transpose(query), jnp.transpose(grad)
        new_q = []
        for a in range(2):
            pick = (lambda x, y: jnp.where(low, x, y)) if a == 0 else (lambda x, y: jnp.where(low, y, x))
            half = slice(64 * a, 64 * a + 64)
            scores = nt(pick(query, zero), keys[:ext])
            probs = jnp.exp(scores - stat[:, a : a + 1])
            last = probs[:, i * BLOCK :]
            r = lax.broadcasted_iota(jnp.int32, last.shape, 0)
            c = lax.broadcasted_iota(jnp.int32, last.shape, 1)
            last = jnp.where(r >= c, last, 0.0)
            probs = jnp.concatenate([probs[:, : i * BLOCK], last], axis=1) if i else last
            inner = jnp.sum(pick(product, 0.0), axis=1, keepdims=True)
            grad_probs = nt(pick(grad, zero), values[:ext])
            grad_scores = (probs * (grad_probs - inner)).astype(bf16)
            more_v = nn(turned_grad[half], probs.astype(bf16))
            more_k = nn(turned_query[half], grad_scores)
            if i:
                acc_v[half, : i * BLOCK] += more_v[:, : i * BLOCK]
                acc_k[half, : i * BLOCK] += more_k[:, : i * BLOCK]
            acc_v[half, cols] = more_v[:, i * BLOCK :]
            acc_k[half, cols] = more_k[:, i * BLOCK :]
            new_q.append(nn(grad_scores, keys[:ext]))
        both = jnp.where(low, new_q[0], new_q[1])
        dqs[cols, place] = (both * 0.125).astype(bf16)
    dks[:, place] = jnp.transpose(acc_k[...].astype(bf16))
    dvs[:, place] = jnp.transpose(acc_v[...].astype(bf16))


def attention_back_kernel(
    ids, q, k_in, v, ctx, stat, w_o, parts, others, g0, g1, g2, g3, mid_own, mid_other, w, n_all, downs,
    gain, down_w, up_w,
    own, send, grad_middle, total,
    gs, mids, os, qs, ks, vs, ctxs, stats, heads, dqs, dks, dvs, acc_k, acc_v,
    ws, ns, tilts, sems,
):
    core, z = ids[0], ids[1]
    go = Copies(sems)
    sources = [(core, 0, g0, mid_own), (core, 1, g1, mid_own), (1 - core, 0, g2, mid_other), (1 - core, 1, g3, mid_other)]
    blocks, loads = [], []
    for at, (side, k, ref, mid) in enumerate(sources):
        blocks.append(rows(2 * side + parity(z, k), BLOCK))
        here = rows(parity(z, k), BLOCK)
        loads.append([go.start(ref, gs.at[at]), go.start(mid.at[1, here], mids.at[at])])
        if at == 0:
            outer = go.start(w_o, os)
    then = [
        go.start(ref, to)
        for ref, to in ((q, qs), (k_in, ks), (v, vs), (ctx, ctxs), (stat, stats))
    ]
    weights = [go.start(w, ws), go.start(n_all, ns)]
    for at in range(4):
        tok = blocks[at]
        wait_all(loads[at])
        hat, inverse = center_scale(mids[at].astype(f32))
        grad = (parts[tok].astype(f32) + others[tok].astype(f32)) * gain[1:2]
        value = (gs[at].astype(f32) + norm_back(hat, inverse, grad)).astype(bf16)
        if at < 2:
            grad_middle[rows(parity(z, at), BLOCK)] = value
        if at == 0:
            outer.wait()
        value = nt(value, os[...]).astype(bf16)
        for pair in range(4):
            heads[pair, tok] = value[:, 128 * pair : 128 * (pair + 1)]
    wait_all(then)

    @pl.loop(0, 4)
    def _(pair):
        attend_back(pair, qs, ks, vs, ctxs, stats, heads, dqs, dks, dvs, acc_k, acc_v)

    wait_all(weights)
    for side, values in ((1 - core, send), (core, own)):
        for i in range(2):
            at = rows(2 * side + i, BLOCK)
            tok = slice(i * BLOCK, (i + 1) * BLOCK)
            gq, gk, gv = dqs[at], dks[at], dvs[at]
            tilt = (nt(gq, up_w[:, :HALF]) + nt(gv, up_w[:, 2 * HALF :])).astype(bf16)
            value = nt(gq, ws[0]) + nt(gk, ws[1]) + nt(gv, ws[2]) + nn(tilt, down_w[...])
            values[tok] = value.astype(bf16)
    tilts[...] = (nt(up_w[:16, :HALF], dqs[...]) + nt(up_w[:16, 2 * HALF :], dvs[...])).astype(bf16)
    down_terms = nn(tilts[...], ns[...])
    total[...] = jnp.zeros_like(total)
    total[0:4] = down_terms[0:4]
    total[8:12] = down_terms[4:8]
    up_q = 8.0 * nn(downs[...], dqs[...])
    up_v = 8.0 * nn(downs[...], dvs[...])
    for pair in range(4):
        here = pl.ds(pl.multiple_of(256 * pair + 128 * core, 128), 128)
        total[4:8, here] = up_q[0:4, 128 * pair : 128 * (pair + 1)]
        total[12:16, here] = up_v[4:8, 128 * pair : 128 * (pair + 1)]


def call_attention_back(
    ids, q, k, v, ctx, stat, w_o, part, other, g_own, g_other, mid_own, mid_other,
    w, n_all, downs, gain, down_w, up_w,
):
    pairs = pltpu.VMEM((4, 1024, 128), bf16)
    wide = pltpu.VMEM((1024, HALF), bf16)
    return call(
        attention_back_kernel,
        out_shape=(
            shape(HALF, 1024),
            shape(HALF, 1024),
            shape(HALF, 1024),
            shape(16, 1024, dtype=f32),
        ),
        in_specs=[SMEM] + [HBM] * 6 + [KEEP] * 2 + [FREE] * 4 + [HBM] * 4 + [VMEM] * 4,
        out_specs=(KEEP, KEEP, KEEP, KEEP),
        scratch_shapes=[
            pltpu.VMEM((4, BLOCK, 1024), bf16),
            pltpu.VMEM((4, BLOCK, 1024), bf16),
            pltpu.VMEM((HALF, 1024), bf16),
            pairs,
            pairs,
            pairs,
            pairs,
            pltpu.VMEM((4, 8, 1024), f32),
            pairs,
            wide,
            wide,
            wide,
            pltpu.VMEM((128, 1024), f32),
            pltpu.VMEM((128, 1024), f32),
            pltpu.VMEM((3, 1024, HALF), bf16),
            pltpu.VMEM((1024, 1024), bf16),
            pltpu.VMEM((16, 1024), bf16),
            pltpu.SemaphoreType.DMA((16,)),
        ],
        compiler_params=params(50),
        name="attention_back",
    )(
        ids, q, k, v, ctx, stat, w_o, part, other, *g_own, *g_other, mid_own, mid_other,
        w, n_all, downs, gain, down_w, up_w,
    )


def low_half(value):
    return lax.broadcasted_iota(jnp.int32, value.shape, 1) < 64


def start_tokens(go, pair, target, z):
    return [go.start(ref, target.at[parity(z, k)]) for k, ref in enumerate(pair)]


def middle_kernel(
    ids, own, other, x0, x1, bias, gain, shift, both, owns, others, xs, lows, ns, sems
):
    go = Copies(sems)
    tokens = start_tokens(go, (x0, x1), xs, ids[1])
    parts = []
    for i in range(2):
        at = slice(i * BLOCK, (i + 1) * BLOCK)
        parts.append([go.start(own.at[at], owns.at[i]), go.start(other.at[at], others.at[i])])
    wait_all(tokens)
    leave = []
    for i in range(2):
        at = slice(i * BLOCK, (i + 1) * BLOCK)
        wait_all(parts[i])
        value = owns[i].astype(f32) + others[i].astype(f32) + xs[i].astype(f32) + bias[2:3]
        lows[i] = value.astype(bf16)
        leave.append(go.start(lows.at[i], both.at[1, at]))
        hat, _ = center_scale(value)
        ns[i] = (hat * gain[1:2] + shift[1:2]).astype(bf16)
        leave.append(go.start(ns.at[i], both.at[0, at]))
    wait_all(leave)


def call_middle(ids, own, other, x_own, bias, gain, shift):
    return call(
        middle_kernel,
        out_shape=shape(2, HALF, 1024),
        in_specs=[SMEM, HBM, FREE, HBM, HBM] + [VMEM] * 3,
        out_specs=HBM,
        scratch_shapes=[
            pltpu.VMEM((2, BLOCK, 1024), bf16),
            pltpu.VMEM((2, BLOCK, 1024), bf16),
            pltpu.VMEM((2, BLOCK, 1024), bf16),
            pltpu.VMEM((2, BLOCK, 1024), bf16),
            pltpu.VMEM((2, BLOCK, 1024), bf16),
            pltpu.SemaphoreType.DMA((12,)),
        ],
        compiler_params=params(40),
        name="middle",
    )(ids, own, other, *x_own, bias, gain, shift)


def start_grads(go, ids, g_own, g_other, gs):
    core, z = ids[0], ids[1]
    return [
        go.start(ref, gs.at[2 * side + parity(z, k)])
        for side, pair in ((core, g_own), (1 - core, g_other))
        for k, ref in enumerate(pair)
    ]


def hidden_kernel(
    ids, n_own, n_other, w0, w1, w2, w3t, w3b, bias, piece,
    acts, slopes, ws, result, ns, wo, sems,
):
    core, chip = ids[0], ids[2]
    go = Copies(sems)
    arrive = [
        go.start(n_own.at[0], ns.at[rows(core, HALF)]),
        go.start(n_other.at[0], ns.at[rows(1 - core, HALF)]),
    ]
    weights = []
    for p in range(4):
        for r, ref in enumerate((w0, w1, w2, (w3t, w3b))):
            part = ref.at[p] if r < 3 else ref[p // 2].at[p % 2]
            weights += start_sides(go, part, ws.at[p], chip ^ r, core, p)
    later = go.start(piece, wo)
    wait_all(arrive)

    def finish(p, i, h):
        at = slice(i * BLOCK, (i + 1) * BLOCK)
        square = h * h
        lift = 0.5 + 0.5 * jnp.tanh(h * (GELU_A + (GELU_A * GELU_B) * square))
        act = h * lift
        acts[p, at] = act.astype(bf16)
        rise = 2.0 * GELU_A + (6.0 * GELU_A * GELU_B) * square
        slopes[p, at] = (lift + (act - act * lift) * rise).astype(bf16)

    before = None
    for p in range(4):
        wait_all([copy for at, copy in weights if at == p])
        shift = bias[pl.ds(2 * p + core, 1)]
        for i in range(4):
            h = nn(ns[i * BLOCK : (i + 1) * BLOCK], ws[p]) + shift
            if before is not None:
                finish(*before)
            before = (p, i, h)
    finish(*before)
    later.wait()
    for i in range(4):
        tok = slice(i * BLOCK, (i + 1) * BLOCK)
        result[tok] = nn(acts[chip, tok], wo[...]).astype(bf16)


def call_hidden(ids, n_own, n_other, pieces, bias, piece):
    return call(
        hidden_kernel,
        out_shape=(shape(4, 1024, HALF),) * 3 + (shape(1024, 1024),),
        in_specs=[SMEM] + [HBM] * 7 + [VMEM, HBM],
        out_specs=(KEEP,) * 4,
        scratch_shapes=[
            pltpu.VMEM((1024, 1024), bf16),
            pltpu.VMEM((HALF, 1024), bf16),
            pltpu.SemaphoreType.DMA((35,)),
        ],
        compiler_params=params(26),
        name="hidden",
    )(ids, n_own, n_other, *pieces, bias, piece)


def feed_kernel(
    ids, g0, g1, g2, g3, acts, slopes, w_ins, own_piece, x_piece, y_piece, old,
    result, grad, gs, w_outs, sems,
):
    core, z, chip = ids[0], ids[1], ids[2]
    go = Copies(sems)
    pieces = (own_piece, x_piece, y_piece)
    sources = [(core, 0, g0), (core, 1, g1), (1 - core, 0, g2), (1 - core, 1, g3)]
    blocks = [2 * side + parity(z, k) for side, k, _ in sources]
    tokens, weights = [], []
    for i in range(4):
        tokens.append(go.start(sources[i][2], gs.at[i]))
        if i < 3:
            weights.append(go.start(pieces[i], w_outs.at[i]))
    for i in range(4):
        tokens[i].wait()
        tok = rows(blocks[i], BLOCK)
        out_sum, grad_sum = old[tok].astype(f32), None
        for r in range(3):
            here = chip ^ r
            if i == 0:
                weights[r].wait()
            back = nt(gs[i], w_outs[r])
            if r:
                out_sum += nn(acts[here, tok], w_outs[r])
            back = (back * slopes[here, tok].astype(f32)).astype(bf16)
            term = nt(back, w_ins[here])
            grad_sum = term if r == 0 else grad_sum + term
        result[tok] = out_sum.astype(bf16)
        grad[tok] = grad_sum.astype(bf16)


def call_feed(ids, g_own, g_other, active, slope, w_in, pieces, old):
    return call(
        feed_kernel,
        out_shape=(shape(1024, 1024),) * 2,
        in_specs=[SMEM] + [FREE] * 4 + [KEEP] * 3 + [HBM] * 3 + [KEEP],
        out_specs=(KEEP, KEEP),
        scratch_shapes=[
            pltpu.VMEM((4, BLOCK, 1024), bf16),
            pltpu.VMEM((3, HALF, 1024), bf16),
            pltpu.SemaphoreType.DMA((7,)),
        ],
        compiler_params=params(30),
        name="feed",
    )(ids, *g_own, *g_other, active, slope, w_in, *pieces, old)


def far_grad_kernel(ids, g0, g1, g2, g3, slopes, w_ins, top, low, old, out, gs, w_outs, sems):
    core, z, far = ids[0], ids[1], ids[2] ^ 3
    go = Copies(sems)
    arrive = [go.start(top, w_outs.at[:BLOCK]), go.start(low, w_outs.at[BLOCK:])]
    sources = [(core, 0, g0), (core, 1, g1), (1 - core, 0, g2), (1 - core, 1, g3)]
    tokens = [go.start(ref, gs.at[i]) for i, (_, _, ref) in enumerate(sources)]
    wait_all(arrive)
    for i, (side, k, _) in enumerate(sources):
        tok = rows(2 * side + parity(z, k), BLOCK)
        tokens[i].wait()
        back = nt(gs[i], w_outs[...]) * slopes[far, tok].astype(f32)
        more = nt(back.astype(bf16), w_ins[far])
        out[tok] = (more + old[tok].astype(f32)).astype(bf16)


def call_far_grad(ids, g_own, g_other, slope, w_in, far, old):
    return call(
        far_grad_kernel,
        out_shape=shape(1024, 1024),
        in_specs=[SMEM] + [FREE] * 4 + [KEEP] * 2 + [HBM] * 2 + [KEEP],
        out_specs=KEEP,
        scratch_shapes=[
            pltpu.VMEM((4, BLOCK, 1024), bf16),
            pltpu.VMEM((HALF, 1024), bf16),
            pltpu.SemaphoreType.DMA((6,)),
        ],
        compiler_params=params(26),
        name="far_grad",
    )(ids, *g_own, *g_other, slope, w_in, *far, old)


def far_result_kernel(ids, acts, top, low, old, own, send, w_outs, sems):
    core, far = ids[0], ids[2] ^ 3
    go = Copies(sems)
    arrive = [go.start(top, w_outs.at[:BLOCK]), go.start(low, w_outs.at[BLOCK:])]
    wait_all(arrive)
    for side, values in ((1 - core, send), (core, own)):
        for i in range(2):
            at = rows(2 * side + i, BLOCK)
            tok = slice(i * BLOCK, (i + 1) * BLOCK)
            values[tok] = (old[at].astype(f32) + nn(acts[far, at], w_outs[...])).astype(bf16)


def call_far_result(ids, active, far, old):
    return call(
        far_result_kernel,
        out_shape=(shape(HALF, 1024), shape(HALF, 1024)),
        in_specs=[SMEM, KEEP, HBM, HBM, KEEP],
        out_specs=(KEEP, KEEP),
        scratch_shapes=[
            pltpu.VMEM((HALF, 1024), bf16),
            pltpu.SemaphoreType.DMA((2,)),
        ],
        compiler_params=params(16),
        name="far_result",
    )(ids, active, *far, old)


def mixed_kernel(ids, own, other, middle, bias, out0, out1, mids, sems):
    z = ids[1]
    go = Copies(sems)
    places = [rows(parity(z, k), BLOCK) for k in range(2)]
    loads = [go.start(middle.at[1, tok], mids.at[k]) for k, tok in enumerate(places)]
    for k, (tok, out) in enumerate(zip(places, (out0, out1), strict=True)):
        loads[k].wait()
        value = own[tok].astype(f32) + other[tok].astype(f32) + mids[k].astype(f32) + bias[3:4]
        out[...] = value.astype(bf16)


def call_mixed(ids, own, other, middle, bias):
    return call(
        mixed_kernel,
        out_shape=(shape(BLOCK, 1024),) * 2,
        in_specs=[SMEM, KEEP, KEEP, HBM, VMEM],
        out_specs=(KEEP, KEEP),
        scratch_shapes=[pltpu.VMEM((2, BLOCK, 1024), bf16), pltpu.SemaphoreType.DMA((2,))],
        compiler_params=params(12),
        name="mixed",
    )(ids, own, other, middle, bias)


def input_grad_kernel(ids, x0, x1, own, other, grad_middle, gain, out0, out1, xs, sems):
    z = ids[1]
    go = Copies(sems)
    loads = [go.start(ref, xs.at[k]) for k, ref in enumerate((x0, x1))]
    for k, out in enumerate((out0, out1)):
        loads[k].wait()
        for h in range(2):
            tok = rows(2 * parity(z, k) + h, 128)
            here = slice(128 * h, 128 * (h + 1))
            grad = (own[tok].astype(f32) + other[tok].astype(f32)) * gain[0:1]
            hat, inverse = center_scale(xs[k, here].astype(f32))
            out[here] = (grad_middle[tok].astype(f32) + norm_back(hat, inverse, grad)).astype(bf16)


def call_input_grad(ids, x_own, own, other, grad_middle, gain):
    return call(
        input_grad_kernel,
        out_shape=(shape(BLOCK, 1024),) * 2,
        in_specs=[SMEM, HBM, HBM, KEEP, KEEP, KEEP, VMEM],
        out_specs=(KEEP, KEEP),
        scratch_shapes=[pltpu.VMEM((2, BLOCK, 1024), bf16), pltpu.SemaphoreType.DMA((2,))],
        compiler_params=params(16),
        name="input_grad",
    )(ids, *x_own, own, other, grad_middle, gain)


def to_core(value):
    return lax.ppermute(value, "core", SWAP)


def total_over(value, axis, *others):
    flip = [lax.ppermute(value, axis, [(i, i ^ by) for i in range(4)]) for by in (1, 2, 3)]
    flip = after(flip, *others)
    return (value + flip[0]) + (flip[1] + flip[2])


def exchange(z, pair):
    sent = []
    for k in range(2):
        perm = [
            (4 * core + at, 4 * (at // 2) + 2 * core + (at + k) % 2)
            for core in range(2)
            for at in range(4)
        ]
        sent.append(lax.ppermute(pair[k], ("core", "seq"), perm))
    return sent


def pick_kernel(ids, value, out0, out1, sems):
    z = ids[1]
    go = Copies(sems)
    wait_all([go.start(value.at[parity(z, k)], out) for k, out in enumerate((out0, out1))])


def call_pick(ids, value):
    return call(
        pick_kernel,
        out_shape=(shape(BLOCK, 1024),) * 2,
        in_specs=[SMEM, HBM],
        out_specs=(KEEP, KEEP),
        scratch_shapes=[pltpu.SemaphoreType.DMA((2,))],
        compiler_params=params(PICK),
        name="pick",
    )(ids, value)


def place_kernel(ids, first, second, out, sems):
    z = ids[1]
    go = Copies(sems)
    wait_all([go.start(ref, out.at[parity(z, k)]) for k, ref in enumerate((first, second))])


def call_place(ids, pair):
    return call(
        place_kernel,
        out_shape=shape(2, BLOCK, 1024),
        in_specs=[SMEM, KEEP, KEEP],
        out_specs=HBM,
        scratch_shapes=[pltpu.SemaphoreType.DMA((2,))],
        compiler_params=params(PICK),
        name="place",
    )(ids, *pair)


def after(value, *others):
    return lax.optimization_barrier((value, *others))[0]


def gather_near(shard):
    return [shard, lax.ppermute(shard, "x", SWAP), lax.ppermute(shard, "y", SWAP)]


def halves(near):
    return call_halves(near[1], near[2])


def halves_kernel(by_x, by_y, first, second, held, sems):
    half = first.shape[0]
    go = Copies(sems)
    loads = [go.start(by_x.at[:half], held.at[0]), go.start(by_y.at[half:], held.at[1])]
    leave = []
    for at, out in enumerate((first, second)):
        loads[at].wait()
        leave.append(go.start(held.at[at], out))
    wait_all(leave)


def call_halves(by_x, by_y):
    dims = (by_x.shape[0] // 2, *by_x.shape[1:])
    return call(
        halves_kernel,
        out_shape=(shape(*dims), shape(*dims)),
        in_specs=[HBM, HBM],
        out_specs=(HBM, HBM),
        scratch_shapes=[pltpu.VMEM((2, *dims), bf16), pltpu.SemaphoreType.DMA((4,))],
        compiler_params=params(8),
        name="halves",
    )(by_x, by_y)


def gather_far(near, parts):
    return near + [lax.ppermute(parts[0], "y", SWAP), lax.ppermute(parts[1], "x", SWAP)]


def on_chip(
    inputs,
    out_grad,
    norm_gain,
    norm_bias,
    proj_bias,
    fc_bias,
    qkv_weight,
    out_weight,
    feed_input_weight,
    proj_weight,
    adapters,
    first_moment,
    second_moment,
):
    width = inputs.shape[2]
    core = lax.axis_index("core")
    z = lax.axis_index("seq")
    chip = 2 * lax.axis_index("y") + lax.axis_index("x")
    ids = jnp.stack([core, z, chip]).astype(jnp.int32)

    qkv_own, qkv_send, out_part = call_cut(ids, qkv_weight, out_weight)
    qkv_got = to_core(qkv_send)
    first_shard = jnp.concatenate([jnp.concatenate([qkv_own, qkv_got], axis=1), out_part], axis=0)
    first_near = gather_near(first_shard)
    x_own = exchange(z, call_pick(ids, after(inputs, first_shard)))
    in_own, in_send = call_cut_feed(ids, after(feed_input_weight, first_shard))
    in_shard = jnp.concatenate([in_own, to_core(in_send)], axis=1)

    def columns(value):
        lead = value.shape[0]
        value = value.reshape(lead, 4, 2, 128)
        return jnp.where(core == 0, value[:, :, 0], value[:, :, 1]).reshape(lead, HALF)

    scale = adapter_alpha / ADAPTER_RANK
    adapters, proj_bias = after((adapters, proj_bias), first_shard)
    up_q, up_v = scale * columns(adapters[1]), scale * columns(adapters[3])
    up_w = jnp.zeros((128, 1536), f32)
    up_w = up_w.at[0:4, :HALF].set(up_q).at[4:8, 2 * HALF :].set(up_v).astype(bf16)
    down_w = jnp.concatenate([adapters[0], adapters[2], jnp.zeros((120, 1024), f32)], axis=0)
    down_w = down_w.astype(bf16)
    head_bias = columns(proj_bias[:2])
    qkv_bias = jnp.concatenate([head_bias[0], jnp.zeros((HALF,), f32), head_bias[1]])[None]

    first_near = after(first_near, up_w, down_w, qkv_bias, in_shard)
    first_halves = halves(first_near)
    first_pieces = gather_far(first_near, first_halves)
    x_own = after(x_own, *first_halves)
    x_other = to_core(jnp.stack(x_own))
    in_near = gather_near(after(in_shard, *first_pieces[3:]))
    q, k, v, n_all, down, w_qkv, w_o, ctx, stat, attn_own, attn_send = call_first(
        ids, x_own, x_other, first_pieces, norm_gain, norm_bias, down_w, up_w, qkv_bias
    )
    in_near = after(in_near, ctx)
    in_halves = halves(in_near)
    in_pieces = gather_far(in_near, in_halves)
    attn_other = to_core(after(attn_send, *in_halves))
    n2_own = call_middle(
        ids, attn_own, after(attn_other, *in_halves), x_own, proj_bias, norm_gain, norm_bias
    )
    g_pair = call_pick(ids, after(out_grad, n2_own))
    in_pieces[3:] = after(in_pieces[3:], *g_pair)
    g_own = exchange(z, g_pair)
    n2_other = to_core(after(n2_own, *in_pieces[3:]))
    proj_near = gather_near(after(proj_weight, *in_pieces[3:]))
    active, slope, w_in, old = call_hidden(
        ids, n2_own, n2_other, in_pieces, fc_bias.reshape(8, HALF), proj_near[0]
    )
    proj_near = after(proj_near, old)
    proj_halves = halves(proj_near)
    far = gather_far(proj_near, proj_halves)[3:]
    near = after(proj_near, *proj_halves)
    g_own = after(g_own, *proj_halves)
    g_other = [to_core(part) for part in g_own]
    result, grad = call_feed(ids, g_own, g_other, active, slope, w_in, near, old)
    result_own, result_send = call_far_result(ids, active, far, result)
    result_other = to_core(result_send)
    part = call_far_grad(ids, g_own, g_other, slope, w_in, after(far, result_own), grad)
    part = after(part, result_other)
    part_other = to_core(part)
    mixed = call_mixed(ids, result_own, after(result_other, part), n2_own, proj_bias)
    part_other = after(part_other, *mixed)
    mixed = exchange(z, mixed)
    own, send, grad_middle, total = call_attention_back(
        ids, q, k, v, ctx, stat, w_o, part, part_other, g_own, g_other, n2_own, n2_other,
        w_qkv, n_all, down, norm_gain, down_w, up_w,
    )
    other = to_core(after(send, *mixed))
    grad_in = call_input_grad(ids, x_own, own, other, grad_middle, norm_gain)
    total = total_over(total, "seq", *grad_in)
    grad_in = exchange(z, grad_in)
    total = total + to_core(total)
    total = total_over(total, ("y", "x"))
    total = total.reshape(4, ADAPTER_RANK, width)
    grad_norm = jnp.sqrt(jnp.sum(total * total))
    clipped, new_weight, new_first, new_second = adam_update(
        total, adapters, first_moment, second_moment, grad_norm
    )
    mixed = call_place(ids, after(mixed, new_weight))
    grad_input = call_place(ids, after(grad_in, mixed, new_weight))
    return (mixed, grad_input, clipped, grad_norm, new_weight, new_first, new_second)


def solution(mesh):
    sizes = dict(mesh.shape)
    if sizes["dp"] == 8 and sizes["seq"] == 4:
        plane = Mesh(mesh.devices.reshape(2, 2, 2, 4), ("y", "x", "core", "seq"))
        return build(plane, ("y", "x", "core"), on_chip)
    return build(mesh, "dp", on_device)


def build(mesh, dp, step):
    tokens, weight = P(dp, "seq", None), P(dp, None)
    return jax.shard_map(
        step,
        mesh=mesh,
        in_specs=(tokens, tokens) + (P(),) * 4 + (weight,) * 4 + (P(),) * 3,
        out_specs=(tokens, tokens) + (P(),) * 5,
        check_vma=False,
    )
```

```python
import functools
import math

import jax
import jax.numpy as jnp
from jax import lax
from jax.experimental import pallas as pl
from jax.experimental.pallas import tpu as pltpu
from jax.sharding import Mesh
from jax.sharding import PartitionSpec as P

HEAD_DIM = 64
ADAPTER_RANK = 4
STEP = 10


highest = lax.Precision.HIGHEST
adapter_alpha = 32.0
beta_one = 0.9
beta_two = 0.999
adam_eps = 1e-08
decay_rate = 0.01
learning_rate = 0.02
clip_bound = 1.0
norm_eps = 1e-05


def layer_norm(value, gain, shift):
    center = jnp.mean(value, axis=-1, keepdims=True)
    centered = value - center
    spread = jnp.mean(centered * centered, axis=-1, keepdims=True)
    return centered * lax.rsqrt(spread + norm_eps) * gain + shift


def dot_trans(left, right):
    return lax.dot_general(
        left, right, (((1,), (1,)), ((), ())), preferred_element_type=jnp.float32
    )


def dot_first(left, right):
    return lax.dot_general(
        left, right, (((0,), (0,)), ((), ())), precision=highest, preferred_element_type=jnp.float32
    )


def adam_update(grad, weight, first, second, norm):
    scale_factor = clip_bound / jnp.maximum(norm, clip_bound)
    clipped = grad * scale_factor
    new_first = beta_one * first + (1.0 - beta_one) * clipped
    new_second = beta_two * second + (1.0 - beta_two) * clipped * clipped
    first_hat = new_first / (1.0 - beta_one**STEP)
    second_hat = new_second / (1.0 - beta_two**STEP)
    new_weight = weight - learning_rate * (
        first_hat / (jnp.sqrt(second_hat) + adam_eps) + decay_rate * weight
    )
    return (clipped, new_weight, new_first, new_second)


def split_heads(packed):
    length = packed.shape[0]
    local_heads = packed.shape[-1] // HEAD_DIM
    query = packed[:, 0, 0].reshape(length, local_heads, HEAD_DIM)
    keys = packed[:, 1, 0].reshape(length, local_heads, HEAD_DIM)
    values = packed[:, 2, 0].reshape(length, local_heads, HEAD_DIM)
    return (query, keys, values)


def doc_forward(packed):
    length = packed.shape[0]
    local_width = packed.shape[-1]
    query, keys, values = split_heads(packed)
    local_heads = query.shape[1]
    span = min(512, length)
    blocks = length // span
    scale = 1.0 / math.sqrt(HEAD_DIM)
    starts = jnp.arange(blocks, dtype=jnp.int32) * span

    def visit(pieces):
        query_block, start = pieces
        scores = (
            jnp.einsum("qhd,khd->hqk", query_block, keys, preferred_element_type=jnp.float32)
            * scale
        )
        causal = (start + jnp.arange(span))[:, None] >= jnp.arange(length)[None, :]
        masked = jnp.where(causal[None], scores, -1e30)
        summit = jnp.max(masked, axis=-1, keepdims=True)
        expo = jnp.where(causal[None], jnp.exp(masked - summit), 0.0)
        totals = jnp.sum(expo, axis=-1, keepdims=True)
        weights = (expo / totals).astype(jnp.bfloat16)
        context = jnp.einsum(
            "hqk,khd->qhd", weights, values, preferred_element_type=jnp.float32
        ).astype(jnp.bfloat16)
        return (context, summit[..., 0] + jnp.log(totals[..., 0]))

    context, log_total = lax.map(
        visit, (query.reshape(blocks, span, local_heads, HEAD_DIM), starts)
    )
    return (context.reshape(length, 1, local_width), log_total)


def doc_backward(args):
    packed, grad_context, log_total = args
    length = packed.shape[0]
    local_width = packed.shape[-1]
    query, keys, values = split_heads(packed)
    local_heads = query.shape[1]
    output_gradient = grad_context[:, 0].reshape(length, local_heads, HEAD_DIM)
    span = min(512, length)
    blocks = length // span
    scale = 1.0 / math.sqrt(HEAD_DIM)
    starts = jnp.arange(blocks, dtype=jnp.int32) * span

    def visit(carry, pieces):
        grad_keys, grad_values = carry
        query_block, grad_block, total_block, start = pieces
        scores = (
            jnp.einsum("qhd,khd->hqk", query_block, keys, preferred_element_type=jnp.float32)
            * scale
        )
        causal = (start + jnp.arange(span))[:, None] >= jnp.arange(length)[None, :]
        masked = jnp.where(causal[None], scores, -1e30)
        probs = jnp.where(causal[None], jnp.exp(masked - total_block[:, :, None]), 0.0)
        weights = probs.astype(jnp.bfloat16)
        grad_probs = jnp.einsum(
            "qhd,khd->hqk", grad_block, values, preferred_element_type=jnp.float32
        )
        inner = jnp.sum(probs * grad_probs, axis=-1, keepdims=True)
        grad_scores = (probs * (grad_probs - inner)).astype(jnp.bfloat16)
        grad_query = (
            jnp.einsum("hqk,khd->qhd", grad_scores, keys, preferred_element_type=jnp.float32)
            * scale
        )
        grad_keys = (
            grad_keys
            + jnp.einsum(
                "hqk,qhd->khd", grad_scores, query_block, preferred_element_type=jnp.float32
            )
            * scale
        )
        grad_values = grad_values + jnp.einsum(
            "hqk,qhd->khd", weights, grad_block, preferred_element_type=jnp.float32
        )
        return ((grad_keys, grad_values), grad_query)

    empty = jnp.zeros((length, local_heads, HEAD_DIM), jnp.float32)
    pieces = (
        query.reshape(blocks, span, local_heads, HEAD_DIM),
        output_gradient.reshape(blocks, span, local_heads, HEAD_DIM),
        log_total,
        starts,
    )
    (grad_keys, grad_values), grad_query = lax.scan(visit, (empty, empty), pieces)
    joined = jnp.stack(
        [
            grad_query.reshape(length, local_width),
            grad_keys.reshape(length, local_width),
            grad_values.reshape(length, local_width),
        ],
        axis=1,
    )
    return joined.astype(jnp.bfloat16)[:, :, None, :]


def on_device(
    inputs,
    out_grad,
    norm_gain,
    norm_bias,
    proj_bias,
    fc_bias,
    qkv_weight,
    out_weight,
    feed_input_weight,
    proj_weight,
    adapters,
    first_moment,
    second_moment,
):
    docs, tokens, width = inputs.shape
    count = docs * tokens
    ranks = lax.axis_size("seq")
    scale_factor = adapter_alpha / ADAPTER_RANK

    def forward(stack):
        qkv_full, out_full, fc_full, proj_full = stack
        flat = inputs.reshape(count, width).astype(jnp.float32)
        normed, norm_one_back = jax.vjp(
            lambda value: layer_norm(value, norm_gain[0], norm_bias[0]), flat
        )
        base = jnp.dot(normed.astype(jnp.bfloat16), qkv_full, preferred_element_type=jnp.float32)
        down_q = jnp.dot(normed, adapters[0].T, precision=highest)
        down_v = jnp.dot(normed, adapters[2].T, precision=highest)
        query = (
            base[:, :width]
            + proj_bias[0]
            + scale_factor * jnp.dot(down_q, adapters[1], precision=highest)
        )
        keys = base[:, width : 2 * width]
        values = (
            base[:, 2 * width :]
            + proj_bias[1]
            + scale_factor * jnp.dot(down_v, adapters[3], precision=highest)
        )
        joined = (
            jnp.concatenate([query, keys, values], axis=1)
            .astype(jnp.bfloat16)
            .reshape(docs, tokens, 3, ranks, width // ranks)
        )
        spread = lax.all_to_all(joined, "seq", split_axis=3, concat_axis=1, tiled=True)
        context, log_total = lax.map(doc_forward, spread)
        context = lax.all_to_all(context, "seq", split_axis=1, concat_axis=2, tiled=True).reshape(
            count, width
        )
        middle = (
            flat + jnp.dot(context, out_full, preferred_element_type=jnp.float32) + proj_bias[2]
        )
        normed_two, norm_two_back = jax.vjp(
            lambda value: layer_norm(value, norm_gain[1], norm_bias[1]), middle
        )
        hidden = (
            jnp.dot(normed_two.astype(jnp.bfloat16), fc_full, preferred_element_type=jnp.float32)
            + fc_bias
        )
        active, gelu_back = jax.vjp(lambda value: jax.nn.gelu(value, approximate=True), hidden)
        result = (
            middle
            + jnp.dot(active.astype(jnp.bfloat16), proj_full, preferred_element_type=jnp.float32)
            + proj_bias[3]
        )
        return (
            result,
            (normed, down_q, down_v, norm_one_back, spread, log_total, norm_two_back, gelu_back),
        )

    stack = (
        lax.all_gather(qkv_weight, "dp", axis=0, tiled=True),
        lax.all_gather(out_weight, "dp", axis=0, tiled=True),
        lax.all_gather(feed_input_weight, "dp", axis=0, tiled=True),
        lax.all_gather(proj_weight, "dp", axis=0, tiled=True),
    )
    result, kept = forward(stack)
    fenced = lax.optimization_barrier((stack, result))
    stack = fenced[0]
    again, kept = forward(stack)
    qkv_full, out_full, fc_full, proj_full = stack
    normed, down_q, down_v, norm_one_back, spread, log_total, norm_two_back, gelu_back = kept
    cotangent = out_grad.reshape(count, width)
    grad_active = dot_trans(cotangent, proj_full)
    grad_hidden = gelu_back(grad_active)[0].astype(jnp.bfloat16)
    grad_normed_two = dot_trans(grad_hidden, fc_full)
    grad_middle = cotangent.astype(jnp.float32) + norm_two_back(grad_normed_two)[0]
    grad_context = dot_trans(grad_middle.astype(jnp.bfloat16), out_full).astype(jnp.bfloat16)
    grad_context = grad_context.reshape(docs, tokens, ranks, width // ranks)
    grad_context = lax.all_to_all(grad_context, "seq", split_axis=2, concat_axis=1, tiled=True)
    grad_joined = lax.map(doc_backward, (spread, grad_context, log_total))
    grad_joined = lax.all_to_all(
        grad_joined, "seq", split_axis=1, concat_axis=3, tiled=True
    ).reshape(count, 3 * width)
    grad_normed = dot_trans(grad_joined, qkv_full)
    grad_query = grad_joined[:, :width].astype(jnp.float32)
    grad_value = grad_joined[:, 2 * width :].astype(jnp.float32)
    tilt_q = scale_factor * jnp.dot(grad_query, adapters[1].T, precision=highest)
    value_adapter_up = scale_factor * jnp.dot(grad_value, adapters[3].T, precision=highest)
    grad_normed = (
        grad_normed
        + jnp.dot(tilt_q, adapters[0], precision=highest)
        + jnp.dot(value_adapter_up, adapters[2], precision=highest)
    )
    grad_input = (
        (grad_middle + norm_one_back(grad_normed)[0])
        .astype(jnp.bfloat16)
        .reshape(docs, tokens, width)
    )
    partial_terms = jnp.stack(
        [
            dot_first(tilt_q, normed),
            scale_factor * dot_first(down_q, grad_query),
            dot_first(value_adapter_up, normed),
            scale_factor * dot_first(down_v, grad_value),
        ]
    )
    total = lax.psum(partial_terms, ("dp", "seq"))
    grad_norm = jnp.sqrt(jnp.sum(total * total))
    clipped, new_weight, new_first, new_second = adam_update(
        total, adapters, first_moment, second_moment, grad_norm
    )
    mixed = result.astype(jnp.bfloat16).reshape(docs, tokens, width)
    return (mixed, grad_input, clipped, grad_norm, new_weight, new_first, new_second)


HALF = 512
BLOCK = 256
PICK = 20
SMEM = pl.BlockSpec(memory_space=pltpu.SMEM)
VMEM = pl.BlockSpec(memory_space=pltpu.VMEM)
HBM = pl.BlockSpec(memory_space=pltpu.HBM)
FREE = pl.BlockSpec(memory_space=pl.ANY)
KEEP = pl.BlockSpec(memory_space=pltpu.VMEM)
f32 = jnp.float32
bf16 = jnp.bfloat16
SWAP = ((0, 1), (1, 0))
GELU_A = math.sqrt(2.0 / math.pi)
GELU_B = 0.044715


def nn(left, right):
    return lax.dot_general(left, right, (((1,), (0,)), ((), ())), preferred_element_type=f32)


def nt(left, right):
    return lax.dot_general(left, right, (((1,), (1,)), ((), ())), preferred_element_type=f32)


def tn(left, right):
    return lax.dot_general(left, right, (((0,), (0,)), ((), ())), preferred_element_type=f32)


def shape(*dims, dtype=bf16):
    return jax.ShapeDtypeStruct(dims, dtype)


def params(mib):
    return pltpu.CompilerParams(vmem_limit_bytes=mib * 2**20)


def call(kernel, *, out_shape, in_specs, out_specs, **options):
    spaces = {id(HBM): pltpu.HBM, id(KEEP): pltpu.VMEM}
    single = not isinstance(out_shape, tuple)
    shapes, specs = ((out_shape,), (out_specs,)) if single else (out_shape, out_specs)
    shapes = tuple(
        spaces[id(spec)](each.shape, each.dtype) if id(spec) in spaces else each
        for each, spec in zip(shapes, specs, strict=True)
    )

    def run(*values):
        values = [
            pltpu.with_memory_space_constraint(value, spaces[id(spec)]) if id(spec) in spaces else value
            for value, spec in zip(values, in_specs, strict=True)
        ]
        return pl.pallas_call(
            kernel,
            out_shape=shapes[0] if single else shapes,
            in_specs=in_specs,
            out_specs=out_specs,
            **options,
        )(*values)

    return run


def rows(index, size):
    return pl.ds(pl.multiple_of(index * size, size), size)


def parity(z, k):
    return lax.rem(z + k, 2)


class Copies:
    def __init__(self, sems):
        self.sems = sems
        self.count = 0

    def start(self, source, target):
        copy = pltpu.make_async_copy(source, target, self.sems.at[self.count])
        self.count += 1
        copy.start()
        return copy


def wait_all(copies):
    for copy in copies:
        copy.wait()


def center_scale(x):
    center = jnp.mean(x, axis=-1, keepdims=True)
    centered = x - center
    spread = jnp.mean(centered * centered, axis=-1, keepdims=True)
    inverse = lax.rsqrt(spread + norm_eps)
    return centered * inverse, inverse


def norm_back(hat, inverse, grad):
    first = jnp.mean(grad, axis=-1, keepdims=True)
    second = jnp.mean(grad * hat, axis=-1, keepdims=True)
    return inverse * (grad - first - hat * second)


def cut_kernel(ids, w, w_o, own, send, out_part):
    core = ids[0]
    for p in range(3):
        for i in range(4):
            base = 1024 * p + 256 * i
            to = slice(128 * i, 128 * (i + 1))
            send[p, :, to] = w[:, pl.ds(pl.multiple_of(base + 128 * (1 - core), 128), 128)]
            own[p, :, to] = w[:, pl.ds(pl.multiple_of(base + 128 * core, 128), 128)]
    out_part[0, :128] = w_o[:, :HALF]
    out_part[0, 128:] = w_o[:, HALF:]


def call_cut(ids, w, w_o):
    return call(
        cut_kernel,
        out_shape=(shape(3, 128, HALF), shape(3, 128, HALF), shape(1, BLOCK, HALF)),
        in_specs=[SMEM, VMEM, VMEM],
        out_specs=(VMEM,) * 3,
        compiler_params=params(60),
        name="cut_qkv",
    )(ids, w, w_o)


def cut_feed_kernel(ids, w, own, send):
    core = ids[0]
    for i in range(4):
        send[i] = w[:, pl.ds(pl.multiple_of(1024 * i + HALF * (1 - core), HALF), HALF)]
        own[i] = w[:, pl.ds(pl.multiple_of(1024 * i + HALF * core, HALF), HALF)]


def call_cut_feed(ids, w):
    return call(
        cut_feed_kernel,
        out_shape=(shape(4, 128, HALF), shape(4, 128, HALF)),
        in_specs=[SMEM, VMEM],
        out_specs=(VMEM,) * 2,
        compiler_params=params(60),
        name="cut_feed",
    )(ids, w)


def start_sides(go, piece, target, chip, core, tag):
    return [
        (tag, go.start(piece.at[:128], target.at[rows(2 * chip + core, 128)])),
        (tag, go.start(piece.at[128:], target.at[rows(2 * chip + 1 - core, 128)])),
    ]


def attend(pair, qs, ks, vs, ctxs, stats):
    keys = ks[pair]
    values = jnp.concatenate([jnp.transpose(vs[pair]), jnp.ones((128, 1024), bf16)], axis=0)
    for i in range(4):
        ext = (i + 1) * BLOCK
        cols = slice(i * BLOCK, ext)
        query = qs[pair, cols]
        low = low_half(query)
        zero = jnp.zeros_like(query)
        parts = []
        for a in range(2):
            part = jnp.where(low, query, zero) if a == 0 else jnp.where(low, zero, query)
            scores = nt(keys[:ext], part)
            last = scores[i * BLOCK :]
            r = lax.broadcasted_iota(jnp.int32, last.shape, 0)
            c = lax.broadcasted_iota(jnp.int32, last.shape, 1)
            last = jnp.where(r <= c, last, -1e30)
            scores = jnp.concatenate([scores[: i * BLOCK], last], axis=0) if i else last
            top = jnp.max(scores, axis=0, keepdims=True)
            expo = jnp.exp(scores - top).astype(bf16)
            wide = nn(values[:, :ext], expo)
            total = wide[128:129]
            parts.append(wide[64 * a : 64 * a + 64] * (1.0 / total))
            stats[pair, a : a + 1, cols] = top + jnp.log(total)
        ctxs[pair, cols] = jnp.transpose(jnp.concatenate(parts, axis=0).astype(bf16))


def first_kernel(
    ids, m0, m1, others, w0, w1, w2, w3t, w3b, gain, shift, down_w, up_w, bias,
    q_out, k_out, v_out, n_out, down_out, w_out, o_out, ctx_out, stat_out, own, send,
    xs, ns, ws, os, qs, ks, vs, downs, ctxs, stats, owns, sends, sems,
):
    core, chip = ids[0], ids[2]
    go = Copies(sems)
    arrive = start_grads(go, ids, (m0, m1), (others.at[0], others.at[1]), xs)
    weights, outer, leave = [], [], []
    pieces = (w0, w1, w2, (w3t, w3b))
    part = lambda r, p: pieces[r].at[p] if r < 3 else pieces[r][p // 2].at[p % 2]
    for p in range(3):
        for r in range(4):
            weights += start_sides(go, part(r, p), ws.at[p], chip ^ r, core, p)
    for r in range(4):
        for h in range(2):
            outer.append(
                go.start(
                    part(r, 3).at[h * 128 : (h + 1) * 128],
                    os.at[rows(chip ^ r, 128), h * HALF : (h + 1) * HALF],
                )
            )
    wait_all(arrive)
    for i in range(4):
        hat, _ = center_scale(xs[i].astype(f32))
        ns[i * BLOCK : (i + 1) * BLOCK] = (hat * gain[0:1] + shift[0:1]).astype(bf16)
    leave.append(go.start(ns, n_out))
    for p, (to, out) in enumerate(((qs, q_out), (ks, k_out), (vs, v_out))):
        wait_all([copy for at, copy in weights if at == p])
        leave.append(go.start(ws.at[p], w_out.at[p]))
        for i in range(4):
            at = slice(i * BLOCK, (i + 1) * BLOCK)
            value = nn(ns[at], ws[p]) + bias[:, p * HALF : (p + 1) * HALF]
            if p == 0:
                downs[at] = nt(ns[at], down_w[...]).astype(bf16)
            if p != 1:
                value += nn(downs[at], up_w[:, p * HALF : (p + 1) * HALF])
            value = value.astype(bf16)
            if p == 0:
                value = value * jnp.asarray(0.125, bf16)
            for pair in range(4):
                to[pair, at] = value[:, 128 * pair : 128 * (pair + 1)]
        leave.append(go.start(to, out))
    down_out[...] = nt(down_w[:16], ns[...]).astype(bf16)

    @pl.loop(0, 4)
    def _(pair):
        attend(pair, qs, ks, vs, ctxs, stats)

    leave.append(go.start(ctxs, ctx_out))
    leave.append(go.start(stats, stat_out))
    wait_all(outer)
    leave.append(go.start(os, o_out))
    for side, to, out in ((1 - core, sends, send), (core, owns, own)):
        for i in range(2):
            at = rows(2 * side + i, BLOCK)
            tok = slice(i * BLOCK, (i + 1) * BLOCK)
            whole = jnp.concatenate([ctxs[p, at] for p in range(4)], axis=1)
            to[tok] = nn(whole, os[...]).astype(to.dtype)
            leave.append(go.start(to.at[tok], out.at[tok]))
    wait_all(leave)


def call_first(ids, x_own, x_other, pieces, gain, shift, down_w, up_w, bias):
    heads = shape(4, 1024, 128)
    return call(
        first_kernel,
        out_shape=(
            heads,
            heads,
            heads,
            shape(1024, 1024),
            shape(16, 1024),
            shape(3, 1024, HALF),
            shape(HALF, 1024),
            heads,
            shape(4, 8, 1024, dtype=f32),
            shape(HALF, 1024),
            shape(HALF, 1024),
        ),
        in_specs=[SMEM] + [HBM] * 8 + [VMEM] * 5,
        out_specs=(HBM,) * 4 + (VMEM,) + (HBM,) * 6,
        scratch_shapes=[
            pltpu.VMEM((4, BLOCK, 1024), bf16),
            pltpu.VMEM((1024, 1024), bf16),
            pltpu.VMEM((3, 1024, HALF), bf16),
            pltpu.VMEM((HALF, 1024), bf16),
            pltpu.VMEM((4, 1024, 128), bf16),
            pltpu.VMEM((4, 1024, 128), bf16),
            pltpu.VMEM((4, 1024, 128), bf16),
            pltpu.VMEM((1024, 128), bf16),
            pltpu.VMEM((4, 1024, 128), bf16),
            pltpu.VMEM((4, 8, 1024), f32),
            pltpu.VMEM((HALF, 1024), bf16),
            pltpu.VMEM((HALF, 1024), bf16),
            pltpu.SemaphoreType.DMA((53,)),
        ],
        compiler_params=params(60),
        name="qkv_attention",
    )(ids, *x_own, x_other, *pieces, gain, shift, down_w, up_w, bias)


def attend_back(pair, qs, ks, vs, ctxs, stats, gs, dqs, dks, dvs, acc_k, acc_v):
    keys, values = ks[pair], vs[pair]
    place = pl.ds(pl.multiple_of(pair * 128, 128), 128)
    for i in range(4):
        ext = (i + 1) * BLOCK
        cols = slice(i * BLOCK, ext)
        query, grad = qs[pair, cols], gs[pair, cols]
        low = low_half(query)
        zero = jnp.zeros_like(query)
        product = grad.astype(f32) * ctxs[pair, cols].astype(f32)
        stat = jnp.transpose(stats[pair, :, cols])
        turned_query, turned_grad = jnp.transpose(query), jnp.transpose(grad)
        new_q = []
        for a in range(2):
            pick = (lambda x, y: jnp.where(low, x, y)) if a == 0 else (lambda x, y: jnp.where(low, y, x))
            half = slice(64 * a, 64 * a + 64)
            scores = nt(pick(query, zero), keys[:ext])
            probs = jnp.exp(scores - stat[:, a : a + 1])
            last = probs[:, i * BLOCK :]
            r = lax.broadcasted_iota(jnp.int32, last.shape, 0)
            c = lax.broadcasted_iota(jnp.int32, last.shape, 1)
            last = jnp.where(r >= c, last, 0.0)
            probs = jnp.concatenate([probs[:, : i * BLOCK], last], axis=1) if i else last
            inner = jnp.sum(pick(product, 0.0), axis=1, keepdims=True)
            grad_probs = nt(pick(grad, zero), values[:ext])
            grad_scores = (probs * (grad_probs - inner)).astype(bf16)
            more_v = nn(turned_grad[half], probs.astype(bf16))
            more_k = nn(turned_query[half], grad_scores)
            if i:
                acc_v[half, : i * BLOCK] += more_v[:, : i * BLOCK]
                acc_k[half, : i * BLOCK] += more_k[:, : i * BLOCK]
            acc_v[half, cols] = more_v[:, i * BLOCK :]
            acc_k[half, cols] = more_k[:, i * BLOCK :]
            new_q.append(nn(grad_scores, keys[:ext]))
        both = jnp.where(low, new_q[0], new_q[1])
        dqs[cols, place] = (both * 0.125).astype(bf16)
    dks[:, place] = jnp.transpose(acc_k[...].astype(bf16))
    dvs[:, place] = jnp.transpose(acc_v[...].astype(bf16))


def attention_back_kernel(
    ids, q, k_in, v, ctx, stat, w_o, parts, others, g0, g1, g2, g3, mid_own, mid_other, w, n_all, downs,
    gain, down_w, up_w,
    own, send, grad_middle, total,
    os, qs, ks, vs, ctxs, stats, heads, dqs, dks, dvs, acc_k, acc_v,
    ws, ns, tilts, sems,
):
    core, z = ids[0], ids[1]
    go = Copies(sems)
    outer = go.start(w_o, os)
    then = [
        go.start(ref, to)
        for ref, to in ((q, qs), (k_in, ks), (v, vs), (ctx, ctxs), (stat, stats))
    ]
    weights = [go.start(w, ws), go.start(n_all, ns)]
    mids = (mid_own, mid_own, mid_other, mid_other)
    for at, (g, tok) in enumerate(token_blocks(ids, (g0, g1), (g2, g3))):
        here = rows(parity(z, at % 2), BLOCK)
        hat, inverse = center_scale(mids[at][1, here].astype(f32))
        grad = (parts[tok].astype(f32) + others[tok].astype(f32)) * gain[1:2]
        value = (g[...].astype(f32) + norm_back(hat, inverse, grad)).astype(bf16)
        if at < 2:
            grad_middle[here] = value
        if at == 0:
            outer.wait()
        value = nt(value, os[...]).astype(bf16)
        for pair in range(4):
            heads[pair, tok] = value[:, 128 * pair : 128 * (pair + 1)]
    wait_all(then)

    @pl.loop(0, 4)
    def _(pair):
        attend_back(pair, qs, ks, vs, ctxs, stats, heads, dqs, dks, dvs, acc_k, acc_v)

    wait_all(weights)
    for side, values in ((1 - core, send), (core, own)):
        for i in range(2):
            at = rows(2 * side + i, BLOCK)
            tok = slice(i * BLOCK, (i + 1) * BLOCK)
            gq, gk, gv = dqs[at], dks[at], dvs[at]
            tilt = (nt(gq, up_w[:, :HALF]) + nt(gv, up_w[:, 2 * HALF :])).astype(bf16)
            value = nt(gq, ws[0]) + nt(gk, ws[1]) + nt(gv, ws[2]) + nn(tilt, down_w[...])
            values[tok] = value.astype(bf16)
    tilts[...] = (nt(up_w[:16, :HALF], dqs[...]) + nt(up_w[:16, 2 * HALF :], dvs[...])).astype(bf16)
    down_terms = nn(tilts[...], ns[...])
    total[...] = jnp.zeros_like(total)
    total[0:4] = down_terms[0:4]
    total[8:12] = down_terms[4:8]
    up_q = 8.0 * nn(downs[...], dqs[...])
    up_v = 8.0 * nn(downs[...], dvs[...])
    for pair in range(4):
        here = pl.ds(pl.multiple_of(256 * pair + 128 * core, 128), 128)
        total[4:8, here] = up_q[0:4, 128 * pair : 128 * (pair + 1)]
        total[12:16, here] = up_v[4:8, 128 * pair : 128 * (pair + 1)]


def call_attention_back(
    ids, q, k, v, ctx, stat, w_o, part, other, g_own, g_other, mid_own, mid_other,
    w, n_all, downs, gain, down_w, up_w,
):
    pairs = pltpu.VMEM((4, 1024, 128), bf16)
    wide = pltpu.VMEM((1024, HALF), bf16)
    return call(
        attention_back_kernel,
        out_shape=(
            shape(HALF, 1024),
            shape(HALF, 1024),
            shape(HALF, 1024),
            shape(16, 1024, dtype=f32),
        ),
        in_specs=[SMEM] + [HBM] * 6 + [KEEP] * 8 + [HBM] * 2 + [VMEM] * 4,
        out_specs=(KEEP, KEEP, KEEP, KEEP),
        scratch_shapes=[
            pltpu.VMEM((HALF, 1024), bf16),
            pairs,
            pairs,
            pairs,
            pairs,
            pltpu.VMEM((4, 8, 1024), f32),
            pairs,
            wide,
            wide,
            wide,
            pltpu.VMEM((128, 1024), f32),
            pltpu.VMEM((128, 1024), f32),
            pltpu.VMEM((3, 1024, HALF), bf16),
            pltpu.VMEM((1024, 1024), bf16),
            pltpu.VMEM((16, 1024), bf16),
            pltpu.SemaphoreType.DMA((8,)),
        ],
        compiler_params=params(36),
        name="attention_back",
    )(
        ids, q, k, v, ctx, stat, w_o, part, other, *g_own, *g_other, mid_own, mid_other,
        w, n_all, downs, gain, down_w, up_w,
    )


def low_half(value):
    return lax.broadcasted_iota(jnp.int32, value.shape, 1) < 64


def start_tokens(go, pair, target, z):
    return [go.start(ref, target.at[parity(z, k)]) for k, ref in enumerate(pair)]


def middle_kernel(
    ids, own, other, x0, x1, bias, gain, shift, both, owns, others, xs, sems
):
    go = Copies(sems)
    tokens = start_tokens(go, (x0, x1), xs, ids[1])
    parts = []
    for i in range(2):
        at = slice(i * BLOCK, (i + 1) * BLOCK)
        parts.append([go.start(own.at[at], owns.at[i]), go.start(other.at[at], others.at[i])])
    wait_all(tokens)
    for i in range(2):
        at = slice(i * BLOCK, (i + 1) * BLOCK)
        wait_all(parts[i])
        value = owns[i].astype(f32) + others[i].astype(f32) + xs[i].astype(f32) + bias[2:3]
        both[1, at] = value.astype(bf16)
        hat, _ = center_scale(value)
        both[0, at] = (hat * gain[1:2] + shift[1:2]).astype(bf16)


def call_middle(ids, own, other, x_own, bias, gain, shift):
    return call(
        middle_kernel,
        out_shape=shape(2, HALF, 1024),
        in_specs=[SMEM, HBM, FREE, HBM, HBM] + [VMEM] * 3,
        out_specs=KEEP,
        scratch_shapes=[pltpu.VMEM((2, BLOCK, 1024), bf16)] * 3 + [pltpu.SemaphoreType.DMA((6,))],
        compiler_params=params(40),
        name="middle",
    )(ids, own, other, *x_own, bias, gain, shift)


def start_grads(go, ids, g_own, g_other, gs):
    core, z = ids[0], ids[1]
    return [
        go.start(ref, gs.at[2 * side + parity(z, k)])
        for side, pair in ((core, g_own), (1 - core, g_other))
        for k, ref in enumerate(pair)
    ]


def hidden_kernel(
    ids, n_own, n_other, w0, w1, w2, w3t, w3b, bias, piece, acts, slopes, ws, result, wo, sems
):
    core, chip = ids[0], ids[2]
    go = Copies(sems)
    weights = []
    for p in range(4):
        for r, ref in enumerate((w0, w1, w2, (w3t, w3b))):
            part = ref.at[p] if r < 3 else ref[p // 2].at[p % 2]
            weights += start_sides(go, part, ws.at[p], chip ^ r, core, p)
    later = go.start(piece, wo)
    tokens = [
        (ref, slice(h * BLOCK, (h + 1) * BLOCK), rows(2 * side + h, BLOCK))
        for ref, side in ((n_own, core), (n_other, 1 - core))
        for h in range(2)
    ]

    def finish(p, at, h):
        square = h * h
        lift = 0.5 + 0.5 * jnp.tanh(h * (GELU_A + (GELU_A * GELU_B) * square))
        act = h * lift
        acts[p, at] = act.astype(bf16)
        rise = 2.0 * GELU_A + (6.0 * GELU_A * GELU_B) * square
        slopes[p, at] = (lift + (act - act * lift) * rise).astype(bf16)

    before = None
    for p in range(4):
        wait_all([copy for at, copy in weights if at == p])
        shift = bias[pl.ds(2 * p + core, 1)]
        for ref, here, at in tokens:
            h = nn(ref[0, here], ws[p]) + shift
            if before is not None:
                finish(*before)
            before = (p, at, h)
    finish(*before)
    later.wait()
    for i in range(4):
        tok = slice(i * BLOCK, (i + 1) * BLOCK)
        result[tok] = nn(acts[chip, tok], wo[...]).astype(bf16)


def call_hidden(ids, n_own, n_other, pieces, bias, piece):
    return call(
        hidden_kernel,
        out_shape=(shape(4, 1024, HALF),) * 3 + (shape(1024, 1024),),
        in_specs=[SMEM] + [KEEP] * 2 + [HBM] * 5 + [VMEM, HBM],
        out_specs=(KEEP,) * 4,
        scratch_shapes=[
            pltpu.VMEM((HALF, 1024), bf16),
            pltpu.SemaphoreType.DMA((33,)),
        ],
        compiler_params=params(26),
        name="hidden",
    )(ids, n_own, n_other, *pieces, bias, piece)


def token_blocks(ids, g_own, g_other):
    core, z = ids[0], ids[1]
    return [
        (ref, rows(2 * side + parity(z, k), BLOCK))
        for side, pair in ((core, g_own), (1 - core, g_other))
        for k, ref in enumerate(pair)
    ]


def feed_kernel(
    ids, g0, g1, g2, g3, acts, slopes, w_ins, own_piece, x_piece, y_piece, old,
    result, grad, own_rows, sems,
):
    chip = ids[2]
    load = Copies(sems).start(own_piece, own_rows)
    for i, (g, tok) in enumerate(token_blocks(ids, (g0, g1), (g2, g3))):
        out_sum, grad_sum = old[tok].astype(f32), None
        for r, piece in ((1, x_piece), (2, y_piece), (0, own_rows)):
            here = chip ^ r
            if i == 0 and r == 0:
                load.wait()
            back = nt(g[...], piece[...])
            if r:
                out_sum += nn(acts[here, tok], piece[...])
            back = (back * slopes[here, tok].astype(f32)).astype(bf16)
            term = nt(back, w_ins[here])
            grad_sum = term if grad_sum is None else grad_sum + term
        result[tok] = out_sum.astype(bf16)
        grad[tok] = grad_sum.astype(bf16)


def call_feed(ids, g_own, g_other, active, slope, w_in, pieces, old):
    return call(
        feed_kernel,
        out_shape=(shape(1024, 1024),) * 2,
        in_specs=[SMEM] + [KEEP] * 7 + [HBM] + [KEEP] * 3,
        out_specs=(KEEP, KEEP),
        scratch_shapes=[pltpu.VMEM((HALF, 1024), bf16), pltpu.SemaphoreType.DMA((1,))],
        compiler_params=params(30),
        name="feed",
    )(ids, *g_own, *g_other, active, slope, w_in, *pieces, old)


def far_grad_kernel(ids, g0, g1, g2, g3, slopes, w_ins, top, low, old, out):
    far = ids[2] ^ 3
    for g, tok in token_blocks(ids, (g0, g1), (g2, g3)):
        back = jnp.concatenate([nt(g[...], top[...]), nt(g[...], low[...])], axis=1)
        back = back * slopes[far, tok].astype(f32)
        more = nt(back.astype(bf16), w_ins[far])
        out[tok] = (more + old[tok].astype(f32)).astype(bf16)


def call_far_grad(ids, g_own, g_other, slope, w_in, far, old):
    return call(
        far_grad_kernel,
        out_shape=shape(1024, 1024),
        in_specs=[SMEM] + [KEEP] * 9,
        out_specs=KEEP,
        compiler_params=params(26),
        name="far_grad",
    )(ids, *g_own, *g_other, slope, w_in, *far, old)


def far_result_kernel(ids, acts, top, low, old, own, send):
    core, far = ids[0], ids[2] ^ 3
    for side, values in ((1 - core, send), (core, own)):
        for i in range(2):
            at = rows(2 * side + i, BLOCK)
            tok = slice(i * BLOCK, (i + 1) * BLOCK)
            more = nn(acts[far, at, :BLOCK], top[...]) + nn(acts[far, at, BLOCK:], low[...])
            values[tok] = (old[at].astype(f32) + more).astype(bf16)


def call_far_result(ids, active, far, old):
    return call(
        far_result_kernel,
        out_shape=(shape(HALF, 1024), shape(HALF, 1024)),
        in_specs=[SMEM] + [KEEP] * 4,
        out_specs=(KEEP, KEEP),
        compiler_params=params(16),
        name="far_result",
    )(ids, active, *far, old)


def mixed_kernel(ids, own, other, middle, bias, out0, out1):
    z = ids[1]
    for k, out in enumerate((out0, out1)):
        tok = rows(parity(z, k), BLOCK)
        value = own[tok].astype(f32) + other[tok].astype(f32) + middle[1, tok].astype(f32)
        out[...] = (value + bias[3:4]).astype(bf16)


def call_mixed(ids, own, other, middle, bias):
    return call(
        mixed_kernel,
        out_shape=(shape(BLOCK, 1024),) * 2,
        in_specs=[SMEM, KEEP, KEEP, KEEP, VMEM],
        out_specs=(KEEP, KEEP),
        compiler_params=params(12),
        name="mixed",
    )(ids, own, other, middle, bias)


def input_grad_kernel(ids, x0, x1, own, other, grad_middle, gain, out0, out1, xs, sems):
    z = ids[1]
    go = Copies(sems)
    loads = [go.start(ref, xs.at[k]) for k, ref in enumerate((x0, x1))]
    for k, out in enumerate((out0, out1)):
        loads[k].wait()
        for h in range(2):
            tok = rows(2 * parity(z, k) + h, 128)
            here = slice(128 * h, 128 * (h + 1))
            grad = (own[tok].astype(f32) + other[tok].astype(f32)) * gain[0:1]
            hat, inverse = center_scale(xs[k, here].astype(f32))
            out[here] = (grad_middle[tok].astype(f32) + norm_back(hat, inverse, grad)).astype(bf16)


def call_input_grad(ids, x_own, own, other, grad_middle, gain):
    return call(
        input_grad_kernel,
        out_shape=(shape(BLOCK, 1024),) * 2,
        in_specs=[SMEM, HBM, HBM, KEEP, KEEP, KEEP, VMEM],
        out_specs=(KEEP, KEEP),
        scratch_shapes=[pltpu.VMEM((2, BLOCK, 1024), bf16), pltpu.SemaphoreType.DMA((2,))],
        compiler_params=params(16),
        name="input_grad",
    )(ids, *x_own, own, other, grad_middle, gain)


def to_core(value):
    return lax.ppermute(value, "core", SWAP)


def total_over(value, axis, *others):
    flip = [lax.ppermute(value, axis, [(i, i ^ by) for i in range(4)]) for by in (1, 2, 3)]
    flip = after(flip, *others)
    return (value + flip[0]) + (flip[1] + flip[2])


def exchange(z, pair):
    sent = []
    for k in range(2):
        perm = [
            (4 * core + at, 4 * (at // 2) + 2 * core + (at + k) % 2)
            for core in range(2)
            for at in range(4)
        ]
        sent.append(lax.ppermute(pair[k], ("core", "seq"), perm))
    return sent


def pick_kernel(ids, value, out0, out1, sems):
    z = ids[1]
    go = Copies(sems)
    wait_all([go.start(value.at[parity(z, k)], out) for k, out in enumerate((out0, out1))])


def call_pick(ids, value):
    return call(
        pick_kernel,
        out_shape=(shape(BLOCK, 1024),) * 2,
        in_specs=[SMEM, HBM],
        out_specs=(KEEP, KEEP),
        scratch_shapes=[pltpu.SemaphoreType.DMA((2,))],
        compiler_params=params(PICK),
        name="pick",
    )(ids, value)


def place_kernel(ids, first, second, out, sems):
    z = ids[1]
    go = Copies(sems)
    wait_all([go.start(ref, out.at[parity(z, k)]) for k, ref in enumerate((first, second))])


def call_place(ids, pair):
    return call(
        place_kernel,
        out_shape=shape(2, BLOCK, 1024),
        in_specs=[SMEM, KEEP, KEEP],
        out_specs=HBM,
        scratch_shapes=[pltpu.SemaphoreType.DMA((2,))],
        compiler_params=params(PICK),
        name="place",
    )(ids, *pair)


def after(value, *others):
    return lax.optimization_barrier((value, *others))[0]


def gather_near(shard):
    return [shard, lax.ppermute(shard, "x", SWAP), lax.ppermute(shard, "y", SWAP)]


def halves(near):
    return call_halves(near[1], near[2])


def halves_kernel(by_x, by_y, first, second, held, sems):
    half = first.shape[0]
    go = Copies(sems)
    loads = [go.start(by_x.at[:half], held.at[0]), go.start(by_y.at[half:], held.at[1])]
    leave = []
    for at, out in enumerate((first, second)):
        loads[at].wait()
        leave.append(go.start(held.at[at], out))
    wait_all(leave)


def call_halves(by_x, by_y):
    dims = (by_x.shape[0] // 2, *by_x.shape[1:])
    return call(
        halves_kernel,
        out_shape=(shape(*dims), shape(*dims)),
        in_specs=[FREE, FREE],
        out_specs=(HBM, HBM),
        scratch_shapes=[pltpu.VMEM((2, *dims), bf16), pltpu.SemaphoreType.DMA((4,))],
        compiler_params=params(8),
        name="halves",
    )(by_x, by_y)


def gather_far(near, parts):
    return near + [lax.ppermute(parts[0], "y", SWAP), lax.ppermute(parts[1], "x", SWAP)]


def on_chip(
    inputs,
    out_grad,
    norm_gain,
    norm_bias,
    proj_bias,
    fc_bias,
    qkv_weight,
    out_weight,
    feed_input_weight,
    proj_weight,
    adapters,
    first_moment,
    second_moment,
):
    width = inputs.shape[2]
    core = lax.axis_index("core")
    z = lax.axis_index("seq")
    chip = 2 * lax.axis_index("y") + lax.axis_index("x")
    ids = jnp.stack([core, z, chip]).astype(jnp.int32)

    qkv_own, qkv_send, out_part = call_cut(ids, qkv_weight, out_weight)
    qkv_got = to_core(qkv_send)
    first_shard = jnp.concatenate([jnp.concatenate([qkv_own, qkv_got], axis=1), out_part], axis=0)
    first_near = gather_near(first_shard)
    x_own = exchange(z, call_pick(ids, after(inputs, first_shard)))
    in_own, in_send = call_cut_feed(ids, after(feed_input_weight, first_shard))
    in_shard = jnp.concatenate([in_own, to_core(in_send)], axis=1)

    def columns(value):
        lead = value.shape[0]
        value = value.reshape(lead, 4, 2, 128)
        return jnp.where(core == 0, value[:, :, 0], value[:, :, 1]).reshape(lead, HALF)

    scale = adapter_alpha / ADAPTER_RANK
    adapters, proj_bias = after((adapters, proj_bias), first_shard)
    up_q, up_v = scale * columns(adapters[1]), scale * columns(adapters[3])
    up_w = jnp.zeros((128, 1536), f32)
    up_w = up_w.at[0:4, :HALF].set(up_q).at[4:8, 2 * HALF :].set(up_v).astype(bf16)
    down_w = jnp.concatenate([adapters[0], adapters[2], jnp.zeros((120, 1024), f32)], axis=0)
    down_w = down_w.astype(bf16)
    head_bias = columns(proj_bias[:2])
    qkv_bias = jnp.concatenate([head_bias[0], jnp.zeros((HALF,), f32), head_bias[1]])[None]

    first_near = after(first_near, up_w, down_w, qkv_bias, in_shard)
    first_halves = halves(first_near)
    first_pieces = gather_far(first_near, first_halves)
    x_own = after(x_own, *first_halves)
    x_other = to_core(jnp.stack(x_own))
    in_near = gather_near(after(in_shard, *first_pieces[3:]))
    q, k, v, n_all, down, w_qkv, w_o, ctx, stat, attn_own, attn_send = call_first(
        ids, x_own, x_other, first_pieces, norm_gain, norm_bias, down_w, up_w, qkv_bias
    )
    in_near = after(in_near, ctx)
    in_halves = halves(in_near)
    in_pieces = gather_far(in_near, in_halves)
    attn_other = to_core(after(attn_send, *in_halves))
    n2_own = call_middle(
        ids, attn_own, after(attn_other, *in_halves), x_own, proj_bias, norm_gain, norm_bias
    )
    g_pair = call_pick(ids, after(out_grad, n2_own))
    in_pieces[3:] = after(in_pieces[3:], *g_pair)
    g_own = exchange(z, g_pair)
    n2_other = to_core(after(n2_own, *in_pieces[3:]))
    proj_near = gather_near(after(proj_weight, *in_pieces[3:]))
    active, slope, w_in, old = call_hidden(
        ids, n2_own, n2_other, in_pieces, fc_bias.reshape(8, HALF), proj_near[0]
    )
    proj_near = after(proj_near, old)
    proj_halves = halves(proj_near)
    far = gather_far(proj_near, proj_halves)[3:]
    near = after(proj_near, *proj_halves)
    g_own = after(g_own, *proj_halves)
    g_other = [to_core(part) for part in g_own]
    result, grad = call_feed(ids, g_own, g_other, active, slope, w_in, near, old)
    result_own, result_send = call_far_result(ids, active, far, result)
    result_other = to_core(result_send)
    part = call_far_grad(ids, g_own, g_other, slope, w_in, after(far, result_own), grad)
    part = after(part, result_other)
    part_other = to_core(part)
    mixed = call_mixed(ids, result_own, after(result_other, part), n2_own, proj_bias)
    part_other = after(part_other, *mixed)
    mixed = exchange(z, mixed)
    own, send, grad_middle, total = call_attention_back(
        ids, q, k, v, ctx, stat, w_o, part, part_other, g_own, g_other, n2_own, n2_other,
        w_qkv, n_all, down, norm_gain, down_w, up_w,
    )
    other = to_core(after(send, *mixed))
    grad_in = call_input_grad(ids, x_own, own, other, grad_middle, norm_gain)
    total = total_over(total, "seq", *grad_in)
    grad_in = exchange(z, grad_in)
    total = total + to_core(total)
    total = total_over(total, ("y", "x"))
    mixed = call_place(ids, after(mixed, total))
    total = after(total, grad_in[0]).reshape(4, ADAPTER_RANK, width)
    grad_norm = jnp.sqrt(jnp.sum(total * total))
    clipped, new_weight, new_first, new_second = adam_update(
        total, adapters, first_moment, second_moment, grad_norm
    )
    grad_input = call_place(ids, after(grad_in, mixed))
    return (mixed, grad_input, clipped, grad_norm, new_weight, new_first, new_second)


def solution(mesh):
    sizes = dict(mesh.shape)
    if sizes["dp"] == 8 and sizes["seq"] == 4:
        plane = Mesh(mesh.devices.reshape(2, 2, 2, 4), ("y", "x", "core", "seq"))
        return build(plane, ("y", "x", "core"), on_chip)
    return build(mesh, "dp", on_device)


def build(mesh, dp, step):
    tokens, weight = P(dp, "seq", None), P(dp, None)
    return jax.shard_map(
        step,
        mesh=mesh,
        in_specs=(tokens, tokens) + (P(),) * 4 + (weight,) * 4 + (P(),) * 3,
        out_specs=(tokens, tokens) + (P(),) * 5,
        check_vma=False,
    )
```

```python
import functools
import math

import jax
import jax.numpy as jnp
from jax import lax
from jax.experimental import pallas as pl
from jax.experimental.pallas import tpu as pltpu
from jax.sharding import Mesh
from jax.sharding import PartitionSpec as P

HEAD_DIM = 64
ADAPTER_RANK = 4
STEP = 10


highest = lax.Precision.HIGHEST
adapter_alpha = 32.0
beta_one = 0.9
beta_two = 0.999
adam_eps = 1e-08
decay_rate = 0.01
learning_rate = 0.02
clip_bound = 1.0
norm_eps = 1e-05


def layer_norm(value, gain, shift):
    center = jnp.mean(value, axis=-1, keepdims=True)
    centered = value - center
    spread = jnp.mean(centered * centered, axis=-1, keepdims=True)
    return centered * lax.rsqrt(spread + norm_eps) * gain + shift


def dot_trans(left, right):
    return lax.dot_general(
        left, right, (((1,), (1,)), ((), ())), preferred_element_type=jnp.float32
    )


def dot_first(left, right):
    return lax.dot_general(
        left, right, (((0,), (0,)), ((), ())), precision=highest, preferred_element_type=jnp.float32
    )


def adam_update(grad, weight, first, second, norm):
    scale_factor = clip_bound / jnp.maximum(norm, clip_bound)
    clipped = grad * scale_factor
    new_first = beta_one * first + (1.0 - beta_one) * clipped
    new_second = beta_two * second + (1.0 - beta_two) * clipped * clipped
    first_hat = new_first / (1.0 - beta_one**STEP)
    second_hat = new_second / (1.0 - beta_two**STEP)
    new_weight = weight - learning_rate * (
        first_hat / (jnp.sqrt(second_hat) + adam_eps) + decay_rate * weight
    )
    return (clipped, new_weight, new_first, new_second)


def split_heads(packed):
    length = packed.shape[0]
    local_heads = packed.shape[-1] // HEAD_DIM
    query = packed[:, 0, 0].reshape(length, local_heads, HEAD_DIM)
    keys = packed[:, 1, 0].reshape(length, local_heads, HEAD_DIM)
    values = packed[:, 2, 0].reshape(length, local_heads, HEAD_DIM)
    return (query, keys, values)


def doc_forward(packed):
    length = packed.shape[0]
    local_width = packed.shape[-1]
    query, keys, values = split_heads(packed)
    local_heads = query.shape[1]
    span = min(512, length)
    blocks = length // span
    scale = 1.0 / math.sqrt(HEAD_DIM)
    starts = jnp.arange(blocks, dtype=jnp.int32) * span

    def visit(pieces):
        query_block, start = pieces
        scores = (
            jnp.einsum("qhd,khd->hqk", query_block, keys, preferred_element_type=jnp.float32)
            * scale
        )
        causal = (start + jnp.arange(span))[:, None] >= jnp.arange(length)[None, :]
        masked = jnp.where(causal[None], scores, -1e30)
        summit = jnp.max(masked, axis=-1, keepdims=True)
        expo = jnp.where(causal[None], jnp.exp(masked - summit), 0.0)
        totals = jnp.sum(expo, axis=-1, keepdims=True)
        weights = (expo / totals).astype(jnp.bfloat16)
        context = jnp.einsum(
            "hqk,khd->qhd", weights, values, preferred_element_type=jnp.float32
        ).astype(jnp.bfloat16)
        return (context, summit[..., 0] + jnp.log(totals[..., 0]))

    context, log_total = lax.map(
        visit, (query.reshape(blocks, span, local_heads, HEAD_DIM), starts)
    )
    return (context.reshape(length, 1, local_width), log_total)


def doc_backward(args):
    packed, grad_context, log_total = args
    length = packed.shape[0]
    local_width = packed.shape[-1]
    query, keys, values = split_heads(packed)
    local_heads = query.shape[1]
    output_gradient = grad_context[:, 0].reshape(length, local_heads, HEAD_DIM)
    span = min(512, length)
    blocks = length // span
    scale = 1.0 / math.sqrt(HEAD_DIM)
    starts = jnp.arange(blocks, dtype=jnp.int32) * span

    def visit(carry, pieces):
        grad_keys, grad_values = carry
        query_block, grad_block, total_block, start = pieces
        scores = (
            jnp.einsum("qhd,khd->hqk", query_block, keys, preferred_element_type=jnp.float32)
            * scale
        )
        causal = (start + jnp.arange(span))[:, None] >= jnp.arange(length)[None, :]
        masked = jnp.where(causal[None], scores, -1e30)
        probs = jnp.where(causal[None], jnp.exp(masked - total_block[:, :, None]), 0.0)
        weights = probs.astype(jnp.bfloat16)
        grad_probs = jnp.einsum(
            "qhd,khd->hqk", grad_block, values, preferred_element_type=jnp.float32
        )
        inner = jnp.sum(probs * grad_probs, axis=-1, keepdims=True)
        grad_scores = (probs * (grad_probs - inner)).astype(jnp.bfloat16)
        grad_query = (
            jnp.einsum("hqk,khd->qhd", grad_scores, keys, preferred_element_type=jnp.float32)
            * scale
        )
        grad_keys = (
            grad_keys
            + jnp.einsum(
                "hqk,qhd->khd", grad_scores, query_block, preferred_element_type=jnp.float32
            )
            * scale
        )
        grad_values = grad_values + jnp.einsum(
            "hqk,qhd->khd", weights, grad_block, preferred_element_type=jnp.float32
        )
        return ((grad_keys, grad_values), grad_query)

    empty = jnp.zeros((length, local_heads, HEAD_DIM), jnp.float32)
    pieces = (
        query.reshape(blocks, span, local_heads, HEAD_DIM),
        output_gradient.reshape(blocks, span, local_heads, HEAD_DIM),
        log_total,
        starts,
    )
    (grad_keys, grad_values), grad_query = lax.scan(visit, (empty, empty), pieces)
    joined = jnp.stack(
        [
            grad_query.reshape(length, local_width),
            grad_keys.reshape(length, local_width),
            grad_values.reshape(length, local_width),
        ],
        axis=1,
    )
    return joined.astype(jnp.bfloat16)[:, :, None, :]


def on_device(
    inputs,
    out_grad,
    norm_gain,
    norm_bias,
    proj_bias,
    fc_bias,
    qkv_weight,
    out_weight,
    feed_input_weight,
    proj_weight,
    adapters,
    first_moment,
    second_moment,
):
    docs, tokens, width = inputs.shape
    count = docs * tokens
    ranks = lax.axis_size("seq")
    scale_factor = adapter_alpha / ADAPTER_RANK

    def forward(stack):
        qkv_full, out_full, fc_full, proj_full = stack
        flat = inputs.reshape(count, width).astype(jnp.float32)
        normed, norm_one_back = jax.vjp(
            lambda value: layer_norm(value, norm_gain[0], norm_bias[0]), flat
        )
        base = jnp.dot(normed.astype(jnp.bfloat16), qkv_full, preferred_element_type=jnp.float32)
        down_q = jnp.dot(normed, adapters[0].T, precision=highest)
        down_v = jnp.dot(normed, adapters[2].T, precision=highest)
        query = (
            base[:, :width]
            + proj_bias[0]
            + scale_factor * jnp.dot(down_q, adapters[1], precision=highest)
        )
        keys = base[:, width : 2 * width]
        values = (
            base[:, 2 * width :]
            + proj_bias[1]
            + scale_factor * jnp.dot(down_v, adapters[3], precision=highest)
        )
        joined = (
            jnp.concatenate([query, keys, values], axis=1)
            .astype(jnp.bfloat16)
            .reshape(docs, tokens, 3, ranks, width // ranks)
        )
        spread = lax.all_to_all(joined, "seq", split_axis=3, concat_axis=1, tiled=True)
        context, log_total = lax.map(doc_forward, spread)
        context = lax.all_to_all(context, "seq", split_axis=1, concat_axis=2, tiled=True).reshape(
            count, width
        )
        middle = (
            flat + jnp.dot(context, out_full, preferred_element_type=jnp.float32) + proj_bias[2]
        )
        normed_two, norm_two_back = jax.vjp(
            lambda value: layer_norm(value, norm_gain[1], norm_bias[1]), middle
        )
        hidden = (
            jnp.dot(normed_two.astype(jnp.bfloat16), fc_full, preferred_element_type=jnp.float32)
            + fc_bias
        )
        active, gelu_back = jax.vjp(lambda value: jax.nn.gelu(value, approximate=True), hidden)
        result = (
            middle
            + jnp.dot(active.astype(jnp.bfloat16), proj_full, preferred_element_type=jnp.float32)
            + proj_bias[3]
        )
        return (
            result,
            (normed, down_q, down_v, norm_one_back, spread, log_total, norm_two_back, gelu_back),
        )

    stack = (
        lax.all_gather(qkv_weight, "dp", axis=0, tiled=True),
        lax.all_gather(out_weight, "dp", axis=0, tiled=True),
        lax.all_gather(feed_input_weight, "dp", axis=0, tiled=True),
        lax.all_gather(proj_weight, "dp", axis=0, tiled=True),
    )
    result, kept = forward(stack)
    fenced = lax.optimization_barrier((stack, result))
    stack = fenced[0]
    again, kept = forward(stack)
    qkv_full, out_full, fc_full, proj_full = stack
    normed, down_q, down_v, norm_one_back, spread, log_total, norm_two_back, gelu_back = kept
    cotangent = out_grad.reshape(count, width)
    grad_active = dot_trans(cotangent, proj_full)
    grad_hidden = gelu_back(grad_active)[0].astype(jnp.bfloat16)
    grad_normed_two = dot_trans(grad_hidden, fc_full)
    grad_middle = cotangent.astype(jnp.float32) + norm_two_back(grad_normed_two)[0]
    grad_context = dot_trans(grad_middle.astype(jnp.bfloat16), out_full).astype(jnp.bfloat16)
    grad_context = grad_context.reshape(docs, tokens, ranks, width // ranks)
    grad_context = lax.all_to_all(grad_context, "seq", split_axis=2, concat_axis=1, tiled=True)
    grad_joined = lax.map(doc_backward, (spread, grad_context, log_total))
    grad_joined = lax.all_to_all(
        grad_joined, "seq", split_axis=1, concat_axis=3, tiled=True
    ).reshape(count, 3 * width)
    grad_normed = dot_trans(grad_joined, qkv_full)
    grad_query = grad_joined[:, :width].astype(jnp.float32)
    grad_value = grad_joined[:, 2 * width :].astype(jnp.float32)
    tilt_q = scale_factor * jnp.dot(grad_query, adapters[1].T, precision=highest)
    value_adapter_up = scale_factor * jnp.dot(grad_value, adapters[3].T, precision=highest)
    grad_normed = (
        grad_normed
        + jnp.dot(tilt_q, adapters[0], precision=highest)
        + jnp.dot(value_adapter_up, adapters[2], precision=highest)
    )
    grad_input = (
        (grad_middle + norm_one_back(grad_normed)[0])
        .astype(jnp.bfloat16)
        .reshape(docs, tokens, width)
    )
    partial_terms = jnp.stack(
        [
            dot_first(tilt_q, normed),
            scale_factor * dot_first(down_q, grad_query),
            dot_first(value_adapter_up, normed),
            scale_factor * dot_first(down_v, grad_value),
        ]
    )
    total = lax.psum(partial_terms, ("dp", "seq"))
    grad_norm = jnp.sqrt(jnp.sum(total * total))
    clipped, new_weight, new_first, new_second = adam_update(
        total, adapters, first_moment, second_moment, grad_norm
    )
    mixed = result.astype(jnp.bfloat16).reshape(docs, tokens, width)
    return (mixed, grad_input, clipped, grad_norm, new_weight, new_first, new_second)


HALF = 512
BLOCK = 256
PICK = 20
SMEM = pl.BlockSpec(memory_space=pltpu.SMEM)
VMEM = pl.BlockSpec(memory_space=pltpu.VMEM)
HBM = pl.BlockSpec(memory_space=pltpu.HBM)
FREE = pl.BlockSpec(memory_space=pl.ANY)
KEEP = pl.BlockSpec(memory_space=pltpu.VMEM)
f32 = jnp.float32
bf16 = jnp.bfloat16
SWAP = ((0, 1), (1, 0))
GELU_A = math.sqrt(2.0 / math.pi)
GELU_B = 0.044715


def nn(left, right):
    return lax.dot_general(left, right, (((1,), (0,)), ((), ())), preferred_element_type=f32)


def nt(left, right):
    return lax.dot_general(left, right, (((1,), (1,)), ((), ())), preferred_element_type=f32)


def tn(left, right):
    return lax.dot_general(left, right, (((0,), (0,)), ((), ())), preferred_element_type=f32)


def shape(*dims, dtype=bf16):
    return jax.ShapeDtypeStruct(dims, dtype)


def params(mib):
    return pltpu.CompilerParams(vmem_limit_bytes=mib * 2**20)


def call(kernel, *, out_shape, in_specs, out_specs, **options):
    spaces = {id(HBM): pltpu.HBM, id(KEEP): pltpu.VMEM}
    single = not isinstance(out_shape, tuple)
    shapes, specs = ((out_shape,), (out_specs,)) if single else (out_shape, out_specs)
    shapes = tuple(
        spaces[id(spec)](each.shape, each.dtype) if id(spec) in spaces else each
        for each, spec in zip(shapes, specs, strict=True)
    )

    def run(*values):
        values = [
            pltpu.with_memory_space_constraint(value, spaces[id(spec)]) if id(spec) in spaces else value
            for value, spec in zip(values, in_specs, strict=True)
        ]
        return pl.pallas_call(
            kernel,
            out_shape=shapes[0] if single else shapes,
            in_specs=in_specs,
            out_specs=out_specs,
            **options,
        )(*values)

    return run


def rows(index, size):
    return pl.ds(pl.multiple_of(index * size, size), size)


def parity(z, k):
    return lax.rem(z + k, 2)


class Copies:
    def __init__(self, sems):
        self.sems = sems
        self.count = 0

    def start(self, source, target):
        copy = pltpu.make_async_copy(source, target, self.sems.at[self.count])
        self.count += 1
        copy.start()
        return copy


def wait_all(copies):
    for copy in copies:
        copy.wait()


def center_scale(x):
    center = jnp.mean(x, axis=-1, keepdims=True)
    centered = x - center
    spread = jnp.mean(centered * centered, axis=-1, keepdims=True)
    inverse = lax.rsqrt(spread + norm_eps)
    return centered * inverse, inverse


def norm_back(hat, inverse, grad):
    first = jnp.mean(grad, axis=-1, keepdims=True)
    second = jnp.mean(grad * hat, axis=-1, keepdims=True)
    return inverse * (grad - first - hat * second)


def cut_kernel(w, w_o, own, send, out_part):
    core = lax.axis_index("core")
    for p in range(3):
        for i in range(4):
            base = 1024 * p + 256 * i
            to = slice(128 * i, 128 * (i + 1))
            send[p, :, to] = w[:, pl.ds(pl.multiple_of(base + 128 * (1 - core), 128), 128)]
            own[p, :, to] = w[:, pl.ds(pl.multiple_of(base + 128 * core, 128), 128)]
    out_part[0, :128] = w_o[:, :HALF]
    out_part[0, 128:] = w_o[:, HALF:]


def call_cut(w, w_o):
    return call(
        cut_kernel,
        out_shape=(shape(3, 128, HALF), shape(3, 128, HALF), shape(1, BLOCK, HALF)),
        in_specs=[VMEM, VMEM],
        out_specs=(KEEP,) * 3,
        compiler_params=params(12),
        name="cut_qkv",
    )(w, w_o)


def join_kernel(own, got, out_part, shard):
    shard[:3, :128] = own[...]
    shard[:3, 128:] = got[...]
    shard[3:] = out_part[...]


def cut_feed_kernel(ids, w, own, send):
    core = ids[0]
    for i in range(4):
        send[i] = w[:, pl.ds(pl.multiple_of(1024 * i + HALF * (1 - core), HALF), HALF)]
        own[i] = w[:, pl.ds(pl.multiple_of(1024 * i + HALF * core, HALF), HALF)]


def call_cut_feed(ids, w):
    return call(
        cut_feed_kernel,
        out_shape=(shape(4, 128, HALF), shape(4, 128, HALF)),
        in_specs=[SMEM, VMEM],
        out_specs=(VMEM,) * 2,
        compiler_params=params(60),
        name="cut_feed",
    )(ids, w)


def start_sides(go, piece, target, chip, core, tag):
    return [
        (tag, go.start(piece.at[:128], target.at[rows(2 * chip + core, 128)])),
        (tag, go.start(piece.at[128:], target.at[rows(2 * chip + 1 - core, 128)])),
    ]


def attend(pair, qs, ks, vs, ctxs, stats):
    keys = ks[pair]
    values = jnp.concatenate([jnp.transpose(vs[pair]), jnp.ones((128, 1024), bf16)], axis=0)
    for i in range(4):
        ext = (i + 1) * BLOCK
        cols = slice(i * BLOCK, ext)
        query = qs[pair, cols]
        low = low_half(query)
        zero = jnp.zeros_like(query)
        parts = []
        for a in range(2):
            part = jnp.where(low, query, zero) if a == 0 else jnp.where(low, zero, query)
            scores = nt(keys[:ext], part)
            last = scores[i * BLOCK :]
            r = lax.broadcasted_iota(jnp.int32, last.shape, 0)
            c = lax.broadcasted_iota(jnp.int32, last.shape, 1)
            last = jnp.where(r <= c, last, -1e30)
            scores = jnp.concatenate([scores[: i * BLOCK], last], axis=0) if i else last
            top = jnp.max(scores, axis=0, keepdims=True)
            expo = jnp.exp(scores - top).astype(bf16)
            wide = nn(values[:, :ext], expo)
            total = wide[128:129]
            parts.append(wide[64 * a : 64 * a + 64] * (1.0 / total))
            stats[pair, a : a + 1, cols] = top + jnp.log(total)
        ctxs[pair, cols] = jnp.transpose(jnp.concatenate(parts, axis=0).astype(bf16))


def first_kernel(
    ids, m0, m1, others, w0, w1, w2, w3t, w3b, gain, shift, down_w, up_w, bias,
    q_out, k_out, v_out, n_out, down_out, w_out, o_out, ctx_out, stat_out, own, send,
    ns, ws, os, qs, ks, vs, ctxs, stats, owns, sends, sems,
):
    core, chip = ids[0], ids[2]
    go = Copies(sems)
    weights, outer, leave = [], [], []
    pieces = (w0, w1, w2, (w3t, w3b))
    part = lambda r, p: pieces[r].at[p] if r < 3 else pieces[r][p // 2].at[p % 2]
    for p in range(3):
        for r in range(4):
            weights += start_sides(go, part(r, p), ws.at[p], chip ^ r, core, p)
    for r in range(4):
        for h in range(2):
            outer.append(
                go.start(
                    part(r, 3).at[h * 128 : (h + 1) * 128],
                    os.at[rows(chip ^ r, 128), h * HALF : (h + 1) * HALF],
                )
            )
    for x, at in token_blocks(ids, (m0, m1), (others.at[0], others.at[1])):
        hat, _ = center_scale(x[...].astype(f32))
        ns[at] = (hat * gain[0:1] + shift[0:1]).astype(bf16)
    leave.append(go.start(ns, n_out))
    for p, (to, out) in enumerate(((qs, q_out), (ks, k_out), (vs, v_out))):
        wait_all([copy for at, copy in weights if at == p])
        if p != 1:
            for i in range(4):
                at = slice(i * BLOCK, (i + 1) * BLOCK)
                more = tn(down_w[:16, at], up_w[:16, p * HALF : (p + 1) * HALF])
                ws[p, at] = (ws[p, at].astype(f32) + more).astype(bf16)
        leave.append(go.start(ws.at[p], w_out.at[p]))
        for i in range(4):
            at = slice(i * BLOCK, (i + 1) * BLOCK)
            value = nn(ns[at], ws[p]) + bias[:, p * HALF : (p + 1) * HALF]
            value = value.astype(bf16)
            if p == 0:
                value = value * jnp.asarray(0.125, bf16)
            for pair in range(4):
                to[pair, at] = value[:, 128 * pair : 128 * (pair + 1)]
        leave.append(go.start(to, out))
    down_out[...] = nt(down_w[:16], ns[...]).astype(bf16)

    @pl.loop(0, 4)
    def _(pair):
        attend(pair, qs, ks, vs, ctxs, stats)

    leave.append(go.start(ctxs, ctx_out))
    leave.append(go.start(stats, stat_out))
    wait_all(outer)
    leave.append(go.start(os, o_out))
    for side, to, out in ((1 - core, sends, send), (core, owns, own)):
        for i in range(2):
            at = rows(2 * side + i, BLOCK)
            tok = slice(i * BLOCK, (i + 1) * BLOCK)
            whole = jnp.concatenate([ctxs[p, at] for p in range(4)], axis=1)
            to[tok] = nn(whole, os[...]).astype(to.dtype)
            leave.append(go.start(to.at[tok], out.at[tok]))
    wait_all(leave)


def call_first(ids, x_own, x_other, pieces, gain, shift, down_w, up_w, bias):
    heads = shape(4, 1024, 128)
    return call(
        first_kernel,
        out_shape=(
            heads,
            heads,
            heads,
            shape(1024, 1024),
            shape(16, 1024),
            shape(3, 1024, HALF),
            shape(HALF, 1024),
            heads,
            shape(4, 8, 1024, dtype=f32),
            shape(HALF, 1024),
            shape(HALF, 1024),
        ),
        in_specs=[SMEM] + [KEEP] * 3 + [FREE] * 5 + [VMEM] * 5,
        out_specs=(HBM,) * 4 + (VMEM,) + (HBM,) * 6,
        scratch_shapes=[
            pltpu.VMEM((1024, 1024), bf16),
            pltpu.VMEM((3, 1024, HALF), bf16),
            pltpu.VMEM((HALF, 1024), bf16),
            pltpu.VMEM((4, 1024, 128), bf16),
            pltpu.VMEM((4, 1024, 128), bf16),
            pltpu.VMEM((4, 1024, 128), bf16),
            pltpu.VMEM((4, 1024, 128), bf16),
            pltpu.VMEM((4, 8, 1024), f32),
            pltpu.VMEM((HALF, 1024), bf16),
            pltpu.VMEM((HALF, 1024), bf16),
            pltpu.SemaphoreType.DMA((53,)),
        ],
        compiler_params=params(44),
        name="qkv_attention",
    )(ids, *x_own, x_other, *pieces, gain, shift, down_w, up_w, bias)


def attend_back(pair, qs, ks, vs, ctxs, stats, gs, dqs, dks, dvs, acc_k, acc_v):
    keys, values = ks[pair], vs[pair]
    place = pl.ds(pl.multiple_of(pair * 128, 128), 128)
    for i in range(4):
        ext = (i + 1) * BLOCK
        cols = slice(i * BLOCK, ext)
        query, grad = qs[pair, cols], gs[pair, cols]
        low = low_half(query)
        zero = jnp.zeros_like(query)
        product = grad.astype(f32) * ctxs[pair, cols].astype(f32)
        stat = jnp.transpose(stats[pair, :, cols])
        turned_query, turned_grad = jnp.transpose(query), jnp.transpose(grad)
        new_q = []
        for a in range(2):
            pick = (lambda x, y: jnp.where(low, x, y)) if a == 0 else (lambda x, y: jnp.where(low, y, x))
            half = slice(64 * a, 64 * a + 64)
            scores = nt(pick(query, zero), keys[:ext])
            probs = jnp.exp(scores - stat[:, a : a + 1])
            last = probs[:, i * BLOCK :]
            r = lax.broadcasted_iota(jnp.int32, last.shape, 0)
            c = lax.broadcasted_iota(jnp.int32, last.shape, 1)
            last = jnp.where(r >= c, last, 0.0)
            probs = jnp.concatenate([probs[:, : i * BLOCK], last], axis=1) if i else last
            inner = jnp.sum(pick(product, 0.0), axis=1, keepdims=True)
            grad_probs = nt(pick(grad, zero), values[:ext])
            grad_scores = (probs * (grad_probs - inner)).astype(bf16)
            more_v = nn(turned_grad[half], probs.astype(bf16))
            more_k = nn(turned_query[half], grad_scores)
            if i:
                acc_v[half, : i * BLOCK] += more_v[:, : i * BLOCK]
                acc_k[half, : i * BLOCK] += more_k[:, : i * BLOCK]
            acc_v[half, cols] = more_v[:, i * BLOCK :]
            acc_k[half, cols] = more_k[:, i * BLOCK :]
            new_q.append(nn(grad_scores, keys[:ext]))
        both = jnp.where(low, new_q[0], new_q[1])
        dqs[cols, place] = (both * 0.125).astype(bf16)
    dks[:, place] = jnp.transpose(acc_k[...].astype(bf16))
    dvs[:, place] = jnp.transpose(acc_v[...].astype(bf16))


def attention_back_kernel(
    ids, q, k_in, v, ctx, stat, w_o, parts, others, g0, g1, g2, g3, mid_own, mid_other, w, n_all, downs,
    gain, down_w, up_w,
    own, send, grad_middle, total,
    os, qs, ks, vs, ctxs, stats, heads, dqs, dks, dvs, acc_k, acc_v,
    ws, ns, tilts, sems,
):
    core, z = ids[0], ids[1]
    go = Copies(sems)
    outer = go.start(w_o, os)
    then = [
        go.start(ref, to)
        for ref, to in ((q, qs), (k_in, ks), (v, vs), (ctx, ctxs), (stat, stats))
    ]
    weights = [go.start(w, ws), go.start(n_all, ns)]
    mids = (mid_own, mid_own, mid_other, mid_other)
    for at, (g, tok) in enumerate(token_blocks(ids, (g0, g1), (g2, g3))):
        here = rows(parity(z, at % 2), BLOCK)
        hat, inverse = center_scale(mids[at][1, here].astype(f32))
        grad = (parts[tok].astype(f32) + others[tok].astype(f32)) * gain[1:2]
        value = (g[...].astype(f32) + norm_back(hat, inverse, grad)).astype(bf16)
        if at < 2:
            grad_middle[here] = value
        if at == 0:
            outer.wait()
        value = nt(value, os[...]).astype(bf16)
        for pair in range(4):
            heads[pair, tok] = value[:, 128 * pair : 128 * (pair + 1)]
    wait_all(then)

    @pl.loop(0, 4)
    def _(pair):
        attend_back(pair, qs, ks, vs, ctxs, stats, heads, dqs, dks, dvs, acc_k, acc_v)

    wait_all(weights)
    for side, values in ((1 - core, send), (core, own)):
        for i in range(2):
            at = rows(2 * side + i, BLOCK)
            tok = slice(i * BLOCK, (i + 1) * BLOCK)
            gq, gk, gv = dqs[at], dks[at], dvs[at]
            value = nt(gq, ws[0]) + nt(gk, ws[1]) + nt(gv, ws[2])
            values[tok] = value.astype(bf16)
    tilts[...] = (nt(up_w[:16, :HALF], dqs[...]) + nt(up_w[:16, 2 * HALF :], dvs[...])).astype(bf16)
    down_terms = nn(tilts[...], ns[...])
    total[...] = jnp.zeros_like(total)
    total[0:4] = down_terms[0:4]
    total[8:12] = down_terms[4:8]
    up_q = 8.0 * nn(downs[...], dqs[...])
    up_v = 8.0 * nn(downs[...], dvs[...])
    for pair in range(4):
        here = pl.ds(pl.multiple_of(256 * pair + 128 * core, 128), 128)
        total[4:8, here] = up_q[0:4, 128 * pair : 128 * (pair + 1)]
        total[12:16, here] = up_v[4:8, 128 * pair : 128 * (pair + 1)]


def call_attention_back(
    ids, q, k, v, ctx, stat, w_o, part, other, g_own, g_other, mid_own, mid_other,
    w, n_all, downs, gain, down_w, up_w,
):
    pairs = pltpu.VMEM((4, 1024, 128), bf16)
    wide = pltpu.VMEM((1024, HALF), bf16)
    return call(
        attention_back_kernel,
        out_shape=(
            shape(HALF, 1024),
            shape(HALF, 1024),
            shape(HALF, 1024),
            shape(16, 1024, dtype=f32),
        ),
        in_specs=[SMEM] + [HBM] * 6 + [KEEP] * 8 + [HBM] * 2 + [VMEM] * 4,
        out_specs=(KEEP, KEEP, KEEP, KEEP),
        scratch_shapes=[
            pltpu.VMEM((HALF, 1024), bf16),
            pairs,
            pairs,
            pairs,
            pairs,
            pltpu.VMEM((4, 8, 1024), f32),
            pairs,
            wide,
            wide,
            wide,
            pltpu.VMEM((128, 1024), f32),
            pltpu.VMEM((128, 1024), f32),
            pltpu.VMEM((3, 1024, HALF), bf16),
            pltpu.VMEM((1024, 1024), bf16),
            pltpu.VMEM((16, 1024), bf16),
            pltpu.SemaphoreType.DMA((8,)),
        ],
        compiler_params=params(36),
        name="attention_back",
    )(
        ids, q, k, v, ctx, stat, w_o, part, other, *g_own, *g_other, mid_own, mid_other,
        w, n_all, downs, gain, down_w, up_w,
    )


def low_half(value):
    return lax.broadcasted_iota(jnp.int32, value.shape, 1) < 64


def start_tokens(go, pair, target, z):
    return [go.start(ref, target.at[parity(z, k)]) for k, ref in enumerate(pair)]


def middle_kernel(
    ids, own, other, x0, x1, bias, gain, shift, both, owns, others, xs, sems
):
    go = Copies(sems)
    tokens = start_tokens(go, (x0, x1), xs, ids[1])
    parts = []
    for i in range(2):
        at = slice(i * BLOCK, (i + 1) * BLOCK)
        parts.append([go.start(own.at[at], owns.at[i]), go.start(other.at[at], others.at[i])])
    wait_all(tokens)
    for i in range(2):
        at = slice(i * BLOCK, (i + 1) * BLOCK)
        wait_all(parts[i])
        value = owns[i].astype(f32) + others[i].astype(f32) + xs[i].astype(f32) + bias[2:3]
        both[1, at] = value.astype(bf16)
        hat, _ = center_scale(value)
        both[0, at] = (hat * gain[1:2] + shift[1:2]).astype(bf16)


def call_middle(ids, own, other, x_own, bias, gain, shift):
    return call(
        middle_kernel,
        out_shape=shape(2, HALF, 1024),
        in_specs=[SMEM, HBM, FREE, HBM, HBM] + [VMEM] * 3,
        out_specs=KEEP,
        scratch_shapes=[pltpu.VMEM((2, BLOCK, 1024), bf16)] * 3 + [pltpu.SemaphoreType.DMA((6,))],
        compiler_params=params(40),
        name="middle",
    )(ids, own, other, *x_own, bias, gain, shift)


def start_grads(go, ids, g_own, g_other, gs):
    core, z = ids[0], ids[1]
    return [
        go.start(ref, gs.at[2 * side + parity(z, k)])
        for side, pair in ((core, g_own), (1 - core, g_other))
        for k, ref in enumerate(pair)
    ]


def hidden_kernel(
    ids, n_own, n_other, w0, w1, w2, w3t, w3b, bias, piece, acts, slopes, ws, result, wo, sems
):
    core, chip = ids[0], ids[2]
    go = Copies(sems)
    weights = []
    for p in range(4):
        for r, ref in enumerate((w0, w1, w2, (w3t, w3b))):
            part = ref.at[p] if r < 3 else ref[p // 2].at[p % 2]
            weights += start_sides(go, part, ws.at[p], chip ^ r, core, p)
    later = go.start(piece, wo)
    tokens = [
        (ref, slice(h * BLOCK, (h + 1) * BLOCK), rows(2 * side + h, BLOCK))
        for ref, side in ((n_own, core), (n_other, 1 - core))
        for h in range(2)
    ]

    def finish(p, at, h):
        square = h * h
        lift = 0.5 + 0.5 * jnp.tanh(h * (GELU_A + (GELU_A * GELU_B) * square))
        act = h * lift
        acts[p, at] = act.astype(bf16)
        rise = 2.0 * GELU_A + (6.0 * GELU_A * GELU_B) * square
        slopes[p, at] = (lift + (act - act * lift) * rise).astype(bf16)

    before = None
    for p in range(4):
        wait_all([copy for at, copy in weights if at == p])
        shift = bias[pl.ds(2 * p + core, 1)]
        for ref, here, at in tokens:
            h = nn(ref[0, here], ws[p]) + shift
            if before is not None:
                finish(*before)
            before = (p, at, h)
    finish(*before)
    later.wait()
    for i in range(4):
        tok = slice(i * BLOCK, (i + 1) * BLOCK)
        result[tok] = nn(acts[chip, tok], wo[...]).astype(bf16)


def call_hidden(ids, n_own, n_other, pieces, bias, piece):
    return call(
        hidden_kernel,
        out_shape=(shape(4, 1024, HALF),) * 3 + (shape(1024, 1024),),
        in_specs=[SMEM] + [KEEP] * 2 + [HBM] * 5 + [VMEM, HBM],
        out_specs=(KEEP,) * 4,
        scratch_shapes=[
            pltpu.VMEM((HALF, 1024), bf16),
            pltpu.SemaphoreType.DMA((33,)),
        ],
        compiler_params=params(26),
        name="hidden",
    )(ids, n_own, n_other, *pieces, bias, piece)


def token_blocks(ids, g_own, g_other):
    core, z = ids[0], ids[1]
    return [
        (ref, rows(2 * side + parity(z, k), BLOCK))
        for side, pair in ((core, g_own), (1 - core, g_other))
        for k, ref in enumerate(pair)
    ]


def feed_kernel(
    ids, g0, g1, g2, g3, acts, slopes, w_ins, own_piece, x_piece, y_piece, old,
    result, grad, own_rows, sems,
):
    chip = ids[2]
    load = Copies(sems).start(own_piece, own_rows)
    for i, (g, tok) in enumerate(token_blocks(ids, (g0, g1), (g2, g3))):
        out_sum, grad_sum = old[tok].astype(f32), None
        for r, piece in ((1, x_piece), (2, y_piece), (0, own_rows)):
            here = chip ^ r
            if i == 0 and r == 0:
                load.wait()
            back = nt(g[...], piece[...])
            if r:
                out_sum += nn(acts[here, tok], piece[...])
            back = (back * slopes[here, tok].astype(f32)).astype(bf16)
            term = nt(back, w_ins[here])
            grad_sum = term if grad_sum is None else grad_sum + term
        result[tok] = out_sum.astype(bf16)
        grad[tok] = grad_sum.astype(bf16)


def call_feed(ids, g_own, g_other, active, slope, w_in, pieces, old):
    return call(
        feed_kernel,
        out_shape=(shape(1024, 1024),) * 2,
        in_specs=[SMEM] + [KEEP] * 7 + [HBM] + [KEEP] * 3,
        out_specs=(KEEP, KEEP),
        scratch_shapes=[pltpu.VMEM((HALF, 1024), bf16), pltpu.SemaphoreType.DMA((1,))],
        compiler_params=params(30),
        name="feed",
    )(ids, *g_own, *g_other, active, slope, w_in, *pieces, old)


def far_grad_kernel(ids, g0, g1, g2, g3, slopes, w_ins, top, low, old, out):
    far = ids[2] ^ 3
    for g, tok in token_blocks(ids, (g0, g1), (g2, g3)):
        back = jnp.concatenate([nt(g[...], top[...]), nt(g[...], low[...])], axis=1)
        back = back * slopes[far, tok].astype(f32)
        more = nt(back.astype(bf16), w_ins[far])
        out[tok] = (more + old[tok].astype(f32)).astype(bf16)


def call_far_grad(ids, g_own, g_other, slope, w_in, far, old):
    return call(
        far_grad_kernel,
        out_shape=shape(1024, 1024),
        in_specs=[SMEM] + [KEEP] * 9,
        out_specs=KEEP,
        compiler_params=params(26),
        name="far_grad",
    )(ids, *g_own, *g_other, slope, w_in, *far, old)


def far_result_kernel(ids, acts, top, low, old, own, send):
    core, far = ids[0], ids[2] ^ 3
    for side, values in ((1 - core, send), (core, own)):
        for i in range(2):
            at = rows(2 * side + i, BLOCK)
            tok = slice(i * BLOCK, (i + 1) * BLOCK)
            more = nn(acts[far, at, :BLOCK], top[...]) + nn(acts[far, at, BLOCK:], low[...])
            values[tok] = (old[at].astype(f32) + more).astype(bf16)


def call_far_result(ids, active, far, old):
    return call(
        far_result_kernel,
        out_shape=(shape(HALF, 1024), shape(HALF, 1024)),
        in_specs=[SMEM] + [KEEP] * 4,
        out_specs=(KEEP, KEEP),
        compiler_params=params(16),
        name="far_result",
    )(ids, active, *far, old)


def mixed_kernel(ids, own, other, middle, bias, out0, out1):
    z = ids[1]
    for k, out in enumerate((out0, out1)):
        tok = rows(parity(z, k), BLOCK)
        value = own[tok].astype(f32) + other[tok].astype(f32) + middle[1, tok].astype(f32)
        out[...] = (value + bias[3:4]).astype(bf16)


def call_mixed(ids, own, other, middle, bias):
    return call(
        mixed_kernel,
        out_shape=(shape(BLOCK, 1024),) * 2,
        in_specs=[SMEM, KEEP, KEEP, KEEP, VMEM],
        out_specs=(KEEP, KEEP),
        compiler_params=params(12),
        name="mixed",
    )(ids, own, other, middle, bias)


def input_grad_kernel(ids, x0, x1, own, other, grad_middle, gain, out0, out1):
    z = ids[1]
    for k, (x, out) in enumerate(((x0, out0), (x1, out1))):
        for h in range(2):
            tok = rows(2 * parity(z, k) + h, 128)
            here = slice(128 * h, 128 * (h + 1))
            grad = (own[tok].astype(f32) + other[tok].astype(f32)) * gain[0:1]
            hat, inverse = center_scale(x[here].astype(f32))
            out[here] = (grad_middle[tok].astype(f32) + norm_back(hat, inverse, grad)).astype(bf16)


def call_input_grad(ids, x_own, own, other, grad_middle, gain):
    return call(
        input_grad_kernel,
        out_shape=(shape(BLOCK, 1024),) * 2,
        in_specs=[SMEM, KEEP, KEEP, KEEP, KEEP, KEEP, VMEM],
        out_specs=(KEEP, KEEP),
        compiler_params=params(16),
        name="input_grad",
    )(ids, *x_own, own, other, grad_middle, gain)


def to_core(value):
    return lax.ppermute(value, "core", SWAP)


def total_over(value, axis, *others):
    flip = [lax.ppermute(value, axis, [(i, i ^ by) for i in range(4)]) for by in (1, 2, 3)]
    flip = after(flip, *others)
    return (value + flip[0]) + (flip[1] + flip[2])


def exchange(z, pair):
    sent = []
    for k in range(2):
        perm = [
            (4 * core + at, 4 * (at // 2) + 2 * core + (at + k) % 2)
            for core in range(2)
            for at in range(4)
        ]
        sent.append(lax.ppermute(pair[k], ("core", "seq"), perm))
    return sent


def pick_kernel(ids, value, out0, out1, sems):
    z = ids[1]
    go = Copies(sems)
    wait_all([go.start(value.at[parity(z, k)], out) for k, out in enumerate((out0, out1))])


def call_pick(ids, value):
    return call(
        pick_kernel,
        out_shape=(shape(BLOCK, 1024),) * 2,
        in_specs=[SMEM, HBM],
        out_specs=(KEEP, KEEP),
        scratch_shapes=[pltpu.SemaphoreType.DMA((2,))],
        compiler_params=params(PICK),
        name="pick",
    )(ids, value)


def place_kernel(ids, first, second, out, sems):
    z = ids[1]
    go = Copies(sems)
    wait_all([go.start(ref, out.at[parity(z, k)]) for k, ref in enumerate((first, second))])


def call_place(ids, pair):
    return call(
        place_kernel,
        out_shape=shape(2, BLOCK, 1024),
        in_specs=[SMEM, KEEP, KEEP],
        out_specs=HBM,
        scratch_shapes=[pltpu.SemaphoreType.DMA((2,))],
        compiler_params=params(PICK),
        name="place",
    )(ids, *pair)


def after(value, *others):
    return lax.optimization_barrier((value, *others))[0]


def gather_near(shard):
    return [shard, lax.ppermute(shard, "x", SWAP), lax.ppermute(shard, "y", SWAP)]


def halves(near, first=False):
    if near[1].shape[0] == 4 and not first:
        return call_halves(near[1], near[2])
    half = near[1].shape[0] // 2
    return call(
        split_kernel,
        out_shape=(shape(half, *near[1].shape[1:]),) * 2,
        in_specs=[KEEP, KEEP],
        out_specs=(KEEP, KEEP),
        compiler_params=params(8),
        name="split",
    )(near[1], near[2])


def split_kernel(by_x, by_y, first, second):
    half = first.shape[0]
    first[...] = by_x[:half]
    second[...] = by_y[half:]


def halves_kernel(by_x, by_y, first, second, held, sems):
    half = first.shape[0]
    go = Copies(sems)
    loads = [go.start(by_x.at[:half], held.at[0]), go.start(by_y.at[half:], held.at[1])]
    leave = []
    for at, out in enumerate((first, second)):
        loads[at].wait()
        leave.append(go.start(held.at[at], out))
    wait_all(leave)


def call_halves(by_x, by_y):
    dims = (by_x.shape[0] // 2, *by_x.shape[1:])
    return call(
        halves_kernel,
        out_shape=(shape(*dims), shape(*dims)),
        in_specs=[FREE, FREE],
        out_specs=(HBM, HBM),
        scratch_shapes=[pltpu.VMEM((2, *dims), bf16), pltpu.SemaphoreType.DMA((4,))],
        compiler_params=params(8),
        name="halves",
    )(by_x, by_y)


def gather_far(near, parts):
    return near + [lax.ppermute(parts[0], "y", SWAP), lax.ppermute(parts[1], "x", SWAP)]


def on_chip(
    inputs,
    out_grad,
    norm_gain,
    norm_bias,
    proj_bias,
    fc_bias,
    qkv_weight,
    out_weight,
    feed_input_weight,
    proj_weight,
    adapters,
    first_moment,
    second_moment,
):
    width = inputs.shape[2]
    core = lax.axis_index("core")
    z = lax.axis_index("seq")
    chip = 2 * lax.axis_index("y") + lax.axis_index("x")
    ids = jnp.stack([core, z, chip]).astype(jnp.int32)

    qkv_own, qkv_send, out_part = call_cut(qkv_weight, out_weight)
    qkv_got = to_core(qkv_send)
    first_shard = call(
        join_kernel,
        out_shape=shape(4, BLOCK, HALF),
        in_specs=[KEEP] * 3,
        out_specs=KEEP,
        compiler_params=params(12),
        name="join",
    )(qkv_own, qkv_got, out_part)
    first_near = gather_near(first_shard)
    x_own = exchange(z, call_pick(ids, after(inputs, first_shard)))
    in_own, in_send = call_cut_feed(ids, after(feed_input_weight, first_shard))
    in_shard = jnp.concatenate([in_own, to_core(in_send)], axis=1)

    def columns(value):
        lead = value.shape[0]
        value = value.reshape(lead, 4, 2, 128)
        return jnp.where(core == 0, value[:, :, 0], value[:, :, 1]).reshape(lead, HALF)

    scale = adapter_alpha / ADAPTER_RANK
    adapters, proj_bias = after((adapters, proj_bias), first_shard)
    up_q, up_v = scale * columns(adapters[1]), scale * columns(adapters[3])
    up_w = jnp.zeros((128, 1536), f32)
    up_w = up_w.at[0:4, :HALF].set(up_q).at[4:8, 2 * HALF :].set(up_v).astype(bf16)
    down_w = jnp.concatenate([adapters[0], adapters[2], jnp.zeros((120, 1024), f32)], axis=0)
    down_w = down_w.astype(bf16)
    head_bias = columns(proj_bias[:2])
    qkv_bias = jnp.concatenate([head_bias[0], jnp.zeros((HALF,), f32), head_bias[1]])[None]

    first_near = after(first_near, up_w, down_w, qkv_bias, in_shard)
    first_halves = halves(first_near, True)
    first_pieces = gather_far(first_near, first_halves)
    x_own = after(x_own, *first_halves)
    x_other = to_core(jnp.stack(x_own))
    in_near = gather_near(after(in_shard, *first_pieces[3:]))
    q, k, v, n_all, down, w_qkv, w_o, ctx, stat, attn_own, attn_send = call_first(
        ids, x_own, x_other, first_pieces, norm_gain, norm_bias, down_w, up_w, qkv_bias
    )
    in_near = after(in_near, ctx)
    in_halves = halves(in_near)
    in_pieces = gather_far(in_near, in_halves)
    attn_other = to_core(after(attn_send, *in_halves))
    n2_own = call_middle(
        ids, attn_own, after(attn_other, *in_halves), x_own, proj_bias, norm_gain, norm_bias
    )
    g_pair = call_pick(ids, after(out_grad, n2_own))
    in_pieces[3:] = after(in_pieces[3:], *g_pair)
    g_own = exchange(z, g_pair)
    proj_near = gather_near(after(proj_weight, *in_pieces[3:]))
    n2_other = to_core(after(n2_own, *in_pieces[3:]))
    active, slope, w_in, old = call_hidden(
        ids, n2_own, n2_other, in_pieces, fc_bias.reshape(8, HALF), proj_near[0]
    )
    proj_near = after(proj_near, old)
    proj_halves = halves(proj_near)
    far = gather_far(proj_near, proj_halves)[3:]
    near = after(proj_near, *proj_halves)
    g_own = after(g_own, *proj_halves)
    g_other = [to_core(part) for part in g_own]
    result, grad = call_feed(ids, g_own, g_other, active, slope, w_in, near, old)
    result_own, result_send = call_far_result(ids, active, far, result)
    result_other = to_core(result_send)
    part = call_far_grad(ids, g_own, g_other, slope, w_in, after(far, result_own), grad)
    part = after(part, result_other)
    part_other = to_core(part)
    mixed = call_mixed(ids, result_own, after(result_other, part), n2_own, proj_bias)
    part_other = after(part_other, *mixed)
    mixed = exchange(z, mixed)
    own, send, grad_middle, total = call_attention_back(
        ids, q, k, v, ctx, stat, w_o, part, part_other, g_own, g_other, n2_own, n2_other,
        w_qkv, n_all, down, norm_gain, down_w, up_w,
    )
    other = to_core(after(send, *mixed))
    grad_in = call_input_grad(ids, x_own, own, other, grad_middle, norm_gain)
    total = total_over(total, "seq", *grad_in)
    grad_in = exchange(z, grad_in)
    total = total + to_core(total)
    total = total_over(total, ("y", "x"))
    mixed = call_place(ids, after(mixed, total))
    total = after(total, grad_in[0]).reshape(4, ADAPTER_RANK, width)
    grad_norm = jnp.sqrt(jnp.sum(total * total))
    clipped, new_weight, new_first, new_second = adam_update(
        total, adapters, first_moment, second_moment, grad_norm
    )
    grad_input = call_place(ids, after(grad_in, mixed, new_weight))
    return (mixed, grad_input, clipped, grad_norm, new_weight, new_first, new_second)


def solution(mesh):
    sizes = dict(mesh.shape)
    if sizes["dp"] == 8 and sizes["seq"] == 4:
        plane = Mesh(mesh.devices.reshape(2, 2, 2, 4), ("y", "x", "core", "seq"))
        return build(plane, ("y", "x", "core"), on_chip)
    return build(mesh, "dp", on_device)


def build(mesh, dp, step):
    tokens, weight = P(dp, "seq", None), P(dp, None)
    return jax.shard_map(
        step,
        mesh=mesh,
        in_specs=(tokens, tokens) + (P(),) * 4 + (weight,) * 4 + (P(),) * 3,
        out_specs=(tokens, tokens) + (P(),) * 5,
        check_vma=False,
    )
```

```python
import functools
import math

import jax
import jax.numpy as jnp
from jax import lax
from jax.experimental import pallas as pl
from jax.experimental.pallas import tpu as pltpu
from jax.sharding import Mesh
from jax.sharding import PartitionSpec as P

HEAD_DIM = 64
ADAPTER_RANK = 4
STEP = 10


highest = lax.Precision.HIGHEST
adapter_alpha = 32.0
beta_one = 0.9
beta_two = 0.999
adam_eps = 1e-08
decay_rate = 0.01
learning_rate = 0.02
clip_bound = 1.0
norm_eps = 1e-05


def layer_norm(value, gain, shift):
    center = jnp.mean(value, axis=-1, keepdims=True)
    centered = value - center
    spread = jnp.mean(centered * centered, axis=-1, keepdims=True)
    return centered * lax.rsqrt(spread + norm_eps) * gain + shift


def dot_trans(left, right):
    return lax.dot_general(
        left, right, (((1,), (1,)), ((), ())), preferred_element_type=jnp.float32
    )


def dot_first(left, right):
    return lax.dot_general(
        left, right, (((0,), (0,)), ((), ())), precision=highest, preferred_element_type=jnp.float32
    )


def adam_update(grad, weight, first, second, norm):
    scale_factor = clip_bound / jnp.maximum(norm, clip_bound)
    clipped = grad * scale_factor
    new_first = beta_one * first + (1.0 - beta_one) * clipped
    new_second = beta_two * second + (1.0 - beta_two) * clipped * clipped
    first_hat = new_first / (1.0 - beta_one**STEP)
    second_hat = new_second / (1.0 - beta_two**STEP)
    new_weight = weight - learning_rate * (
        first_hat / (jnp.sqrt(second_hat) + adam_eps) + decay_rate * weight
    )
    return (clipped, new_weight, new_first, new_second)


def split_heads(packed):
    length = packed.shape[0]
    local_heads = packed.shape[-1] // HEAD_DIM
    query = packed[:, 0, 0].reshape(length, local_heads, HEAD_DIM)
    keys = packed[:, 1, 0].reshape(length, local_heads, HEAD_DIM)
    values = packed[:, 2, 0].reshape(length, local_heads, HEAD_DIM)
    return (query, keys, values)


def doc_forward(packed):
    length = packed.shape[0]
    local_width = packed.shape[-1]
    query, keys, values = split_heads(packed)
    local_heads = query.shape[1]
    span = min(512, length)
    blocks = length // span
    scale = 1.0 / math.sqrt(HEAD_DIM)
    starts = jnp.arange(blocks, dtype=jnp.int32) * span

    def visit(pieces):
        query_block, start = pieces
        scores = (
            jnp.einsum("qhd,khd->hqk", query_block, keys, preferred_element_type=jnp.float32)
            * scale
        )
        causal = (start + jnp.arange(span))[:, None] >= jnp.arange(length)[None, :]
        masked = jnp.where(causal[None], scores, -1e30)
        summit = jnp.max(masked, axis=-1, keepdims=True)
        expo = jnp.where(causal[None], jnp.exp(masked - summit), 0.0)
        totals = jnp.sum(expo, axis=-1, keepdims=True)
        weights = (expo / totals).astype(jnp.bfloat16)
        context = jnp.einsum(
            "hqk,khd->qhd", weights, values, preferred_element_type=jnp.float32
        ).astype(jnp.bfloat16)
        return (context, summit[..., 0] + jnp.log(totals[..., 0]))

    context, log_total = lax.map(
        visit, (query.reshape(blocks, span, local_heads, HEAD_DIM), starts)
    )
    return (context.reshape(length, 1, local_width), log_total)


def doc_backward(args):
    packed, grad_context, log_total = args
    length = packed.shape[0]
    local_width = packed.shape[-1]
    query, keys, values = split_heads(packed)
    local_heads = query.shape[1]
    output_gradient = grad_context[:, 0].reshape(length, local_heads, HEAD_DIM)
    span = min(512, length)
    blocks = length // span
    scale = 1.0 / math.sqrt(HEAD_DIM)
    starts = jnp.arange(blocks, dtype=jnp.int32) * span

    def visit(carry, pieces):
        grad_keys, grad_values = carry
        query_block, grad_block, total_block, start = pieces
        scores = (
            jnp.einsum("qhd,khd->hqk", query_block, keys, preferred_element_type=jnp.float32)
            * scale
        )
        causal = (start + jnp.arange(span))[:, None] >= jnp.arange(length)[None, :]
        masked = jnp.where(causal[None], scores, -1e30)
        probs = jnp.where(causal[None], jnp.exp(masked - total_block[:, :, None]), 0.0)
        weights = probs.astype(jnp.bfloat16)
        grad_probs = jnp.einsum(
            "qhd,khd->hqk", grad_block, values, preferred_element_type=jnp.float32
        )
        inner = jnp.sum(probs * grad_probs, axis=-1, keepdims=True)
        grad_scores = (probs * (grad_probs - inner)).astype(jnp.bfloat16)
        grad_query = (
            jnp.einsum("hqk,khd->qhd", grad_scores, keys, preferred_element_type=jnp.float32)
            * scale
        )
        grad_keys = (
            grad_keys
            + jnp.einsum(
                "hqk,qhd->khd", grad_scores, query_block, preferred_element_type=jnp.float32
            )
            * scale
        )
        grad_values = grad_values + jnp.einsum(
            "hqk,qhd->khd", weights, grad_block, preferred_element_type=jnp.float32
        )
        return ((grad_keys, grad_values), grad_query)

    empty = jnp.zeros((length, local_heads, HEAD_DIM), jnp.float32)
    pieces = (
        query.reshape(blocks, span, local_heads, HEAD_DIM),
        output_gradient.reshape(blocks, span, local_heads, HEAD_DIM),
        log_total,
        starts,
    )
    (grad_keys, grad_values), grad_query = lax.scan(visit, (empty, empty), pieces)
    joined = jnp.stack(
        [
            grad_query.reshape(length, local_width),
            grad_keys.reshape(length, local_width),
            grad_values.reshape(length, local_width),
        ],
        axis=1,
    )
    return joined.astype(jnp.bfloat16)[:, :, None, :]


def on_device(
    inputs,
    out_grad,
    norm_gain,
    norm_bias,
    proj_bias,
    fc_bias,
    qkv_weight,
    out_weight,
    feed_input_weight,
    proj_weight,
    adapters,
    first_moment,
    second_moment,
):
    docs, tokens, width = inputs.shape
    count = docs * tokens
    ranks = lax.axis_size("seq")
    scale_factor = adapter_alpha / ADAPTER_RANK

    def forward(stack):
        qkv_full, out_full, fc_full, proj_full = stack
        flat = inputs.reshape(count, width).astype(jnp.float32)
        normed, norm_one_back = jax.vjp(
            lambda value: layer_norm(value, norm_gain[0], norm_bias[0]), flat
        )
        base = jnp.dot(normed.astype(jnp.bfloat16), qkv_full, preferred_element_type=jnp.float32)
        down_q = jnp.dot(normed, adapters[0].T, precision=highest)
        down_v = jnp.dot(normed, adapters[2].T, precision=highest)
        query = (
            base[:, :width]
            + proj_bias[0]
            + scale_factor * jnp.dot(down_q, adapters[1], precision=highest)
        )
        keys = base[:, width : 2 * width]
        values = (
            base[:, 2 * width :]
            + proj_bias[1]
            + scale_factor * jnp.dot(down_v, adapters[3], precision=highest)
        )
        joined = (
            jnp.concatenate([query, keys, values], axis=1)
            .astype(jnp.bfloat16)
            .reshape(docs, tokens, 3, ranks, width // ranks)
        )
        spread = lax.all_to_all(joined, "seq", split_axis=3, concat_axis=1, tiled=True)
        context, log_total = lax.map(doc_forward, spread)
        context = lax.all_to_all(context, "seq", split_axis=1, concat_axis=2, tiled=True).reshape(
            count, width
        )
        middle = (
            flat + jnp.dot(context, out_full, preferred_element_type=jnp.float32) + proj_bias[2]
        )
        normed_two, norm_two_back = jax.vjp(
            lambda value: layer_norm(value, norm_gain[1], norm_bias[1]), middle
        )
        hidden = (
            jnp.dot(normed_two.astype(jnp.bfloat16), fc_full, preferred_element_type=jnp.float32)
            + fc_bias
        )
        active, gelu_back = jax.vjp(lambda value: jax.nn.gelu(value, approximate=True), hidden)
        result = (
            middle
            + jnp.dot(active.astype(jnp.bfloat16), proj_full, preferred_element_type=jnp.float32)
            + proj_bias[3]
        )
        return (
            result,
            (normed, down_q, down_v, norm_one_back, spread, log_total, norm_two_back, gelu_back),
        )

    stack = (
        lax.all_gather(qkv_weight, "dp", axis=0, tiled=True),
        lax.all_gather(out_weight, "dp", axis=0, tiled=True),
        lax.all_gather(feed_input_weight, "dp", axis=0, tiled=True),
        lax.all_gather(proj_weight, "dp", axis=0, tiled=True),
    )
    result, kept = forward(stack)
    fenced = lax.optimization_barrier((stack, result))
    stack = fenced[0]
    again, kept = forward(stack)
    qkv_full, out_full, fc_full, proj_full = stack
    normed, down_q, down_v, norm_one_back, spread, log_total, norm_two_back, gelu_back = kept
    cotangent = out_grad.reshape(count, width)
    grad_active = dot_trans(cotangent, proj_full)
    grad_hidden = gelu_back(grad_active)[0].astype(jnp.bfloat16)
    grad_normed_two = dot_trans(grad_hidden, fc_full)
    grad_middle = cotangent.astype(jnp.float32) + norm_two_back(grad_normed_two)[0]
    grad_context = dot_trans(grad_middle.astype(jnp.bfloat16), out_full).astype(jnp.bfloat16)
    grad_context = grad_context.reshape(docs, tokens, ranks, width // ranks)
    grad_context = lax.all_to_all(grad_context, "seq", split_axis=2, concat_axis=1, tiled=True)
    grad_joined = lax.map(doc_backward, (spread, grad_context, log_total))
    grad_joined = lax.all_to_all(
        grad_joined, "seq", split_axis=1, concat_axis=3, tiled=True
    ).reshape(count, 3 * width)
    grad_normed = dot_trans(grad_joined, qkv_full)
    grad_query = grad_joined[:, :width].astype(jnp.float32)
    grad_value = grad_joined[:, 2 * width :].astype(jnp.float32)
    tilt_q = scale_factor * jnp.dot(grad_query, adapters[1].T, precision=highest)
    value_adapter_up = scale_factor * jnp.dot(grad_value, adapters[3].T, precision=highest)
    grad_normed = (
        grad_normed
        + jnp.dot(tilt_q, adapters[0], precision=highest)
        + jnp.dot(value_adapter_up, adapters[2], precision=highest)
    )
    grad_input = (
        (grad_middle + norm_one_back(grad_normed)[0])
        .astype(jnp.bfloat16)
        .reshape(docs, tokens, width)
    )
    partial_terms = jnp.stack(
        [
            dot_first(tilt_q, normed),
            scale_factor * dot_first(down_q, grad_query),
            dot_first(value_adapter_up, normed),
            scale_factor * dot_first(down_v, grad_value),
        ]
    )
    total = lax.psum(partial_terms, ("dp", "seq"))
    grad_norm = jnp.sqrt(jnp.sum(total * total))
    clipped, new_weight, new_first, new_second = adam_update(
        total, adapters, first_moment, second_moment, grad_norm
    )
    mixed = result.astype(jnp.bfloat16).reshape(docs, tokens, width)
    return (mixed, grad_input, clipped, grad_norm, new_weight, new_first, new_second)


HALF = 512
BLOCK = 256
PICK = 20
SMEM = pl.BlockSpec(memory_space=pltpu.SMEM)
VMEM = pl.BlockSpec(memory_space=pltpu.VMEM)
HBM = pl.BlockSpec(memory_space=pltpu.HBM)
FREE = pl.BlockSpec(memory_space=pl.ANY)
KEEP = pl.BlockSpec(memory_space=pltpu.VMEM)
f32 = jnp.float32
bf16 = jnp.bfloat16
SWAP = ((0, 1), (1, 0))
GELU_A = math.sqrt(2.0 / math.pi)
GELU_B = 0.044715


def nn(left, right):
    return lax.dot_general(left, right, (((1,), (0,)), ((), ())), preferred_element_type=f32)


def nt(left, right):
    return lax.dot_general(left, right, (((1,), (1,)), ((), ())), preferred_element_type=f32)


def tn(left, right):
    return lax.dot_general(left, right, (((0,), (0,)), ((), ())), preferred_element_type=f32)


def shape(*dims, dtype=bf16):
    return jax.ShapeDtypeStruct(dims, dtype)


def params(mib):
    return pltpu.CompilerParams(vmem_limit_bytes=mib * 2**20)


def call(kernel, *, out_shape, in_specs, out_specs, **options):
    spaces = {id(HBM): pltpu.HBM, id(KEEP): pltpu.VMEM}
    single = not isinstance(out_shape, tuple)
    shapes, specs = ((out_shape,), (out_specs,)) if single else (out_shape, out_specs)
    shapes = tuple(
        spaces[id(spec)](each.shape, each.dtype) if id(spec) in spaces else each
        for each, spec in zip(shapes, specs, strict=True)
    )

    def run(*values):
        values = [
            pltpu.with_memory_space_constraint(value, spaces[id(spec)]) if id(spec) in spaces else value
            for value, spec in zip(values, in_specs, strict=True)
        ]
        return pl.pallas_call(
            kernel,
            out_shape=shapes[0] if single else shapes,
            in_specs=in_specs,
            out_specs=out_specs,
            **options,
        )(*values)

    return run


def rows(index, size):
    return pl.ds(pl.multiple_of(index * size, size), size)


def parity(z, k):
    return lax.rem(z + k, 2)


class Copies:
    def __init__(self, sems):
        self.sems = sems
        self.count = 0

    def start(self, source, target):
        copy = pltpu.make_async_copy(source, target, self.sems.at[self.count])
        self.count += 1
        copy.start()
        return copy


def wait_all(copies):
    for copy in copies:
        copy.wait()


def center_scale(x):
    center = jnp.mean(x, axis=-1, keepdims=True)
    centered = x - center
    spread = jnp.mean(centered * centered, axis=-1, keepdims=True)
    inverse = lax.rsqrt(spread + norm_eps)
    return centered * inverse, inverse


def norm_back(hat, inverse, grad):
    first = jnp.mean(grad, axis=-1, keepdims=True)
    second = jnp.mean(grad * hat, axis=-1, keepdims=True)
    return inverse * (grad - first - hat * second)


def cut_kernel(w, w_o, own, send, out_part):
    core = lax.axis_index("core")
    for p in range(3):
        for i in range(4):
            base = 1024 * p + 256 * i
            to = slice(128 * i, 128 * (i + 1))
            send[p, :, to] = w[:, pl.ds(pl.multiple_of(base + 128 * (1 - core), 128), 128)]
            own[p, :, to] = w[:, pl.ds(pl.multiple_of(base + 128 * core, 128), 128)]
    out_part[0, :128] = w_o[:, :HALF]
    out_part[0, 128:] = w_o[:, HALF:]


def call_cut(w, w_o):
    return call(
        cut_kernel,
        out_shape=(shape(3, 128, HALF), shape(3, 128, HALF), shape(1, BLOCK, HALF)),
        in_specs=[VMEM, VMEM],
        out_specs=(KEEP,) * 3,
        compiler_params=params(12),
        name="cut_qkv",
    )(w, w_o)


def join_kernel(own, got, out_part, shard):
    shard[:3, :128] = own[...]
    shard[:3, 128:] = got[...]
    shard[3:] = out_part[...]


def cut_feed_kernel(ids, w, own, send):
    core = ids[0]
    for i in range(4):
        send[i] = w[:, pl.ds(pl.multiple_of(1024 * i + HALF * (1 - core), HALF), HALF)]
        own[i] = w[:, pl.ds(pl.multiple_of(1024 * i + HALF * core, HALF), HALF)]


def call_cut_feed(ids, w):
    return call(
        cut_feed_kernel,
        out_shape=(shape(4, 128, HALF), shape(4, 128, HALF)),
        in_specs=[SMEM, VMEM],
        out_specs=(VMEM,) * 2,
        compiler_params=params(60),
        name="cut_feed",
    )(ids, w)


def start_sides(go, piece, target, chip, core, tag):
    return [
        (tag, go.start(piece.at[:128], target.at[rows(2 * chip + core, 128)])),
        (tag, go.start(piece.at[128:], target.at[rows(2 * chip + 1 - core, 128)])),
    ]


def attend(pair, qs, ks, vs, ctxs, stats):
    keys = ks[pair]
    values = jnp.concatenate([jnp.transpose(vs[pair]), jnp.ones((128, 1024), bf16)], axis=0)
    for i in range(4):
        ext = (i + 1) * BLOCK
        cols = slice(i * BLOCK, ext)
        query = qs[pair, cols]
        low = low_half(query)
        zero = jnp.zeros_like(query)
        parts = []
        for a in range(2):
            part = jnp.where(low, query, zero) if a == 0 else jnp.where(low, zero, query)
            scores = nt(keys[:ext], part)
            last = scores[i * BLOCK :]
            r = lax.broadcasted_iota(jnp.int32, last.shape, 0)
            c = lax.broadcasted_iota(jnp.int32, last.shape, 1)
            last = jnp.where(r <= c, last, -1e30)
            scores = jnp.concatenate([scores[: i * BLOCK], last], axis=0) if i else last
            top = jnp.max(scores, axis=0, keepdims=True)
            expo = jnp.exp(scores - top).astype(bf16)
            wide = nn(values[:, :ext], expo)
            total = wide[128:129]
            parts.append(wide[64 * a : 64 * a + 64] * (1.0 / total))
            stats[pair, a : a + 1, cols] = top + jnp.log(total)
        ctxs[pair, cols] = jnp.transpose(jnp.concatenate(parts, axis=0).astype(bf16))


def split_down(both):
    down = both + pltpu.roll(both, 120, 1)
    upper = down.astype(bf16).astype(f32)
    lower = down - upper
    lane = lax.broadcasted_iota(jnp.int32, both.shape, 1)
    packed = jnp.where(lane < 8, upper, jnp.where(lane < 16, pltpu.roll(lower, 8, 1), pltpu.roll(upper, 16, 1)))
    return jnp.where(lane < 24, packed, 0.0).astype(bf16)


def fold_kernel(w, down_w, up_w, out, ws, sems):
    go = Copies(sems)
    loads = [go.start(w.at[p], ws.at[p]) for p in range(3)]
    leave = []
    for p in (1, 0, 2):
        loads[p].wait()
        if p != 1:
            for i in range(4):
                at = slice(i * BLOCK, (i + 1) * BLOCK)
                more = tn(down_w[:8, at], up_w[:8, p * HALF : (p + 1) * HALF])
                ws[p, at] = (ws[p, at].astype(f32) + more).astype(bf16)
        leave.append(go.start(ws.at[p], out.at[p]))
    wait_all(leave)


def call_fold(w, down_w, up_w):
    return call(
        fold_kernel,
        out_shape=shape(3, 1024, HALF),
        in_specs=[HBM, VMEM, VMEM],
        out_specs=HBM,
        scratch_shapes=[pltpu.VMEM((3, 1024, HALF), bf16), pltpu.SemaphoreType.DMA((6,))],
        compiler_params=params(16),
        name="fold",
    )(w, down_w, up_w)


def first_kernel(
    ids, m0, m1, others, w0, w1, w2, w3t, w3b, gain, shift, down_w, up_w, bias,
    q_out, k_out, v_out, n_out, down_out, w_out, o_out, ctx_out, stat_out, own, send,
    ns, rest, ws, os, qs, ks, vs, downs, ctxs, stats, owns, sends, sems,
):
    core, chip = ids[0], ids[2]
    go = Copies(sems)
    weights, outer, leave = [], [], []
    pieces = (w0, w1, w2, (w3t, w3b))
    part = lambda r, p: pieces[r].at[p] if r < 3 else pieces[r][p // 2].at[p % 2]
    for p in range(3):
        for r in range(4):
            weights += start_sides(go, part(r, p), ws.at[p], chip ^ r, core, p)
    for r in range(4):
        for h in range(2):
            outer.append(
                go.start(
                    part(r, 3).at[h * 128 : (h + 1) * 128],
                    os.at[rows(chip ^ r, 128), h * HALF : (h + 1) * HALF],
                )
            )
    for x, at in token_blocks(ids, (m0, m1), (others.at[0], others.at[1])):
        hat, _ = center_scale(x[...].astype(f32))
        value = hat * gain[0:1] + shift[0:1]
        upper = value.astype(bf16)
        ns[at] = upper
        rest[at] = (value - upper.astype(f32)).astype(bf16)
    leave.append(go.start(ns, n_out))
    for p, (to, out) in enumerate(((qs, q_out), (ks, k_out), (vs, v_out))):
        wait_all([copy for at, copy in weights if at == p])
        leave.append(go.start(ws.at[p], w_out.at[p]))
        for i in range(4):
            at = slice(i * BLOCK, (i + 1) * BLOCK)
            value = nn(ns[at], ws[p]) + bias[:, p * HALF : (p + 1) * HALF]
            if p == 0:
                down = split_down(nt(ns[at], down_w[...]) + nt(rest[at], down_w[...]))
                downs[at] = down
                down_out[:, at] = jnp.transpose(down)[:16]
            if p != 1:
                value += nn(downs[at], up_w[:, p * HALF : (p + 1) * HALF])
            value = value.astype(bf16)
            if p == 0:
                value = value * jnp.asarray(0.125, bf16)
            for pair in range(4):
                to[pair, at] = value[:, 128 * pair : 128 * (pair + 1)]
        leave.append(go.start(to, out))

    @pl.loop(0, 4)
    def _(pair):
        attend(pair, qs, ks, vs, ctxs, stats)

    leave.append(go.start(ctxs, ctx_out))
    leave.append(go.start(stats, stat_out))
    wait_all(outer)
    leave.append(go.start(os, o_out))
    for side, to, out in ((1 - core, sends, send), (core, owns, own)):
        for i in range(2):
            at = rows(2 * side + i, BLOCK)
            tok = slice(i * BLOCK, (i + 1) * BLOCK)
            whole = jnp.concatenate([ctxs[p, at] for p in range(4)], axis=1)
            to[tok] = nn(whole, os[...]).astype(to.dtype)
            leave.append(go.start(to.at[tok], out.at[tok]))
    wait_all(leave)


def call_first(ids, x_own, x_other, pieces, gain, shift, down_w, up_w, bias):
    heads = shape(4, 1024, 128)
    return call(
        first_kernel,
        out_shape=(
            heads,
            heads,
            heads,
            shape(1024, 1024),
            shape(16, 1024),
            shape(3, 1024, HALF),
            shape(HALF, 1024),
            heads,
            shape(4, 8, 1024, dtype=f32),
            shape(HALF, 1024),
            shape(HALF, 1024),
        ),
        in_specs=[SMEM] + [KEEP] * 3 + [FREE] * 5 + [VMEM] * 5,
        out_specs=(HBM,) * 4 + (VMEM,) + (HBM,) * 6,
        scratch_shapes=[
            pltpu.VMEM((1024, 1024), bf16),
            pltpu.VMEM((1024, 1024), bf16),
            pltpu.VMEM((3, 1024, HALF), bf16),
            pltpu.VMEM((HALF, 1024), bf16),
            pltpu.VMEM((4, 1024, 128), bf16),
            pltpu.VMEM((4, 1024, 128), bf16),
            pltpu.VMEM((4, 1024, 128), bf16),
            pltpu.VMEM((1024, 128), bf16),
            pltpu.VMEM((4, 1024, 128), bf16),
            pltpu.VMEM((4, 8, 1024), f32),
            pltpu.VMEM((HALF, 1024), bf16),
            pltpu.VMEM((HALF, 1024), bf16),
            pltpu.SemaphoreType.DMA((53,)),
        ],
        compiler_params=params(44),
        name="qkv_attention",
    )(ids, *x_own, x_other, *pieces, gain, shift, down_w, up_w, bias)


def attend_back(pair, qs, ks, vs, ctxs, stats, gs, dqs, dks, dvs, acc_k, acc_v):
    keys, values = ks[pair], vs[pair]
    place = pl.ds(pl.multiple_of(pair * 128, 128), 128)
    for i in range(4):
        ext = (i + 1) * BLOCK
        cols = slice(i * BLOCK, ext)
        query, grad = qs[pair, cols], gs[pair, cols]
        low = low_half(query)
        zero = jnp.zeros_like(query)
        product = grad.astype(f32) * ctxs[pair, cols].astype(f32)
        stat = jnp.transpose(stats[pair, :, cols])
        turned_query, turned_grad = jnp.transpose(query), jnp.transpose(grad)
        new_q = []
        for a in range(2):
            pick = (lambda x, y: jnp.where(low, x, y)) if a == 0 else (lambda x, y: jnp.where(low, y, x))
            half = slice(64 * a, 64 * a + 64)
            scores = nt(pick(query, zero), keys[:ext])
            probs = jnp.exp(scores - stat[:, a : a + 1])
            last = probs[:, i * BLOCK :]
            r = lax.broadcasted_iota(jnp.int32, last.shape, 0)
            c = lax.broadcasted_iota(jnp.int32, last.shape, 1)
            last = jnp.where(r >= c, last, 0.0)
            probs = jnp.concatenate([probs[:, : i * BLOCK], last], axis=1) if i else last
            inner = jnp.sum(pick(product, 0.0), axis=1, keepdims=True)
            grad_probs = nt(pick(grad, zero), values[:ext])
            grad_scores = (probs * (grad_probs - inner)).astype(bf16)
            more_v = nn(turned_grad[half], probs.astype(bf16))
            more_k = nn(turned_query[half], grad_scores)
            if i:
                acc_v[half, : i * BLOCK] += more_v[:, : i * BLOCK]
                acc_k[half, : i * BLOCK] += more_k[:, : i * BLOCK]
            acc_v[half, cols] = more_v[:, i * BLOCK :]
            acc_k[half, cols] = more_k[:, i * BLOCK :]
            new_q.append(nn(grad_scores, keys[:ext]))
        both = jnp.where(low, new_q[0], new_q[1])
        dqs[cols, place] = (both * 0.125).astype(bf16)
    dks[:, place] = jnp.transpose(acc_k[...].astype(bf16))
    dvs[:, place] = jnp.transpose(acc_v[...].astype(bf16))


def attention_back_kernel(
    ids, q, k_in, v, ctx, stat, w_o, parts, others, g0, g1, g2, g3, mid_own, mid_other, w, n_all, downs,
    gain, down_w, up_w,
    own, send, grad_middle, total,
    os, qs, ks, vs, ctxs, stats, heads, dqs, dks, dvs, acc_k, acc_v,
    ws, ns, tilts, sems,
):
    core, z = ids[0], ids[1]
    go = Copies(sems)
    outer = go.start(w_o, os)
    then = [
        go.start(ref, to)
        for ref, to in ((q, qs), (k_in, ks), (v, vs), (ctx, ctxs), (stat, stats))
    ]
    weights = [go.start(w, ws), go.start(n_all, ns)]
    mids = (mid_own, mid_own, mid_other, mid_other)
    for at, (g, tok) in enumerate(token_blocks(ids, (g0, g1), (g2, g3))):
        here = rows(parity(z, at % 2), BLOCK)
        hat, inverse = center_scale(mids[at][1, here].astype(f32))
        grad = (parts[tok].astype(f32) + others[tok].astype(f32)) * gain[1:2]
        value = (g[...].astype(f32) + norm_back(hat, inverse, grad)).astype(bf16)
        if at < 2:
            grad_middle[here] = value
        if at == 0:
            outer.wait()
        value = nt(value, os[...]).astype(bf16)
        for pair in range(4):
            heads[pair, tok] = value[:, 128 * pair : 128 * (pair + 1)]
    wait_all(then)

    @pl.loop(0, 4)
    def _(pair):
        attend_back(pair, qs, ks, vs, ctxs, stats, heads, dqs, dks, dvs, acc_k, acc_v)

    wait_all(weights)
    for side, values in ((1 - core, send), (core, own)):
        for i in range(2):
            at = rows(2 * side + i, BLOCK)
            tok = slice(i * BLOCK, (i + 1) * BLOCK)
            gq, gk, gv = dqs[at], dks[at], dvs[at]
            value = nt(gq, ws[0]) + nt(gk, ws[1]) + nt(gv, ws[2])
            values[tok] = value.astype(bf16)
    tilts[...] = (nt(up_w[:16, :HALF], dqs[...]) + nt(up_w[:16, 2 * HALF :], dvs[...])).astype(bf16)
    down_terms = nn(tilts[...], ns[...])
    total[...] = jnp.zeros_like(total)
    total[0:4] = down_terms[0:4]
    total[8:12] = down_terms[4:8]
    up_q = 8.0 * nn(downs[...], dqs[...])
    up_v = 8.0 * nn(downs[...], dvs[...])
    for pair in range(4):
        here = pl.ds(pl.multiple_of(256 * pair + 128 * core, 128), 128)
        total[4:8, here] = up_q[0:4, 128 * pair : 128 * (pair + 1)]
        total[12:16, here] = up_v[4:8, 128 * pair : 128 * (pair + 1)]


def call_attention_back(
    ids, q, k, v, ctx, stat, w_o, part, other, g_own, g_other, mid_own, mid_other,
    w, n_all, downs, gain, down_w, up_w,
):
    pairs = pltpu.VMEM((4, 1024, 128), bf16)
    wide = pltpu.VMEM((1024, HALF), bf16)
    return call(
        attention_back_kernel,
        out_shape=(
            shape(HALF, 1024),
            shape(HALF, 1024),
            shape(HALF, 1024),
            shape(16, 1024, dtype=f32),
        ),
        in_specs=[SMEM] + [HBM] * 6 + [KEEP] * 8 + [HBM] * 2 + [VMEM] * 4,
        out_specs=(KEEP, KEEP, KEEP, KEEP),
        scratch_shapes=[
            pltpu.VMEM((HALF, 1024), bf16),
            pairs,
            pairs,
            pairs,
            pairs,
            pltpu.VMEM((4, 8, 1024), f32),
            pairs,
            wide,
            wide,
            wide,
            pltpu.VMEM((128, 1024), f32),
            pltpu.VMEM((128, 1024), f32),
            pltpu.VMEM((3, 1024, HALF), bf16),
            pltpu.VMEM((1024, 1024), bf16),
            pltpu.VMEM((16, 1024), bf16),
            pltpu.SemaphoreType.DMA((8,)),
        ],
        compiler_params=params(36),
        name="attention_back",
    )(
        ids, q, k, v, ctx, stat, w_o, part, other, *g_own, *g_other, mid_own, mid_other,
        w, n_all, downs, gain, down_w, up_w,
    )


def low_half(value):
    return lax.broadcasted_iota(jnp.int32, value.shape, 1) < 64


def start_tokens(go, pair, target, z):
    return [go.start(ref, target.at[parity(z, k)]) for k, ref in enumerate(pair)]


def middle_kernel(
    ids, own, other, x0, x1, bias, gain, shift, both, owns, others, xs, sems
):
    go = Copies(sems)
    tokens = start_tokens(go, (x0, x1), xs, ids[1])
    parts = []
    for i in range(2):
        at = slice(i * BLOCK, (i + 1) * BLOCK)
        parts.append([go.start(own.at[at], owns.at[i]), go.start(other.at[at], others.at[i])])
    wait_all(tokens)
    for i in range(2):
        at = slice(i * BLOCK, (i + 1) * BLOCK)
        wait_all(parts[i])
        value = owns[i].astype(f32) + others[i].astype(f32) + xs[i].astype(f32) + bias[2:3]
        both[1, at] = value.astype(bf16)
        hat, _ = center_scale(value)
        both[0, at] = (hat * gain[1:2] + shift[1:2]).astype(bf16)


def call_middle(ids, own, other, x_own, bias, gain, shift):
    return call(
        middle_kernel,
        out_shape=shape(2, HALF, 1024),
        in_specs=[SMEM, HBM, FREE, HBM, HBM] + [VMEM] * 3,
        out_specs=KEEP,
        scratch_shapes=[pltpu.VMEM((2, BLOCK, 1024), bf16)] * 3 + [pltpu.SemaphoreType.DMA((6,))],
        compiler_params=params(40),
        name="middle",
    )(ids, own, other, *x_own, bias, gain, shift)


def start_grads(go, ids, g_own, g_other, gs):
    core, z = ids[0], ids[1]
    return [
        go.start(ref, gs.at[2 * side + parity(z, k)])
        for side, pair in ((core, g_own), (1 - core, g_other))
        for k, ref in enumerate(pair)
    ]


def hidden_kernel(
    ids, n_own, n_other, w0, w1, w2, w3t, w3b, bias, piece, acts, slopes, ws, result, wo, sems
):
    core, chip = ids[0], ids[2]
    go = Copies(sems)
    weights = []
    for p in range(4):
        for r, ref in enumerate((w0, w1, w2, (w3t, w3b))):
            part = ref.at[p] if r < 3 else ref[p // 2].at[p % 2]
            weights += start_sides(go, part, ws.at[p], chip ^ r, core, p)
    later = go.start(piece, wo)
    tokens = [
        (ref, slice(h * BLOCK, (h + 1) * BLOCK), rows(2 * side + h, BLOCK))
        for ref, side in ((n_own, core), (n_other, 1 - core))
        for h in range(2)
    ]

    def finish(p, at, h):
        square = h * h
        lift = 0.5 + 0.5 * jnp.tanh(h * (GELU_A + (GELU_A * GELU_B) * square))
        act = h * lift
        acts[p, at] = act.astype(bf16)
        rise = 2.0 * GELU_A + (6.0 * GELU_A * GELU_B) * square
        slopes[p, at] = (lift + (act - act * lift) * rise).astype(bf16)

    before = None
    for p in range(4):
        wait_all([copy for at, copy in weights if at == p])
        shift = bias[pl.ds(2 * p + core, 1)]
        for ref, here, at in tokens:
            h = nn(ref[0, here], ws[p]) + shift
            if before is not None:
                finish(*before)
            before = (p, at, h)
    finish(*before)
    later.wait()
    for i in range(4):
        tok = slice(i * BLOCK, (i + 1) * BLOCK)
        result[tok] = nn(acts[chip, tok], wo[...])


def call_hidden(ids, n_own, n_other, pieces, bias, piece):
    return call(
        hidden_kernel,
        out_shape=(shape(4, 1024, HALF),) * 3 + (shape(1024, 1024, dtype=f32),),
        in_specs=[SMEM] + [KEEP] * 2 + [HBM] * 5 + [VMEM, HBM],
        out_specs=(KEEP,) * 4,
        scratch_shapes=[
            pltpu.VMEM((HALF, 1024), bf16),
            pltpu.SemaphoreType.DMA((33,)),
        ],
        compiler_params=params(26),
        name="hidden",
    )(ids, n_own, n_other, *pieces, bias, piece)


def token_blocks(ids, g_own, g_other):
    core, z = ids[0], ids[1]
    return [
        (ref, rows(2 * side + parity(z, k), BLOCK))
        for side, pair in ((core, g_own), (1 - core, g_other))
        for k, ref in enumerate(pair)
    ]


def feed_kernel(
    ids, g0, g1, g2, g3, acts, slopes, w_ins, own_piece, x_piece, y_piece, old,
    result, grad, own_rows, sems,
):
    chip = ids[2]
    load = Copies(sems).start(own_piece, own_rows)
    for i, (g, tok) in enumerate(token_blocks(ids, (g0, g1), (g2, g3))):
        out_sum, grad_sum = old[tok], None
        for r, piece in ((1, x_piece), (2, y_piece), (0, own_rows)):
            here = chip ^ r
            if i == 0 and r == 0:
                load.wait()
            back = nt(g[...], piece[...])
            if r:
                out_sum += nn(acts[here, tok], piece[...])
            back = (back * slopes[here, tok].astype(f32)).astype(bf16)
            term = nt(back, w_ins[here])
            grad_sum = term if grad_sum is None else grad_sum + term
        result[tok] = out_sum
        grad[tok] = grad_sum


def call_feed(ids, g_own, g_other, active, slope, w_in, pieces, old):
    return call(
        feed_kernel,
        out_shape=(shape(1024, 1024, dtype=f32),) * 2,
        in_specs=[SMEM] + [KEEP] * 7 + [HBM] + [KEEP] * 3,
        out_specs=(KEEP, KEEP),
        scratch_shapes=[pltpu.VMEM((HALF, 1024), bf16), pltpu.SemaphoreType.DMA((1,))],
        compiler_params=params(18),
        name="feed",
    )(ids, *g_own, *g_other, active, slope, w_in, *pieces, old)


def far_grad_kernel(ids, g0, g1, g2, g3, slopes, w_ins, top, low, old, out):
    far = ids[2] ^ 3
    for g, tok in token_blocks(ids, (g0, g1), (g2, g3)):
        back = jnp.concatenate([nt(g[...], top[...]), nt(g[...], low[...])], axis=1)
        back = back * slopes[far, tok].astype(f32)
        more = nt(back.astype(bf16), w_ins[far])
        out[tok] = (more + old[tok]).astype(bf16)


def call_far_grad(ids, g_own, g_other, slope, w_in, far, old):
    return call(
        far_grad_kernel,
        out_shape=shape(1024, 1024),
        in_specs=[SMEM] + [KEEP] * 9,
        out_specs=KEEP,
        compiler_params=params(18),
        name="far_grad",
    )(ids, *g_own, *g_other, slope, w_in, *far, old)


def far_result_kernel(ids, acts, top, low, old, own, send):
    core, far = ids[0], ids[2] ^ 3
    for side, values in ((1 - core, send), (core, own)):
        for i in range(2):
            at = rows(2 * side + i, BLOCK)
            tok = slice(i * BLOCK, (i + 1) * BLOCK)
            more = nn(acts[far, at, :BLOCK], top[...]) + nn(acts[far, at, BLOCK:], low[...])
            values[tok] = (old[at] + more).astype(values.dtype)


def call_far_result(ids, active, far, old):
    return call(
        far_result_kernel,
        out_shape=(shape(HALF, 1024, dtype=f32), shape(HALF, 1024)),
        in_specs=[SMEM] + [KEEP] * 4,
        out_specs=(KEEP, KEEP),
        compiler_params=params(16),
        name="far_result",
    )(ids, active, *far, old)


def mixed_kernel(ids, own, other, middle, bias, out0, out1):
    z = ids[1]
    for k, out in enumerate((out0, out1)):
        tok = rows(parity(z, k), BLOCK)
        value = own[tok] + other[tok].astype(f32) + middle[1, tok].astype(f32)
        out[...] = (value + bias[3:4]).astype(bf16)


def call_mixed(ids, own, other, middle, bias):
    return call(
        mixed_kernel,
        out_shape=(shape(BLOCK, 1024),) * 2,
        in_specs=[SMEM, KEEP, KEEP, KEEP, VMEM],
        out_specs=(KEEP, KEEP),
        compiler_params=params(12),
        name="mixed",
    )(ids, own, other, middle, bias)


def input_grad_kernel(ids, x0, x1, own, other, grad_middle, gain, out0, out1):
    z = ids[1]
    for k, (x, out) in enumerate(((x0, out0), (x1, out1))):
        for h in range(2):
            tok = rows(2 * parity(z, k) + h, 128)
            here = slice(128 * h, 128 * (h + 1))
            grad = (own[tok].astype(f32) + other[tok].astype(f32)) * gain[0:1]
            hat, inverse = center_scale(x[here].astype(f32))
            out[here] = (grad_middle[tok].astype(f32) + norm_back(hat, inverse, grad)).astype(bf16)


def call_input_grad(ids, x_own, own, other, grad_middle, gain):
    return call(
        input_grad_kernel,
        out_shape=(shape(BLOCK, 1024),) * 2,
        in_specs=[SMEM, KEEP, KEEP, KEEP, KEEP, KEEP, VMEM],
        out_specs=(KEEP, KEEP),
        compiler_params=params(16),
        name="input_grad",
    )(ids, *x_own, own, other, grad_middle, gain)


def to_core(value):
    return lax.ppermute(value, "core", SWAP)


def total_over(value, axis, *others):
    flip = [lax.ppermute(value, axis, [(i, i ^ by) for i in range(4)]) for by in (1, 2, 3)]
    flip = after(flip, *others)
    return (value + flip[0]) + (flip[1] + flip[2])


def exchange(z, pair):
    sent = []
    for k in range(2):
        perm = [
            (4 * core + at, 4 * (at // 2) + 2 * core + (at + k) % 2)
            for core in range(2)
            for at in range(4)
        ]
        sent.append(lax.ppermute(pair[k], ("core", "seq"), perm))
    return sent


def pick_kernel(ids, value, out0, out1, sems):
    z = ids[1]
    go = Copies(sems)
    wait_all([go.start(value.at[parity(z, k)], out) for k, out in enumerate((out0, out1))])


def call_pick(ids, value):
    return call(
        pick_kernel,
        out_shape=(shape(BLOCK, 1024),) * 2,
        in_specs=[SMEM, HBM],
        out_specs=(KEEP, KEEP),
        scratch_shapes=[pltpu.SemaphoreType.DMA((2,))],
        compiler_params=params(PICK),
        name="pick",
    )(ids, value)


def place_kernel(ids, first, second, out, sems):
    z = ids[1]
    go = Copies(sems)
    wait_all([go.start(ref, out.at[parity(z, k)]) for k, ref in enumerate((first, second))])


def call_place(ids, pair):
    return call(
        place_kernel,
        out_shape=shape(2, BLOCK, 1024),
        in_specs=[SMEM, KEEP, KEEP],
        out_specs=HBM,
        scratch_shapes=[pltpu.SemaphoreType.DMA((2,))],
        compiler_params=params(PICK),
        name="place",
    )(ids, *pair)


def after(value, *others):
    return lax.optimization_barrier((value, *others))[0]


def gather_near(shard):
    return [shard, lax.ppermute(shard, "x", SWAP), lax.ppermute(shard, "y", SWAP)]


def halves(near, first=False):
    if near[1].shape[0] == 4 and not first:
        return call_halves(near[1], near[2])
    half = near[1].shape[0] // 2
    return call(
        split_kernel,
        out_shape=(shape(half, *near[1].shape[1:]),) * 2,
        in_specs=[KEEP, KEEP],
        out_specs=(KEEP, KEEP),
        compiler_params=params(8),
        name="split",
    )(near[1], near[2])


def split_kernel(by_x, by_y, first, second):
    half = first.shape[0]
    first[...] = by_x[:half]
    second[...] = by_y[half:]


def halves_kernel(by_x, by_y, first, second, held, sems):
    half = first.shape[0]
    go = Copies(sems)
    loads = [go.start(by_x.at[:half], held.at[0]), go.start(by_y.at[half:], held.at[1])]
    leave = []
    for at, out in enumerate((first, second)):
        loads[at].wait()
        leave.append(go.start(held.at[at], out))
    wait_all(leave)


def call_halves(by_x, by_y):
    dims = (by_x.shape[0] // 2, *by_x.shape[1:])
    return call(
        halves_kernel,
        out_shape=(shape(*dims), shape(*dims)),
        in_specs=[FREE, FREE],
        out_specs=(HBM, HBM),
        scratch_shapes=[pltpu.VMEM((2, *dims), bf16), pltpu.SemaphoreType.DMA((4,))],
        compiler_params=params(8),
        name="halves",
    )(by_x, by_y)


def gather_far(near, parts):
    return near + [lax.ppermute(parts[0], "y", SWAP), lax.ppermute(parts[1], "x", SWAP)]


def parts_of(value):
    upper = lax.reduce_precision(value, 8, 7)
    return upper.astype(bf16), (value - upper).astype(bf16)


def on_chip(
    inputs,
    out_grad,
    norm_gain,
    norm_bias,
    proj_bias,
    fc_bias,
    qkv_weight,
    out_weight,
    feed_input_weight,
    proj_weight,
    adapters,
    first_moment,
    second_moment,
):
    width = inputs.shape[2]
    core = lax.axis_index("core")
    z = lax.axis_index("seq")
    chip = 2 * lax.axis_index("y") + lax.axis_index("x")
    ids = jnp.stack([core, z, chip]).astype(jnp.int32)

    qkv_own, qkv_send, out_part = call_cut(qkv_weight, out_weight)
    qkv_got = to_core(qkv_send)
    first_shard = call(
        join_kernel,
        out_shape=shape(4, BLOCK, HALF),
        in_specs=[KEEP] * 3,
        out_specs=KEEP,
        compiler_params=params(12),
        name="join",
    )(qkv_own, qkv_got, out_part)
    first_near = gather_near(first_shard)
    x_own = exchange(z, call_pick(ids, after(inputs, first_shard)))
    in_own, in_send = call_cut_feed(ids, after(feed_input_weight, first_shard))
    in_shard = jnp.concatenate([in_own, to_core(in_send)], axis=1)

    def columns(value):
        lead = value.shape[0]
        value = value.reshape(lead, 4, 2, 128)
        return jnp.where(core == 0, value[:, :, 0], value[:, :, 1]).reshape(lead, HALF)

    scale = adapter_alpha / ADAPTER_RANK
    adapters, proj_bias = after((adapters, proj_bias), first_shard)
    up_q, up_v = scale * columns(adapters[1]), scale * columns(adapters[3])
    up = jnp.zeros((8, 1536), f32).at[0:4, :HALF].set(up_q).at[4:8, 2 * HALF :].set(up_v)
    upper, lower = parts_of(up)
    up_w = jnp.concatenate([upper, upper, lower, jnp.zeros((104, 1536), bf16)], axis=0)
    upper, lower = parts_of(jnp.concatenate([adapters[0], adapters[2]], axis=0))
    down_w = jnp.concatenate([upper, lower, jnp.zeros((112, 1024), bf16)], axis=0)
    head_bias = columns(proj_bias[:2])
    qkv_bias = jnp.concatenate([head_bias[0], jnp.zeros((HALF,), f32), head_bias[1]])[None]

    first_near = after(first_near, up_w, down_w, qkv_bias, in_shard)
    first_halves = halves(first_near, True)
    first_pieces = gather_far(first_near, first_halves)
    x_own = after(x_own, *first_halves)
    x_other = to_core(jnp.stack(x_own))
    in_near = gather_near(after(in_shard, *first_pieces[3:]))
    q, k, v, n_all, down, w_qkv, w_o, ctx, stat, attn_own, attn_send = call_first(
        ids, x_own, x_other, first_pieces, norm_gain, norm_bias, down_w, up_w, qkv_bias
    )
    in_near = after(in_near, ctx)
    in_halves = halves(in_near)
    in_pieces = gather_far(in_near, in_halves)
    attn_other = to_core(after(attn_send, *in_halves))
    n2_own = call_middle(
        ids, attn_own, after(attn_other, *in_halves), x_own, proj_bias, norm_gain, norm_bias
    )
    g_pair = call_pick(ids, after(out_grad, n2_own))
    w_qkv = call_fold(after(w_qkv, *g_pair), down_w, up_w)
    in_pieces[3:] = after(in_pieces[3:], w_qkv)
    g_own = exchange(z, g_pair)
    proj_near = gather_near(after(proj_weight, *in_pieces[3:]))
    n2_other = to_core(after(n2_own, *in_pieces[3:]))
    active, slope, w_in, old = call_hidden(
        ids, n2_own, n2_other, in_pieces, fc_bias.reshape(8, HALF), proj_near[0]
    )
    proj_near = after(proj_near, old)
    proj_halves = halves(proj_near)
    far = gather_far(proj_near, proj_halves)[3:]
    near = after(proj_near, *proj_halves)
    g_own = after(g_own, *proj_halves)
    g_other = [to_core(part) for part in g_own]
    result, grad = call_feed(ids, g_own, g_other, active, slope, w_in, near, old)
    result_own, result_send = call_far_result(ids, active, far, result)
    result_other = to_core(result_send)
    part = call_far_grad(ids, g_own, g_other, slope, w_in, after(far, result_own), grad)
    part = after(part, result_other)
    part_other = to_core(part)
    mixed = call_mixed(ids, result_own, after(result_other, part), n2_own, proj_bias)
    part_other = after(part_other, *mixed)
    mixed = exchange(z, mixed)
    own, send, grad_middle, total = call_attention_back(
        ids, q, k, v, ctx, stat, w_o, part, part_other, g_own, g_other, n2_own, n2_other,
        w_qkv, n_all, down, norm_gain, down_w, up_w,
    )
    other = to_core(after(send, *mixed))
    grad_in = call_input_grad(ids, x_own, own, other, grad_middle, norm_gain)
    total = total_over(total, "seq", *grad_in)
    grad_in = exchange(z, grad_in)
    total = total + to_core(total)
    total = total_over(total, ("y", "x"))
    mixed = call_place(ids, after(mixed, total))
    total = after(total, grad_in[0]).reshape(4, ADAPTER_RANK, width)
    grad_norm = jnp.sqrt(jnp.sum(total * total))
    clipped, new_weight, new_first, new_second = adam_update(
        total, adapters, first_moment, second_moment, grad_norm
    )
    grad_input = call_place(ids, after(grad_in, mixed, new_weight))
    return (mixed, grad_input, clipped, grad_norm, new_weight, new_first, new_second)


def solution(mesh):
    sizes = dict(mesh.shape)
    if sizes["dp"] == 8 and sizes["seq"] == 4:
        plane = Mesh(mesh.devices.reshape(2, 2, 2, 4), ("y", "x", "core", "seq"))
        return build(plane, ("y", "x", "core"), on_chip)
    return build(mesh, "dp", on_device)


def build(mesh, dp, step):
    tokens, weight = P(dp, "seq", None), P(dp, None)
    return jax.shard_map(
        step,
        mesh=mesh,
        in_specs=(tokens, tokens) + (P(),) * 4 + (weight,) * 4 + (P(),) * 3,
        out_specs=(tokens, tokens) + (P(),) * 5,
        check_vma=False,
    )
```

```python
import functools
import math

import jax
import jax.numpy as jnp
from jax import lax
from jax.experimental import pallas as pl
from jax.experimental.pallas import tpu as pltpu
from jax.sharding import Mesh
from jax.sharding import PartitionSpec as P

HEAD_DIM = 64
ADAPTER_RANK = 4
STEP = 10


highest = lax.Precision.HIGHEST
adapter_alpha = 32.0
beta_one = 0.9
beta_two = 0.999
adam_eps = 1e-08
decay_rate = 0.01
learning_rate = 0.02
clip_bound = 1.0
norm_eps = 1e-05


def layer_norm(value, gain, shift):
    center = jnp.mean(value, axis=-1, keepdims=True)
    centered = value - center
    spread = jnp.mean(centered * centered, axis=-1, keepdims=True)
    return centered * lax.rsqrt(spread + norm_eps) * gain + shift


def dot_trans(left, right):
    return lax.dot_general(
        left, right, (((1,), (1,)), ((), ())), preferred_element_type=jnp.float32
    )


def dot_first(left, right):
    return lax.dot_general(
        left, right, (((0,), (0,)), ((), ())), precision=highest, preferred_element_type=jnp.float32
    )


def adam_update(grad, weight, first, second, norm):
    scale_factor = clip_bound / jnp.maximum(norm, clip_bound)
    clipped = grad * scale_factor
    new_first = beta_one * first + (1.0 - beta_one) * clipped
    new_second = beta_two * second + (1.0 - beta_two) * clipped * clipped
    first_hat = new_first / (1.0 - beta_one**STEP)
    second_hat = new_second / (1.0 - beta_two**STEP)
    new_weight = weight - learning_rate * (
        first_hat / (jnp.sqrt(second_hat) + adam_eps) + decay_rate * weight
    )
    return (clipped, new_weight, new_first, new_second)


def split_heads(packed):
    length = packed.shape[0]
    local_heads = packed.shape[-1] // HEAD_DIM
    query = packed[:, 0, 0].reshape(length, local_heads, HEAD_DIM)
    keys = packed[:, 1, 0].reshape(length, local_heads, HEAD_DIM)
    values = packed[:, 2, 0].reshape(length, local_heads, HEAD_DIM)
    return (query, keys, values)


def doc_forward(packed):
    length = packed.shape[0]
    local_width = packed.shape[-1]
    query, keys, values = split_heads(packed)
    local_heads = query.shape[1]
    span = min(512, length)
    blocks = length // span
    scale = 1.0 / math.sqrt(HEAD_DIM)
    starts = jnp.arange(blocks, dtype=jnp.int32) * span

    def visit(pieces):
        query_block, start = pieces
        scores = (
            jnp.einsum("qhd,khd->hqk", query_block, keys, preferred_element_type=jnp.float32)
            * scale
        )
        causal = (start + jnp.arange(span))[:, None] >= jnp.arange(length)[None, :]
        masked = jnp.where(causal[None], scores, -1e30)
        summit = jnp.max(masked, axis=-1, keepdims=True)
        expo = jnp.where(causal[None], jnp.exp(masked - summit), 0.0)
        totals = jnp.sum(expo, axis=-1, keepdims=True)
        weights = (expo / totals).astype(jnp.bfloat16)
        context = jnp.einsum(
            "hqk,khd->qhd", weights, values, preferred_element_type=jnp.float32
        ).astype(jnp.bfloat16)
        return (context, summit[..., 0] + jnp.log(totals[..., 0]))

    context, log_total = lax.map(
        visit, (query.reshape(blocks, span, local_heads, HEAD_DIM), starts)
    )
    return (context.reshape(length, 1, local_width), log_total)


def doc_backward(args):
    packed, grad_context, log_total = args
    length = packed.shape[0]
    local_width = packed.shape[-1]
    query, keys, values = split_heads(packed)
    local_heads = query.shape[1]
    output_gradient = grad_context[:, 0].reshape(length, local_heads, HEAD_DIM)
    span = min(512, length)
    blocks = length // span
    scale = 1.0 / math.sqrt(HEAD_DIM)
    starts = jnp.arange(blocks, dtype=jnp.int32) * span

    def visit(carry, pieces):
        grad_keys, grad_values = carry
        query_block, grad_block, total_block, start = pieces
        scores = (
            jnp.einsum("qhd,khd->hqk", query_block, keys, preferred_element_type=jnp.float32)
            * scale
        )
        causal = (start + jnp.arange(span))[:, None] >= jnp.arange(length)[None, :]
        masked = jnp.where(causal[None], scores, -1e30)
        probs = jnp.where(causal[None], jnp.exp(masked - total_block[:, :, None]), 0.0)
        weights = probs.astype(jnp.bfloat16)
        grad_probs = jnp.einsum(
            "qhd,khd->hqk", grad_block, values, preferred_element_type=jnp.float32
        )
        inner = jnp.sum(probs * grad_probs, axis=-1, keepdims=True)
        grad_scores = (probs * (grad_probs - inner)).astype(jnp.bfloat16)
        grad_query = (
            jnp.einsum("hqk,khd->qhd", grad_scores, keys, preferred_element_type=jnp.float32)
            * scale
        )
        grad_keys = (
            grad_keys
            + jnp.einsum(
                "hqk,qhd->khd", grad_scores, query_block, preferred_element_type=jnp.float32
            )
            * scale
        )
        grad_values = grad_values + jnp.einsum(
            "hqk,qhd->khd", weights, grad_block, preferred_element_type=jnp.float32
        )
        return ((grad_keys, grad_values), grad_query)

    empty = jnp.zeros((length, local_heads, HEAD_DIM), jnp.float32)
    pieces = (
        query.reshape(blocks, span, local_heads, HEAD_DIM),
        output_gradient.reshape(blocks, span, local_heads, HEAD_DIM),
        log_total,
        starts,
    )
    (grad_keys, grad_values), grad_query = lax.scan(visit, (empty, empty), pieces)
    joined = jnp.stack(
        [
            grad_query.reshape(length, local_width),
            grad_keys.reshape(length, local_width),
            grad_values.reshape(length, local_width),
        ],
        axis=1,
    )
    return joined.astype(jnp.bfloat16)[:, :, None, :]


def on_device(
    inputs,
    out_grad,
    norm_gain,
    norm_bias,
    proj_bias,
    fc_bias,
    qkv_weight,
    out_weight,
    feed_input_weight,
    proj_weight,
    adapters,
    first_moment,
    second_moment,
):
    docs, tokens, width = inputs.shape
    count = docs * tokens
    ranks = lax.axis_size("seq")
    scale_factor = adapter_alpha / ADAPTER_RANK

    def forward(stack):
        qkv_full, out_full, fc_full, proj_full = stack
        flat = inputs.reshape(count, width).astype(jnp.float32)
        normed, norm_one_back = jax.vjp(
            lambda value: layer_norm(value, norm_gain[0], norm_bias[0]), flat
        )
        base = jnp.dot(normed.astype(jnp.bfloat16), qkv_full, preferred_element_type=jnp.float32)
        down_q = jnp.dot(normed, adapters[0].T, precision=highest)
        down_v = jnp.dot(normed, adapters[2].T, precision=highest)
        query = (
            base[:, :width]
            + proj_bias[0]
            + scale_factor * jnp.dot(down_q, adapters[1], precision=highest)
        )
        keys = base[:, width : 2 * width]
        values = (
            base[:, 2 * width :]
            + proj_bias[1]
            + scale_factor * jnp.dot(down_v, adapters[3], precision=highest)
        )
        joined = (
            jnp.concatenate([query, keys, values], axis=1)
            .astype(jnp.bfloat16)
            .reshape(docs, tokens, 3, ranks, width // ranks)
        )
        spread = lax.all_to_all(joined, "seq", split_axis=3, concat_axis=1, tiled=True)
        context, log_total = lax.map(doc_forward, spread)
        context = lax.all_to_all(context, "seq", split_axis=1, concat_axis=2, tiled=True).reshape(
            count, width
        )
        middle = (
            flat + jnp.dot(context, out_full, preferred_element_type=jnp.float32) + proj_bias[2]
        )
        normed_two, norm_two_back = jax.vjp(
            lambda value: layer_norm(value, norm_gain[1], norm_bias[1]), middle
        )
        hidden = (
            jnp.dot(normed_two.astype(jnp.bfloat16), fc_full, preferred_element_type=jnp.float32)
            + fc_bias
        )
        active, gelu_back = jax.vjp(lambda value: jax.nn.gelu(value, approximate=True), hidden)
        result = (
            middle
            + jnp.dot(active.astype(jnp.bfloat16), proj_full, preferred_element_type=jnp.float32)
            + proj_bias[3]
        )
        return (
            result,
            (normed, down_q, down_v, norm_one_back, spread, log_total, norm_two_back, gelu_back),
        )

    stack = (
        lax.all_gather(qkv_weight, "dp", axis=0, tiled=True),
        lax.all_gather(out_weight, "dp", axis=0, tiled=True),
        lax.all_gather(feed_input_weight, "dp", axis=0, tiled=True),
        lax.all_gather(proj_weight, "dp", axis=0, tiled=True),
    )
    result, kept = forward(stack)
    fenced = lax.optimization_barrier((stack, result))
    stack = fenced[0]
    again, kept = forward(stack)
    qkv_full, out_full, fc_full, proj_full = stack
    normed, down_q, down_v, norm_one_back, spread, log_total, norm_two_back, gelu_back = kept
    cotangent = out_grad.reshape(count, width)
    grad_active = dot_trans(cotangent, proj_full)
    grad_hidden = gelu_back(grad_active)[0].astype(jnp.bfloat16)
    grad_normed_two = dot_trans(grad_hidden, fc_full)
    grad_middle = cotangent.astype(jnp.float32) + norm_two_back(grad_normed_two)[0]
    grad_context = dot_trans(grad_middle.astype(jnp.bfloat16), out_full).astype(jnp.bfloat16)
    grad_context = grad_context.reshape(docs, tokens, ranks, width // ranks)
    grad_context = lax.all_to_all(grad_context, "seq", split_axis=2, concat_axis=1, tiled=True)
    grad_joined = lax.map(doc_backward, (spread, grad_context, log_total))
    grad_joined = lax.all_to_all(
        grad_joined, "seq", split_axis=1, concat_axis=3, tiled=True
    ).reshape(count, 3 * width)
    grad_normed = dot_trans(grad_joined, qkv_full)
    grad_query = grad_joined[:, :width].astype(jnp.float32)
    grad_value = grad_joined[:, 2 * width :].astype(jnp.float32)
    tilt_q = scale_factor * jnp.dot(grad_query, adapters[1].T, precision=highest)
    value_adapter_up = scale_factor * jnp.dot(grad_value, adapters[3].T, precision=highest)
    grad_normed = (
        grad_normed
        + jnp.dot(tilt_q, adapters[0], precision=highest)
        + jnp.dot(value_adapter_up, adapters[2], precision=highest)
    )
    grad_input = (
        (grad_middle + norm_one_back(grad_normed)[0])
        .astype(jnp.bfloat16)
        .reshape(docs, tokens, width)
    )
    partial_terms = jnp.stack(
        [
            dot_first(tilt_q, normed),
            scale_factor * dot_first(down_q, grad_query),
            dot_first(value_adapter_up, normed),
            scale_factor * dot_first(down_v, grad_value),
        ]
    )
    total = lax.psum(partial_terms, ("dp", "seq"))
    grad_norm = jnp.sqrt(jnp.sum(total * total))
    clipped, new_weight, new_first, new_second = adam_update(
        total, adapters, first_moment, second_moment, grad_norm
    )
    mixed = result.astype(jnp.bfloat16).reshape(docs, tokens, width)
    return (mixed, grad_input, clipped, grad_norm, new_weight, new_first, new_second)


HALF = 512
BLOCK = 256
PICK = 20
SMEM = pl.BlockSpec(memory_space=pltpu.SMEM)
VMEM = pl.BlockSpec(memory_space=pltpu.VMEM)
HBM = pl.BlockSpec(memory_space=pltpu.HBM)
FREE = pl.BlockSpec(memory_space=pl.ANY)
KEEP = pl.BlockSpec(memory_space=pltpu.VMEM)
f32 = jnp.float32
bf16 = jnp.bfloat16
SWAP = ((0, 1), (1, 0))
GELU_A = math.sqrt(2.0 / math.pi)
GELU_B = 0.044715


def nn(left, right):
    return lax.dot_general(left, right, (((1,), (0,)), ((), ())), preferred_element_type=f32)


def nt(left, right):
    return lax.dot_general(left, right, (((1,), (1,)), ((), ())), preferred_element_type=f32)


def tn(left, right):
    return lax.dot_general(left, right, (((0,), (0,)), ((), ())), preferred_element_type=f32)


def shape(*dims, dtype=bf16):
    return jax.ShapeDtypeStruct(dims, dtype)


def params(mib):
    return pltpu.CompilerParams(vmem_limit_bytes=mib * 2**20)


def call(kernel, *, out_shape, in_specs, out_specs, **options):
    spaces = {id(HBM): pltpu.HBM, id(KEEP): pltpu.VMEM}
    single = not isinstance(out_shape, tuple)
    shapes, specs = ((out_shape,), (out_specs,)) if single else (out_shape, out_specs)
    shapes = tuple(
        spaces[id(spec)](each.shape, each.dtype) if id(spec) in spaces else each
        for each, spec in zip(shapes, specs, strict=True)
    )

    def run(*values):
        values = [
            pltpu.with_memory_space_constraint(value, spaces[id(spec)]) if id(spec) in spaces else value
            for value, spec in zip(values, in_specs, strict=True)
        ]
        return pl.pallas_call(
            kernel,
            out_shape=shapes[0] if single else shapes,
            in_specs=in_specs,
            out_specs=out_specs,
            **options,
        )(*values)

    return run


def rows(index, size):
    return pl.ds(pl.multiple_of(index * size, size), size)


def parity(z, k):
    return lax.rem(z + k, 2)


class Copies:
    def __init__(self, sems):
        self.sems = sems
        self.count = 0

    def start(self, source, target):
        copy = pltpu.make_async_copy(source, target, self.sems.at[self.count])
        self.count += 1
        copy.start()
        return copy


def wait_all(copies):
    for copy in copies:
        copy.wait()


def center_scale(x):
    center = jnp.mean(x, axis=-1, keepdims=True)
    centered = x - center
    spread = jnp.mean(centered * centered, axis=-1, keepdims=True)
    inverse = lax.rsqrt(spread + norm_eps)
    return centered * inverse, inverse


def norm_back(hat, inverse, grad):
    first = jnp.mean(grad, axis=-1, keepdims=True)
    second = jnp.mean(grad * hat, axis=-1, keepdims=True)
    return inverse * (grad - first - hat * second)


def cut_kernel(w, w_o, own, send, out_part):
    core = lax.axis_index("core")
    for p in range(3):
        for i in range(4):
            base = 1024 * p + 256 * i
            to = slice(128 * i, 128 * (i + 1))
            send[p, :, to] = w[:, pl.ds(pl.multiple_of(base + 128 * (1 - core), 128), 128)]
            own[p, :, to] = w[:, pl.ds(pl.multiple_of(base + 128 * core, 128), 128)]
    out_part[0, :128] = w_o[:, :HALF]
    out_part[0, 128:] = w_o[:, HALF:]


def call_cut(w, w_o):
    return call(
        cut_kernel,
        out_shape=(shape(3, 128, HALF), shape(3, 128, HALF), shape(1, BLOCK, HALF)),
        in_specs=[VMEM, VMEM],
        out_specs=(KEEP,) * 3,
        compiler_params=params(12),
        name="cut_qkv",
    )(w, w_o)


def join_kernel(own, got, out_part, shard):
    shard[:3, :128] = own[...]
    shard[:3, 128:] = got[...]
    shard[3:] = out_part[...]


def cut_feed_kernel(ids, w, own, send):
    core = ids[0]
    for i in range(4):
        send[i] = w[:, pl.ds(pl.multiple_of(1024 * i + HALF * (1 - core), HALF), HALF)]
        own[i] = w[:, pl.ds(pl.multiple_of(1024 * i + HALF * core, HALF), HALF)]


def call_cut_feed(ids, w):
    return call(
        cut_feed_kernel,
        out_shape=(shape(4, 128, HALF), shape(4, 128, HALF)),
        in_specs=[SMEM, VMEM],
        out_specs=(VMEM,) * 2,
        compiler_params=params(60),
        name="cut_feed",
    )(ids, w)


def start_sides(go, piece, target, chip, core, tag):
    return [
        (tag, go.start(piece.at[:128], target.at[rows(2 * chip + core, 128)])),
        (tag, go.start(piece.at[128:], target.at[rows(2 * chip + 1 - core, 128)])),
    ]


def attend(pair, qs, ks, vs, ctxs, stats):
    keys = ks[pair]
    values = jnp.concatenate([jnp.transpose(vs[pair]), jnp.ones((128, 1024), bf16)], axis=0)
    for i in range(4):
        ext = (i + 1) * BLOCK
        cols = slice(i * BLOCK, ext)
        query = qs[pair, cols]
        low = low_half(query)
        zero = jnp.zeros_like(query)
        parts = []
        for a in range(2):
            part = jnp.where(low, query, zero) if a == 0 else jnp.where(low, zero, query)
            scores = nt(keys[:ext], part)
            last = scores[i * BLOCK :]
            r = lax.broadcasted_iota(jnp.int32, last.shape, 0)
            c = lax.broadcasted_iota(jnp.int32, last.shape, 1)
            last = jnp.where(r <= c, last, -1e30)
            scores = jnp.concatenate([scores[: i * BLOCK], last], axis=0) if i else last
            top = jnp.max(scores, axis=0, keepdims=True)
            expo = jnp.exp(scores - top).astype(bf16)
            wide = nn(values[:, :ext], expo)
            total = wide[128:129]
            parts.append(wide[64 * a : 64 * a + 64] * (1.0 / total))
            stats[pair, a : a + 1, cols] = top + jnp.log(total)
        ctxs[pair, cols] = jnp.transpose(jnp.concatenate(parts, axis=0).astype(bf16))


def split_down(both):
    down = both[:8] + both[8:16]
    upper = down.astype(bf16).astype(f32)
    zero = jnp.zeros((104, both.shape[1]), f32)
    packed = jnp.concatenate([upper, down - upper, upper, zero], axis=0)
    return jnp.concatenate([upper, zero[:8]], axis=0).astype(bf16), jnp.transpose(packed).astype(bf16)


def fold_kernel(w, down_w, up_w, out, ws, sems):
    go = Copies(sems)
    loads = [go.start(w.at[p], ws.at[p]) for p in range(3)]
    leave = []
    for p in (1, 0, 2):
        loads[p].wait()
        if p != 1:
            for i in range(4):
                at = slice(i * BLOCK, (i + 1) * BLOCK)
                more = tn(down_w[:16, at], up_w[:16, p * HALF : (p + 1) * HALF])
                ws[p, at] = (ws[p, at].astype(f32) + more).astype(bf16)
        leave.append(go.start(ws.at[p], out.at[p]))
    wait_all(leave)


def call_fold(w, down_w, up_w):
    return call(
        fold_kernel,
        out_shape=shape(3, 1024, HALF),
        in_specs=[HBM, VMEM, VMEM],
        out_specs=HBM,
        scratch_shapes=[pltpu.VMEM((3, 1024, HALF), bf16), pltpu.SemaphoreType.DMA((6,))],
        compiler_params=params(16),
        name="fold",
    )(w, down_w, up_w)


def first_kernel(
    ids, m0, m1, others, w0, w1, w2, w3t, w3b, gain, shift, down_w, up_w, bias,
    q_out, k_out, v_out, n_out, down_out, w_out, o_out, ctx_out, stat_out, own, send,
    ns, rest, ws, os, qs, ks, vs, downs, ctxs, stats, owns, sends, sems,
):
    core, chip = ids[0], ids[2]
    go = Copies(sems)
    leave = []
    pieces = (w0, w1, w2, (w3t, w3b))
    part = lambda r, p: pieces[r].at[p] if r < 3 else pieces[r][p // 2].at[p % 2]
    for x, at in token_blocks(ids, (m0, m1), (others.at[0], others.at[1])):
        hat, _ = center_scale(x[...].astype(f32))
        value = hat * gain[0:1] + shift[0:1]
        upper = value.astype(bf16)
        ns[at] = upper
        rest[at] = (value - upper.astype(f32)).astype(bf16)
    leave.append(go.start(ns, n_out))
    for p, (to, out) in enumerate(((qs, q_out), (ks, k_out), (vs, v_out))):
        for r in range(4):
            piece = part(r, p)
            ws[p, rows(2 * (chip ^ r) + core, 128)] = piece[:128]
            ws[p, rows(2 * (chip ^ r) + 1 - core, 128)] = piece[128:]
        leave.append(go.start(ws.at[p], w_out.at[p]))
        for i in range(4):
            at = slice(i * BLOCK, (i + 1) * BLOCK)
            value = nn(ns[at], ws[p]) + bias[:, p * HALF : (p + 1) * HALF]
            if p == 0:
                both = nt(down_w[:16], ns[at]) + nt(down_w[:16], rest[at])
                down_out[:, at], downs[at] = split_down(both)
            if p != 1:
                value += nn(downs[at], up_w[:, p * HALF : (p + 1) * HALF])
            value = value.astype(bf16)
            if p == 0:
                value = value * jnp.asarray(0.125, bf16)
            for pair in range(4):
                to[pair, at] = value[:, 128 * pair : 128 * (pair + 1)]
        leave.append(go.start(to, out))

    @pl.loop(0, 4)
    def _(pair):
        attend(pair, qs, ks, vs, ctxs, stats)

    leave.append(go.start(ctxs, ctx_out))
    leave.append(go.start(stats, stat_out))
    for r in range(4):
        for h in range(2):
            os[rows(chip ^ r, 128), h * HALF : (h + 1) * HALF] = part(r, 3)[h * 128 : (h + 1) * 128]
    leave.append(go.start(os, o_out))
    for side, to, out in ((1 - core, sends, send), (core, owns, own)):
        for i in range(2):
            at = rows(2 * side + i, BLOCK)
            tok = slice(i * BLOCK, (i + 1) * BLOCK)
            whole = jnp.concatenate([ctxs[p, at] for p in range(4)], axis=1)
            to[tok] = nn(whole, os[...]).astype(to.dtype)
            leave.append(go.start(to.at[tok], out.at[tok]))
    wait_all(leave)


def call_first(ids, x_own, x_other, pieces, gain, shift, down_w, up_w, bias):
    heads = shape(4, 1024, 128)
    return call(
        first_kernel,
        out_shape=(
            heads,
            heads,
            heads,
            shape(1024, 1024),
            shape(16, 1024),
            shape(3, 1024, HALF),
            shape(HALF, 1024),
            heads,
            shape(4, 8, 1024, dtype=f32),
            shape(HALF, 1024),
            shape(HALF, 1024),
        ),
        in_specs=[SMEM] + [KEEP] * 3 + [KEEP] * 5 + [VMEM] * 5,
        out_specs=(HBM,) * 4 + (VMEM,) + (HBM,) * 6,
        scratch_shapes=[
            pltpu.VMEM((1024, 1024), bf16),
            pltpu.VMEM((1024, 1024), bf16),
            pltpu.VMEM((3, 1024, HALF), bf16),
            pltpu.VMEM((HALF, 1024), bf16),
            pltpu.VMEM((4, 1024, 128), bf16),
            pltpu.VMEM((4, 1024, 128), bf16),
            pltpu.VMEM((4, 1024, 128), bf16),
            pltpu.VMEM((1024, 128), bf16),
            pltpu.VMEM((4, 1024, 128), bf16),
            pltpu.VMEM((4, 8, 1024), f32),
            pltpu.VMEM((HALF, 1024), bf16),
            pltpu.VMEM((HALF, 1024), bf16),
            pltpu.SemaphoreType.DMA((53,)),
        ],
        compiler_params=params(44),
        name="qkv_attention",
    )(ids, *x_own, x_other, *pieces, gain, shift, down_w, up_w, bias)


def attend_back(pair, qs, ks, vs, ctxs, stats, gs, dqs, dks, dvs, acc_k, acc_v):
    keys, values = ks[pair], vs[pair]
    place = pl.ds(pl.multiple_of(pair * 128, 128), 128)
    for i in range(4):
        ext = (i + 1) * BLOCK
        cols = slice(i * BLOCK, ext)
        query, grad = qs[pair, cols], gs[pair, cols]
        low = low_half(query)
        zero = jnp.zeros_like(query)
        product = grad.astype(f32) * ctxs[pair, cols].astype(f32)
        stat = jnp.transpose(stats[pair, :, cols])
        turned_query, turned_grad = jnp.transpose(query), jnp.transpose(grad)
        new_q = []
        for a in range(2):
            pick = (lambda x, y: jnp.where(low, x, y)) if a == 0 else (lambda x, y: jnp.where(low, y, x))
            half = slice(64 * a, 64 * a + 64)
            scores = nt(pick(query, zero), keys[:ext])
            probs = jnp.exp(scores - stat[:, a : a + 1])
            last = probs[:, i * BLOCK :]
            r = lax.broadcasted_iota(jnp.int32, last.shape, 0)
            c = lax.broadcasted_iota(jnp.int32, last.shape, 1)
            last = jnp.where(r >= c, last, 0.0)
            probs = jnp.concatenate([probs[:, : i * BLOCK], last], axis=1) if i else last
            inner = jnp.sum(pick(product, 0.0), axis=1, keepdims=True)
            grad_probs = nt(pick(grad, zero), values[:ext])
            grad_scores = (probs * (grad_probs - inner)).astype(bf16)
            more_v = nn(turned_grad[half], probs.astype(bf16))
            more_k = nn(turned_query[half], grad_scores)
            if i:
                acc_v[half, : i * BLOCK] += more_v[:, : i * BLOCK]
                acc_k[half, : i * BLOCK] += more_k[:, : i * BLOCK]
            acc_v[half, cols] = more_v[:, i * BLOCK :]
            acc_k[half, cols] = more_k[:, i * BLOCK :]
            new_q.append(nn(grad_scores, keys[:ext]))
        both = jnp.where(low, new_q[0], new_q[1])
        dqs[cols, place] = (both * 0.125).astype(bf16)
    dks[:, place] = jnp.transpose(acc_k[...].astype(bf16))
    dvs[:, place] = jnp.transpose(acc_v[...].astype(bf16))


def attention_back_kernel(
    ids, q, k_in, v, ctx, stat, w_o, parts, others, g0, g1, g2, g3, mid_own, mid_other, w, n_all, downs,
    gain, down_w, up_w,
    own, send, grad_middle, total,
    os, qs, ks, vs, ctxs, stats, heads, dqs, dks, dvs, acc_k, acc_v,
    ws, ns, tilts, sems,
):
    core, z = ids[0], ids[1]
    go = Copies(sems)
    outer = go.start(w_o, os)
    then = [
        go.start(ref, to)
        for ref, to in ((q, qs), (k_in, ks), (v, vs), (ctx, ctxs), (stat, stats))
    ]
    weights = [go.start(w, ws), go.start(n_all, ns)]
    mids = (mid_own, mid_own, mid_other, mid_other)
    for at, (g, tok) in enumerate(token_blocks(ids, (g0, g1), (g2, g3))):
        here = rows(parity(z, at % 2), BLOCK)
        hat, inverse = center_scale(mids[at][1, here].astype(f32))
        grad = (parts[tok].astype(f32) + others[tok].astype(f32)) * gain[1:2]
        value = (g[...].astype(f32) + norm_back(hat, inverse, grad)).astype(bf16)
        if at < 2:
            grad_middle[here] = value
        if at == 0:
            outer.wait()
        value = nt(value, os[...]).astype(bf16)
        for pair in range(4):
            heads[pair, tok] = value[:, 128 * pair : 128 * (pair + 1)]
    wait_all(then)

    @pl.loop(0, 4)
    def _(pair):
        attend_back(pair, qs, ks, vs, ctxs, stats, heads, dqs, dks, dvs, acc_k, acc_v)

    wait_all(weights)
    for side, values in ((1 - core, send), (core, own)):
        for i in range(2):
            at = rows(2 * side + i, BLOCK)
            tok = slice(i * BLOCK, (i + 1) * BLOCK)
            gq, gk, gv = dqs[at], dks[at], dvs[at]
            value = nt(gq, ws[0]) + nt(gk, ws[1]) + nt(gv, ws[2])
            values[tok] = value.astype(bf16)
    tilts[...] = (nt(up_w[:16, :HALF], dqs[...]) + nt(up_w[:16, 2 * HALF :], dvs[...])).astype(bf16)
    down_terms = nn(tilts[...], ns[...])
    total[...] = jnp.zeros_like(total)
    total[0:4] = down_terms[0:4]
    total[8:12] = down_terms[4:8]
    up_q = 8.0 * nn(downs[...], dqs[...])
    up_v = 8.0 * nn(downs[...], dvs[...])
    for pair in range(4):
        here = pl.ds(pl.multiple_of(256 * pair + 128 * core, 128), 128)
        total[4:8, here] = up_q[0:4, 128 * pair : 128 * (pair + 1)]
        total[12:16, here] = up_v[4:8, 128 * pair : 128 * (pair + 1)]


def call_attention_back(
    ids, q, k, v, ctx, stat, w_o, part, other, g_own, g_other, mid_own, mid_other,
    w, n_all, downs, gain, down_w, up_w,
):
    pairs = pltpu.VMEM((4, 1024, 128), bf16)
    wide = pltpu.VMEM((1024, HALF), bf16)
    return call(
        attention_back_kernel,
        out_shape=(
            shape(HALF, 1024),
            shape(HALF, 1024),
            shape(HALF, 1024),
            shape(16, 1024, dtype=f32),
        ),
        in_specs=[SMEM] + [HBM] * 6 + [KEEP] * 8 + [HBM] * 2 + [VMEM] * 4,
        out_specs=(KEEP, KEEP, KEEP, KEEP),
        scratch_shapes=[
            pltpu.VMEM((HALF, 1024), bf16),
            pairs,
            pairs,
            pairs,
            pairs,
            pltpu.VMEM((4, 8, 1024), f32),
            pairs,
            wide,
            wide,
            wide,
            pltpu.VMEM((128, 1024), f32),
            pltpu.VMEM((128, 1024), f32),
            pltpu.VMEM((3, 1024, HALF), bf16),
            pltpu.VMEM((1024, 1024), bf16),
            pltpu.VMEM((16, 1024), bf16),
            pltpu.SemaphoreType.DMA((8,)),
        ],
        compiler_params=params(36),
        name="attention_back",
    )(
        ids, q, k, v, ctx, stat, w_o, part, other, *g_own, *g_other, mid_own, mid_other,
        w, n_all, downs, gain, down_w, up_w,
    )


def low_half(value):
    return lax.broadcasted_iota(jnp.int32, value.shape, 1) < 64


def start_tokens(go, pair, target, z):
    return [go.start(ref, target.at[parity(z, k)]) for k, ref in enumerate(pair)]


def middle_kernel(
    ids, own, other, x0, x1, bias, gain, shift, both, owns, others, xs, sems
):
    go = Copies(sems)
    tokens = start_tokens(go, (x0, x1), xs, ids[1])
    parts = []
    for i in range(2):
        at = slice(i * BLOCK, (i + 1) * BLOCK)
        parts.append([go.start(own.at[at], owns.at[i]), go.start(other.at[at], others.at[i])])
    wait_all(tokens)
    for i in range(2):
        at = slice(i * BLOCK, (i + 1) * BLOCK)
        wait_all(parts[i])
        value = owns[i].astype(f32) + others[i].astype(f32) + xs[i].astype(f32) + bias[2:3]
        both[1, at] = value.astype(bf16)
        hat, _ = center_scale(value)
        both[0, at] = (hat * gain[1:2] + shift[1:2]).astype(bf16)


def call_middle(ids, own, other, x_own, bias, gain, shift):
    return call(
        middle_kernel,
        out_shape=shape(2, HALF, 1024),
        in_specs=[SMEM, HBM, FREE, HBM, HBM] + [VMEM] * 3,
        out_specs=KEEP,
        scratch_shapes=[pltpu.VMEM((2, BLOCK, 1024), bf16)] * 3 + [pltpu.SemaphoreType.DMA((6,))],
        compiler_params=params(40),
        name="middle",
    )(ids, own, other, *x_own, bias, gain, shift)


def start_grads(go, ids, g_own, g_other, gs):
    core, z = ids[0], ids[1]
    return [
        go.start(ref, gs.at[2 * side + parity(z, k)])
        for side, pair in ((core, g_own), (1 - core, g_other))
        for k, ref in enumerate(pair)
    ]


def hidden_kernel(
    ids, n_own, n_other, w0, w1, w2, w3t, w3b, bias, piece, acts, slopes, ws, result, wo, sems
):
    core, chip = ids[0], ids[2]
    go = Copies(sems)
    weights = []
    for p in range(4):
        for r, ref in enumerate((w0, w1, w2, (w3t, w3b))):
            part = ref.at[p] if r < 3 else ref[p // 2].at[p % 2]
            weights += start_sides(go, part, ws.at[p], chip ^ r, core, p)
    later = go.start(piece, wo)
    tokens = [
        (ref, slice(h * BLOCK, (h + 1) * BLOCK), rows(2 * side + h, BLOCK))
        for ref, side in ((n_own, core), (n_other, 1 - core))
        for h in range(2)
    ]

    def finish(p, at, h):
        square = h * h
        lift = 0.5 + 0.5 * jnp.tanh(h * (GELU_A + (GELU_A * GELU_B) * square))
        act = h * lift
        acts[p, at] = act.astype(bf16)
        rise = 2.0 * GELU_A + (6.0 * GELU_A * GELU_B) * square
        slopes[p, at] = (lift + (act - act * lift) * rise).astype(bf16)

    before = None
    for p in range(4):
        wait_all([copy for at, copy in weights if at == p])
        shift = bias[pl.ds(2 * p + core, 1)]
        for ref, here, at in tokens:
            h = nn(ref[0, here], ws[p]) + shift
            if before is not None:
                finish(*before)
            before = (p, at, h)
    finish(*before)
    later.wait()
    for i in range(4):
        tok = slice(i * BLOCK, (i + 1) * BLOCK)
        result[tok] = nn(acts[chip, tok], wo[...])


def call_hidden(ids, n_own, n_other, pieces, bias, piece):
    return call(
        hidden_kernel,
        out_shape=(shape(4, 1024, HALF),) * 3 + (shape(1024, 1024, dtype=f32),),
        in_specs=[SMEM] + [KEEP] * 2 + [HBM] * 5 + [VMEM, HBM],
        out_specs=(KEEP,) * 4,
        scratch_shapes=[
            pltpu.VMEM((HALF, 1024), bf16),
            pltpu.SemaphoreType.DMA((33,)),
        ],
        compiler_params=params(26),
        name="hidden",
    )(ids, n_own, n_other, *pieces, bias, piece)


def token_blocks(ids, g_own, g_other):
    core, z = ids[0], ids[1]
    return [
        (ref, rows(2 * side + parity(z, k), BLOCK))
        for side, pair in ((core, g_own), (1 - core, g_other))
        for k, ref in enumerate(pair)
    ]


def feed_kernel(
    ids, g0, g1, g2, g3, acts, slopes, w_ins, own_piece, x_piece, y_piece, old,
    result, grad, own_rows, sems,
):
    chip = ids[2]
    load = Copies(sems).start(own_piece, own_rows)
    for i, (g, tok) in enumerate(token_blocks(ids, (g0, g1), (g2, g3))):
        out_sum, grad_sum = old[tok], None
        for r, piece in ((1, x_piece), (2, y_piece), (0, own_rows)):
            here = chip ^ r
            if i == 0 and r == 0:
                load.wait()
            back = nt(g[...], piece[...])
            if r:
                out_sum += nn(acts[here, tok], piece[...])
            back = (back * slopes[here, tok].astype(f32)).astype(bf16)
            term = nt(back, w_ins[here])
            grad_sum = term if grad_sum is None else grad_sum + term
        result[tok] = out_sum
        grad[tok] = grad_sum


def call_feed(ids, g_own, g_other, active, slope, w_in, pieces, old):
    return call(
        feed_kernel,
        out_shape=(shape(1024, 1024, dtype=f32),) * 2,
        in_specs=[SMEM] + [KEEP] * 7 + [HBM] + [KEEP] * 3,
        out_specs=(KEEP, KEEP),
        scratch_shapes=[pltpu.VMEM((HALF, 1024), bf16), pltpu.SemaphoreType.DMA((1,))],
        compiler_params=params(18),
        name="feed",
    )(ids, *g_own, *g_other, active, slope, w_in, *pieces, old)


def far_grad_kernel(ids, g0, g1, g2, g3, slopes, w_ins, top, low, old, out):
    far = ids[2] ^ 3
    for g, tok in token_blocks(ids, (g0, g1), (g2, g3)):
        back = jnp.concatenate([nt(g[...], top[...]), nt(g[...], low[...])], axis=1)
        back = back * slopes[far, tok].astype(f32)
        more = nt(back.astype(bf16), w_ins[far])
        out[tok] = (more + old[tok]).astype(bf16)


def call_far_grad(ids, g_own, g_other, slope, w_in, far, old):
    return call(
        far_grad_kernel,
        out_shape=shape(1024, 1024),
        in_specs=[SMEM] + [KEEP] * 9,
        out_specs=KEEP,
        compiler_params=params(18),
        name="far_grad",
    )(ids, *g_own, *g_other, slope, w_in, *far, old)


def far_result_kernel(ids, acts, top, low, old, own, send):
    core, far = ids[0], ids[2] ^ 3
    for side, values in ((1 - core, send), (core, own)):
        for i in range(2):
            at = rows(2 * side + i, BLOCK)
            tok = slice(i * BLOCK, (i + 1) * BLOCK)
            more = nn(acts[far, at, :BLOCK], top[...]) + nn(acts[far, at, BLOCK:], low[...])
            values[tok] = (old[at] + more).astype(values.dtype)


def call_far_result(ids, active, far, old):
    return call(
        far_result_kernel,
        out_shape=(shape(HALF, 1024, dtype=f32), shape(HALF, 1024)),
        in_specs=[SMEM] + [KEEP] * 4,
        out_specs=(KEEP, KEEP),
        compiler_params=params(16),
        name="far_result",
    )(ids, active, *far, old)


def mixed_kernel(ids, own, other, middle, bias, out0, out1):
    z = ids[1]
    for k, out in enumerate((out0, out1)):
        tok = rows(parity(z, k), BLOCK)
        value = own[tok] + other[tok].astype(f32) + middle[1, tok].astype(f32)
        out[...] = (value + bias[3:4]).astype(bf16)


def call_mixed(ids, own, other, middle, bias):
    return call(
        mixed_kernel,
        out_shape=(shape(BLOCK, 1024),) * 2,
        in_specs=[SMEM, KEEP, KEEP, KEEP, VMEM],
        out_specs=(KEEP, KEEP),
        compiler_params=params(12),
        name="mixed",
    )(ids, own, other, middle, bias)


def input_grad_kernel(ids, x0, x1, own, other, grad_middle, gain, out0, out1):
    z = ids[1]
    for k, (x, out) in enumerate(((x0, out0), (x1, out1))):
        for h in range(2):
            tok = rows(2 * parity(z, k) + h, 128)
            here = slice(128 * h, 128 * (h + 1))
            grad = (own[tok].astype(f32) + other[tok].astype(f32)) * gain[0:1]
            hat, inverse = center_scale(x[here].astype(f32))
            out[here] = (grad_middle[tok].astype(f32) + norm_back(hat, inverse, grad)).astype(bf16)


def call_input_grad(ids, x_own, own, other, grad_middle, gain):
    return call(
        input_grad_kernel,
        out_shape=(shape(BLOCK, 1024),) * 2,
        in_specs=[SMEM, KEEP, KEEP, KEEP, KEEP, KEEP, VMEM],
        out_specs=(KEEP, KEEP),
        compiler_params=params(16),
        name="input_grad",
    )(ids, *x_own, own, other, grad_middle, gain)


def to_core(value):
    return lax.ppermute(value, "core", SWAP)


def total_over(value, axis, *others):
    flip = [lax.ppermute(value, axis, [(i, i ^ by) for i in range(4)]) for by in (1, 2, 3)]
    flip = after(flip, *others)
    return (value + flip[0]) + (flip[1] + flip[2])


def exchange(z, pair):
    sent = []
    for k in range(2):
        perm = [
            (4 * core + at, 4 * (at // 2) + 2 * core + (at + k) % 2)
            for core in range(2)
            for at in range(4)
        ]
        sent.append(lax.ppermute(pair[k], ("core", "seq"), perm))
    return sent


def pick_kernel(ids, value, out0, out1, sems):
    z = ids[1]
    go = Copies(sems)
    wait_all([go.start(value.at[parity(z, k)], out) for k, out in enumerate((out0, out1))])


def call_pick(ids, value):
    return call(
        pick_kernel,
        out_shape=(shape(BLOCK, 1024),) * 2,
        in_specs=[SMEM, HBM],
        out_specs=(KEEP, KEEP),
        scratch_shapes=[pltpu.SemaphoreType.DMA((2,))],
        compiler_params=params(PICK),
        name="pick",
    )(ids, value)


def place_kernel(ids, first, second, out, sems):
    z = ids[1]
    go = Copies(sems)
    wait_all([go.start(ref, out.at[parity(z, k)]) for k, ref in enumerate((first, second))])


def call_place(ids, pair):
    return call(
        place_kernel,
        out_shape=shape(2, BLOCK, 1024),
        in_specs=[SMEM, KEEP, KEEP],
        out_specs=HBM,
        scratch_shapes=[pltpu.SemaphoreType.DMA((2,))],
        compiler_params=params(PICK),
        name="place",
    )(ids, *pair)


def after(value, *others):
    return lax.optimization_barrier((value, *others))[0]


def gather_near(shard):
    return [shard, lax.ppermute(shard, "x", SWAP), lax.ppermute(shard, "y", SWAP)]


def halves(near, first=False):
    if near[1].shape[0] == 4 and not first:
        return call_halves(near[1], near[2])
    half = near[1].shape[0] // 2
    return call(
        split_kernel,
        out_shape=(shape(half, *near[1].shape[1:]),) * 2,
        in_specs=[KEEP, KEEP],
        out_specs=(KEEP, KEEP),
        compiler_params=params(8),
        name="split",
    )(near[1], near[2])


def split_kernel(by_x, by_y, first, second):
    half = first.shape[0]
    first[...] = by_x[:half]
    second[...] = by_y[half:]


def halves_kernel(by_x, by_y, first, second, held, sems):
    half = first.shape[0]
    go = Copies(sems)
    loads = [go.start(by_x.at[:half], held.at[0]), go.start(by_y.at[half:], held.at[1])]
    leave = []
    for at, out in enumerate((first, second)):
        loads[at].wait()
        leave.append(go.start(held.at[at], out))
    wait_all(leave)


def call_halves(by_x, by_y):
    dims = (by_x.shape[0] // 2, *by_x.shape[1:])
    return call(
        halves_kernel,
        out_shape=(shape(*dims), shape(*dims)),
        in_specs=[FREE, FREE],
        out_specs=(HBM, HBM),
        scratch_shapes=[pltpu.VMEM((2, *dims), bf16), pltpu.SemaphoreType.DMA((4,))],
        compiler_params=params(8),
        name="halves",
    )(by_x, by_y)


def gather_far(near, parts):
    return near + [lax.ppermute(parts[0], "y", SWAP), lax.ppermute(parts[1], "x", SWAP)]


def parts_of(value):
    upper = lax.reduce_precision(value, 8, 7)
    return upper.astype(bf16), (value - upper).astype(bf16)


def on_chip(
    inputs,
    out_grad,
    norm_gain,
    norm_bias,
    proj_bias,
    fc_bias,
    qkv_weight,
    out_weight,
    feed_input_weight,
    proj_weight,
    adapters,
    first_moment,
    second_moment,
):
    width = inputs.shape[2]
    core = lax.axis_index("core")
    z = lax.axis_index("seq")
    chip = 2 * lax.axis_index("y") + lax.axis_index("x")
    ids = jnp.stack([core, z, chip]).astype(jnp.int32)

    qkv_own, qkv_send, out_part = call_cut(qkv_weight, out_weight)
    qkv_got = to_core(qkv_send)
    first_shard = call(
        join_kernel,
        out_shape=shape(4, BLOCK, HALF),
        in_specs=[KEEP] * 3,
        out_specs=KEEP,
        compiler_params=params(12),
        name="join",
    )(qkv_own, qkv_got, out_part)
    first_near = gather_near(first_shard)
    x_own = exchange(z, call_pick(ids, after(inputs, first_shard)))
    in_own, in_send = call_cut_feed(ids, after(feed_input_weight, first_shard))
    in_shard = jnp.concatenate([in_own, to_core(in_send)], axis=1)

    def columns(value):
        lead = value.shape[0]
        value = value.reshape(lead, 4, 2, 128)
        return jnp.where(core == 0, value[:, :, 0], value[:, :, 1]).reshape(lead, HALF)

    scale = adapter_alpha / ADAPTER_RANK
    adapters, proj_bias = after((adapters, proj_bias), first_shard)
    up_q, up_v = scale * columns(adapters[1]), scale * columns(adapters[3])
    up = jnp.zeros((8, 1536), f32).at[0:4, :HALF].set(up_q).at[4:8, 2 * HALF :].set(up_v)
    upper, lower = parts_of(up)
    up_w = jnp.concatenate([upper, upper, lower, jnp.zeros((104, 1536), bf16)], axis=0)
    upper, lower = parts_of(jnp.concatenate([adapters[0], adapters[2]], axis=0))
    down_w = jnp.concatenate([upper, lower, jnp.zeros((112, 1024), bf16)], axis=0)
    head_bias = columns(proj_bias[:2])
    qkv_bias = jnp.concatenate([head_bias[0], jnp.zeros((HALF,), f32), head_bias[1]])[None]

    first_near = after(first_near, up_w, down_w, qkv_bias, in_shard)
    first_halves = halves(first_near, True)
    first_pieces = gather_far(first_near, first_halves)
    x_own = after(x_own, *first_halves)
    x_other = to_core(jnp.stack(x_own))
    in_near = gather_near(after(in_shard, *first_pieces[3:]))
    q, k, v, n_all, down, w_qkv, w_o, ctx, stat, attn_own, attn_send = call_first(
        ids, x_own, x_other, first_pieces, norm_gain, norm_bias, down_w, up_w, qkv_bias
    )
    in_near = after(in_near, ctx)
    in_halves = halves(in_near)
    in_pieces = gather_far(in_near, in_halves)
    attn_other = to_core(after(attn_send, *in_halves))
    n2_own = call_middle(
        ids, attn_own, after(attn_other, *in_halves), x_own, proj_bias, norm_gain, norm_bias
    )
    g_pair = call_pick(ids, after(out_grad, n2_own))
    w_qkv = call_fold(after(w_qkv, *g_pair), down_w, up_w)
    in_pieces[3:] = after(in_pieces[3:], w_qkv)
    g_own = exchange(z, g_pair)
    proj_near = gather_near(after(proj_weight, *in_pieces[3:]))
    n2_other = to_core(after(n2_own, *in_pieces[3:]))
    active, slope, w_in, old = call_hidden(
        ids, n2_own, n2_other, in_pieces, fc_bias.reshape(8, HALF), proj_near[0]
    )
    proj_near = after(proj_near, old)
    proj_halves = halves(proj_near)
    far = gather_far(proj_near, proj_halves)[3:]
    near = after(proj_near, *proj_halves)
    g_own = after(g_own, *proj_halves)
    g_other = [to_core(part) for part in g_own]
    result, grad = call_feed(ids, g_own, g_other, active, slope, w_in, near, old)
    result_own, result_send = call_far_result(ids, active, far, result)
    result_other = to_core(result_send)
    part = call_far_grad(ids, g_own, g_other, slope, w_in, after(far, result_own), grad)
    part = after(part, result_other)
    part_other = to_core(part)
    mixed = call_mixed(ids, result_own, after(result_other, part), n2_own, proj_bias)
    part_other = after(part_other, *mixed)
    mixed = exchange(z, mixed)
    own, send, grad_middle, total = call_attention_back(
        ids, q, k, v, ctx, stat, w_o, part, part_other, g_own, g_other, n2_own, n2_other,
        w_qkv, n_all, down, norm_gain, down_w, up_w,
    )
    other = to_core(after(send, *mixed))
    grad_in = call_input_grad(ids, x_own, own, other, grad_middle, norm_gain)
    total = total_over(total, "seq", *grad_in)
    grad_in = exchange(z, grad_in)
    total = total + to_core(total)
    total = total_over(total, ("y", "x"))
    mixed = call_place(ids, after(mixed, total))
    total = after(total, grad_in[0]).reshape(4, ADAPTER_RANK, width)
    grad_norm = jnp.sqrt(jnp.sum(total * total))
    clipped, new_weight, new_first, new_second = adam_update(
        total, adapters, first_moment, second_moment, grad_norm
    )
    grad_input = call_place(ids, after(grad_in, mixed, new_weight))
    return (mixed, grad_input, clipped, grad_norm, new_weight, new_first, new_second)


def solution(mesh):
    sizes = dict(mesh.shape)
    if sizes["dp"] == 8 and sizes["seq"] == 4:
        plane = Mesh(mesh.devices.reshape(2, 2, 2, 4), ("y", "x", "core", "seq"))
        return build(plane, ("y", "x", "core"), on_chip)
    return build(mesh, "dp", on_device)


def build(mesh, dp, step):
    tokens, weight = P(dp, "seq", None), P(dp, None)
    return jax.shard_map(
        step,
        mesh=mesh,
        in_specs=(tokens, tokens) + (P(),) * 4 + (weight,) * 4 + (P(),) * 3,
        out_specs=(tokens, tokens) + (P(),) * 5,
        check_vma=False,
    )
```

```python
import functools
import math

import jax
import jax.numpy as jnp
from jax import lax
from jax.experimental import pallas as pl
from jax.experimental.pallas import tpu as pltpu
from jax.sharding import Mesh
from jax.sharding import PartitionSpec as P

HEAD_DIM = 64
ADAPTER_RANK = 4
STEP = 10


highest = lax.Precision.HIGHEST
adapter_alpha = 32.0
beta_one = 0.9
beta_two = 0.999
adam_eps = 1e-08
decay_rate = 0.01
learning_rate = 0.02
clip_bound = 1.0
norm_eps = 1e-05


def layer_norm(value, gain, shift):
    center = jnp.mean(value, axis=-1, keepdims=True)
    centered = value - center
    spread = jnp.mean(centered * centered, axis=-1, keepdims=True)
    return centered * lax.rsqrt(spread + norm_eps) * gain + shift


def dot_trans(left, right):
    return lax.dot_general(
        left, right, (((1,), (1,)), ((), ())), preferred_element_type=jnp.float32
    )


def dot_first(left, right):
    return lax.dot_general(
        left, right, (((0,), (0,)), ((), ())), precision=highest, preferred_element_type=jnp.float32
    )


def adam_update(grad, weight, first, second, norm):
    scale_factor = clip_bound / jnp.maximum(norm, clip_bound)
    clipped = grad * scale_factor
    new_first = beta_one * first + (1.0 - beta_one) * clipped
    new_second = beta_two * second + (1.0 - beta_two) * clipped * clipped
    first_hat = new_first / (1.0 - beta_one**STEP)
    second_hat = new_second / (1.0 - beta_two**STEP)
    new_weight = weight - learning_rate * (
        first_hat / (jnp.sqrt(second_hat) + adam_eps) + decay_rate * weight
    )
    return (clipped, new_weight, new_first, new_second)


def split_heads(packed):
    length = packed.shape[0]
    local_heads = packed.shape[-1] // HEAD_DIM
    query = packed[:, 0, 0].reshape(length, local_heads, HEAD_DIM)
    keys = packed[:, 1, 0].reshape(length, local_heads, HEAD_DIM)
    values = packed[:, 2, 0].reshape(length, local_heads, HEAD_DIM)
    return (query, keys, values)


def doc_forward(packed):
    length = packed.shape[0]
    local_width = packed.shape[-1]
    query, keys, values = split_heads(packed)
    local_heads = query.shape[1]
    span = min(512, length)
    blocks = length // span
    scale = 1.0 / math.sqrt(HEAD_DIM)
    starts = jnp.arange(blocks, dtype=jnp.int32) * span

    def visit(pieces):
        query_block, start = pieces
        scores = (
            jnp.einsum("qhd,khd->hqk", query_block, keys, preferred_element_type=jnp.float32)
            * scale
        )
        causal = (start + jnp.arange(span))[:, None] >= jnp.arange(length)[None, :]
        masked = jnp.where(causal[None], scores, -1e30)
        summit = jnp.max(masked, axis=-1, keepdims=True)
        expo = jnp.where(causal[None], jnp.exp(masked - summit), 0.0)
        totals = jnp.sum(expo, axis=-1, keepdims=True)
        weights = (expo / totals).astype(jnp.bfloat16)
        context = jnp.einsum(
            "hqk,khd->qhd", weights, values, preferred_element_type=jnp.float32
        ).astype(jnp.bfloat16)
        return (context, summit[..., 0] + jnp.log(totals[..., 0]))

    context, log_total = lax.map(
        visit, (query.reshape(blocks, span, local_heads, HEAD_DIM), starts)
    )
    return (context.reshape(length, 1, local_width), log_total)


def doc_backward(args):
    packed, grad_context, log_total = args
    length = packed.shape[0]
    local_width = packed.shape[-1]
    query, keys, values = split_heads(packed)
    local_heads = query.shape[1]
    output_gradient = grad_context[:, 0].reshape(length, local_heads, HEAD_DIM)
    span = min(512, length)
    blocks = length // span
    scale = 1.0 / math.sqrt(HEAD_DIM)
    starts = jnp.arange(blocks, dtype=jnp.int32) * span

    def visit(carry, pieces):
        grad_keys, grad_values = carry
        query_block, grad_block, total_block, start = pieces
        scores = (
            jnp.einsum("qhd,khd->hqk", query_block, keys, preferred_element_type=jnp.float32)
            * scale
        )
        causal = (start + jnp.arange(span))[:, None] >= jnp.arange(length)[None, :]
        masked = jnp.where(causal[None], scores, -1e30)
        probs = jnp.where(causal[None], jnp.exp(masked - total_block[:, :, None]), 0.0)
        weights = probs.astype(jnp.bfloat16)
        grad_probs = jnp.einsum(
            "qhd,khd->hqk", grad_block, values, preferred_element_type=jnp.float32
        )
        inner = jnp.sum(probs * grad_probs, axis=-1, keepdims=True)
        grad_scores = (probs * (grad_probs - inner)).astype(jnp.bfloat16)
        grad_query = (
            jnp.einsum("hqk,khd->qhd", grad_scores, keys, preferred_element_type=jnp.float32)
            * scale
        )
        grad_keys = (
            grad_keys
            + jnp.einsum(
                "hqk,qhd->khd", grad_scores, query_block, preferred_element_type=jnp.float32
            )
            * scale
        )
        grad_values = grad_values + jnp.einsum(
            "hqk,qhd->khd", weights, grad_block, preferred_element_type=jnp.float32
        )
        return ((grad_keys, grad_values), grad_query)

    empty = jnp.zeros((length, local_heads, HEAD_DIM), jnp.float32)
    pieces = (
        query.reshape(blocks, span, local_heads, HEAD_DIM),
        output_gradient.reshape(blocks, span, local_heads, HEAD_DIM),
        log_total,
        starts,
    )
    (grad_keys, grad_values), grad_query = lax.scan(visit, (empty, empty), pieces)
    joined = jnp.stack(
        [
            grad_query.reshape(length, local_width),
            grad_keys.reshape(length, local_width),
            grad_values.reshape(length, local_width),
        ],
        axis=1,
    )
    return joined.astype(jnp.bfloat16)[:, :, None, :]


def on_device(
    inputs,
    out_grad,
    norm_gain,
    norm_bias,
    proj_bias,
    fc_bias,
    qkv_weight,
    out_weight,
    feed_input_weight,
    proj_weight,
    adapters,
    first_moment,
    second_moment,
):
    docs, tokens, width = inputs.shape
    count = docs * tokens
    ranks = lax.axis_size("seq")
    scale_factor = adapter_alpha / ADAPTER_RANK

    def forward(stack):
        qkv_full, out_full, fc_full, proj_full = stack
        flat = inputs.reshape(count, width).astype(jnp.float32)
        normed, norm_one_back = jax.vjp(
            lambda value: layer_norm(value, norm_gain[0], norm_bias[0]), flat
        )
        base = jnp.dot(normed.astype(jnp.bfloat16), qkv_full, preferred_element_type=jnp.float32)
        down_q = jnp.dot(normed, adapters[0].T, precision=highest)
        down_v = jnp.dot(normed, adapters[2].T, precision=highest)
        query = (
            base[:, :width]
            + proj_bias[0]
            + scale_factor * jnp.dot(down_q, adapters[1], precision=highest)
        )
        keys = base[:, width : 2 * width]
        values = (
            base[:, 2 * width :]
            + proj_bias[1]
            + scale_factor * jnp.dot(down_v, adapters[3], precision=highest)
        )
        joined = (
            jnp.concatenate([query, keys, values], axis=1)
            .astype(jnp.bfloat16)
            .reshape(docs, tokens, 3, ranks, width // ranks)
        )
        spread = lax.all_to_all(joined, "seq", split_axis=3, concat_axis=1, tiled=True)
        context, log_total = lax.map(doc_forward, spread)
        context = lax.all_to_all(context, "seq", split_axis=1, concat_axis=2, tiled=True).reshape(
            count, width
        )
        middle = (
            flat + jnp.dot(context, out_full, preferred_element_type=jnp.float32) + proj_bias[2]
        )
        normed_two, norm_two_back = jax.vjp(
            lambda value: layer_norm(value, norm_gain[1], norm_bias[1]), middle
        )
        hidden = (
            jnp.dot(normed_two.astype(jnp.bfloat16), fc_full, preferred_element_type=jnp.float32)
            + fc_bias
        )
        active, gelu_back = jax.vjp(lambda value: jax.nn.gelu(value, approximate=True), hidden)
        result = (
            middle
            + jnp.dot(active.astype(jnp.bfloat16), proj_full, preferred_element_type=jnp.float32)
            + proj_bias[3]
        )
        return (
            result,
            (normed, down_q, down_v, norm_one_back, spread, log_total, norm_two_back, gelu_back),
        )

    stack = (
        lax.all_gather(qkv_weight, "dp", axis=0, tiled=True),
        lax.all_gather(out_weight, "dp", axis=0, tiled=True),
        lax.all_gather(feed_input_weight, "dp", axis=0, tiled=True),
        lax.all_gather(proj_weight, "dp", axis=0, tiled=True),
    )
    result, kept = forward(stack)
    fenced = lax.optimization_barrier((stack, result))
    stack = fenced[0]
    again, kept = forward(stack)
    qkv_full, out_full, fc_full, proj_full = stack
    normed, down_q, down_v, norm_one_back, spread, log_total, norm_two_back, gelu_back = kept
    cotangent = out_grad.reshape(count, width)
    grad_active = dot_trans(cotangent, proj_full)
    grad_hidden = gelu_back(grad_active)[0].astype(jnp.bfloat16)
    grad_normed_two = dot_trans(grad_hidden, fc_full)
    grad_middle = cotangent.astype(jnp.float32) + norm_two_back(grad_normed_two)[0]
    grad_context = dot_trans(grad_middle.astype(jnp.bfloat16), out_full).astype(jnp.bfloat16)
    grad_context = grad_context.reshape(docs, tokens, ranks, width // ranks)
    grad_context = lax.all_to_all(grad_context, "seq", split_axis=2, concat_axis=1, tiled=True)
    grad_joined = lax.map(doc_backward, (spread, grad_context, log_total))
    grad_joined = lax.all_to_all(
        grad_joined, "seq", split_axis=1, concat_axis=3, tiled=True
    ).reshape(count, 3 * width)
    grad_normed = dot_trans(grad_joined, qkv_full)
    grad_query = grad_joined[:, :width].astype(jnp.float32)
    grad_value = grad_joined[:, 2 * width :].astype(jnp.float32)
    tilt_q = scale_factor * jnp.dot(grad_query, adapters[1].T, precision=highest)
    value_adapter_up = scale_factor * jnp.dot(grad_value, adapters[3].T, precision=highest)
    grad_normed = (
        grad_normed
        + jnp.dot(tilt_q, adapters[0], precision=highest)
        + jnp.dot(value_adapter_up, adapters[2], precision=highest)
    )
    grad_input = (
        (grad_middle + norm_one_back(grad_normed)[0])
        .astype(jnp.bfloat16)
        .reshape(docs, tokens, width)
    )
    partial_terms = jnp.stack(
        [
            dot_first(tilt_q, normed),
            scale_factor * dot_first(down_q, grad_query),
            dot_first(value_adapter_up, normed),
            scale_factor * dot_first(down_v, grad_value),
        ]
    )
    total = lax.psum(partial_terms, ("dp", "seq"))
    grad_norm = jnp.sqrt(jnp.sum(total * total))
    clipped, new_weight, new_first, new_second = adam_update(
        total, adapters, first_moment, second_moment, grad_norm
    )
    mixed = result.astype(jnp.bfloat16).reshape(docs, tokens, width)
    return (mixed, grad_input, clipped, grad_norm, new_weight, new_first, new_second)


HALF = 512
BLOCK = 256
PICK = 20
SMEM = pl.BlockSpec(memory_space=pltpu.SMEM)
VMEM = pl.BlockSpec(memory_space=pltpu.VMEM)
HBM = pl.BlockSpec(memory_space=pltpu.HBM)
FREE = pl.BlockSpec(memory_space=pl.ANY)
KEEP = pl.BlockSpec(memory_space=pltpu.VMEM)
f32 = jnp.float32
bf16 = jnp.bfloat16
SWAP = ((0, 1), (1, 0))
GELU_A = math.sqrt(2.0 / math.pi)
GELU_B = 0.044715


def nn(left, right):
    return lax.dot_general(left, right, (((1,), (0,)), ((), ())), preferred_element_type=f32)


def nt(left, right):
    return lax.dot_general(left, right, (((1,), (1,)), ((), ())), preferred_element_type=f32)


def tn(left, right):
    return lax.dot_general(left, right, (((0,), (0,)), ((), ())), preferred_element_type=f32)


def shape(*dims, dtype=bf16):
    return jax.ShapeDtypeStruct(dims, dtype)


def params(mib):
    return pltpu.CompilerParams(vmem_limit_bytes=mib * 2**20)


def call(kernel, *, out_shape, in_specs, out_specs, **options):
    spaces = {id(HBM): pltpu.HBM, id(KEEP): pltpu.VMEM}
    single = not isinstance(out_shape, tuple)
    shapes, specs = ((out_shape,), (out_specs,)) if single else (out_shape, out_specs)
    shapes = tuple(
        spaces[id(spec)](each.shape, each.dtype) if id(spec) in spaces else each
        for each, spec in zip(shapes, specs, strict=True)
    )

    def run(*values):
        values = [
            pltpu.with_memory_space_constraint(value, spaces[id(spec)]) if id(spec) in spaces else value
            for value, spec in zip(values, in_specs, strict=True)
        ]
        return pl.pallas_call(
            kernel,
            out_shape=shapes[0] if single else shapes,
            in_specs=in_specs,
            out_specs=out_specs,
            **options,
        )(*values)

    return run


def rows(index, size):
    return pl.ds(pl.multiple_of(index * size, size), size)


def parity(z, k):
    return lax.rem(z + k, 2)


class Copies:
    def __init__(self, sems):
        self.sems = sems
        self.count = 0

    def start(self, source, target):
        copy = pltpu.make_async_copy(source, target, self.sems.at[self.count])
        self.count += 1
        copy.start()
        return copy


def wait_all(copies):
    for copy in copies:
        copy.wait()


def center_scale(x):
    center = jnp.mean(x, axis=-1, keepdims=True)
    centered = x - center
    spread = jnp.mean(centered * centered, axis=-1, keepdims=True)
    inverse = lax.rsqrt(spread + norm_eps)
    return centered * inverse, inverse


def norm_back(hat, inverse, grad):
    first = jnp.mean(grad, axis=-1, keepdims=True)
    second = jnp.mean(grad * hat, axis=-1, keepdims=True)
    return inverse * (grad - first - hat * second)


def cut_kernel(w, w_o, own, send, out_part, sems):
    core = lax.axis_index("core")
    go = Copies(sems)
    copies = []
    for out, side in ((send, 1 - core), (own, core)):
        for p in range(3):
            for i in range(4):
                from_ = pl.ds(pl.multiple_of(1024 * p + 256 * i + 128 * side, 128), 128)
                copies.append(go.start(w.at[:, from_], out.at[p, :, 128 * i : 128 * (i + 1)]))
    for h in range(2):
        to = out_part.at[0, 128 * h : 128 * (h + 1)]
        copies.append(go.start(w_o.at[:, h * HALF : (h + 1) * HALF], to))
    wait_all(copies)


def call_cut(w, w_o):
    return call(
        cut_kernel,
        out_shape=(shape(3, 128, HALF), shape(3, 128, HALF), shape(1, BLOCK, HALF)),
        in_specs=[HBM, HBM],
        out_specs=(KEEP,) * 3,
        scratch_shapes=[pltpu.SemaphoreType.DMA((26,))],
        compiler_params=params(12),
        name="cut_qkv",
    )(w, w_o)


def join_kernel(own, got, out_part, shard):
    shard[:3, :128] = own[...]
    shard[:3, 128:] = got[...]
    shard[3:] = out_part[...]


def cut_feed_kernel(ids, w, own, send):
    core = ids[0]
    for i in range(4):
        send[i] = w[:, pl.ds(pl.multiple_of(1024 * i + HALF * (1 - core), HALF), HALF)]
        own[i] = w[:, pl.ds(pl.multiple_of(1024 * i + HALF * core, HALF), HALF)]


def call_cut_feed(ids, w):
    return call(
        cut_feed_kernel,
        out_shape=(shape(4, 128, HALF), shape(4, 128, HALF)),
        in_specs=[SMEM, VMEM],
        out_specs=(VMEM,) * 2,
        compiler_params=params(60),
        name="cut_feed",
    )(ids, w)


def start_sides(go, piece, target, chip, core, tag):
    return [
        (tag, go.start(piece.at[:128], target.at[rows(2 * chip + core, 128)])),
        (tag, go.start(piece.at[128:], target.at[rows(2 * chip + 1 - core, 128)])),
    ]


def attend(pair, qs, ks, vs, ctxs, stats):
    keys = ks[pair]
    values = jnp.concatenate([jnp.transpose(vs[pair]), jnp.ones((128, 1024), bf16)], axis=0)
    for i in range(4):
        ext = (i + 1) * BLOCK
        cols = slice(i * BLOCK, ext)
        query = qs[pair, cols]
        low = low_half(query)
        zero = jnp.zeros_like(query)
        parts = []
        for a in range(2):
            part = jnp.where(low, query, zero) if a == 0 else jnp.where(low, zero, query)
            scores = nt(keys[:ext], part)
            last = scores[i * BLOCK :]
            r = lax.broadcasted_iota(jnp.int32, last.shape, 0)
            c = lax.broadcasted_iota(jnp.int32, last.shape, 1)
            last = jnp.where(r <= c, last, -1e30)
            scores = jnp.concatenate([scores[: i * BLOCK], last], axis=0) if i else last
            top = jnp.max(scores, axis=0, keepdims=True)
            expo = jnp.exp(scores - top).astype(bf16)
            wide = nn(values[:, :ext], expo)
            total = wide[128:129]
            parts.append(wide[64 * a : 64 * a + 64] * (1.0 / total))
            stats[pair, a : a + 1, cols] = top + jnp.log(total)
        ctxs[pair, cols] = jnp.transpose(jnp.concatenate(parts, axis=0).astype(bf16))


def split_down(both):
    down = both[:8] + both[8:16]
    upper = down.astype(bf16).astype(f32)
    zero = jnp.zeros((104, both.shape[1]), f32)
    packed = jnp.concatenate([upper, down - upper, upper, zero], axis=0)
    return jnp.concatenate([upper, zero[:8]], axis=0).astype(bf16), jnp.transpose(packed).astype(bf16)


def fold_kernel(w, down_w, up_w, out, ws, sems):
    go = Copies(sems)
    loads = [go.start(w.at[p], ws.at[p]) for p in range(3)]
    leave = []
    for p in (1, 0, 2):
        loads[p].wait()
        if p != 1:
            for i in range(4):
                at = slice(i * BLOCK, (i + 1) * BLOCK)
                more = tn(down_w[:16, at], up_w[:16, p * HALF : (p + 1) * HALF])
                ws[p, at] = (ws[p, at].astype(f32) + more).astype(bf16)
        leave.append(go.start(ws.at[p], out.at[p]))
    wait_all(leave)


def call_fold(w, down_w, up_w):
    return call(
        fold_kernel,
        out_shape=shape(3, 1024, HALF),
        in_specs=[HBM, VMEM, VMEM],
        out_specs=HBM,
        scratch_shapes=[pltpu.VMEM((3, 1024, HALF), bf16), pltpu.SemaphoreType.DMA((6,))],
        compiler_params=params(16),
        name="fold",
    )(w, down_w, up_w)


def first_kernel(
    ids, m0, m1, others, w0, w1, w2, w3t, w3b, gain, shift, down_w, up_w, bias,
    q_out, k_out, v_out, n_out, down_out, w_out, o_out, ctx_out, stat_out, own, send,
    ns, rest, ws, os, qs, ks, vs, downs, ctxs, stats, owns, sends, sems,
):
    core, chip = ids[0], ids[2]
    go = Copies(sems)
    leave = []
    pieces = (w0, w1, w2, (w3t, w3b))
    part = lambda r, p: pieces[r].at[p] if r < 3 else pieces[r][p // 2].at[p % 2]
    for x, at in token_blocks(ids, (m0, m1), (others.at[0], others.at[1])):
        hat, _ = center_scale(x[...].astype(f32))
        value = hat * gain[0:1] + shift[0:1]
        upper = value.astype(bf16)
        ns[at] = upper
        rest[at] = (value - upper.astype(f32)).astype(bf16)
    leave.append(go.start(ns, n_out))
    for p, (to, out) in enumerate(((qs, q_out), (ks, k_out), (vs, v_out))):
        for r in range(4):
            piece = part(r, p)
            ws[p, rows(2 * (chip ^ r) + core, 128)] = piece[:128]
            ws[p, rows(2 * (chip ^ r) + 1 - core, 128)] = piece[128:]
        leave.append(go.start(ws.at[p], w_out.at[p]))
        for i in range(4):
            at = slice(i * BLOCK, (i + 1) * BLOCK)
            value = nn(ns[at], ws[p]) + bias[:, p * HALF : (p + 1) * HALF]
            if p == 0:
                both = nt(down_w[:16], ns[at]) + nt(down_w[:16], rest[at])
                down_out[:, at], downs[at] = split_down(both)
            if p != 1:
                value += nn(downs[at], up_w[:, p * HALF : (p + 1) * HALF])
            value = value.astype(bf16)
            if p == 0:
                value = value * jnp.asarray(0.125, bf16)
            for pair in range(4):
                to[pair, at] = value[:, 128 * pair : 128 * (pair + 1)]
        leave.append(go.start(to, out))

    @pl.loop(0, 4)
    def _(pair):
        attend(pair, qs, ks, vs, ctxs, stats)

    leave.append(go.start(ctxs, ctx_out))
    leave.append(go.start(stats, stat_out))
    for r in range(4):
        for h in range(2):
            os[rows(chip ^ r, 128), h * HALF : (h + 1) * HALF] = part(r, 3)[h * 128 : (h + 1) * 128]
    leave.append(go.start(os, o_out))
    for side, to, out in ((1 - core, sends, send), (core, owns, own)):
        for i in range(2):
            at = rows(2 * side + i, BLOCK)
            tok = slice(i * BLOCK, (i + 1) * BLOCK)
            whole = jnp.concatenate([ctxs[p, at] for p in range(4)], axis=1)
            to[tok] = nn(whole, os[...]).astype(to.dtype)
            leave.append(go.start(to.at[tok], out.at[tok]))
    wait_all(leave)


def call_first(ids, x_own, x_other, pieces, gain, shift, down_w, up_w, bias):
    heads = shape(4, 1024, 128)
    return call(
        first_kernel,
        out_shape=(
            heads,
            heads,
            heads,
            shape(1024, 1024),
            shape(16, 1024),
            shape(3, 1024, HALF),
            shape(HALF, 1024),
            heads,
            shape(4, 8, 1024, dtype=f32),
            shape(HALF, 1024),
            shape(HALF, 1024),
        ),
        in_specs=[SMEM] + [KEEP] * 3 + [KEEP] * 5 + [VMEM] * 5,
        out_specs=(HBM,) * 4 + (VMEM,) + (HBM,) * 6,
        scratch_shapes=[
            pltpu.VMEM((1024, 1024), bf16),
            pltpu.VMEM((1024, 1024), bf16),
            pltpu.VMEM((3, 1024, HALF), bf16),
            pltpu.VMEM((HALF, 1024), bf16),
            pltpu.VMEM((4, 1024, 128), bf16),
            pltpu.VMEM((4, 1024, 128), bf16),
            pltpu.VMEM((4, 1024, 128), bf16),
            pltpu.VMEM((1024, 128), bf16),
            pltpu.VMEM((4, 1024, 128), bf16),
            pltpu.VMEM((4, 8, 1024), f32),
            pltpu.VMEM((HALF, 1024), bf16),
            pltpu.VMEM((HALF, 1024), bf16),
            pltpu.SemaphoreType.DMA((53,)),
        ],
        compiler_params=params(44),
        name="qkv_attention",
    )(ids, *x_own, x_other, *pieces, gain, shift, down_w, up_w, bias)


def attend_back(pair, qs, ks, vs, ctxs, stats, gs, dqs, dks, dvs, acc_k, acc_v):
    keys, values = ks[pair], vs[pair]
    place = pl.ds(pl.multiple_of(pair * 128, 128), 128)
    for i in range(4):
        ext = (i + 1) * BLOCK
        cols = slice(i * BLOCK, ext)
        query, grad = qs[pair, cols], gs[pair, cols]
        low = low_half(query)
        zero = jnp.zeros_like(query)
        product = grad.astype(f32) * ctxs[pair, cols].astype(f32)
        stat = jnp.transpose(stats[pair, :, cols])
        turned_query, turned_grad = jnp.transpose(query), jnp.transpose(grad)
        new_q = []
        for a in range(2):
            pick = (lambda x, y: jnp.where(low, x, y)) if a == 0 else (lambda x, y: jnp.where(low, y, x))
            half = slice(64 * a, 64 * a + 64)
            scores = nt(pick(query, zero), keys[:ext])
            probs = jnp.exp(scores - stat[:, a : a + 1])
            last = probs[:, i * BLOCK :]
            r = lax.broadcasted_iota(jnp.int32, last.shape, 0)
            c = lax.broadcasted_iota(jnp.int32, last.shape, 1)
            last = jnp.where(r >= c, last, 0.0)
            probs = jnp.concatenate([probs[:, : i * BLOCK], last], axis=1) if i else last
            inner = jnp.sum(pick(product, 0.0), axis=1, keepdims=True)
            grad_probs = nt(pick(grad, zero), values[:ext])
            grad_scores = (probs * (grad_probs - inner)).astype(bf16)
            more_v = nn(turned_grad[half], probs.astype(bf16))
            more_k = nn(turned_query[half], grad_scores)
            if i:
                acc_v[half, : i * BLOCK] += more_v[:, : i * BLOCK]
                acc_k[half, : i * BLOCK] += more_k[:, : i * BLOCK]
            acc_v[half, cols] = more_v[:, i * BLOCK :]
            acc_k[half, cols] = more_k[:, i * BLOCK :]
            new_q.append(nn(grad_scores, keys[:ext]))
        both = jnp.where(low, new_q[0], new_q[1])
        dqs[cols, place] = (both * 0.125).astype(bf16)
    dks[:, place] = jnp.transpose(acc_k[...].astype(bf16))
    dvs[:, place] = jnp.transpose(acc_v[...].astype(bf16))


def attention_back_kernel(
    ids, q, k_in, v, ctx, stat, w_o, parts, others, g0, g1, g2, g3, mid_own, mid_other, w, n_all, downs,
    gain, down_w, up_w,
    own, send, grad_middle, total,
    os, qs, ks, vs, ctxs, stats, heads, dqs, dks, dvs, acc_k, acc_v,
    ws, ns, tilts, sems,
):
    core, z = ids[0], ids[1]
    go = Copies(sems)
    outer = go.start(w_o, os)
    then = [
        go.start(ref, to)
        for ref, to in ((q, qs), (k_in, ks), (v, vs), (ctx, ctxs), (stat, stats))
    ]
    weights = [go.start(w, ws), go.start(n_all, ns)]
    mids = (mid_own, mid_own, mid_other, mid_other)
    for at, (g, tok) in enumerate(token_blocks(ids, (g0, g1), (g2, g3))):
        here = rows(parity(z, at % 2), BLOCK)
        hat, inverse = center_scale(mids[at][1, here].astype(f32))
        grad = (parts[tok].astype(f32) + others[tok].astype(f32)) * gain[1:2]
        value = (g[...].astype(f32) + norm_back(hat, inverse, grad)).astype(bf16)
        if at < 2:
            grad_middle[here] = value
        if at == 0:
            outer.wait()
        value = nt(value, os[...]).astype(bf16)
        for pair in range(4):
            heads[pair, tok] = value[:, 128 * pair : 128 * (pair + 1)]
    wait_all(then)

    @pl.loop(0, 4)
    def _(pair):
        attend_back(pair, qs, ks, vs, ctxs, stats, heads, dqs, dks, dvs, acc_k, acc_v)

    wait_all(weights)
    for side, values in ((1 - core, send), (core, own)):
        for i in range(2):
            at = rows(2 * side + i, BLOCK)
            tok = slice(i * BLOCK, (i + 1) * BLOCK)
            gq, gk, gv = dqs[at], dks[at], dvs[at]
            value = nt(gq, ws[0]) + nt(gk, ws[1]) + nt(gv, ws[2])
            values[tok] = value.astype(bf16)
    tilts[...] = (nt(up_w[:16, :HALF], dqs[...]) + nt(up_w[:16, 2 * HALF :], dvs[...])).astype(bf16)
    down_terms = nn(tilts[...], ns[...])
    total[...] = jnp.zeros_like(total)
    total[0:4] = down_terms[0:4]
    total[8:12] = down_terms[4:8]
    up_q = 8.0 * nn(downs[...], dqs[...])
    up_v = 8.0 * nn(downs[...], dvs[...])
    for pair in range(4):
        here = pl.ds(pl.multiple_of(256 * pair + 128 * core, 128), 128)
        total[4:8, here] = up_q[0:4, 128 * pair : 128 * (pair + 1)]
        total[12:16, here] = up_v[4:8, 128 * pair : 128 * (pair + 1)]


def call_attention_back(
    ids, q, k, v, ctx, stat, w_o, part, other, g_own, g_other, mid_own, mid_other,
    w, n_all, downs, gain, down_w, up_w,
):
    pairs = pltpu.VMEM((4, 1024, 128), bf16)
    wide = pltpu.VMEM((1024, HALF), bf16)
    return call(
        attention_back_kernel,
        out_shape=(
            shape(HALF, 1024),
            shape(HALF, 1024),
            shape(HALF, 1024),
            shape(16, 1024, dtype=f32),
        ),
        in_specs=[SMEM] + [HBM] * 6 + [KEEP] * 8 + [HBM] * 2 + [VMEM] * 4,
        out_specs=(KEEP, KEEP, KEEP, KEEP),
        scratch_shapes=[
            pltpu.VMEM((HALF, 1024), bf16),
            pairs,
            pairs,
            pairs,
            pairs,
            pltpu.VMEM((4, 8, 1024), f32),
            pairs,
            wide,
            wide,
            wide,
            pltpu.VMEM((128, 1024), f32),
            pltpu.VMEM((128, 1024), f32),
            pltpu.VMEM((3, 1024, HALF), bf16),
            pltpu.VMEM((1024, 1024), bf16),
            pltpu.VMEM((16, 1024), bf16),
            pltpu.SemaphoreType.DMA((8,)),
        ],
        compiler_params=params(36),
        name="attention_back",
    )(
        ids, q, k, v, ctx, stat, w_o, part, other, *g_own, *g_other, mid_own, mid_other,
        w, n_all, downs, gain, down_w, up_w,
    )


def low_half(value):
    return lax.broadcasted_iota(jnp.int32, value.shape, 1) < 64


def start_tokens(go, pair, target, z):
    return [go.start(ref, target.at[parity(z, k)]) for k, ref in enumerate(pair)]


def middle_kernel(
    ids, own, other, x0, x1, bias, gain, shift, both, owns, others, xs, sems
):
    go = Copies(sems)
    tokens = start_tokens(go, (x0, x1), xs, ids[1])
    parts = []
    for i in range(2):
        at = slice(i * BLOCK, (i + 1) * BLOCK)
        parts.append([go.start(own.at[at], owns.at[i]), go.start(other.at[at], others.at[i])])
    wait_all(tokens)
    for i in range(2):
        at = slice(i * BLOCK, (i + 1) * BLOCK)
        wait_all(parts[i])
        value = owns[i].astype(f32) + others[i].astype(f32) + xs[i].astype(f32) + bias[2:3]
        both[1, at] = value.astype(bf16)
        hat, _ = center_scale(value)
        both[0, at] = (hat * gain[1:2] + shift[1:2]).astype(bf16)


def call_middle(ids, own, other, x_own, bias, gain, shift):
    return call(
        middle_kernel,
        out_shape=shape(2, HALF, 1024),
        in_specs=[SMEM, HBM, FREE, HBM, HBM] + [VMEM] * 3,
        out_specs=KEEP,
        scratch_shapes=[pltpu.VMEM((2, BLOCK, 1024), bf16)] * 3 + [pltpu.SemaphoreType.DMA((6,))],
        compiler_params=params(40),
        name="middle",
    )(ids, own, other, *x_own, bias, gain, shift)


def start_grads(go, ids, g_own, g_other, gs):
    core, z = ids[0], ids[1]
    return [
        go.start(ref, gs.at[2 * side + parity(z, k)])
        for side, pair in ((core, g_own), (1 - core, g_other))
        for k, ref in enumerate(pair)
    ]


def hidden_kernel(
    ids, n_own, n_other, w0, w1, w2, w3t, w3b, bias, piece, acts, slopes, ws, result, wo, sems
):
    core, chip = ids[0], ids[2]
    go = Copies(sems)
    weights = []
    for p in range(4):
        for r, ref in enumerate((w0, w1, w2, (w3t, w3b))):
            part = ref.at[p] if r < 3 else ref[p // 2].at[p % 2]
            weights += start_sides(go, part, ws.at[p], chip ^ r, core, p)
    later = go.start(piece, wo)
    tokens = [
        (ref, slice(h * BLOCK, (h + 1) * BLOCK), rows(2 * side + h, BLOCK))
        for ref, side in ((n_own, core), (n_other, 1 - core))
        for h in range(2)
    ]

    def finish(p, at, h):
        square = h * h
        lift = 0.5 + 0.5 * jnp.tanh(h * (GELU_A + (GELU_A * GELU_B) * square))
        act = h * lift
        acts[p, at] = act.astype(bf16)
        rise = 2.0 * GELU_A + (6.0 * GELU_A * GELU_B) * square
        slopes[p, at] = (lift + (act - act * lift) * rise).astype(bf16)

    before = None
    for p in range(4):
        wait_all([copy for at, copy in weights if at == p])
        shift = bias[pl.ds(2 * p + core, 1)]
        for ref, here, at in tokens:
            h = nn(ref[0, here], ws[p]) + shift
            if before is not None:
                finish(*before)
            before = (p, at, h)
    finish(*before)
    later.wait()
    for i in range(4):
        tok = slice(i * BLOCK, (i + 1) * BLOCK)
        result[tok] = nn(acts[chip, tok], wo[...])


def call_hidden(ids, n_own, n_other, pieces, bias, piece):
    return call(
        hidden_kernel,
        out_shape=(shape(4, 1024, HALF),) * 3 + (shape(1024, 1024, dtype=f32),),
        in_specs=[SMEM] + [KEEP] * 2 + [HBM] * 5 + [VMEM, HBM],
        out_specs=(KEEP,) * 4,
        scratch_shapes=[
            pltpu.VMEM((HALF, 1024), bf16),
            pltpu.SemaphoreType.DMA((33,)),
        ],
        compiler_params=params(26),
        name="hidden",
    )(ids, n_own, n_other, *pieces, bias, piece)


def token_blocks(ids, g_own, g_other):
    core, z = ids[0], ids[1]
    return [
        (ref, rows(2 * side + parity(z, k), BLOCK))
        for side, pair in ((core, g_own), (1 - core, g_other))
        for k, ref in enumerate(pair)
    ]


def feed_kernel(
    ids, g0, g1, g2, g3, acts, slopes, w_ins, own_piece, x_piece, y_piece, old,
    result, grad, own_rows, sems,
):
    chip = ids[2]
    load = Copies(sems).start(own_piece, own_rows)
    for i, (g, tok) in enumerate(token_blocks(ids, (g0, g1), (g2, g3))):
        out_sum, grad_sum = old[tok], None
        for r, piece in ((1, x_piece), (2, y_piece), (0, own_rows)):
            here = chip ^ r
            if i == 0 and r == 0:
                load.wait()
            back = nt(g[...], piece[...])
            if r:
                out_sum += nn(acts[here, tok], piece[...])
            back = (back * slopes[here, tok].astype(f32)).astype(bf16)
            term = nt(back, w_ins[here])
            grad_sum = term if grad_sum is None else grad_sum + term
        result[tok] = out_sum
        grad[tok] = grad_sum


def call_feed(ids, g_own, g_other, active, slope, w_in, pieces, old):
    return call(
        feed_kernel,
        out_shape=(shape(1024, 1024, dtype=f32),) * 2,
        in_specs=[SMEM] + [KEEP] * 7 + [HBM] + [KEEP] * 3,
        out_specs=(KEEP, KEEP),
        scratch_shapes=[pltpu.VMEM((HALF, 1024), bf16), pltpu.SemaphoreType.DMA((1,))],
        compiler_params=params(18),
        name="feed",
    )(ids, *g_own, *g_other, active, slope, w_in, *pieces, old)


def far_grad_kernel(ids, g0, g1, g2, g3, slopes, w_ins, top, low, old, out):
    far = ids[2] ^ 3
    for g, tok in token_blocks(ids, (g0, g1), (g2, g3)):
        back = jnp.concatenate([nt(g[...], top[...]), nt(g[...], low[...])], axis=1)
        back = back * slopes[far, tok].astype(f32)
        more = nt(back.astype(bf16), w_ins[far])
        out[tok] = (more + old[tok]).astype(bf16)


def call_far_grad(ids, g_own, g_other, slope, w_in, far, old):
    return call(
        far_grad_kernel,
        out_shape=shape(1024, 1024),
        in_specs=[SMEM] + [KEEP] * 9,
        out_specs=KEEP,
        compiler_params=params(18),
        name="far_grad",
    )(ids, *g_own, *g_other, slope, w_in, *far, old)


def far_result_kernel(ids, acts, top, low, old, own, send):
    core, far = ids[0], ids[2] ^ 3
    for side, values in ((1 - core, send), (core, own)):
        for i in range(2):
            at = rows(2 * side + i, BLOCK)
            tok = slice(i * BLOCK, (i + 1) * BLOCK)
            more = nn(acts[far, at, :BLOCK], top[...]) + nn(acts[far, at, BLOCK:], low[...])
            values[tok] = (old[at] + more).astype(values.dtype)


def call_far_result(ids, active, far, old):
    return call(
        far_result_kernel,
        out_shape=(shape(HALF, 1024, dtype=f32), shape(HALF, 1024)),
        in_specs=[SMEM] + [KEEP] * 4,
        out_specs=(KEEP, KEEP),
        compiler_params=params(16),
        name="far_result",
    )(ids, active, *far, old)


def mixed_kernel(ids, own, other, middle, bias, out0, out1):
    z = ids[1]
    for k, out in enumerate((out0, out1)):
        tok = rows(parity(z, k), BLOCK)
        value = own[tok] + other[tok].astype(f32) + middle[1, tok].astype(f32)
        out[...] = (value + bias[3:4]).astype(bf16)


def call_mixed(ids, own, other, middle, bias):
    return call(
        mixed_kernel,
        out_shape=(shape(BLOCK, 1024),) * 2,
        in_specs=[SMEM, KEEP, KEEP, KEEP, VMEM],
        out_specs=(KEEP, KEEP),
        compiler_params=params(12),
        name="mixed",
    )(ids, own, other, middle, bias)


def input_grad_kernel(ids, x0, x1, own, other, grad_middle, gain, out0, out1):
    z = ids[1]
    for k, (x, out) in enumerate(((x0, out0), (x1, out1))):
        for h in range(2):
            tok = rows(2 * parity(z, k) + h, 128)
            here = slice(128 * h, 128 * (h + 1))
            grad = (own[tok].astype(f32) + other[tok].astype(f32)) * gain[0:1]
            hat, inverse = center_scale(x[here].astype(f32))
            out[here] = (grad_middle[tok].astype(f32) + norm_back(hat, inverse, grad)).astype(bf16)


def call_input_grad(ids, x_own, own, other, grad_middle, gain):
    return call(
        input_grad_kernel,
        out_shape=(shape(BLOCK, 1024),) * 2,
        in_specs=[SMEM, KEEP, KEEP, KEEP, KEEP, KEEP, VMEM],
        out_specs=(KEEP, KEEP),
        compiler_params=params(16),
        name="input_grad",
    )(ids, *x_own, own, other, grad_middle, gain)


def to_core(value):
    return lax.ppermute(value, "core", SWAP)


def total_over(value, axis, *others):
    flip = [lax.ppermute(value, axis, [(i, i ^ by) for i in range(4)]) for by in (1, 2, 3)]
    flip = after(flip, *others)
    return (value + flip[0]) + (flip[1] + flip[2])


def exchange(z, pair):
    sent = []
    for k in range(2):
        perm = [
            (4 * core + at, 4 * (at // 2) + 2 * core + (at + k) % 2)
            for core in range(2)
            for at in range(4)
        ]
        sent.append(lax.ppermute(pair[k], ("core", "seq"), perm))
    return sent


def pick_kernel(ids, value, out0, out1, sems):
    z = ids[1]
    go = Copies(sems)
    wait_all([go.start(value.at[parity(z, k)], out) for k, out in enumerate((out0, out1))])


def call_pick(ids, value):
    return call(
        pick_kernel,
        out_shape=(shape(BLOCK, 1024),) * 2,
        in_specs=[SMEM, HBM],
        out_specs=(KEEP, KEEP),
        scratch_shapes=[pltpu.SemaphoreType.DMA((2,))],
        compiler_params=params(PICK),
        name="pick",
    )(ids, value)


def place_kernel(ids, first, second, out, sems):
    z = ids[1]
    go = Copies(sems)
    wait_all([go.start(ref, out.at[parity(z, k)]) for k, ref in enumerate((first, second))])


def call_place(ids, pair):
    return call(
        place_kernel,
        out_shape=shape(2, BLOCK, 1024),
        in_specs=[SMEM, KEEP, KEEP],
        out_specs=HBM,
        scratch_shapes=[pltpu.SemaphoreType.DMA((2,))],
        compiler_params=params(PICK),
        name="place",
    )(ids, *pair)


def after(value, *others):
    return lax.optimization_barrier((value, *others))[0]


def gather_near(shard):
    return [shard, lax.ppermute(shard, "x", SWAP), lax.ppermute(shard, "y", SWAP)]


def halves(near, first=False):
    if near[1].shape[0] == 4 and not first:
        return call_halves(near[1], near[2])
    half = near[1].shape[0] // 2
    return call(
        split_kernel,
        out_shape=(shape(half, *near[1].shape[1:]),) * 2,
        in_specs=[KEEP, KEEP],
        out_specs=(KEEP, KEEP),
        compiler_params=params(8),
        name="split",
    )(near[1], near[2])


def split_kernel(by_x, by_y, first, second):
    half = first.shape[0]
    first[...] = by_x[:half]
    second[...] = by_y[half:]


def halves_kernel(by_x, by_y, first, second, held, sems):
    half = first.shape[0]
    go = Copies(sems)
    loads = [go.start(by_x.at[:half], held.at[0]), go.start(by_y.at[half:], held.at[1])]
    leave = []
    for at, out in enumerate((first, second)):
        loads[at].wait()
        leave.append(go.start(held.at[at], out))
    wait_all(leave)


def call_halves(by_x, by_y):
    dims = (by_x.shape[0] // 2, *by_x.shape[1:])
    return call(
        halves_kernel,
        out_shape=(shape(*dims), shape(*dims)),
        in_specs=[FREE, FREE],
        out_specs=(HBM, HBM),
        scratch_shapes=[pltpu.VMEM((2, *dims), bf16), pltpu.SemaphoreType.DMA((4,))],
        compiler_params=params(8),
        name="halves",
    )(by_x, by_y)


def gather_far(near, parts):
    return near + [lax.ppermute(parts[0], "y", SWAP), lax.ppermute(parts[1], "x", SWAP)]


def parts_of(value):
    upper = lax.reduce_precision(value, 8, 7)
    return upper.astype(bf16), (value - upper).astype(bf16)


def on_chip(
    inputs,
    out_grad,
    norm_gain,
    norm_bias,
    proj_bias,
    fc_bias,
    qkv_weight,
    out_weight,
    feed_input_weight,
    proj_weight,
    adapters,
    first_moment,
    second_moment,
):
    width = inputs.shape[2]
    core = lax.axis_index("core")
    z = lax.axis_index("seq")
    chip = 2 * lax.axis_index("y") + lax.axis_index("x")
    ids = jnp.stack([core, z, chip]).astype(jnp.int32)

    qkv_own, qkv_send, out_part = call_cut(qkv_weight, out_weight)
    qkv_got = to_core(qkv_send)
    first_shard = call(
        join_kernel,
        out_shape=shape(4, BLOCK, HALF),
        in_specs=[KEEP] * 3,
        out_specs=KEEP,
        compiler_params=params(12),
        name="join",
    )(qkv_own, qkv_got, out_part)
    first_near = gather_near(first_shard)
    x_own = exchange(z, call_pick(ids, after(inputs, first_shard)))
    in_own, in_send = call_cut_feed(ids, after(feed_input_weight, first_shard))
    in_shard = jnp.concatenate([in_own, to_core(in_send)], axis=1)

    def columns(value):
        lead = value.shape[0]
        value = value.reshape(lead, 4, 2, 128)
        return jnp.where(core == 0, value[:, :, 0], value[:, :, 1]).reshape(lead, HALF)

    scale = adapter_alpha / ADAPTER_RANK
    adapters, proj_bias = after((adapters, proj_bias), first_shard)
    up_q, up_v = scale * columns(adapters[1]), scale * columns(adapters[3])
    up = jnp.zeros((8, 1536), f32).at[0:4, :HALF].set(up_q).at[4:8, 2 * HALF :].set(up_v)
    upper, lower = parts_of(up)
    up_w = jnp.concatenate([upper, upper, lower, jnp.zeros((104, 1536), bf16)], axis=0)
    upper, lower = parts_of(jnp.concatenate([adapters[0], adapters[2]], axis=0))
    down_w = jnp.concatenate([upper, lower, jnp.zeros((112, 1024), bf16)], axis=0)
    head_bias = columns(proj_bias[:2])
    qkv_bias = jnp.concatenate([head_bias[0], jnp.zeros((HALF,), f32), head_bias[1]])[None]

    first_near = after(first_near, up_w, down_w, qkv_bias, in_shard)
    first_halves = halves(first_near, True)
    first_pieces = gather_far(first_near, first_halves)
    x_own = after(x_own, *first_halves)
    x_other = to_core(jnp.stack(x_own))
    in_near = gather_near(after(in_shard, *first_pieces[3:]))
    q, k, v, n_all, down, w_qkv, w_o, ctx, stat, attn_own, attn_send = call_first(
        ids, x_own, x_other, first_pieces, norm_gain, norm_bias, down_w, up_w, qkv_bias
    )
    in_near = after(in_near, ctx)
    in_halves = halves(in_near)
    in_pieces = gather_far(in_near, in_halves)
    attn_other = to_core(after(attn_send, *in_halves))
    n2_own = call_middle(
        ids, attn_own, after(attn_other, *in_halves), x_own, proj_bias, norm_gain, norm_bias
    )
    g_pair = call_pick(ids, after(out_grad, n2_own))
    w_qkv = call_fold(after(w_qkv, *g_pair), down_w, up_w)
    in_pieces[3:] = after(in_pieces[3:], w_qkv)
    g_own = exchange(z, g_pair)
    proj_near = gather_near(after(proj_weight, *in_pieces[3:]))
    n2_other = to_core(after(n2_own, *in_pieces[3:]))
    active, slope, w_in, old = call_hidden(
        ids, n2_own, n2_other, in_pieces, fc_bias.reshape(8, HALF), proj_near[0]
    )
    proj_near = after(proj_near, old)
    proj_halves = halves(proj_near)
    far = gather_far(proj_near, proj_halves)[3:]
    near = after(proj_near, *proj_halves)
    g_own = after(g_own, *proj_halves)
    g_other = [to_core(part) for part in g_own]
    result, grad = call_feed(ids, g_own, g_other, active, slope, w_in, near, old)
    result_own, result_send = call_far_result(ids, active, far, result)
    result_other = to_core(result_send)
    part = call_far_grad(ids, g_own, g_other, slope, w_in, after(far, result_own), grad)
    part = after(part, result_other)
    part_other = to_core(part)
    mixed = call_mixed(ids, result_own, after(result_other, part), n2_own, proj_bias)
    part_other = after(part_other, *mixed)
    mixed = exchange(z, mixed)
    own, send, grad_middle, total = call_attention_back(
        ids, q, k, v, ctx, stat, w_o, part, part_other, g_own, g_other, n2_own, n2_other,
        w_qkv, n_all, down, norm_gain, down_w, up_w,
    )
    other = to_core(after(send, *mixed))
    grad_in = call_input_grad(ids, x_own, own, other, grad_middle, norm_gain)
    total = total_over(total, "seq", *grad_in)
    grad_in = exchange(z, grad_in)
    total = total + to_core(total)
    total = total_over(total, ("y", "x"))
    mixed = call_place(ids, after(mixed, total))
    total = after(total, grad_in[0]).reshape(4, ADAPTER_RANK, width)
    grad_norm = jnp.sqrt(jnp.sum(total * total))
    clipped, new_weight, new_first, new_second = adam_update(
        total, adapters, first_moment, second_moment, grad_norm
    )
    grad_input = call_place(ids, after(grad_in, mixed, new_weight))
    return (mixed, grad_input, clipped, grad_norm, new_weight, new_first, new_second)


def solution(mesh):
    sizes = dict(mesh.shape)
    if sizes["dp"] == 8 and sizes["seq"] == 4:
        plane = Mesh(mesh.devices.reshape(2, 2, 2, 4), ("y", "x", "core", "seq"))
        return build(plane, ("y", "x", "core"), on_chip)
    return build(mesh, "dp", on_device)


def build(mesh, dp, step):
    tokens, weight = P(dp, "seq", None), P(dp, None)
    return jax.shard_map(
        step,
        mesh=mesh,
        in_specs=(tokens, tokens) + (P(),) * 4 + (weight,) * 4 + (P(),) * 3,
        out_specs=(tokens, tokens) + (P(),) * 5,
        check_vma=False,
    )
```
